32 devices in a mesh: groups: 2 (over y), hash: 16 (over z, x, core).
Axes of the slice: x: 2, y: 2, z: 4, core: 2. Of those that a mesh axis runs over, the one named last changes fastest.
Arguments:
- passages: bfloat16 [16384, 4096], P(('groups', 'hash')), parts along dimension 0, may hold values from -100 to 100
- queries: bfloat16 [32, 4096], P(('groups', 'hash')), parts along dimension 0, may hold values from -100 to 100
- gain: float32 [4096], replicated, may hold values from 0.5 to 1.5
- candidates: int32 [32, 128], P(('groups', 'hash')), parts along dimension 0, may hold values from 0 to 8191, as said below
- teacher: int32 [32, 128], P(('groups', 'hash')), parts along dimension 0, may hold values from 0 to 40
Outputs:
- d_passages: float32 [16384, 4096], P(('groups', 'hash')), parts along dimension 0
- d_queries: float32 [32, 4096], P(('groups', 'hash')), parts along dimension 0
- d_gain: float32 [8192], P('groups'), parts along dimension 0
The draws below stay inside these ranges and needn't reach their ends.
There are 2 independent parts, one for each index of `groups`. The reference program is written for one: setup_inputs(seed, part) draws one part's arguments, and reference() takes and returns one part's arrays. A program takes and returns all parts, laid end to end along the dimension named above; an argument that names none is the same for every part. Nothing has to cross between parts.
Inputs may be any that keep to these rules, and one draw needn't show every extreme that they name: `candidates`: each query's 128 candidate ids are distinct, and exactly 8 of them lie in each hash index's block of 512 consecutive ids (owner = id // 512).
All inputs are finite; a program needn't handle non-finite values.
Results may differ from the reference program's by a relative error of at most 0.0095.
Values may be sent and summed in bfloat16 or wider, within the bound.
No kernel may reach another device: no remote copies, remote signals or barrier semaphores. Data moves between devices by JAX's collectives and lax.ppermute only.
A program may use at most 64 MiB of HBM per device.

```python
import math
import jax
import jax.numpy as jnp
from jax import lax

D = 4096
C = 128
P_DEV = 512
PASSAGES = 8192
QUERIES = 16
N_HASH = 16


def draw_passages(key, part):
    key = jax.random.fold_in(key, 5)
    first = jax.random.fold_in(key, 0)
    second = jax.random.fold_in(key, 1)
    fourth = jax.random.fold_in(key, 3)
    row_scale = jnp.exp(jax.random.uniform(second, (PASSAGES, 1), jnp.float32, 0.0, math.log(10.0)))
    col_scale = jnp.exp(jax.random.uniform(fourth, (1, D), jnp.float32, 0.0, math.log(10.0)))
    base = jnp.clip(jax.random.normal(first, (PASSAGES, D), jnp.float32), -5.0, 5.0)
    values = base * row_scale * jnp.sqrt(col_scale) / 1.6
    return values.astype(jnp.bfloat16)


def draw_queries(key, part):
    key = jax.random.fold_in(key, 7)
    first = jax.random.fold_in(key, 0)
    second = jax.random.fold_in(key, 1)
    fourth = jax.random.fold_in(key, 3)
    row_scale = jnp.exp(jax.random.uniform(second, (QUERIES, 1), jnp.float32, 0.0, math.log(10.0)))
    col_scale = jnp.exp(jax.random.uniform(fourth, (1, D), jnp.float32, 0.0, math.log(10.0)))
    base = jnp.clip(jax.random.normal(first, (QUERIES, D), jnp.float32), -5.0, 5.0)
    values = base * row_scale * jnp.sqrt(col_scale) / 1.6
    return values.astype(jnp.bfloat16)


def draw_candidates(key, part):
    key = jax.random.fold_in(key, 11)
    first, second, third, fourth, fifth = jax.random.split(key, 5)
    shifts = jax.random.randint(first, (QUERIES, 1), 0, N_HASH)
    picks_one = jax.random.randint(second, (QUERIES, N_HASH), 0, P_DEV)
    picks_two = jax.random.randint(third, (QUERIES, N_HASH), 0, P_DEV)
    picks_three = jax.random.randint(fourth, (QUERIES, N_HASH), 0, P_DEV)
    bases = jnp.minimum(jnp.minimum(picks_one, picks_two), picks_three)
    slots = jnp.arange(C, dtype=jnp.int32)
    owner = (slots[None, :] % N_HASH + shifts) % N_HASH
    within = slots[None, :] // N_HASH
    start_rows = jnp.take_along_axis(bases, owner, axis=1)
    rows = (start_rows + within) % P_DEV
    ids = (owner * P_DEV + rows).astype(jnp.int32)
    row_keys = jax.random.split(fifth, QUERIES)
    shuffled = jax.vmap(lambda k, r: jax.random.permutation(k, r))(row_keys, ids)
    return shuffled.astype(jnp.int32)


def touch_ends(array, stream_key, smallest, top_value):
    dims = array.shape
    index_at = [jax.random.randint(jax.random.fold_in(stream_key, axis), (), 0, dims[axis]) for axis in range(len(dims))]
    array = array.at[tuple(index_at)].set(smallest)
    longest = dims.index(max(dims))
    index_at[longest] = (index_at[longest] + 1) % dims[longest]
    return array.at[tuple(index_at)].set(top_value)


def setup_inputs(seed: int = 0, part: int = 0) -> dict:
    keys = jax.random.split(jax.random.key(seed), 6)
    part_splits = jax.random.split(jax.random.fold_in(keys[5], part), 6)
    passages = draw_passages(jax.random.fold_in(jax.random.fold_in(keys[5], part), 71), part)
    queries = draw_queries(jax.random.fold_in(jax.random.fold_in(keys[5], part), 71), part)
    gain = jnp.clip(1.0 + 0.1 * jax.random.normal(keys[2], (D,), jnp.float32), 0.5, 1.5)
    candidates = draw_candidates(jax.random.fold_in(jax.random.fold_in(keys[5], part), 71), part)
    teacher = touch_ends(jax.random.randint(part_splits[4], (QUERIES, C), 0, 41), jax.random.fold_in(part_splits[4], 1), 0, 40).astype(jnp.int32)
    return {"passages": passages, "queries": queries, "gain": gain, "candidates": candidates, "teacher": teacher}


score_scale = 20.0
loss_scale = 8192.0
teacher_div = 2.0

def reference(passages, queries, gain, candidates, teacher):
    gain_f = gain.astype(jnp.float32)
    passage_f = passages.astype(jnp.float32)
    lifted = passage_f * gain_f[None, :]
    p_norm = jnp.sqrt(lax.optimization_barrier(jnp.sum(lifted * lifted, axis=-1, keepdims=True)))
    p_unit = lifted / p_norm
    table = p_unit.astype(jnp.bfloat16)
    query_f = queries.astype(jnp.float32)
    q_norm = jnp.sqrt(lax.optimization_barrier(jnp.sum(query_f * query_f, axis=-1, keepdims=True)))
    q_unit = query_f / q_norm
    q_send = q_unit.astype(jnp.bfloat16)
    block = math.gcd(QUERIES, 64)
    steps_count = QUERIES // block

    def one_block(d_table, index):
        start = (index * block).astype(jnp.int32)
        ids = lax.dynamic_slice_in_dim(candidates, start, block, 0)
        marks = lax.dynamic_slice_in_dim(teacher, start, block, 0)
        q_block = lax.dynamic_slice_in_dim(q_send, start, block, 0).astype(jnp.float32)
        unit_block = lax.dynamic_slice_in_dim(q_unit, start, block, 0)
        norm_block = lax.dynamic_slice_in_dim(q_norm, start, block, 0)
        rows = table[ids].astype(jnp.float32)
        scores = jnp.einsum('bcd,bd->bc', rows, q_block) * score_scale
        weights = jnp.exp(scores)
        student = weights / lax.optimization_barrier(jnp.sum(weights, axis=-1, keepdims=True))
        t_weights = jnp.exp(marks.astype(jnp.float32) / teacher_div)
        teach = t_weights / lax.optimization_barrier(jnp.sum(t_weights, axis=-1, keepdims=True))
        coef = loss_scale * score_scale * (student - teach)
        d_unit = jnp.einsum('bc,bcd->bd', coef, rows)
        d_query = (d_unit - unit_block * lax.optimization_barrier(jnp.sum(unit_block * d_unit, axis=-1, keepdims=True))) / norm_block
        terms = coef[:, :, None] * q_block[:, None, :]
        d_table = d_table.at[ids.reshape(-1)].add(terms.reshape(-1, D))
        return (d_table, d_query)
    zeros = jnp.zeros((PASSAGES, D), jnp.float32)
    d_table, d_blocks = lax.scan(one_block, zeros, jnp.arange(steps_count, dtype=jnp.int32))
    d_queries = d_blocks.reshape(QUERIES, D)
    d_lifted = (d_table - p_unit * lax.optimization_barrier(jnp.sum(p_unit * d_table, axis=-1, keepdims=True))) / p_norm
    d_passages = d_lifted * gain_f[None, :]
    d_gain = lax.optimization_barrier(jnp.sum(d_lifted * passage_f, axis=0))
    return (d_passages, d_queries, d_gain)
```

```python
import functools

import jax
import jax.numpy as jnp
from jax import lax
from jax.experimental import pallas as pl
from jax.experimental.pallas import tpu as pltpu
from jax.sharding import PartitionSpec as P

score_scale = 20.0
loss_scale = 8192.0
teacher_div = 2.0
coef_scale = loss_scale * score_scale
f32 = jnp.float32
bf16 = jnp.bfloat16
vmem = pltpu.VMEM
nt_dims = (((1,), (1,)), ((), ()))
nn_dims = (((1,), (0,)), ((), ()))


def dot(a, b, dims):
    return lax.dot_general(a, b, dims, preferred_element_type=f32)


def split(x):
    high = x.astype(bf16)
    low = (x - high.astype(f32)).astype(bf16)
    return high, low


def params(megabytes):
    return pltpu.CompilerParams(vmem_limit_bytes=megabytes * 1024 * 1024)


def whole():
    return pl.BlockSpec(memory_space=vmem)


def pack_kernel(queries_ref, candidates_ref, teacher_ref, out_ref):
    half = queries_ref.shape[1] // 2
    query = queries_ref[...].astype(f32)
    ids = candidates_ref[...]
    first = jnp.concatenate(
        [query[:, :half], (ids >> 8).astype(f32), (ids & 255).astype(f32)], axis=1
    )
    second = jnp.concatenate(
        [query[:, half:], teacher_ref[...].astype(f32), jnp.zeros(ids.shape, f32)], axis=1
    )
    both = jnp.concatenate([first, second], axis=0).astype(bf16)
    out_ref[...] = jnp.broadcast_to(both[None], out_ref.shape)


def table_kernel(passages_ref, gain_ref, table_ref, square_ref, inverse_ref):
    lifted = passages_ref[...].astype(f32) * gain_ref[...]
    norm = jnp.sqrt(jnp.sum(lifted * lifted, axis=1, keepdims=True))
    inverse = 1.0 / norm
    unit = lifted * inverse
    table_ref[...] = unit.astype(bf16)
    square_ref[...] = (unit * unit).astype(bf16)
    rows = unit.shape[0]
    inverse_ref[...] = jnp.transpose(jnp.broadcast_to(inverse, (rows, 128)))[:1, :]


def score_kernel(got_ref, start_ref, table_ref, cos_ref, weight_ref, teach_ref, sums_ref, unit_ref):
    queries = got_ref.shape[0]
    half = got_ref.shape[2] - 256
    listed = 128
    rows = table_ref.shape[0]
    got = got_ref[...].astype(f32)
    query = jnp.concatenate([got[:, 0, :half], got[:, 1, :half]], axis=1)
    norm = jnp.sqrt(jnp.sum(query * query, axis=1, keepdims=True))
    unit = (query / norm).astype(bf16)
    unit_ref[...] = unit
    ids = (got[:, 0, half : half + listed] * 256.0 + got[:, 0, half + listed :]).astype(jnp.int32)
    marks = jnp.exp(got[:, 1, half : half + listed] * (1.0 / teacher_div))
    marks = marks / jnp.sum(marks, axis=1, keepdims=True)
    here = ids - start_ref[0]
    places = lax.broadcasted_iota(jnp.int32, (queries, rows), 1)
    teach = jnp.zeros((queries, rows), f32)
    for c in range(listed):
        teach = teach + jnp.where(here[:, c : c + 1] == places, marks[:, c : c + 1], 0.0)
    teach_ref[...] = teach
    cos = dot(unit, table_ref[...], nt_dims)
    cos_ref[...] = cos
    weight = jnp.where(teach > 0.0, jnp.exp(cos * score_scale), 0.0)
    weight_ref[...] = weight
    total = jnp.sum(weight, axis=1, keepdims=True)
    flipped = jnp.transpose(jnp.broadcast_to(total, (queries, 128)))[:1, :queries]
    sums_ref[...] = jnp.broadcast_to(flipped[None], sums_ref.shape)


def mix_kernel(unit_ref, cos_ref, weight_ref, teach_ref, table_ref, square_ref, by_weight_ref, by_teach_ref, gain_weight_ref, gain_teach_ref):
    queries = unit_ref.shape[0]
    weight, teach, cos = weight_ref[...], teach_ref[...], cos_ref[...]
    stacked = jnp.concatenate([*split(weight), *split(teach)], axis=0)
    mixed = dot(stacked, table_ref[...], nn_dims)
    by_weight = mixed[:queries] + mixed[queries : 2 * queries]
    by_teach = mixed[2 * queries : 3 * queries] + mixed[3 * queries :]
    stacked = jnp.concatenate([*split(weight * cos), *split(teach * cos)], axis=0)
    along = dot(stacked, square_ref[...], nn_dims)
    unit = unit_ref[...].astype(f32)
    by_weight_ref[...] = by_weight
    by_teach_ref[...] = by_teach
    gain_weight_ref[...] = unit * by_weight - (along[:queries] + along[queries : 2 * queries])
    terms = unit * by_teach - (along[2 * queries : 3 * queries] + along[3 * queries :])
    gain_teach_ref[...] = jnp.sum(terms, axis=0, keepdims=True)


def partial_kernel(sums_ref, by_weight_ref, by_teach_ref, gain_weight_ref, gain_teach_ref, out_ref, inverse_ref):
    queries = by_weight_ref.shape[0]
    total = jnp.sum(sums_ref[...][:, 0, :], axis=0, keepdims=True)
    inverse = jnp.transpose(jnp.broadcast_to(1.0 / total, (128, queries)))[:, :1]
    inverse_ref[...] = inverse
    partial = coef_scale * (by_weight_ref[...] * inverse - by_teach_ref[...])
    gain_part = jnp.sum(gain_weight_ref[...] * inverse, axis=0, keepdims=True) - gain_teach_ref[...]
    gain_part = coef_scale * gain_part
    out_ref[...] = jnp.concatenate(
        [partial[:, None, :], jnp.broadcast_to(gain_part[None], (queries, 1, partial.shape[1]))], axis=1
    ).astype(bf16)


def passage_kernel(unit_ref, gain_ref, cos_ref, weight_ref, teach_ref, inverse_ref, norm_ref, table_ref, out_ref):
    coef = coef_scale * (weight_ref[...] * inverse_ref[...] - teach_ref[...])
    scaled = coef * norm_ref[...]
    along = jnp.sum(scaled * cos_ref[...], axis=0, keepdims=True)
    queries, rows = coef.shape
    column = jnp.transpose(jnp.broadcast_to(along, (128, rows)))[:, :1]
    high, low = split(jnp.transpose(scaled))
    unit = unit_ref[...]
    whole_part = dot(
        jnp.concatenate([high, low], axis=1), jnp.concatenate([unit, unit], axis=0), nn_dims
    )
    out_ref[...] = (whole_part - table_ref[...].astype(f32) * column) * gain_ref[...]


def final_kernel(got_ref, queries_ref, gain_ref, d_queries_ref, d_gain_ref):
    got = jnp.sum(got_ref[...].astype(f32), axis=0)
    query = queries_ref[...].astype(f32)
    norm = jnp.sqrt(jnp.sum(query * query, axis=1, keepdims=True))
    unit = query / norm
    d_unit = got[:1]
    d_queries_ref[...] = (d_unit - unit * jnp.sum(unit * d_unit, axis=1, keepdims=True)) / norm
    d_gain_ref[...] = got[1:] / gain_ref[...]


def shape(dims, dtype=f32):
    return jax.ShapeDtypeStruct(dims, dtype)


def exchange(x):
    return lax.all_to_all(x, "hash", split_axis=0, concat_axis=0, tiled=True)


def local(passages, queries, gain, candidates, teacher):
    count = lax.axis_size("hash")
    rows, width = passages.shape
    listed = candidates.shape[1]
    gain = gain.reshape(1, width)

    packed = pl.pallas_call(
        pack_kernel,
        out_shape=shape((count, 2, width // 2 + 2 * listed), bf16),
        name="pack",
    )(queries, candidates, teacher)
    got = exchange(packed)

    block = 128
    row_block = pl.BlockSpec((block, width), lambda i: (i, 0))
    table, square, norms = pl.pallas_call(
        table_kernel,
        grid=(rows // block,),
        in_specs=[row_block, pl.BlockSpec((1, width), lambda i: (0, 0))],
        out_specs=[row_block, row_block, pl.BlockSpec((1, block), lambda i: (0, i))],
        out_shape=[shape((rows, width), bf16), shape((rows, width), bf16), shape((1, rows))],
        compiler_params=params(48),
        name="table",
        cost_estimate=pl.CostEstimate(
            flops=6 * rows * width, bytes_accessed=6 * rows * width, transcendentals=0
        ),
    )(passages, gain)

    start = (lax.axis_index("hash") * rows).astype(jnp.int32).reshape(1)
    small = shape((count, rows))
    cos, weight, teach, sums, unit = pl.pallas_call(
        score_kernel,
        in_specs=[whole(), pl.BlockSpec(memory_space=pltpu.SMEM), whole()],
        out_shape=[small, small, small, shape((count, 1, count)), shape((count, width), bf16)],
        compiler_params=params(48),
        name="score",
    )(got, start, table)
    got_sums = exchange(sums)

    wide = shape((count, width))
    by_weight, by_teach, gain_weight, gain_teach = pl.pallas_call(
        mix_kernel,
        out_shape=[wide, wide, wide, shape((1, width))],
        compiler_params=params(48),
        name="mix",
        cost_estimate=pl.CostEstimate(
            flops=16 * count * rows * width, bytes_accessed=4 * rows * width, transcendentals=0
        ),
    )(unit, cos, weight, teach, table, square)

    partial, inverse = pl.pallas_call(
        partial_kernel,
        out_shape=[shape((count, 2, width), bf16), shape((count, 1))],
        compiler_params=params(48),
        name="partial",
    )(got_sums, by_weight, by_teach, gain_weight, gain_teach)
    got_partial = exchange(partial)

    fixed = lambda dims: pl.BlockSpec(dims, lambda i: (0, 0))
    cols = pl.BlockSpec((count, block), lambda i: (0, i))
    d_passages = pl.pallas_call(
        passage_kernel,
        grid=(rows // block,),
        in_specs=[
            fixed((count, width)),
            fixed((1, width)),
            cols,
            cols,
            cols,
            fixed((count, 1)),
            pl.BlockSpec((1, block), lambda i: (0, i)),
            row_block,
        ],
        out_specs=row_block,
        out_shape=shape((rows, width)),
        compiler_params=params(48),
        name="d_passages",
        cost_estimate=pl.CostEstimate(
            flops=4 * count * rows * width, bytes_accessed=6 * rows * width, transcendentals=0
        ),
    )(unit, gain, cos, weight, teach, inverse, norms, table)

    d_queries, d_gain = pl.pallas_call(
        final_kernel,
        out_shape=[shape((1, width)), shape((1, width))],
        compiler_params=params(48),
        name="final",
    )(got_partial, queries, gain)
    return (d_passages, d_queries, d_gain.reshape(width))


def solution(mesh):
    in_specs = (
        P(("groups", "hash"), None),
        P(("groups", "hash"), None),
        P(),
        P(("groups", "hash"), None),
        P(("groups", "hash"), None),
    )
    out_specs = (P(("groups", "hash"), None), P(("groups", "hash"), None), P("groups"))
    return jax.shard_map(local, mesh=mesh, in_specs=in_specs, out_specs=out_specs, check_vma=False)
```

```python
import functools

import jax
import jax.numpy as jnp
from jax import lax
from jax.experimental import pallas as pl
from jax.experimental.pallas import tpu as pltpu
from jax.sharding import PartitionSpec as P

score_scale = 20.0
loss_scale = 8192.0
teacher_div = 2.0
coef_scale = loss_scale * score_scale
f32 = jnp.float32
bf16 = jnp.bfloat16
vmem = pltpu.VMEM
nt_dims = (((1,), (1,)), ((), ()))
nn_dims = (((1,), (0,)), ((), ()))


def dot(a, b, dims):
    return lax.dot_general(a, b, dims, preferred_element_type=f32)


def split(x):
    high = x.astype(bf16)
    low = (x - high.astype(f32)).astype(bf16)
    return high, low


def params(megabytes):
    return pltpu.CompilerParams(vmem_limit_bytes=int(megabytes * 1024 * 1024))


def whole():
    return pl.BlockSpec(memory_space=vmem)


def pack_kernel(queries_ref, candidates_ref, teacher_ref, out_ref):
    half = queries_ref.shape[1] // 2
    query = queries_ref[...].astype(f32)
    ids = candidates_ref[...]
    first = jnp.concatenate(
        [query[:, :half], (ids >> 8).astype(f32), (ids & 255).astype(f32)], axis=1
    )
    second = jnp.concatenate(
        [query[:, half:], teacher_ref[...].astype(f32), jnp.zeros(ids.shape, f32)], axis=1
    )
    both = jnp.concatenate([first, second], axis=0).astype(bf16)
    out_ref[...] = jnp.broadcast_to(both[None], out_ref.shape)


def table_kernel(passages_ref, gain_ref, table_ref, square_ref, inverse_ref):
    lifted = passages_ref[...].astype(f32) * gain_ref[...]
    norm = jnp.sqrt(jnp.sum(lifted * lifted, axis=1, keepdims=True))
    inverse = 1.0 / norm
    unit = lifted * inverse
    table_ref[...] = unit.astype(bf16)
    square_ref[...] = (unit * unit).astype(bf16)
    rows = unit.shape[0]
    inverse_ref[...] = jnp.transpose(jnp.broadcast_to(inverse, (rows, 128)))[:1, :]


def score_kernel(got_ref, start_ref, table_ref, cos_ref, weight_ref, teach_ref, sums_ref, unit_ref):
    queries = got_ref.shape[0]
    half = got_ref.shape[2] - 256
    listed = 128
    rows = table_ref.shape[0]
    got = got_ref[...].astype(f32)
    query = jnp.concatenate([got[:, 0, :half], got[:, 1, :half]], axis=1)
    norm = jnp.sqrt(jnp.sum(query * query, axis=1, keepdims=True))
    unit = (query / norm).astype(bf16)
    unit_ref[...] = unit
    ids = (got[:, 0, half : half + listed] * 256.0 + got[:, 0, half + listed :]).astype(jnp.int32)
    marks = jnp.exp(got[:, 1, half : half + listed] * (1.0 / teacher_div))
    marks = marks / jnp.sum(marks, axis=1, keepdims=True)
    here = ids - start_ref[0]
    places = lax.broadcasted_iota(jnp.int32, (queries, rows), 1)
    teach = jnp.zeros((queries, rows), f32)
    for c in range(listed):
        teach = teach + jnp.where(here[:, c : c + 1] == places, marks[:, c : c + 1], 0.0)
    teach_ref[...] = teach
    cos = dot(unit, table_ref[...], nt_dims)
    cos_ref[...] = cos
    weight = jnp.where(teach > 0.0, jnp.exp(cos * score_scale), 0.0)
    weight_ref[...] = weight
    total = jnp.sum(weight, axis=1, keepdims=True)
    sums_ref[...] = jnp.broadcast_to(total, sums_ref.shape)


def mix_kernel(unit_ref, cos_ref, weight_ref, teach_ref, table_ref, square_ref, by_weight_ref, by_teach_ref, gain_weight_ref, gain_teach_ref):
    queries = unit_ref.shape[0]
    weight, teach, cos = weight_ref[...], teach_ref[...], cos_ref[...]
    stacked = jnp.concatenate([*split(weight), *split(teach)], axis=0)
    mixed = dot(stacked, table_ref[...], nn_dims)
    by_weight = mixed[:queries] + mixed[queries : 2 * queries]
    by_teach = mixed[2 * queries : 3 * queries] + mixed[3 * queries :]
    stacked = jnp.concatenate([*split(weight * cos), *split(teach * cos)], axis=0)
    along = dot(stacked, square_ref[...], nn_dims)
    unit = unit_ref[...].astype(f32)
    by_weight_ref[...] = by_weight
    by_teach_ref[...] = by_teach
    gain_weight_ref[...] = unit * by_weight - (along[:queries] + along[queries : 2 * queries])
    terms = unit * by_teach - (along[2 * queries : 3 * queries] + along[3 * queries :])
    gain_teach_ref[...] = jnp.sum(terms, axis=0, keepdims=True)


def partial_kernel(sums_ref, by_weight_ref, by_teach_ref, gain_weight_ref, gain_teach_ref, out_ref, inverse_ref):
    queries = by_weight_ref.shape[0]
    inverse = 1.0 / sums_ref[...][:, :1]
    inverse_ref[...] = inverse
    partial = coef_scale * (by_weight_ref[...] * inverse - by_teach_ref[...])
    gain_part = jnp.sum(gain_weight_ref[...] * inverse, axis=0, keepdims=True) - gain_teach_ref[...]
    gain_part = coef_scale * gain_part
    out_ref[...] = jnp.concatenate(
        [partial[:, None, :], jnp.broadcast_to(gain_part[None], (queries, 1, partial.shape[1]))], axis=1
    ).astype(bf16)


def passage_kernel(unit_ref, gain_ref, cos_ref, weight_ref, teach_ref, inverse_ref, norm_ref, table_ref, out_ref):
    coef = coef_scale * (weight_ref[...] * inverse_ref[...] - teach_ref[...])
    scaled = coef * norm_ref[...]
    along = jnp.sum(scaled * cos_ref[...], axis=0, keepdims=True)
    queries, rows = coef.shape
    column = jnp.transpose(jnp.broadcast_to(along, (128, rows)))[:, :1]
    high, low = split(jnp.transpose(scaled))
    unit = unit_ref[...]
    whole_part = dot(
        jnp.concatenate([high, low], axis=1), jnp.concatenate([unit, unit], axis=0), nn_dims
    )
    out_ref[...] = (whole_part - table_ref[...].astype(f32) * column) * gain_ref[...]


def final_kernel(got_ref, queries_ref, gain_ref, d_queries_ref, d_gain_ref):
    got = jnp.sum(got_ref[...].astype(f32), axis=0)
    query = queries_ref[...].astype(f32)
    norm = jnp.sqrt(jnp.sum(query * query, axis=1, keepdims=True))
    unit = query / norm
    d_unit = got[:1]
    d_queries_ref[...] = (d_unit - unit * jnp.sum(unit * d_unit, axis=1, keepdims=True)) / norm
    d_gain_ref[...] = got[1:] / gain_ref[...]


def shape(dims, dtype=f32):
    return jax.ShapeDtypeStruct(dims, dtype)


def exchange(x):
    return lax.all_to_all(x, "hash", split_axis=0, concat_axis=0, tiled=True)


def add_up(x):
    count = lax.axis_size("hash")
    step = 1
    while step < count:
        x = x + lax.ppermute(x, "hash", [(i, i ^ step) for i in range(count)])
        step *= 2
    return x


def local(passages, queries, gain, candidates, teacher):
    count = lax.axis_size("hash")
    rows, width = passages.shape
    listed = candidates.shape[1]
    gain = gain.reshape(1, width)

    packed = pl.pallas_call(
        pack_kernel,
        out_shape=shape((count, 2, width // 2 + 2 * listed), bf16),
        name="pack",
    )(queries, candidates, teacher)
    got = exchange(packed)

    block = 128
    row_block = pl.BlockSpec((block, width), lambda i: (i, 0))
    table, square, norms = pl.pallas_call(
        table_kernel,
        grid=(rows // block,),
        in_specs=[row_block, pl.BlockSpec((1, width), lambda i: (0, 0))],
        out_specs=[row_block, row_block, pl.BlockSpec((1, block), lambda i: (0, i))],
        out_shape=[shape((rows, width), bf16), shape((rows, width), bf16), shape((1, rows))],
        compiler_params=params(24),
        name="table",
        cost_estimate=pl.CostEstimate(
            flops=6 * rows * width, bytes_accessed=6 * rows * width, transcendentals=0
        ),
    )(passages, gain)

    start = (lax.axis_index("hash") * rows).astype(jnp.int32).reshape(1)
    small = shape((count, rows))
    cos, weight, teach, sums, unit = pl.pallas_call(
        score_kernel,
        in_specs=[whole(), pl.BlockSpec(memory_space=pltpu.SMEM), whole()],
        out_shape=[small, small, small, shape((count, 128)), shape((count, width), bf16)],
        compiler_params=params(12 + count // 4),
        name="score",
    )(got, start, table)
    got_sums = add_up(sums)

    wide = shape((count, width))
    by_weight, by_teach, gain_weight, gain_teach = pl.pallas_call(
        mix_kernel,
        out_shape=[wide, wide, wide, shape((1, width))],
        compiler_params=params(12 + count // 4),
        name="mix",
        cost_estimate=pl.CostEstimate(
            flops=16 * count * rows * width, bytes_accessed=4 * rows * width, transcendentals=0
        ),
    )(unit, cos, weight, teach, table, square)

    partial, inverse = pl.pallas_call(
        partial_kernel,
        out_shape=[shape((count, 2, width), bf16), shape((count, 1))],
        compiler_params=params(12 + count // 4),
        name="partial",
    )(got_sums, by_weight, by_teach, gain_weight, gain_teach)
    got_partial = exchange(partial)

    fixed = lambda dims: pl.BlockSpec(dims, lambda i: (0, 0))
    cols = pl.BlockSpec((count, block), lambda i: (0, i))
    d_passages = pl.pallas_call(
        passage_kernel,
        grid=(rows // block,),
        in_specs=[
            fixed((count, width)),
            fixed((1, width)),
            cols,
            cols,
            cols,
            fixed((count, 1)),
            pl.BlockSpec((1, block), lambda i: (0, i)),
            row_block,
        ],
        out_specs=row_block,
        out_shape=shape((rows, width)),
        compiler_params=params(16 + count // 8),
        name="d_passages",
        cost_estimate=pl.CostEstimate(
            flops=4 * count * rows * width, bytes_accessed=6 * rows * width, transcendentals=0
        ),
    )(unit, gain, cos, weight, teach, inverse, norms, table)

    d_queries, d_gain = pl.pallas_call(
        final_kernel,
        out_shape=[shape((1, width)), shape((1, width))],
        compiler_params=params(12 + count // 4),
        name="final",
    )(got_partial, queries, gain)
    return (d_passages, d_queries, d_gain.reshape(width))


def solution(mesh):
    in_specs = (
        P(("groups", "hash"), None),
        P(("groups", "hash"), None),
        P(),
        P(("groups", "hash"), None),
        P(("groups", "hash"), None),
    )
    out_specs = (P(("groups", "hash"), None), P(("groups", "hash"), None), P("groups"))
    return jax.shard_map(local, mesh=mesh, in_specs=in_specs, out_specs=out_specs, check_vma=False)
```

```python
import functools

import jax
import jax.numpy as jnp
from jax import lax
from jax.experimental import pallas as pl
from jax.experimental.pallas import tpu as pltpu
from jax.sharding import PartitionSpec as P

score_scale = 20.0
loss_scale = 8192.0
teacher_div = 2.0
coef_scale = loss_scale * score_scale
chunks = 4
f32 = jnp.float32
bf16 = jnp.bfloat16
vmem = pltpu.VMEM
nt_dims = (((1,), (1,)), ((), ()))
nn_dims = (((1,), (0,)), ((), ()))


def dot(a, b, dims):
    return lax.dot_general(a, b, dims, preferred_element_type=f32)


def split(x):
    high = x.astype(bf16)
    low = (x - high.astype(f32)).astype(bf16)
    return high, low


def params(megabytes):
    return pltpu.CompilerParams(vmem_limit_bytes=megabytes * 1024 * 1024)


def whole():
    return pl.BlockSpec(memory_space=vmem)


def outside():
    return pl.BlockSpec(memory_space=pltpu.HBM)


def pack_kernel(queries_ref, candidates_ref, teacher_ref, out_ref):
    half = queries_ref.shape[1] // 2
    query = queries_ref[...].astype(f32)
    ids = candidates_ref[...]
    first = jnp.concatenate(
        [query[:, :half], (ids >> 8).astype(f32), (ids & 255).astype(f32)], axis=1
    )
    second = jnp.concatenate(
        [query[:, half:], teacher_ref[...].astype(f32), jnp.zeros(ids.shape, f32)], axis=1
    )
    both = jnp.concatenate([first, second], axis=0).astype(bf16)
    out_ref[...] = jnp.broadcast_to(both[None], out_ref.shape)


def table_kernel(passages_ref, gain_ref, table_ref, inverse_ref, raw, held, sems_in, sems_out):
    gain = gain_ref[...]
    chunk = raw.shape[0] // chunks
    copies_in, copies_out = [], []
    for k in range(chunks):
        part = pl.ds(k * chunk, chunk)
        copies_in.append(pltpu.make_async_copy(passages_ref.at[part], raw.at[part], sems_in.at[k]))
        copies_out.append(pltpu.make_async_copy(held.at[part], table_ref.at[part], sems_out.at[k]))
        copies_in[-1].start()
    for k in range(chunks):
        part = pl.ds(k * chunk, chunk)
        copies_in[k].wait()
        lifted = raw[part, :].astype(f32) * gain
        norm = jnp.sqrt(jnp.sum(lifted * lifted, axis=1, keepdims=True))
        inverse = 1.0 / norm
        held[part, :] = (lifted * inverse).astype(bf16)
        copies_out[k].start()
        inverse_ref[:, part] = jnp.transpose(jnp.broadcast_to(inverse, (chunk, 128)))[:1, :]
    for k in range(chunks):
        copies_out[k].wait()


def score_kernel(got_ref, start_ref, table_ref, cos_ref, weight_ref, teach_ref, sums_ref, unit_ref, held, sems):
    queries = got_ref.shape[0]
    half = got_ref.shape[2] - 256
    listed = 128
    rows = table_ref.shape[0]
    chunk = rows // chunks
    copies = []
    for k in range(chunks):
        part = pl.ds(k * chunk, chunk)
        copies.append(pltpu.make_async_copy(table_ref.at[part], held.at[part], sems.at[k]))
        copies[-1].start()
    got = got_ref[...].astype(f32)
    query = jnp.concatenate([got[:, 0, :half], got[:, 1, :half]], axis=1)
    norm = jnp.sqrt(jnp.sum(query * query, axis=1, keepdims=True))
    unit = (query / norm).astype(bf16)
    unit_ref[...] = unit
    ids = (got[:, 0, half : half + listed] * 256.0 + got[:, 0, half + listed :]).astype(jnp.int32)
    marks = jnp.exp(got[:, 1, half : half + listed] * (1.0 / teacher_div))
    marks = marks / jnp.sum(marks, axis=1, keepdims=True)
    here = ids - start_ref[0]
    places = lax.broadcasted_iota(jnp.int32, (queries, rows), 1)
    teach = jnp.zeros((queries, rows), f32)
    for c in range(listed):
        teach = teach + jnp.where(here[:, c : c + 1] == places, marks[:, c : c + 1], 0.0)
    teach_ref[...] = teach
    for k in range(chunks):
        copies[k].wait()
        part = pl.ds(k * chunk, chunk)
        cos_ref[:, part] = dot(unit, held[part, :], nt_dims)
    weight = jnp.where(teach > 0.0, jnp.exp(cos_ref[...] * score_scale), 0.0)
    weight_ref[...] = weight
    total = jnp.sum(weight, axis=1, keepdims=True)
    flipped = jnp.transpose(jnp.broadcast_to(total, (queries, 128)))[:1, :queries]
    sums_ref[...] = jnp.broadcast_to(flipped[None], sums_ref.shape)


def mix_kernel(
    unit_ref, cos_ref, weight_ref, teach_ref, table_ref,
    by_weight_ref, by_teach_ref, gain_weight_ref, gain_teach_ref, held, sems,
):
    queries = unit_ref.shape[0]
    chunk = table_ref.shape[1] // chunks
    copies = []
    for k in range(chunks):
        part = pl.ds(k * chunk, chunk)
        copies.append(pltpu.make_async_copy(table_ref.at[:, part], held.at[:, part], sems.at[k]))
        copies[-1].start()
    weight, teach, cos = weight_ref[...], teach_ref[...], cos_ref[...]
    plain = jnp.concatenate([*split(weight), *split(teach)], axis=0)
    scored = jnp.concatenate([*split(weight * cos), *split(teach * cos)], axis=0)
    for k in range(chunks):
        copies[k].wait()
        part = pl.ds(k * chunk, chunk)
        table = held[:, part]
        mixed = dot(plain, table, nn_dims)
        by_weight = mixed[:queries] + mixed[queries : 2 * queries]
        by_teach = mixed[2 * queries : 3 * queries] + mixed[3 * queries :]
        table = table.astype(f32)
        along = dot(scored, (table * table).astype(bf16), nn_dims)
        unit = unit_ref[:, part].astype(f32)
        by_weight_ref[:, part] = by_weight
        by_teach_ref[:, part] = by_teach
        gain_weight_ref[:, part] = unit * by_weight - (along[:queries] + along[queries : 2 * queries])
        terms = unit * by_teach - (along[2 * queries : 3 * queries] + along[3 * queries :])
        gain_teach_ref[:, part] = jnp.sum(terms, axis=0, keepdims=True)


def partial_kernel(sums_ref, by_weight_ref, by_teach_ref, gain_weight_ref, gain_teach_ref, out_ref, inverse_ref):
    queries = by_weight_ref.shape[0]
    total = jnp.sum(sums_ref[...][:, 0, :], axis=0, keepdims=True)
    inverse = jnp.transpose(jnp.broadcast_to(1.0 / total, (128, queries)))[:, :1]
    inverse_ref[...] = inverse
    partial = coef_scale * (by_weight_ref[...] * inverse - by_teach_ref[...])
    gain_part = jnp.sum(gain_weight_ref[...] * inverse, axis=0, keepdims=True) - gain_teach_ref[...]
    gain_part = coef_scale * gain_part
    out_ref[...] = jnp.concatenate(
        [partial[:, None, :], jnp.broadcast_to(gain_part[None], (queries, 1, partial.shape[1]))], axis=1
    ).astype(bf16)


def passage_kernel(unit_ref, gain_ref, cos_ref, weight_ref, teach_ref, inverse_ref, norm_ref, table_ref, out_ref, held, sems):
    step = pl.program_id(0)
    chunk = out_ref.shape[0]
    part = pl.ds(pl.multiple_of(step * chunk, chunk), chunk)

    @pl.when(step == 0)
    def _():
        for k in range(chunks):
            first = pl.ds(k * chunk, chunk)
            pltpu.make_async_copy(table_ref.at[first], held.at[first], sems.at[k]).start()

    coef = coef_scale * (weight_ref[...] * inverse_ref[...] - teach_ref[...])
    scaled = coef * norm_ref[...]
    along = jnp.sum(scaled * cos_ref[...], axis=0, keepdims=True)
    column = jnp.transpose(jnp.broadcast_to(along, (128, chunk)))[:, :1]
    high, low = split(jnp.transpose(scaled))
    unit = unit_ref[...]
    whole_part = dot(
        jnp.concatenate([high, low], axis=1), jnp.concatenate([unit, unit], axis=0), nn_dims
    )
    pltpu.make_async_copy(table_ref.at[part], held.at[part], sems.at[step]).wait()
    out_ref[...] = (whole_part - held[part, :].astype(f32) * column) * gain_ref[...]


def final_kernel(got_ref, queries_ref, gain_ref, d_queries_ref, d_gain_ref):
    got = jnp.sum(got_ref[...].astype(f32), axis=0)
    query = queries_ref[...].astype(f32)
    norm = jnp.sqrt(jnp.sum(query * query, axis=1, keepdims=True))
    unit = query / norm
    d_unit = got[:1]
    d_queries_ref[...] = (d_unit - unit * jnp.sum(unit * d_unit, axis=1, keepdims=True)) / norm
    d_gain_ref[...] = got[1:] / gain_ref[...]


def shape(dims, dtype=f32):
    return jax.ShapeDtypeStruct(dims, dtype)


def exchange(x):
    return lax.all_to_all(x, "hash", split_axis=0, concat_axis=0, tiled=True)


def local(passages, queries, gain, candidates, teacher):
    count = lax.axis_size("hash")
    rows, width = passages.shape
    listed = candidates.shape[1]
    gain = gain.reshape(1, width)

    packed = pl.pallas_call(
        pack_kernel,
        out_shape=shape((count, 2, width // 2 + 2 * listed), bf16),
        compiler_params=params(60),
        name="pack",
    )(queries, candidates, teacher)
    got = exchange(packed)

    block = 128
    row_block = pl.BlockSpec((block, width), lambda i: (i, 0))
    held = pltpu.VMEM((rows, width), bf16)
    sems = pltpu.SemaphoreType.DMA((chunks,))
    table, norms = pl.pallas_call(
        table_kernel,
        in_specs=[outside(), whole()],
        out_specs=[outside(), whole()],
        out_shape=[shape((rows, width), bf16), shape((1, rows))],
        scratch_shapes=[held, held, sems, sems],
        compiler_params=params(60),
        name="table",
        cost_estimate=pl.CostEstimate(
            flops=6 * rows * width, bytes_accessed=4 * rows * width, transcendentals=0
        ),
    )(passages, gain)

    start = (lax.axis_index("hash") * rows).astype(jnp.int32).reshape(1)
    small = shape((count, rows))
    cos, weight, teach, sums, unit = pl.pallas_call(
        score_kernel,
        in_specs=[whole(), pl.BlockSpec(memory_space=pltpu.SMEM), outside()],
        out_shape=[small, small, small, shape((count, 1, count)), shape((count, width), bf16)],
        scratch_shapes=[held, sems],
        compiler_params=params(60),
        name="score",
    )(got, start, table)
    got_sums = exchange(sums)

    wide = shape((count, width))
    by_weight, by_teach, gain_weight, gain_teach = pl.pallas_call(
        mix_kernel,
        in_specs=[whole(), whole(), whole(), whole(), outside()],
        out_shape=[wide, wide, wide, shape((1, width))],
        scratch_shapes=[held, sems],
        compiler_params=params(60),
        name="mix",
        cost_estimate=pl.CostEstimate(
            flops=16 * count * rows * width, bytes_accessed=2 * rows * width, transcendentals=0
        ),
    )(unit, cos, weight, teach, table)

    partial, inverse = pl.pallas_call(
        partial_kernel,
        out_shape=[shape((count, 2, width), bf16), shape((count, 1))],
        compiler_params=params(60),
        name="partial",
    )(got_sums, by_weight, by_teach, gain_weight, gain_teach)
    got_partial = exchange(partial)

    block = rows // chunks
    fixed = lambda dims: pl.BlockSpec(dims, lambda i: (0, 0))
    cols = pl.BlockSpec((count, block), lambda i: (0, i))
    d_passages = pl.pallas_call(
        passage_kernel,
        grid=(rows // block,),
        in_specs=[
            fixed((count, width)),
            fixed((1, width)),
            cols,
            cols,
            cols,
            fixed((count, 1)),
            pl.BlockSpec((1, block), lambda i: (0, i)),
            outside(),
        ],
        out_specs=pl.BlockSpec((block, width), lambda i: (i, 0)),
        out_shape=shape((rows, width)),
        scratch_shapes=[held, sems],
        compiler_params=params(60),
        name="d_passages",
        cost_estimate=pl.CostEstimate(
            flops=4 * count * rows * width, bytes_accessed=6 * rows * width, transcendentals=0
        ),
    )(unit, gain, cos, weight, teach, inverse, norms, table)

    d_queries, d_gain = pl.pallas_call(
        final_kernel,
        out_shape=[shape((1, width)), shape((1, width))],
        compiler_params=params(60),
        name="final",
    )(got_partial, queries, gain)
    return (d_passages, d_queries, d_gain.reshape(width))


def solution(mesh):
    in_specs = (
        P(("groups", "hash"), None),
        P(("groups", "hash"), None),
        P(),
        P(("groups", "hash"), None),
        P(("groups", "hash"), None),
    )
    out_specs = (P(("groups", "hash"), None), P(("groups", "hash"), None), P("groups"))
    return jax.shard_map(local, mesh=mesh, in_specs=in_specs, out_specs=out_specs, check_vma=False)
```

```python
import functools

import jax
import jax.numpy as jnp
from jax import lax
from jax.experimental import pallas as pl
from jax.experimental.pallas import tpu as pltpu
from jax.sharding import PartitionSpec as P

score_scale = 20.0
loss_scale = 8192.0
teacher_div = 2.0
coef_scale = loss_scale * score_scale
chunks = 4
f32 = jnp.float32
bf16 = jnp.bfloat16
vmem = pltpu.VMEM
nt_dims = (((1,), (1,)), ((), ()))
nn_dims = (((1,), (0,)), ((), ()))


def dot(a, b, dims):
    return lax.dot_general(a, b, dims, preferred_element_type=f32)


def split(x):
    high = x.astype(bf16)
    low = (x - high.astype(f32)).astype(bf16)
    return high, low


def params(megabytes):
    return pltpu.CompilerParams(vmem_limit_bytes=megabytes * 1024 * 1024)


def whole():
    return pl.BlockSpec(memory_space=vmem)


def outside():
    return pl.BlockSpec(memory_space=pltpu.HBM)


def pack_kernel(queries_ref, candidates_ref, teacher_ref, out_ref):
    half = queries_ref.shape[1] // 2
    query = queries_ref[...].astype(f32)
    ids = candidates_ref[...]
    first = jnp.concatenate(
        [query[:, :half], (ids >> 8).astype(f32), (ids & 255).astype(f32)], axis=1
    )
    second = jnp.concatenate(
        [query[:, half:], teacher_ref[...].astype(f32), jnp.zeros(ids.shape, f32)], axis=1
    )
    both = jnp.concatenate([first, second], axis=0).astype(bf16)
    out_ref[...] = jnp.broadcast_to(both[None], out_ref.shape)


def table_kernel(passages_ref, gain_ref, table_ref, inverse_ref, raw, held, sems_in, sems_out):
    gain = gain_ref[...]
    chunk = raw.shape[0] // chunks
    copies_in, copies_out = [], []
    for k in range(chunks):
        part = pl.ds(k * chunk, chunk)
        copies_in.append(pltpu.make_async_copy(passages_ref.at[part], raw.at[part], sems_in.at[k]))
        copies_out.append(pltpu.make_async_copy(held.at[part], table_ref.at[part], sems_out.at[k]))
        copies_in[-1].start()
    for k in range(chunks):
        part = pl.ds(k * chunk, chunk)
        copies_in[k].wait()
        lifted = raw[part, :].astype(f32) * gain
        norm = jnp.sqrt(jnp.sum(lifted * lifted, axis=1, keepdims=True))
        inverse = 1.0 / norm
        held[part, :] = (lifted * inverse).astype(bf16)
        copies_out[k].start()
        inverse_ref[:, part] = jnp.transpose(jnp.broadcast_to(inverse, (chunk, 128)))[:1, :]
    for k in range(chunks):
        copies_out[k].wait()


def score_kernel(got_ref, start_ref, table_ref, cos_ref, weight_ref, teach_ref, sums_ref, unit_ref, held, sems):
    queries = got_ref.shape[0]
    half = got_ref.shape[2] - 256
    listed = 128
    rows = held.shape[0]
    chunk = rows // chunks
    copies = []
    for k in range(chunks):
        part = pl.ds(k * chunk, chunk)
        copies.append(pltpu.make_async_copy(table_ref.at[part], held.at[part], sems.at[k]))
        copies[-1].start()
    got = got_ref[...].astype(f32)
    query = jnp.concatenate([got[:, 0, :half], got[:, 1, :half]], axis=1)
    norm = jnp.sqrt(jnp.sum(query * query, axis=1, keepdims=True))
    unit = (query / norm).astype(bf16)
    unit_ref[...] = unit
    ids = (got[:, 0, half : half + listed] * 256.0 + got[:, 0, half + listed :]).astype(jnp.int32)
    marks = jnp.exp(got[:, 1, half : half + listed] * (1.0 / teacher_div))
    marks = marks / jnp.sum(marks, axis=1, keepdims=True)
    here = ids - start_ref[0]
    places = lax.broadcasted_iota(jnp.int32, (queries, rows), 1)
    teach = jnp.zeros((queries, rows), f32)
    for c in range(listed):
        teach = teach + jnp.where(here[:, c : c + 1] == places, marks[:, c : c + 1], 0.0)
    teach_ref[...] = teach
    for k in range(chunks):
        copies[k].wait()
        part = pl.ds(k * chunk, chunk)
        cos_ref[:, part] = dot(unit, held[part, :], nt_dims)
    weight = jnp.where(teach > 0.0, jnp.exp(cos_ref[...] * score_scale), 0.0)
    weight_ref[...] = weight
    total = jnp.sum(weight, axis=1, keepdims=True)
    flipped = jnp.transpose(jnp.broadcast_to(total, (queries, 128)))[:1, :queries]
    sums_ref[...] = jnp.broadcast_to(flipped[None], sums_ref.shape)


def mix_kernel(
    unit_ref, cos_ref, weight_ref, teach_ref, table_ref,
    by_weight_ref, by_teach_ref, gain_weight_ref, gain_teach_ref, held, sems,
):
    queries = unit_ref.shape[0]
    chunk = table_ref.shape[1] // chunks
    copies = []
    for k in range(chunks):
        part = pl.ds(k * chunk, chunk)
        copies.append(pltpu.make_async_copy(table_ref.at[pl.ds(0, held.shape[0]), part], held.at[:, part], sems.at[k]))
        copies[-1].start()
    weight, teach, cos = weight_ref[...], teach_ref[...], cos_ref[...]
    plain = jnp.concatenate([*split(weight), *split(teach)], axis=0)
    scored = jnp.concatenate([*split(weight * cos), *split(teach * cos)], axis=0)
    for k in range(chunks):
        copies[k].wait()
        part = pl.ds(k * chunk, chunk)
        table = held[:, part]
        mixed = dot(plain, table, nn_dims)
        by_weight = mixed[:queries] + mixed[queries : 2 * queries]
        by_teach = mixed[2 * queries : 3 * queries] + mixed[3 * queries :]
        table = table.astype(f32)
        along = dot(scored, (table * table).astype(bf16), nn_dims)
        unit = unit_ref[:, part].astype(f32)
        by_weight_ref[:, part] = by_weight
        by_teach_ref[:, part] = by_teach
        gain_weight_ref[:, part] = unit * by_weight - (along[:queries] + along[queries : 2 * queries])
        terms = unit * by_teach - (along[2 * queries : 3 * queries] + along[3 * queries :])
        gain_teach_ref[:, part] = jnp.sum(terms, axis=0, keepdims=True)


def partial_kernel(sums_ref, by_weight_ref, by_teach_ref, gain_weight_ref, gain_teach_ref, out_ref, inverse_ref):
    queries = by_weight_ref.shape[0]
    total = jnp.sum(sums_ref[...][:, 0, :], axis=0, keepdims=True)
    inverse = jnp.transpose(jnp.broadcast_to(1.0 / total, (128, queries)))[:, :1]
    inverse_ref[...] = inverse
    partial = coef_scale * (by_weight_ref[...] * inverse - by_teach_ref[...])
    gain_part = jnp.sum(gain_weight_ref[...] * inverse, axis=0, keepdims=True) - gain_teach_ref[...]
    gain_part = coef_scale * gain_part
    out_ref[...] = jnp.concatenate(
        [partial[:, None, :], jnp.broadcast_to(gain_part[None], (queries, 1, partial.shape[1]))], axis=1
    ).astype(bf16)


def passage_kernel(unit_ref, gain_ref, cos_ref, weight_ref, teach_ref, inverse_ref, norm_ref, table_ref, out_ref, held, sems):
    step = pl.program_id(0)
    chunk = out_ref.shape[0]
    part = pl.ds(pl.multiple_of(step * chunk, chunk), chunk)

    @pl.when(step == 0)
    def _():
        for k in range(chunks):
            first = pl.ds(k * chunk, chunk)
            pltpu.make_async_copy(table_ref.at[first], held.at[first], sems.at[k]).start()

    coef = coef_scale * (weight_ref[...] * inverse_ref[...] - teach_ref[...])
    scaled = coef * norm_ref[...]
    along = jnp.sum(scaled * cos_ref[...], axis=0, keepdims=True)
    column = jnp.transpose(jnp.broadcast_to(along, (128, chunk)))[:, :1]
    high, low = split(jnp.transpose(scaled))
    unit = unit_ref[...]
    whole_part = dot(
        jnp.concatenate([high, low], axis=1), jnp.concatenate([unit, unit], axis=0), nn_dims
    )
    pltpu.make_async_copy(table_ref.at[part], held.at[part], sems.at[step]).wait()
    out_ref[...] = (whole_part - held[part, :].astype(f32) * column) * gain_ref[...]


def final_kernel(got_ref, queries_ref, gain_ref, d_queries_ref, d_gain_ref):
    got = jnp.sum(got_ref[...].astype(f32), axis=0)
    query = queries_ref[...].astype(f32)
    norm = jnp.sqrt(jnp.sum(query * query, axis=1, keepdims=True))
    unit = query / norm
    d_unit = got[:1]
    d_queries_ref[...] = (d_unit - unit * jnp.sum(unit * d_unit, axis=1, keepdims=True)) / norm
    d_gain_ref[...] = got[1:] / gain_ref[...]


def shape(dims, dtype=f32):
    return jax.ShapeDtypeStruct(dims, dtype)


def exchange(x):
    return lax.all_to_all(x, "hash", split_axis=0, concat_axis=0, tiled=True)


def local(passages, queries, gain, candidates, teacher):
    count = lax.axis_size("hash")
    rows, width = passages.shape
    listed = candidates.shape[1]
    gain = gain.reshape(1, width)

    packed = pl.pallas_call(
        pack_kernel,
        out_shape=shape((count, 2, width // 2 + 2 * listed), bf16),
        compiler_params=params(48),
        name="pack",
    )(queries, candidates, teacher)
    got = exchange(packed)

    block = 128
    row_block = pl.BlockSpec((block, width), lambda i: (i, 0))
    held = pltpu.VMEM((rows, width), bf16)
    sems = pltpu.SemaphoreType.DMA((chunks,))
    table, norms = pl.pallas_call(
        table_kernel,
        in_specs=[outside(), whole()],
        out_specs=[outside(), whole()],
        out_shape=[shape((5 * rows, width), bf16), shape((1, rows))],
        scratch_shapes=[held, held, sems, sems],
        compiler_params=params(60),
        name="table",
        cost_estimate=pl.CostEstimate(
            flops=6 * rows * width, bytes_accessed=4 * rows * width, transcendentals=0
        ),
    )(passages, gain)

    start = (lax.axis_index("hash") * rows).astype(jnp.int32).reshape(1)
    small = shape((count, rows))
    cos, weight, teach, sums, unit = pl.pallas_call(
        score_kernel,
        in_specs=[whole(), pl.BlockSpec(memory_space=pltpu.SMEM), outside()],
        out_shape=[small, small, small, shape((count, 1, count)), shape((count, width), bf16)],
        scratch_shapes=[held, sems],
        compiler_params=params(48),
        name="score",
    )(got, start, table)
    got_sums = exchange(sums)

    wide = shape((count, width))
    by_weight, by_teach, gain_weight, gain_teach = pl.pallas_call(
        mix_kernel,
        in_specs=[whole(), whole(), whole(), whole(), outside()],
        out_shape=[wide, wide, wide, shape((1, width))],
        scratch_shapes=[held, sems],
        compiler_params=params(48),
        name="mix",
        cost_estimate=pl.CostEstimate(
            flops=16 * count * rows * width, bytes_accessed=2 * rows * width, transcendentals=0
        ),
    )(unit, cos, weight, teach, table)

    partial, inverse = pl.pallas_call(
        partial_kernel,
        out_shape=[shape((count, 2, width), bf16), shape((count, 1))],
        compiler_params=params(48),
        name="partial",
    )(got_sums, by_weight, by_teach, gain_weight, gain_teach)
    got_partial = exchange(partial)

    block = rows // chunks
    fixed = lambda dims: pl.BlockSpec(dims, lambda i: (0, 0))
    cols = pl.BlockSpec((count, block), lambda i: (0, i))
    d_passages = pl.pallas_call(
        passage_kernel,
        grid=(rows // block,),
        in_specs=[
            fixed((count, width)),
            fixed((1, width)),
            cols,
            cols,
            cols,
            fixed((count, 1)),
            pl.BlockSpec((1, block), lambda i: (0, i)),
            outside(),
        ],
        out_specs=pl.BlockSpec((block, width), lambda i: (i, 0)),
        out_shape=shape((rows, width)),
        scratch_shapes=[held, sems],
        compiler_params=params(48),
        name="d_passages",
        cost_estimate=pl.CostEstimate(
            flops=4 * count * rows * width, bytes_accessed=6 * rows * width, transcendentals=0
        ),
    )(unit, gain, cos, weight, teach, inverse, norms, table)

    d_queries, d_gain = pl.pallas_call(
        final_kernel,
        out_shape=[shape((1, width)), shape((1, width))],
        compiler_params=params(48),
        name="final",
    )(got_partial, queries, gain)
    return (d_passages, d_queries, d_gain.reshape(width))


def solution(mesh):
    in_specs = (
        P(("groups", "hash"), None),
        P(("groups", "hash"), None),
        P(),
        P(("groups", "hash"), None),
        P(("groups", "hash"), None),
    )
    out_specs = (P(("groups", "hash"), None), P(("groups", "hash"), None), P("groups"))
    return jax.shard_map(local, mesh=mesh, in_specs=in_specs, out_specs=out_specs, check_vma=False)
```

```python
import functools

import jax
import jax.numpy as jnp
from jax import lax
from jax.experimental import pallas as pl
from jax.experimental.pallas import tpu as pltpu
from jax.sharding import PartitionSpec as P

score_scale = 20.0
loss_scale = 8192.0
teacher_div = 2.0
coef_scale = loss_scale * score_scale
chunks = 4
f32 = jnp.float32
bf16 = jnp.bfloat16
vmem = pltpu.VMEM
nt_dims = (((1,), (1,)), ((), ()))
nn_dims = (((1,), (0,)), ((), ()))


def dot(a, b, dims):
    return lax.dot_general(a, b, dims, preferred_element_type=f32)


def split(x):
    high = x.astype(bf16)
    low = (x - high.astype(f32)).astype(bf16)
    return high, low


def params(megabytes):
    return pltpu.CompilerParams(vmem_limit_bytes=megabytes * 1024 * 1024)


def whole():
    return pl.BlockSpec(memory_space=vmem)


def outside():
    return pl.BlockSpec(memory_space=pltpu.HBM)


def pack_kernel(queries_ref, candidates_ref, teacher_ref, out_ref):
    half = queries_ref.shape[1] // 2
    query = queries_ref[...].astype(f32)
    ids = candidates_ref[...]
    first = jnp.concatenate(
        [query[:, :half], (ids >> 8).astype(f32), (ids & 255).astype(f32)], axis=1
    )
    second = jnp.concatenate(
        [query[:, half:], teacher_ref[...].astype(f32), jnp.zeros(ids.shape, f32)], axis=1
    )
    both = jnp.concatenate([first, second], axis=0).astype(bf16)
    out_ref[...] = jnp.broadcast_to(both[None], out_ref.shape)


def table_kernel(passages_ref, gain_ref, table_ref, inverse_ref, raw, held, sems_in, sems_out):
    gain = gain_ref[...]
    chunk = raw.shape[0] // chunks
    copies_in, copies_out = [], []
    for k in range(chunks):
        part = pl.ds(k * chunk, chunk)
        copies_in.append(pltpu.make_async_copy(passages_ref.at[part], raw.at[part], sems_in.at[k]))
        copies_out.append(pltpu.make_async_copy(held.at[part], table_ref.at[part], sems_out.at[k]))
        copies_in[-1].start()
    for k in range(chunks):
        part = pl.ds(k * chunk, chunk)
        copies_in[k].wait()
        lifted = raw[part, :].astype(f32) * gain
        norm = jnp.sqrt(jnp.sum(lifted * lifted, axis=1, keepdims=True))
        inverse = 1.0 / norm
        held[part, :] = (lifted * inverse).astype(bf16)
        copies_out[k].start()
        inverse_ref[:, part] = jnp.transpose(jnp.broadcast_to(inverse, (chunk, 128)))[:1, :]
    for k in range(chunks):
        copies_out[k].wait()


def score_kernel(got_ref, start_ref, table_ref, cos_ref, weight_ref, teach_ref, sums_ref, unit_ref, held, sems):
    queries = got_ref.shape[0]
    half = got_ref.shape[2] - 256
    listed = 128
    rows = held.shape[0]
    chunk = held.shape[1] // chunks
    copies = []
    for k in range(chunks):
        part = pl.ds(k * chunk, chunk)
        copies.append(
            pltpu.make_async_copy(table_ref.at[pl.ds(0, rows), part], held.at[:, part], sems.at[k])
        )
        copies[-1].start()
    got = got_ref[...].astype(f32)
    query = jnp.concatenate([got[:, 0, :half], got[:, 1, :half]], axis=1)
    norm = jnp.sqrt(jnp.sum(query * query, axis=1, keepdims=True))
    unit = (query / norm).astype(bf16)
    unit_ref[...] = unit
    ids = (got[:, 0, half : half + listed] * 256.0 + got[:, 0, half + listed :]).astype(jnp.int32)
    marks = jnp.exp(got[:, 1, half : half + listed] * (1.0 / teacher_div))
    marks = marks / jnp.sum(marks, axis=1, keepdims=True)
    here = ids - start_ref[0]
    places = lax.broadcasted_iota(jnp.int32, (queries, rows), 1)
    teach = jnp.zeros((queries, rows), f32)
    for c in range(listed):
        teach = teach + jnp.where(here[:, c : c + 1] == places, marks[:, c : c + 1], 0.0)
    teach_ref[...] = teach
    cos = jnp.zeros((queries, rows), f32)
    for k in range(chunks):
        copies[k].wait()
        part = slice(k * chunk, (k + 1) * chunk)
        cos = cos + dot(unit[:, part], held[:, part], nt_dims)
    cos_ref[...] = cos
    weight = jnp.where(teach > 0.0, jnp.exp(cos * score_scale), 0.0)
    weight_ref[...] = weight
    total = jnp.sum(weight, axis=1, keepdims=True)
    flipped = jnp.transpose(jnp.broadcast_to(total, (queries, 128)))[:1, :queries]
    sums_ref[...] = jnp.broadcast_to(flipped[None], sums_ref.shape)


def mix_kernel(
    unit_ref, cos_ref, weight_ref, teach_ref, table_ref,
    by_weight_ref, by_teach_ref, gain_weight_ref, gain_teach_ref, held, sems,
):
    queries = unit_ref.shape[0]
    chunk = table_ref.shape[1] // chunks
    copies = []
    for k in range(chunks):
        part = pl.ds(k * chunk, chunk)
        copies.append(pltpu.make_async_copy(table_ref.at[pl.ds(0, held.shape[0]), part], held.at[:, part], sems.at[k]))
        copies[-1].start()
    weight, teach, cos = weight_ref[...], teach_ref[...], cos_ref[...]
    plain = jnp.concatenate([*split(weight), *split(teach)], axis=0)
    scored = jnp.concatenate([*split(weight * cos), *split(teach * cos)], axis=0)
    for k in range(chunks):
        copies[k].wait()
        part = pl.ds(k * chunk, chunk)
        table = held[:, part]
        mixed = dot(plain, table, nn_dims)
        by_weight = mixed[:queries] + mixed[queries : 2 * queries]
        by_teach = mixed[2 * queries : 3 * queries] + mixed[3 * queries :]
        table = table.astype(f32)
        along = dot(scored, (table * table).astype(bf16), nn_dims)
        unit = unit_ref[:, part].astype(f32)
        by_weight_ref[:, part] = by_weight
        by_teach_ref[:, part] = by_teach
        gain_weight_ref[:, part] = unit * by_weight - (along[:queries] + along[queries : 2 * queries])
        terms = unit * by_teach - (along[2 * queries : 3 * queries] + along[3 * queries :])
        gain_teach_ref[:, part] = jnp.sum(terms, axis=0, keepdims=True)


def partial_kernel(sums_ref, by_weight_ref, by_teach_ref, gain_weight_ref, gain_teach_ref, out_ref, inverse_ref):
    queries = by_weight_ref.shape[0]
    total = jnp.sum(sums_ref[...][:, 0, :], axis=0, keepdims=True)
    inverse = jnp.transpose(jnp.broadcast_to(1.0 / total, (128, queries)))[:, :1]
    inverse_ref[...] = inverse
    partial = coef_scale * (by_weight_ref[...] * inverse - by_teach_ref[...])
    gain_part = jnp.sum(gain_weight_ref[...] * inverse, axis=0, keepdims=True) - gain_teach_ref[...]
    gain_part = coef_scale * gain_part
    out_ref[...] = jnp.concatenate(
        [partial[:, None, :], jnp.broadcast_to(gain_part[None], (queries, 1, partial.shape[1]))], axis=1
    ).astype(bf16)


def passage_kernel(unit_ref, gain_ref, cos_ref, weight_ref, teach_ref, inverse_ref, norm_ref, table_ref, out_ref, held, sems):
    step = pl.program_id(0)
    chunk = out_ref.shape[0]
    part = pl.ds(pl.multiple_of(step * chunk, chunk), chunk)

    @pl.when(step == 0)
    def _():
        for k in range(chunks):
            first = pl.ds(k * chunk, chunk)
            pltpu.make_async_copy(table_ref.at[first], held.at[first], sems.at[k]).start()

    coef = coef_scale * (weight_ref[...] * inverse_ref[...] - teach_ref[...])
    scaled = coef * norm_ref[...]
    along = jnp.sum(scaled * cos_ref[...], axis=0, keepdims=True)
    column = jnp.transpose(jnp.broadcast_to(along, (128, chunk)))[:, :1]
    high, low = split(jnp.transpose(scaled))
    unit = unit_ref[...]
    whole_part = dot(
        jnp.concatenate([high, low], axis=1), jnp.concatenate([unit, unit], axis=0), nn_dims
    )
    pltpu.make_async_copy(table_ref.at[part], held.at[part], sems.at[step]).wait()
    out_ref[...] = (whole_part - held[part, :].astype(f32) * column) * gain_ref[...]


def final_kernel(got_ref, queries_ref, gain_ref, d_queries_ref, d_gain_ref):
    got = jnp.sum(got_ref[...].astype(f32), axis=0)
    query = queries_ref[...].astype(f32)
    norm = jnp.sqrt(jnp.sum(query * query, axis=1, keepdims=True))
    unit = query / norm
    d_unit = got[:1]
    d_queries_ref[...] = (d_unit - unit * jnp.sum(unit * d_unit, axis=1, keepdims=True)) / norm
    d_gain_ref[...] = got[1:] / gain_ref[...]


def shape(dims, dtype=f32):
    return jax.ShapeDtypeStruct(dims, dtype)


def exchange(x):
    count = lax.axis_size("hash")
    order = [(i + count // 2 + 1) % count for i in range(count)]
    return lax.all_to_all(
        x, "hash", split_axis=0, concat_axis=0, axis_index_groups=[order], tiled=True
    )


def local(passages, queries, gain, candidates, teacher):
    count = lax.axis_size("hash")
    rows, width = passages.shape
    listed = candidates.shape[1]
    gain = gain.reshape(1, width)

    packed = pl.pallas_call(
        pack_kernel,
        out_shape=shape((count, 2, width // 2 + 2 * listed), bf16),
        compiler_params=params(48),
        name="pack",
    )(queries, candidates, teacher)
    got = exchange(packed)

    block = 128
    row_block = pl.BlockSpec((block, width), lambda i: (i, 0))
    held = pltpu.VMEM((rows, width), bf16)
    sems = pltpu.SemaphoreType.DMA((chunks,))
    table, norms = pl.pallas_call(
        table_kernel,
        in_specs=[outside(), whole()],
        out_specs=[outside(), whole()],
        out_shape=[shape((5 * rows, width), bf16), shape((1, rows))],
        scratch_shapes=[held, held, sems, sems],
        compiler_params=params(60),
        name="table",
        cost_estimate=pl.CostEstimate(
            flops=6 * rows * width, bytes_accessed=4 * rows * width, transcendentals=0
        ),
    )(passages, gain)

    start = (lax.axis_index("hash") * rows).astype(jnp.int32).reshape(1)
    small = shape((count, rows))
    cos, weight, teach, sums, unit = pl.pallas_call(
        score_kernel,
        in_specs=[whole(), pl.BlockSpec(memory_space=pltpu.SMEM), outside()],
        out_shape=[small, small, small, shape((count, 1, count)), shape((count, width), bf16)],
        scratch_shapes=[held, sems],
        compiler_params=params(48),
        name="score",
    )(got, start, table)
    got_sums = exchange(sums)

    wide = shape((count, width))
    by_weight, by_teach, gain_weight, gain_teach = pl.pallas_call(
        mix_kernel,
        in_specs=[whole(), whole(), whole(), whole(), outside()],
        out_shape=[wide, wide, wide, shape((1, width))],
        scratch_shapes=[held, sems],
        compiler_params=params(48),
        name="mix",
        cost_estimate=pl.CostEstimate(
            flops=16 * count * rows * width, bytes_accessed=2 * rows * width, transcendentals=0
        ),
    )(unit, cos, weight, teach, table)

    partial, inverse = pl.pallas_call(
        partial_kernel,
        out_shape=[shape((count, 2, width), bf16), shape((count, 1))],
        compiler_params=params(48),
        name="partial",
    )(got_sums, by_weight, by_teach, gain_weight, gain_teach)
    got_partial = exchange(partial)

    block = rows // chunks
    fixed = lambda dims: pl.BlockSpec(dims, lambda i: (0, 0))
    cols = pl.BlockSpec((count, block), lambda i: (0, i))
    d_passages = pl.pallas_call(
        passage_kernel,
        grid=(rows // block,),
        in_specs=[
            fixed((count, width)),
            fixed((1, width)),
            cols,
            cols,
            cols,
            fixed((count, 1)),
            pl.BlockSpec((1, block), lambda i: (0, i)),
            outside(),
        ],
        out_specs=pl.BlockSpec((block, width), lambda i: (i, 0)),
        out_shape=shape((rows, width)),
        scratch_shapes=[held, sems],
        compiler_params=params(48),
        name="d_passages",
        cost_estimate=pl.CostEstimate(
            flops=4 * count * rows * width, bytes_accessed=6 * rows * width, transcendentals=0
        ),
    )(unit, gain, cos, weight, teach, inverse, norms, table)

    d_queries, d_gain = pl.pallas_call(
        final_kernel,
        out_shape=[shape((1, width)), shape((1, width))],
        compiler_params=params(48),
        name="final",
    )(got_partial, queries, gain)
    return (d_passages, d_queries, d_gain.reshape(width))


def solution(mesh):
    in_specs = (
        P(("groups", "hash"), None),
        P(("groups", "hash"), None),
        P(),
        P(("groups", "hash"), None),
        P(("groups", "hash"), None),
    )
    out_specs = (P(("groups", "hash"), None), P(("groups", "hash"), None), P("groups"))
    return jax.shard_map(local, mesh=mesh, in_specs=in_specs, out_specs=out_specs, check_vma=False)
```

```python
import functools

import jax
import jax.numpy as jnp
from jax import lax
from jax.experimental import pallas as pl
from jax.experimental.pallas import tpu as pltpu
from jax.sharding import PartitionSpec as P

score_scale = 20.0
loss_scale = 8192.0
teacher_div = 2.0
coef_scale = loss_scale * score_scale
chunks = 4
pieces = 8
f32 = jnp.float32
bf16 = jnp.bfloat16
vmem = pltpu.VMEM
nt_dims = (((1,), (1,)), ((), ()))
nn_dims = (((1,), (0,)), ((), ()))


def dot(a, b, dims):
    return lax.dot_general(a, b, dims, preferred_element_type=f32)


def split(x):
    high = x.astype(bf16)
    low = (x - high.astype(f32)).astype(bf16)
    return high, low


def params(megabytes):
    return pltpu.CompilerParams(vmem_limit_bytes=megabytes * 1024 * 1024)


def whole():
    return pl.BlockSpec(memory_space=vmem)


def outside():
    return pl.BlockSpec(memory_space=pltpu.HBM)


def pack_kernel(queries_ref, candidates_ref, teacher_ref, out_ref):
    ids = candidates_ref[...]
    listed = ids.shape[1]
    width = queries_ref.shape[1] // 8
    query = queries_ref[...].astype(f32)
    query = jnp.concatenate([query[:, k * width : (k + 1) * width] for k in range(8)], axis=0)
    lists = [(ids >> 8).astype(f32), (ids & 255).astype(f32), teacher_ref[...].astype(f32)]
    lists = jnp.concatenate([*lists, jnp.zeros((5, listed), f32)], axis=0)
    both = jnp.concatenate([query, lists], axis=1).astype(bf16)
    out_ref[...] = jnp.broadcast_to(both[None], out_ref.shape)


def table_kernel(passages_ref, gain_ref, table_ref, inverse_ref, raw, held, sems_in, sems_out):
    gain = gain_ref[...]
    chunk = raw.shape[0] // pieces
    copies_in, copies_out, inverses = [], [], []
    for k in range(pieces):
        part = pl.ds(k * chunk, chunk)
        copies_in.append(pltpu.make_async_copy(passages_ref.at[part], raw.at[part], sems_in.at[k]))
        copies_out.append(pltpu.make_async_copy(held.at[part], table_ref.at[part], sems_out.at[k]))
        copies_in[-1].start()
    for k in range(pieces):
        part = pl.ds(k * chunk, chunk)
        copies_in[k].wait()
        lifted = raw[part, :].astype(f32) * gain
        norm = jnp.sqrt(jnp.sum(lifted * lifted, axis=1, keepdims=True))
        inverse = 1.0 / norm
        held[part, :] = (lifted * inverse).astype(bf16)
        copies_out[k].start()
        inverses.append(inverse)
    inverse = jnp.concatenate(inverses, axis=0)
    inverse_ref[...] = jnp.transpose(jnp.broadcast_to(inverse, (inverse.shape[0], 128)))[:1, :]
    for k in range(pieces):
        copies_out[k].wait()


def score_kernel(
    got_ref, start_ref, table_ref, cos_ref, weight_ref, teach_ref, sums_ref, unit_ref, held, wide, sems
):
    queries = unit_ref.shape[0]
    rows, width = held.shape
    chunk = width // chunks
    copies = []
    for k in range(chunks):
        part = pl.ds(k * chunk, chunk)
        copies.append(
            pltpu.make_async_copy(table_ref.at[pl.ds(0, rows), part], held.at[:, part], sems.at[k])
        )
        copies[-1].start()
    listed = wide.shape[2]
    tiles = wide.shape[0]
    for j in range(tiles):
        wide[j] = got_ref[:, j * listed : (j + 1) * listed].astype(f32)
    every = [[wide[j, pl.ds(k, queries, stride=8), :] for j in range(tiles)] for k in range(8)]
    query = jnp.concatenate([x for row in every for x in row[:-1]], axis=1)
    norm = jnp.sqrt(jnp.sum(query * query, axis=1, keepdims=True))
    unit = query / norm
    unit_ref[...] = unit.astype(bf16)
    flipped = jnp.transpose(unit).astype(bf16)
    ids = (every[0][-1] * 256.0 + every[1][-1]).astype(jnp.int32)
    marks = jnp.exp(every[2][-1] * (1.0 / teacher_div))
    marks = marks / jnp.sum(marks, axis=1, keepdims=True)
    here = ids - start_ref[0]
    places = lax.broadcasted_iota(jnp.int32, (queries, rows), 1)
    teach = jnp.zeros((queries, rows), f32)
    for c in range(listed):
        teach = teach + jnp.where(here[:, c : c + 1] == places, marks[:, c : c + 1], 0.0)
    teach_ref[...] = teach
    cos = jnp.zeros((rows, queries), f32)
    for k in range(chunks):
        copies[k].wait()
        part = slice(k * chunk, (k + 1) * chunk)
        cos = cos + dot(held[:, part], flipped[part, :], nn_dims)
    cos = jnp.transpose(cos)
    cos_ref[...] = cos
    weight = jnp.where(teach > 0.0, jnp.exp(cos * score_scale), 0.0)
    weight_ref[...] = weight
    total = jnp.sum(weight, axis=1, keepdims=True)
    flipped = jnp.transpose(jnp.broadcast_to(total, (queries, 128)))[:1, :queries]
    sums_ref[...] = jnp.broadcast_to(flipped[None], sums_ref.shape)


def mix_kernel(
    unit_ref, cos_ref, weight_ref, teach_ref, table_ref,
    by_weight_ref, by_teach_ref, gain_weight_ref, gain_teach_ref, held, sems,
):
    queries = unit_ref.shape[0]
    chunk = table_ref.shape[1] // chunks
    copies = []
    for k in range(chunks):
        part = pl.ds(k * chunk, chunk)
        copies.append(pltpu.make_async_copy(table_ref.at[pl.ds(0, held.shape[0]), part], held.at[:, part], sems.at[k]))
        copies[-1].start()
    weight, teach, cos = weight_ref[...], teach_ref[...], cos_ref[...]
    plain = jnp.concatenate([*split(weight), *split(teach)], axis=0)
    scored = jnp.concatenate([*split(weight * cos), *split(teach * cos)], axis=0)
    for k in range(chunks):
        copies[k].wait()
        part = pl.ds(k * chunk, chunk)
        table = held[:, part]
        mixed = dot(plain, table, nn_dims)
        by_weight = mixed[:queries] + mixed[queries : 2 * queries]
        by_teach = mixed[2 * queries : 3 * queries] + mixed[3 * queries :]
        table = table.astype(f32)
        along = dot(scored, (table * table).astype(bf16), nn_dims)
        unit = unit_ref[:, part].astype(f32)
        by_weight_ref[:, part] = by_weight
        by_teach_ref[:, part] = by_teach
        gain_weight_ref[:, part] = unit * by_weight - (along[:queries] + along[queries : 2 * queries])
        terms = unit * by_teach - (along[2 * queries : 3 * queries] + along[3 * queries :])
        gain_teach_ref[:, part] = jnp.sum(terms, axis=0, keepdims=True)


def partial_kernel(sums_ref, by_weight_ref, by_teach_ref, gain_weight_ref, gain_teach_ref, out_ref, inverse_ref):
    queries = by_weight_ref.shape[0]
    total = jnp.sum(sums_ref[...][:, 0, :], axis=0, keepdims=True)
    inverse = jnp.transpose(jnp.broadcast_to(1.0 / total, (128, queries)))[:, :1]
    inverse_ref[...] = inverse
    partial = coef_scale * (by_weight_ref[...] * inverse - by_teach_ref[...])
    gain_part = jnp.sum(gain_weight_ref[...] * inverse, axis=0, keepdims=True) - gain_teach_ref[...]
    gain_part = coef_scale * gain_part
    out_ref[...] = jnp.concatenate(
        [partial[:, None, :], jnp.broadcast_to(gain_part[None], (queries, 1, partial.shape[1]))], axis=1
    ).astype(bf16)


def passage_kernel(
    unit_ref, gain_ref, cos_ref, weight_ref, teach_ref, inverse_ref, norm_ref, table_ref,
    out_ref, held, made, sems_in, sems_out,
):
    rows = held.shape[0]
    piece = rows // pieces
    parts = [pl.ds(k * piece, piece) for k in range(pieces)]
    copies_in = [
        pltpu.make_async_copy(table_ref.at[part], held.at[part], sems_in.at[k])
        for k, part in enumerate(parts)
    ]
    copies_out = [
        pltpu.make_async_copy(made.at[part], out_ref.at[part], sems_out.at[k])
        for k, part in enumerate(parts)
    ]
    for copy in copies_in:
        copy.start()
    coef = coef_scale * (weight_ref[...] * inverse_ref[...] - teach_ref[...])
    scaled = coef * norm_ref[...]
    along = jnp.sum(scaled * cos_ref[...], axis=0, keepdims=True)
    column = jnp.transpose(jnp.broadcast_to(along, (128, rows)))[:, :1]
    left = jnp.concatenate(split(jnp.transpose(scaled)), axis=1)
    right = jnp.concatenate([unit_ref[...], unit_ref[...]], axis=0)
    gain = gain_ref[...]
    for k, part in enumerate(parts):
        inside = slice(k * piece, (k + 1) * piece)
        mixed = dot(left[inside], right, nn_dims)
        copies_in[k].wait()
        made[part, :] = (mixed - held[part, :].astype(f32) * column[inside]) * gain
        copies_out[k].start()
    for copy in copies_out:
        copy.wait()


def final_kernel(got_ref, queries_ref, gain_ref, d_queries_ref, d_gain_ref):
    got = jnp.sum(got_ref[...].astype(f32), axis=0)
    query = queries_ref[...].astype(f32)
    norm = jnp.sqrt(jnp.sum(query * query, axis=1, keepdims=True))
    unit = query / norm
    d_unit = got[:1]
    d_queries_ref[...] = (d_unit - unit * jnp.sum(unit * d_unit, axis=1, keepdims=True)) / norm
    d_gain_ref[...] = got[1:] / gain_ref[...]


def shape(dims, dtype=f32):
    return jax.ShapeDtypeStruct(dims, dtype)


def exchange(x):
    count = lax.axis_size("hash")
    order = [(i + count // 2 + 1) % count for i in range(count)]
    return lax.all_to_all(
        x, "hash", split_axis=0, concat_axis=0, axis_index_groups=[order], tiled=True
    )


def local(passages, queries, gain, candidates, teacher):
    count = lax.axis_size("hash")
    rows, width = passages.shape
    listed = candidates.shape[1]
    gain = gain.reshape(1, width)

    packed = pl.pallas_call(
        pack_kernel,
        out_shape=shape((count, 8, width // 8 + listed), bf16),
        compiler_params=params(60),
        name="pack",
    )(queries, candidates, teacher)
    got = exchange(packed).reshape(count * 8, width // 8 + listed)

    held = pltpu.VMEM((rows, width), bf16)
    sems = pltpu.SemaphoreType.DMA((chunks,))
    many = pltpu.SemaphoreType.DMA((pieces,))
    table, norms = pl.pallas_call(
        table_kernel,
        in_specs=[outside(), whole()],
        out_specs=[outside(), whole()],
        out_shape=[shape((5 * rows, width), bf16), shape((1, rows))],
        scratch_shapes=[held, held, many, many],
        compiler_params=params(60),
        name="table",
        cost_estimate=pl.CostEstimate(
            flops=6 * rows * width, bytes_accessed=4 * rows * width, transcendentals=0
        ),
    )(passages, gain)

    start = (lax.axis_index("hash") * rows).astype(jnp.int32).reshape(1)
    small = shape((count, rows))
    cos, weight, teach, sums, unit = pl.pallas_call(
        score_kernel,
        in_specs=[whole(), pl.BlockSpec(memory_space=pltpu.SMEM), outside()],
        out_shape=[small, small, small, shape((count, 1, count)), shape((count, width), bf16)],
        scratch_shapes=[held, pltpu.VMEM((width // 8 // listed + 1, count * 8, listed), f32), sems],
        compiler_params=params(48),
        name="score",
    )(got, start, table)
    got_sums = exchange(sums)

    wide = shape((count, width))
    by_weight, by_teach, gain_weight, gain_teach = pl.pallas_call(
        mix_kernel,
        in_specs=[whole(), whole(), whole(), whole(), outside()],
        out_shape=[wide, wide, wide, shape((1, width))],
        scratch_shapes=[held, sems],
        compiler_params=params(48),
        name="mix",
        cost_estimate=pl.CostEstimate(
            flops=16 * count * rows * width, bytes_accessed=2 * rows * width, transcendentals=0
        ),
    )(unit, cos, weight, teach, table)

    partial, inverse = pl.pallas_call(
        partial_kernel,
        out_shape=[shape((count, 2, width), bf16), shape((count, 1))],
        compiler_params=params(48),
        name="partial",
    )(got_sums, by_weight, by_teach, gain_weight, gain_teach)
    got_partial = exchange(partial)

    d_passages = pl.pallas_call(
        passage_kernel,
        in_specs=[whole()] * 7 + [outside()],
        out_specs=outside(),
        out_shape=shape((rows, width)),
        scratch_shapes=[held, pltpu.VMEM((rows, width), f32), many, many],
        compiler_params=params(48),
        name="d_passages",
        cost_estimate=pl.CostEstimate(
            flops=4 * count * rows * width, bytes_accessed=6 * rows * width, transcendentals=0
        ),
    )(unit, gain, cos, weight, teach, inverse, norms, table)

    d_queries, d_gain = pl.pallas_call(
        final_kernel,
        out_shape=[shape((1, width)), shape((1, width))],
        compiler_params=params(48),
        name="final",
    )(got_partial, queries, gain)
    return (d_passages, d_queries, d_gain.reshape(width))


def solution(mesh):
    in_specs = (
        P(("groups", "hash"), None),
        P(("groups", "hash"), None),
        P(),
        P(("groups", "hash"), None),
        P(("groups", "hash"), None),
    )
    out_specs = (P(("groups", "hash"), None), P(("groups", "hash"), None), P("groups"))
    return jax.shard_map(local, mesh=mesh, in_specs=in_specs, out_specs=out_specs, check_vma=False)
```

```python
import functools

import jax
import jax.numpy as jnp
from jax import lax
from jax.experimental import pallas as pl
from jax.experimental.pallas import tpu as pltpu
from jax.sharding import PartitionSpec as P

score_scale = 20.0
loss_scale = 8192.0
teacher_div = 2.0
coef_scale = loss_scale * score_scale
chunks = 4
pieces = 8
f32 = jnp.float32
bf16 = jnp.bfloat16
vmem = pltpu.VMEM
nt_dims = (((1,), (1,)), ((), ()))
nn_dims = (((1,), (0,)), ((), ()))


def dot(a, b, dims):
    return lax.dot_general(a, b, dims, preferred_element_type=f32)


def split(x):
    high = x.astype(bf16)
    low = (x - high.astype(f32)).astype(bf16)
    return high, low


def member_order(count):
    return [(i + count // 2 + 1) % count for i in range(count)]


def params(megabytes):
    return pltpu.CompilerParams(vmem_limit_bytes=megabytes * 1024 * 1024)


def whole():
    return pl.BlockSpec(memory_space=vmem)


def outside():
    return pl.BlockSpec(memory_space=pltpu.HBM)


def pack_kernel(rows, queries_ref, candidates_ref, teacher_ref, out_ref):
    ids = candidates_ref[...]
    listed = ids.shape[1]
    count = out_ref.shape[0]
    width = queries_ref.shape[1] // 8
    query = queries_ref[...].astype(f32)
    query = jnp.concatenate([query[:, k * width : (k + 1) * width] for k in range(8)], axis=0)
    owner = lax.div(ids, rows)
    inside = ids - owner * rows
    marks = jnp.exp(teacher_ref[...].astype(f32) * (1.0 / teacher_div))
    marks = marks / jnp.sum(marks, axis=1, keepdims=True)
    high, low = split(marks)
    values = jnp.concatenate(
        [
            (inside >> 8).astype(f32),
            (inside & 255).astype(f32),
            high.astype(f32),
            low.astype(f32),
            jnp.zeros((4, listed), f32),
        ],
        axis=0,
    )
    square = (listed, listed)
    across = jnp.broadcast_to(owner.astype(f32), square)
    down = jnp.transpose(across)
    lane = lax.broadcasted_iota(jnp.int32, square, 1)
    earlier = (across == down) & (lane < lax.broadcasted_iota(jnp.int32, square, 0))
    rank = jnp.sum(jnp.where(earlier, 1.0, 0.0), axis=1, keepdims=True)
    places = jnp.where(rank == lane.astype(f32), 1.0, 0.0).astype(bf16)
    spread = jnp.concatenate(
        [jnp.where(owner == k, values, 0.0).astype(bf16) for k in member_order(count)], axis=0
    )
    lists = dot(spread, places, nn_dims).reshape(count, 8, listed)
    out_ref[:, :, :width] = jnp.broadcast_to(query.astype(bf16)[None], (count, 8, width))
    out_ref[:, :, width:] = lists.astype(bf16)


def table_kernel(passages_ref, gain_ref, table_ref, inverse_ref, raw, held, sems_in, sems_out):
    gain = gain_ref[...]
    chunk = raw.shape[0] // pieces
    copies_in, copies_out, inverses = [], [], []
    for k in range(pieces):
        part = pl.ds(k * chunk, chunk)
        copies_in.append(pltpu.make_async_copy(passages_ref.at[part], raw.at[part], sems_in.at[k]))
        copies_out.append(pltpu.make_async_copy(held.at[part], table_ref.at[part], sems_out.at[k]))
        copies_in[-1].start()
    for k in range(pieces):
        part = pl.ds(k * chunk, chunk)
        copies_in[k].wait()
        lifted = raw[part, :].astype(f32) * gain
        norm = jnp.sqrt(jnp.sum(lifted * lifted, axis=1, keepdims=True))
        inverse = 1.0 / norm
        held[part, :] = (lifted * inverse).astype(bf16)
        copies_out[k].start()
        inverses.append(inverse)
    inverse = jnp.concatenate(inverses, axis=0)
    inverse_ref[...] = jnp.transpose(jnp.broadcast_to(inverse, (inverse.shape[0], 128)))[:1, :]
    for k in range(pieces):
        copies_out[k].wait()


def score_kernel(
    got_ref, table_ref, cos_ref, weight_ref, teach_ref, sums_ref, unit_ref, held, wide, sems
):
    queries = unit_ref.shape[0]
    rows, width = held.shape
    chunk = width // chunks
    copies = []
    for k in range(chunks):
        part = pl.ds(k * chunk, chunk)
        copies.append(
            pltpu.make_async_copy(table_ref.at[pl.ds(0, rows), part], held.at[:, part], sems.at[k])
        )
        copies[-1].start()
    listed = wide.shape[2]
    tiles = wide.shape[0]
    for j in range(tiles):
        wide[j] = got_ref[:, j * listed : (j + 1) * listed].astype(f32)
    every = [[wide[j, pl.ds(k, queries, stride=8), :] for j in range(tiles)] for k in range(8)]
    query = jnp.concatenate([x for row in every for x in row[:-1]], axis=1)
    norm = jnp.sqrt(jnp.sum(query * query, axis=1, keepdims=True))
    unit = query / norm
    unit_ref[...] = unit.astype(bf16)
    flipped = jnp.transpose(unit).astype(bf16)
    here = (every[0][-1] * 256.0 + every[1][-1]).astype(jnp.int32)
    marks = every[2][-1] + every[3][-1]
    places = lax.broadcasted_iota(jnp.int32, (queries, rows), 1)
    teach = jnp.zeros((queries, rows), f32)
    for c in range(listed // queries):
        teach = teach + jnp.where(here[:, c : c + 1] == places, marks[:, c : c + 1], 0.0)
    teach_ref[...] = teach
    cos = jnp.zeros((rows, queries), f32)
    for k in range(chunks):
        copies[k].wait()
        part = slice(k * chunk, (k + 1) * chunk)
        cos = cos + dot(held[:, part], flipped[part, :], nn_dims)
    cos = jnp.transpose(cos)
    cos_ref[...] = cos
    weight = jnp.where(teach > 0.0, jnp.exp(cos * score_scale), 0.0)
    weight_ref[...] = weight
    total = jnp.sum(weight, axis=1, keepdims=True)
    flipped = jnp.transpose(jnp.broadcast_to(total, (queries, 128)))[:1, :queries]
    sums_ref[...] = jnp.broadcast_to(flipped[None], sums_ref.shape)


def mix_kernel(
    unit_ref, cos_ref, weight_ref, teach_ref, table_ref,
    by_weight_ref, by_teach_ref, gain_weight_ref, gain_teach_ref, held, sems,
):
    queries = unit_ref.shape[0]
    chunk = table_ref.shape[1] // chunks
    copies = []
    for k in range(chunks):
        part = pl.ds(k * chunk, chunk)
        copies.append(pltpu.make_async_copy(table_ref.at[pl.ds(0, held.shape[0]), part], held.at[:, part], sems.at[k]))
        copies[-1].start()
    weight, teach, cos = weight_ref[...], teach_ref[...], cos_ref[...]
    plain = jnp.concatenate([*split(weight), *split(teach)], axis=0)
    scored = jnp.concatenate([*split(weight * cos), *split(teach * cos)], axis=0)
    for k in range(chunks):
        copies[k].wait()
        part = pl.ds(k * chunk, chunk)
        table = held[:, part]
        mixed = dot(plain, table, nn_dims)
        by_weight = mixed[:queries] + mixed[queries : 2 * queries]
        by_teach = mixed[2 * queries : 3 * queries] + mixed[3 * queries :]
        table = table.astype(f32)
        along = dot(scored, (table * table).astype(bf16), nn_dims)
        unit = unit_ref[:, part].astype(f32)
        by_weight_ref[:, part] = by_weight
        by_teach_ref[:, part] = by_teach
        gain_weight_ref[:, part] = unit * by_weight - (along[:queries] + along[queries : 2 * queries])
        terms = unit * by_teach - (along[2 * queries : 3 * queries] + along[3 * queries :])
        gain_teach_ref[:, part] = jnp.sum(terms, axis=0, keepdims=True)


def partial_kernel(
    sums_ref, by_weight_ref, by_teach_ref, gain_weight_ref, gain_teach_ref, out_ref, inverse_ref, laid
):
    queries, width = by_weight_ref.shape
    total = jnp.sum(sums_ref[...][:, 0, :], axis=0, keepdims=True)
    inverse = jnp.transpose(jnp.broadcast_to(1.0 / total, (128, queries)))[:, :1]
    inverse_ref[...] = inverse
    partial = coef_scale * (by_weight_ref[...] * inverse - by_teach_ref[...])
    gain_part = jnp.sum(gain_weight_ref[...] * inverse, axis=0, keepdims=True) - gain_teach_ref[...]
    gain_part = coef_scale * gain_part
    tiles = laid.shape[0]
    for k in range(width // 128):
        row, tile = k // tiles, k % tiles
        part = slice(k * 128, (k + 1) * 128)
        laid[tile, pl.ds(row, queries, stride=8), :] = partial[:, part]
        laid[tile, pl.ds(4 + row, queries, stride=8), :] = jnp.broadcast_to(
            gain_part[:, part], (queries, 128)
        )
    for tile in range(tiles):
        out_ref[:, tile * 128 : (tile + 1) * 128] = laid[tile].astype(bf16)


def passage_kernel(
    unit_ref, gain_ref, cos_ref, weight_ref, teach_ref, inverse_ref, norm_ref, table_ref,
    out_ref, held, made, sems_in, sems_out,
):
    rows = held.shape[0]
    piece = rows // pieces
    parts = [pl.ds(k * piece, piece) for k in range(pieces)]
    copies_in = [
        pltpu.make_async_copy(table_ref.at[part], held.at[part], sems_in.at[k])
        for k, part in enumerate(parts)
    ]
    copies_out = [
        pltpu.make_async_copy(made.at[part], out_ref.at[part], sems_out.at[k])
        for k, part in enumerate(parts)
    ]
    for copy in copies_in:
        copy.start()
    coef = coef_scale * (weight_ref[...] * inverse_ref[...] - teach_ref[...])
    scaled = coef * norm_ref[...]
    along = jnp.sum(scaled * cos_ref[...], axis=0, keepdims=True)
    column = jnp.transpose(jnp.broadcast_to(along, (128, rows)))[:, :1]
    left = jnp.concatenate(split(jnp.transpose(scaled)), axis=1)
    right = jnp.concatenate([unit_ref[...], unit_ref[...]], axis=0)
    gain = gain_ref[...]
    for k, part in enumerate(parts):
        inside = slice(k * piece, (k + 1) * piece)
        mixed = dot(left[inside], right, nn_dims)
        copies_in[k].wait()
        made[part, :] = (mixed - held[part, :].astype(f32) * column[inside]) * gain
        copies_out[k].start()
    for copy in copies_out:
        copy.wait()


def final_kernel(got_ref, queries_ref, gain_ref, d_queries_ref, d_gain_ref):
    got = jnp.sum(got_ref[...].astype(f32), axis=0)
    query = queries_ref[...].astype(f32)
    norm = jnp.sqrt(jnp.sum(query * query, axis=1, keepdims=True))
    unit = query / norm
    d_unit = jnp.concatenate([got[k : k + 1] for k in range(4)], axis=1)
    d_queries_ref[...] = (d_unit - unit * jnp.sum(unit * d_unit, axis=1, keepdims=True)) / norm
    d_gain_ref[...] = jnp.concatenate([got[k : k + 1] for k in range(4, 8)], axis=1) / gain_ref[...]


def shape(dims, dtype=f32):
    return jax.ShapeDtypeStruct(dims, dtype)


def exchange(x):
    order = member_order(lax.axis_size("hash"))
    return lax.all_to_all(
        x, "hash", split_axis=0, concat_axis=0, axis_index_groups=[order], tiled=True
    )


def local(passages, queries, gain, candidates, teacher):
    count = lax.axis_size("hash")
    rows, width = passages.shape
    listed = candidates.shape[1]
    gain = gain.reshape(1, width)

    packed = pl.pallas_call(
        functools.partial(pack_kernel, rows),
        out_shape=shape((count, 8, width // 8 + listed), bf16),
        compiler_params=params(60),
        name="pack",
    )(queries, candidates, teacher)
    got = exchange(packed).reshape(count * 8, width // 8 + listed)

    held = pltpu.VMEM((rows, width), bf16)
    sems = pltpu.SemaphoreType.DMA((chunks,))
    many = pltpu.SemaphoreType.DMA((pieces,))
    table, norms = pl.pallas_call(
        table_kernel,
        in_specs=[outside(), whole()],
        out_specs=[outside(), whole()],
        out_shape=[shape((5 * rows, width), bf16), shape((1, rows))],
        scratch_shapes=[held, held, many, many],
        compiler_params=params(60),
        name="table",
        cost_estimate=pl.CostEstimate(
            flops=6 * rows * width, bytes_accessed=4 * rows * width, transcendentals=0
        ),
    )(passages, gain)

    small = shape((count, rows))
    cos, weight, teach, sums, unit = pl.pallas_call(
        score_kernel,
        in_specs=[whole(), outside()],
        out_shape=[small, small, small, shape((count, 1, count)), shape((count, width), bf16)],
        scratch_shapes=[held, pltpu.VMEM((width // 8 // listed + 1, count * 8, listed), f32), sems],
        compiler_params=params(48),
        name="score",
    )(got, table)
    got_sums = exchange(sums)

    wide = shape((count, width))
    by_weight, by_teach, gain_weight, gain_teach = pl.pallas_call(
        mix_kernel,
        in_specs=[whole(), whole(), whole(), whole(), outside()],
        out_shape=[wide, wide, wide, shape((1, width))],
        scratch_shapes=[held, sems],
        compiler_params=params(48),
        name="mix",
        cost_estimate=pl.CostEstimate(
            flops=16 * count * rows * width, bytes_accessed=2 * rows * width, transcendentals=0
        ),
    )(unit, cos, weight, teach, table)

    partial, inverse = pl.pallas_call(
        partial_kernel,
        out_shape=[shape((count * 8, width // 4), bf16), shape((count, 1))],
        scratch_shapes=[pltpu.VMEM((width // 512, count * 8, 128), f32)],
        compiler_params=params(48),
        name="partial",
    )(got_sums, by_weight, by_teach, gain_weight, gain_teach)
    got_partial = exchange(partial.reshape(count, 8, width // 4))

    d_passages = pl.pallas_call(
        passage_kernel,
        in_specs=[whole()] * 7 + [outside()],
        out_specs=outside(),
        out_shape=shape((rows, width)),
        scratch_shapes=[held, pltpu.VMEM((rows, width), f32), many, many],
        compiler_params=params(48),
        name="d_passages",
        cost_estimate=pl.CostEstimate(
            flops=4 * count * rows * width, bytes_accessed=6 * rows * width, transcendentals=0
        ),
    )(unit, gain, cos, weight, teach, inverse, norms, table)

    d_queries, d_gain = pl.pallas_call(
        final_kernel,
        out_shape=[shape((1, width)), shape((1, width))],
        compiler_params=params(48),
        name="final",
    )(got_partial, queries, gain)
    return (d_passages, d_queries, d_gain.reshape(width))


def solution(mesh):
    in_specs = (
        P(("groups", "hash"), None),
        P(("groups", "hash"), None),
        P(),
        P(("groups", "hash"), None),
        P(("groups", "hash"), None),
    )
    out_specs = (P(("groups", "hash"), None), P(("groups", "hash"), None), P("groups"))
    return jax.shard_map(local, mesh=mesh, in_specs=in_specs, out_specs=out_specs, check_vma=False)
```

```python
import functools

import jax
import jax.numpy as jnp
from jax import lax
from jax.experimental import pallas as pl
from jax.experimental.pallas import tpu as pltpu
from jax.sharding import PartitionSpec as P

score_scale = 20.0
loss_scale = 8192.0
teacher_div = 2.0
coef_scale = loss_scale * score_scale
chunks = 4
pieces = 8
f32 = jnp.float32
bf16 = jnp.bfloat16
vmem = pltpu.VMEM
nn_dims = (((1,), (0,)), ((), ()))


def dot(a, b, dims):
    return lax.dot_general(a, b, dims, preferred_element_type=f32)


def split(x):
    high = x.astype(bf16)
    low = (x - high.astype(f32)).astype(bf16)
    return high, low


def member_order(count):
    return [(i + count // 2 + 1) % count for i in range(count)]


def params(megabytes):
    return pltpu.CompilerParams(vmem_limit_bytes=megabytes * 1024 * 1024)


def whole():
    return pl.BlockSpec(memory_space=vmem)


def outside():
    return pl.BlockSpec(memory_space=pltpu.HBM)


def pack_kernel(rows, queries_ref, candidates_ref, teacher_ref, out_ref):
    ids = candidates_ref[...]
    listed = ids.shape[1]
    count = out_ref.shape[0]
    width = queries_ref.shape[1] // 8
    query = queries_ref[...].astype(f32)
    query = jnp.concatenate([query[:, k * width : (k + 1) * width] for k in range(8)], axis=0)
    owner = lax.div(ids, rows)
    inside = ids - owner * rows
    slot = lax.rem(owner + (count - member_order(count)[0]), count)
    marks = jnp.exp(teacher_ref[...].astype(f32) * (1.0 / teacher_div))
    marks = marks / jnp.sum(marks, axis=1, keepdims=True)
    high, low = split(marks)
    values = jnp.concatenate(
        [
            (inside >> 8).astype(f32),
            (inside & 255).astype(f32),
            high.astype(f32),
            low.astype(f32),
            jnp.zeros((listed - 4, listed), f32),
        ],
        axis=0,
    )
    square = (listed, listed)
    across = jnp.broadcast_to(slot.astype(f32), square)
    same = across == jnp.transpose(across)
    earlier = same & (lax.broadcasted_iota(jnp.int32, square, 0) < lax.broadcasted_iota(jnp.int32, square, 1))
    rank = jnp.sum(jnp.where(earlier, 1.0, 0.0), axis=0, keepdims=True)
    place = slot * 8 + rank.astype(jnp.int32)
    spread = jnp.where(place == lax.broadcasted_iota(jnp.int32, (count * 8, listed), 0), 1.0, 0.0)
    lists = dot(spread.astype(bf16), jnp.transpose(values).astype(bf16), nn_dims)
    out_ref[:, :, :width] = jnp.broadcast_to(query.astype(bf16)[None], (count, 8, width))
    out_ref[:, :, width:] = lists.astype(bf16).reshape(count, 8, listed)


def belongs(dims, pair_axis):
    pair = lax.broadcasted_iota(jnp.int32, dims, pair_axis) >> 3
    return pair == lax.broadcasted_iota(jnp.int32, dims, 1 - pair_axis)


def score_kernel(got_ref, gain_ref, passages_ref, raw_ref, unit_ref, cols_ref, rows_ref, sums_ref, held, wide, sems):
    queries, width = unit_ref.shape
    pairs = queries * 8
    rows = held.shape[0]
    chunk = width // chunks
    copies = []
    for k in range(chunks):
        part = pl.ds(k * chunk, chunk)
        copies.append(pltpu.make_async_copy(passages_ref.at[:, part], held.at[:, part], sems.at[k]))
        copies[-1].start()
    tiles = wide.shape[0]
    loaded = [got_ref[:, j * 128 : (j + 1) * 128].astype(f32) for j in range(tiles + 1)]
    squares = sum(x * x for x in loaded[:-1])
    norm = jnp.sum(squares, axis=1, keepdims=True).reshape(queries, 8, 1)
    norm = jnp.sqrt(jnp.broadcast_to(jnp.sum(norm, axis=1, keepdims=True), (queries, 8, 1)))
    norm = norm.reshape(pairs, 1)
    for j in range(tiles):
        wide[j] = loaded[j] / norm
    unit = [wide[j, pl.ds(k, queries, stride=8), :] for k in range(8) for j in range(tiles)]
    unit = jnp.concatenate(unit, axis=1).astype(bf16)
    unit_ref[...] = unit
    lists = loaded[-1]
    inside = lists[:, 0:1] * 256.0 + lists[:, 1:2]
    mark = lists[:, 2:3] + lists[:, 3:4]
    lane = lax.broadcasted_iota(jnp.int32, (pairs, rows), 1).astype(f32)
    pick = jnp.where(inside == lane, 1.0, 0.0).astype(bf16)
    repeat = jnp.where(belongs((pairs, queries), 0), 1.0, 0.0).astype(bf16)
    size = jnp.zeros((pairs, 128), f32)
    along = jnp.zeros((pairs, 128), f32)
    for k in range(chunks):
        part = slice(k * chunk, (k + 1) * chunk)
        repeated = dot(repeat, unit[:, part], nn_dims)
        copies[k].wait()
        raw = dot(pick, held[:, part], nn_dims)
        raw_ref[:, part] = raw.astype(bf16)
        lifted = raw * gain_ref[:, part]
        for j in range(chunk // 128):
            tile = slice(j * 128, (j + 1) * 128)
            size = size + lifted[:, tile] * lifted[:, tile]
            along = along + lifted[:, tile] * repeated[:, tile]
    inverse = 1.0 / jnp.sqrt(jnp.sum(size, axis=1, keepdims=True))
    cos = jnp.sum(along, axis=1, keepdims=True) * inverse
    weight = jnp.where(mark > 0.0, jnp.exp(cos * score_scale), 0.0)
    lane = lax.broadcasted_iota(jnp.int32, (pairs, 128), 1)
    cols = jnp.zeros((pairs, 128), f32)
    for k, column in enumerate((weight, mark, cos, inverse, inside)):
        cols = jnp.where(lane == k, column, cols)
    cols_ref[...] = cols
    flipped = jnp.transpose(cols)[:8]
    rows_ref[...] = flipped
    sums_ref[...] = jnp.broadcast_to(flipped[None, :1], sums_ref.shape)


def mix_kernel(
    unit_ref, gain_ref, raw_ref, cols_ref, rows_ref, by_weight_ref, by_teach_ref, gain_weight_ref, gain_teach_ref
):
    queries, width = unit_ref.shape
    pairs = raw_ref.shape[0]
    chunk = width // chunks
    cos, inverse = cols_ref[:, 2:3], cols_ref[:, 3:4]
    weight, mark = rows_ref[0:1, :], rows_ref[1:2, :]
    own = belongs((queries, pairs), 1)
    by_weight = split(jnp.where(own, weight, 0.0))
    by_mark = split(jnp.where(own, mark, 0.0))
    plain = jnp.concatenate([*by_weight, *by_mark], axis=0)
    repeat = jnp.where(belongs((pairs, queries), 0), 1.0, 0.0).astype(bf16)
    for k in range(chunks):
        part = slice(k * chunk, (k + 1) * chunk)
        row = (raw_ref[:, part].astype(f32) * gain_ref[:, part] * inverse).astype(bf16)
        mixed = dot(plain, row, nn_dims)
        by_weight_ref[:, part] = mixed[:queries] + mixed[queries : 2 * queries]
        by_teach_ref[:, part] = mixed[2 * queries : 3 * queries] + mixed[3 * queries :]
        row = row.astype(f32)
        turned = row * (dot(repeat, unit_ref[:, part], nn_dims) - cos * row)
        mixed = dot(plain, turned.astype(bf16), nn_dims)
        gain_weight_ref[:, part] = mixed[:queries] + mixed[queries : 2 * queries]
        gain_teach_ref[:, part] = jnp.sum(mixed[2 * queries :], axis=0, keepdims=True)


def partial_kernel(sums_ref, by_weight_ref, by_teach_ref, gain_weight_ref, gain_teach_ref, out_ref, laid):
    queries, width = by_weight_ref.shape
    total = jnp.sum(sums_ref[...][:, 0, :], axis=0, keepdims=True)
    own = belongs((queries, total.shape[1]), 1)
    inverse = 1.0 / jnp.sum(jnp.where(own, total, 0.0), axis=1, keepdims=True)
    partial = coef_scale * (by_weight_ref[...] * inverse - by_teach_ref[...])
    gain_part = jnp.sum(gain_weight_ref[...] * inverse, axis=0, keepdims=True) - gain_teach_ref[...]
    gain_part = coef_scale * gain_part
    tiles = laid.shape[0]
    for k in range(width // 128):
        row, tile = k // tiles, k % tiles
        part = slice(k * 128, (k + 1) * 128)
        laid[tile, pl.ds(row, queries, stride=8), :] = partial[:, part]
        laid[tile, pl.ds(4 + row, queries, stride=8), :] = jnp.broadcast_to(
            gain_part[:, part], (queries, 128)
        )
    for tile in range(tiles):
        out_ref[:, tile * 128 : (tile + 1) * 128] = laid[tile].astype(bf16)


def passage_kernel(sums_ref, unit_ref, gain_ref, raw_ref, cols_ref, rows_ref, out_ref, made, sems):
    queries, width = unit_ref.shape
    rows, pairs = made.shape[0], raw_ref.shape[0]
    piece = width // pieces
    weight, mark = cols_ref[:, 0:1], cols_ref[:, 1:2]
    cos, inverse = cols_ref[:, 2:3], cols_ref[:, 3:4]
    total = jnp.sum(sums_ref[...][:, 0, :], axis=0, keepdims=True)
    square = (pairs, pairs)
    alike = (lax.broadcasted_iota(jnp.int32, square, 0) >> 3) == (
        lax.broadcasted_iota(jnp.int32, square, 1) >> 3
    )
    total = jnp.sum(jnp.where(alike, total, 0.0), axis=1, keepdims=True)
    scale = coef_scale * (weight / total - mark) * inverse
    inside = rows_ref[4:5, :]
    spread = lax.broadcasted_iota(jnp.int32, (rows, pairs), 0).astype(f32) == inside
    spread = jnp.where(spread, 1.0, 0.0).astype(bf16)
    spread = jnp.concatenate([spread, spread], axis=1)
    repeat = jnp.where(belongs((pairs, queries), 0), 1.0, 0.0).astype(bf16)
    copies = []
    for k in range(pieces):
        part = slice(k * piece, (k + 1) * piece)
        gain = gain_ref[:, part]
        row = (raw_ref[:, part].astype(f32) * gain * inverse).astype(bf16).astype(f32)
        term = (dot(repeat, unit_ref[:, part], nn_dims) - cos * row) * scale * gain
        made[:, part] = dot(spread, jnp.concatenate(split(term), axis=0), nn_dims)
        part = pl.ds(k * piece, piece)
        copies.append(pltpu.make_async_copy(made.at[:, part], out_ref.at[:, part], sems.at[k]))
        copies[-1].start()
    for copy in copies:
        copy.wait()


def final_kernel(got_ref, queries_ref, gain_ref, d_queries_ref, d_gain_ref):
    got = jnp.sum(got_ref[...].astype(f32), axis=0)
    query = queries_ref[...].astype(f32)
    norm = jnp.sqrt(jnp.sum(query * query, axis=1, keepdims=True))
    unit = query / norm
    d_unit = jnp.concatenate([got[k : k + 1] for k in range(4)], axis=1)
    d_queries_ref[...] = (d_unit - unit * jnp.sum(unit * d_unit, axis=1, keepdims=True)) / norm
    d_gain_ref[...] = jnp.concatenate([got[k : k + 1] for k in range(4, 8)], axis=1) / gain_ref[...]


def shape(dims, dtype=f32):
    return jax.ShapeDtypeStruct(dims, dtype)


def exchange(x):
    order = member_order(lax.axis_size("hash"))
    return lax.all_to_all(
        x, "hash", split_axis=0, concat_axis=0, axis_index_groups=[order], tiled=True
    )


def local(passages, queries, gain, candidates, teacher):
    count = lax.axis_size("hash")
    rows, width = passages.shape
    listed = candidates.shape[1]
    gain = gain.reshape(1, width)

    packed = pl.pallas_call(
        functools.partial(pack_kernel, rows),
        out_shape=shape((count, 8, width // 8 + listed), bf16),
        compiler_params=params(60),
        name="pack",
    )(queries, candidates, teacher)
    got = exchange(packed).reshape(count * 8, width // 8 + listed)

    pairs = count * 8
    raw, unit, cols, lines, sums = pl.pallas_call(
        score_kernel,
        in_specs=[whole(), whole(), outside()],
        out_shape=[
            shape((pairs, width), bf16),
            shape((count, width), bf16),
            shape((pairs, 128)),
            shape((8, pairs)),
            shape((count, 1, pairs)),
        ],
        scratch_shapes=[
            pltpu.VMEM((rows, width), bf16),
            pltpu.VMEM((width // 1024, pairs, 128), f32),
            pltpu.SemaphoreType.DMA((chunks,)),
        ],
        compiler_params=params(57),
        name="score",
    )(got, gain, passages)
    got_sums = exchange(sums)

    wide = shape((count, width))
    by_weight, by_teach, gain_weight, gain_teach = pl.pallas_call(
        mix_kernel,
        out_shape=[wide, wide, wide, shape((1, width))],
        compiler_params=params(48),
        name="mix",
        cost_estimate=pl.CostEstimate(
            flops=16 * count * pairs * width, bytes_accessed=8 * pairs * width, transcendentals=0
        ),
    )(unit, gain, raw, cols, lines)

    partial = pl.pallas_call(
        partial_kernel,
        out_shape=shape((pairs, width // 4), bf16),
        scratch_shapes=[pltpu.VMEM((width // 512, pairs, 128), f32)],
        compiler_params=params(48),
        name="partial",
    )(got_sums, by_weight, by_teach, gain_weight, gain_teach)
    got_partial = exchange(partial.reshape(count, 8, width // 4))

    d_passages = pl.pallas_call(
        passage_kernel,
        in_specs=[whole()] * 6,
        out_specs=outside(),
        out_shape=shape((rows, width)),
        scratch_shapes=[pltpu.VMEM((rows, width), f32), pltpu.SemaphoreType.DMA((pieces,))],
        compiler_params=params(48),
        name="d_passages",
        cost_estimate=pl.CostEstimate(
            flops=4 * pairs * rows * width, bytes_accessed=4 * rows * width, transcendentals=0
        ),
    )(got_sums, unit, gain, raw, cols, lines)

    d_queries, d_gain = pl.pallas_call(
        final_kernel,
        out_shape=[shape((1, width)), shape((1, width))],
        compiler_params=params(48),
        name="final",
    )(got_partial, queries, gain)
    return (d_passages, d_queries, d_gain.reshape(width))


def solution(mesh):
    in_specs = (
        P(("groups", "hash"), None),
        P(("groups", "hash"), None),
        P(),
        P(("groups", "hash"), None),
        P(("groups", "hash"), None),
    )
    out_specs = (P(("groups", "hash"), None), P(("groups", "hash"), None), P("groups"))
    return jax.shard_map(local, mesh=mesh, in_specs=in_specs, out_specs=out_specs, check_vma=False)
```

```python
import functools

import jax
import jax.numpy as jnp
from jax import lax
from jax.experimental import pallas as pl
from jax.experimental.pallas import tpu as pltpu
from jax.sharding import PartitionSpec as P

score_scale = 20.0
loss_scale = 8192.0
teacher_div = 2.0
coef_scale = loss_scale * score_scale
chunks = 4
pieces = 8
f32 = jnp.float32
bf16 = jnp.bfloat16
vmem = pltpu.VMEM
nn_dims = (((1,), (0,)), ((), ()))


def dot(a, b, dims):
    return lax.dot_general(a, b, dims, preferred_element_type=f32)


def split(x):
    high = x.astype(bf16)
    low = (x - high.astype(f32)).astype(bf16)
    return high, low


def member_order(count):
    return [(i + count // 2 + 1) % count for i in range(count)]


def params(megabytes):
    return pltpu.CompilerParams(vmem_limit_bytes=megabytes * 1024 * 1024)


def whole():
    return pl.BlockSpec(memory_space=vmem)


def outside():
    return pl.BlockSpec(memory_space=pltpu.HBM)


def pack_kernel(rows, queries_ref, candidates_ref, teacher_ref, out_ref):
    ids = candidates_ref[...]
    listed = ids.shape[1]
    count = out_ref.shape[0]
    width = queries_ref.shape[1] // 8
    query = queries_ref[...].astype(f32)
    query = jnp.concatenate([query[:, k * width : (k + 1) * width] for k in range(8)], axis=0)
    owner = lax.div(ids, rows)
    inside = ids - owner * rows
    slot = lax.rem(owner + (count - member_order(count)[0]), count)
    marks = jnp.exp(teacher_ref[...].astype(f32) * (1.0 / teacher_div))
    marks = marks / jnp.sum(marks, axis=1, keepdims=True)
    high, low = split(marks)
    values = jnp.concatenate(
        [
            (inside >> 8).astype(f32),
            (inside & 255).astype(f32),
            high.astype(f32),
            low.astype(f32),
            jnp.zeros((listed - 4, listed), f32),
        ],
        axis=0,
    )
    square = (listed, listed)
    across = jnp.broadcast_to(slot.astype(f32), square)
    same = across == jnp.transpose(across)
    earlier = same & (lax.broadcasted_iota(jnp.int32, square, 0) < lax.broadcasted_iota(jnp.int32, square, 1))
    rank = jnp.sum(jnp.where(earlier, 1.0, 0.0), axis=0, keepdims=True)
    place = slot * 8 + rank.astype(jnp.int32)
    spread = jnp.where(place == lax.broadcasted_iota(jnp.int32, (count * 8, listed), 0), 1.0, 0.0)
    lists = dot(spread.astype(bf16), jnp.transpose(values).astype(bf16), nn_dims)
    out_ref[:, :, :width] = jnp.broadcast_to(query.astype(bf16)[None], (count, 8, width))
    out_ref[:, :, width:] = lists.astype(bf16).reshape(count, 8, listed)


def belongs(dims, pair_axis):
    pair = lax.broadcasted_iota(jnp.int32, dims, pair_axis) >> 3
    return pair == lax.broadcasted_iota(jnp.int32, dims, 1 - pair_axis)


def stage_kernel(passages_ref, near_ref, far_ref, sems):
    rows, width = near_ref.shape
    half = rows // 2
    copies = []
    for k in range(2):
        part = pl.ds(k * half, half)
        near = passages_ref.at[part, pl.ds(0, width)]
        far = passages_ref.at[part, pl.ds(width, width)]
        copies.append(pltpu.make_async_copy(near, near_ref.at[part], sems.at[2 * k]))
        copies.append(pltpu.make_async_copy(far, far_ref.at[part], sems.at[2 * k + 1]))
    for copy in copies:
        copy.start()
    for copy in copies:
        copy.wait()


def score_kernel(
    got_ref, gain_ref, near_ref, far_ref, raw_ref, unit_ref, cols_ref, rows_ref, sums_ref, held, wide, sems
):
    queries, width = unit_ref.shape
    pairs = queries * 8
    rows = held.shape[0]
    chunk = width // chunks
    half = chunks // 2
    copies = []
    for k in range(half):
        part = pl.ds(k * chunk, chunk)
        copies.append(pltpu.make_async_copy(far_ref.at[pl.ds(0, rows), part], held.at[:, part], sems.at[k]))
        copies[-1].start()
    tiles = wide.shape[0]
    loaded = [got_ref[:, j * 128 : (j + 1) * 128].astype(f32) for j in range(tiles + 1)]
    squares = sum(x * x for x in loaded[:-1])
    norm = jnp.sum(squares, axis=1, keepdims=True).reshape(queries, 8, 1)
    norm = jnp.sqrt(jnp.broadcast_to(jnp.sum(norm, axis=1, keepdims=True), (queries, 8, 1)))
    norm = norm.reshape(pairs, 1)
    for j in range(tiles):
        wide[j] = loaded[j] / norm
    unit = [wide[j, pl.ds(k, queries, stride=8), :] for k in range(8) for j in range(tiles)]
    unit = jnp.concatenate(unit, axis=1).astype(bf16)
    unit_ref[...] = unit
    lists = loaded[-1]
    inside = lists[:, 0:1] * 256.0 + lists[:, 1:2]
    mark = lists[:, 2:3] + lists[:, 3:4]
    lane = lax.broadcasted_iota(jnp.int32, (pairs, rows), 1).astype(f32)
    pick = jnp.where(inside == lane, 1.0, 0.0).astype(bf16)
    repeat = jnp.where(belongs((pairs, queries), 0), 1.0, 0.0).astype(bf16)
    size = jnp.zeros((pairs, 128), f32)
    along = jnp.zeros((pairs, 128), f32)
    for k in range(chunks):
        part = slice(k * chunk, (k + 1) * chunk)
        repeated = dot(repeat, unit[:, part], nn_dims)
        if k < half:
            passages = near_ref[:, part]
        else:
            copies[k - half].wait()
            passages = held[:, slice((k - half) * chunk, (k - half + 1) * chunk)]
        raw = dot(pick, passages, nn_dims)
        raw_ref[:, part] = raw.astype(bf16)
        lifted = raw * gain_ref[:, part]
        for j in range(chunk // 128):
            tile = slice(j * 128, (j + 1) * 128)
            size = size + lifted[:, tile] * lifted[:, tile]
            along = along + lifted[:, tile] * repeated[:, tile]
    inverse = 1.0 / jnp.sqrt(jnp.sum(size, axis=1, keepdims=True))
    cos = jnp.sum(along, axis=1, keepdims=True) * inverse
    weight = jnp.where(mark > 0.0, jnp.exp(cos * score_scale), 0.0)
    lane = lax.broadcasted_iota(jnp.int32, (pairs, 128), 1)
    cols = jnp.zeros((pairs, 128), f32)
    for k, column in enumerate((weight, mark, cos, inverse, inside)):
        cols = jnp.where(lane == k, column, cols)
    cols_ref[...] = cols
    flipped = jnp.transpose(cols)[:8]
    rows_ref[...] = flipped
    sums_ref[...] = jnp.broadcast_to(flipped[None, :1], sums_ref.shape)


def mix_kernel(
    unit_ref, gain_ref, raw_ref, cols_ref, rows_ref, by_weight_ref, by_teach_ref, gain_weight_ref, gain_teach_ref
):
    queries, width = unit_ref.shape
    pairs = raw_ref.shape[0]
    chunk = width // chunks
    cos, inverse = cols_ref[:, 2:3], cols_ref[:, 3:4]
    weight, mark = rows_ref[0:1, :], rows_ref[1:2, :]
    own = belongs((queries, pairs), 1)
    by_weight = split(jnp.where(own, weight, 0.0))
    by_mark = split(jnp.where(own, mark, 0.0))
    plain = jnp.concatenate([*by_weight, *by_mark], axis=0)
    repeat = jnp.where(belongs((pairs, queries), 0), 1.0, 0.0).astype(bf16)
    for k in range(chunks):
        part = slice(k * chunk, (k + 1) * chunk)
        row = (raw_ref[:, part].astype(f32) * gain_ref[:, part] * inverse).astype(bf16)
        mixed = dot(plain, row, nn_dims)
        by_weight_ref[:, part] = mixed[:queries] + mixed[queries : 2 * queries]
        by_teach_ref[:, part] = mixed[2 * queries : 3 * queries] + mixed[3 * queries :]
        row = row.astype(f32)
        turned = row * (dot(repeat, unit_ref[:, part], nn_dims) - cos * row)
        mixed = dot(plain, turned.astype(bf16), nn_dims)
        gain_weight_ref[:, part] = mixed[:queries] + mixed[queries : 2 * queries]
        gain_teach_ref[:, part] = jnp.sum(mixed[2 * queries :], axis=0, keepdims=True)


def partial_kernel(sums_ref, by_weight_ref, by_teach_ref, gain_weight_ref, gain_teach_ref, out_ref, laid):
    queries, width = by_weight_ref.shape
    total = jnp.sum(sums_ref[...][:, 0, :], axis=0, keepdims=True)
    own = belongs((queries, total.shape[1]), 1)
    inverse = 1.0 / jnp.sum(jnp.where(own, total, 0.0), axis=1, keepdims=True)
    partial = coef_scale * (by_weight_ref[...] * inverse - by_teach_ref[...])
    gain_part = jnp.sum(gain_weight_ref[...] * inverse, axis=0, keepdims=True) - gain_teach_ref[...]
    gain_part = coef_scale * gain_part
    tiles = laid.shape[0]
    for k in range(width // 128):
        row, tile = k // tiles, k % tiles
        part = slice(k * 128, (k + 1) * 128)
        laid[tile, pl.ds(row, queries, stride=8), :] = partial[:, part]
        laid[tile, pl.ds(4 + row, queries, stride=8), :] = jnp.broadcast_to(
            gain_part[:, part], (queries, 128)
        )
    for tile in range(tiles):
        out_ref[:, tile * 128 : (tile + 1) * 128] = laid[tile].astype(bf16)


def passage_kernel(sums_ref, unit_ref, gain_ref, raw_ref, cols_ref, rows_ref, out_ref, made, sems):
    queries, width = unit_ref.shape
    rows, pairs = made.shape[0], raw_ref.shape[0]
    piece = width // pieces
    weight, mark = cols_ref[:, 0:1], cols_ref[:, 1:2]
    cos, inverse = cols_ref[:, 2:3], cols_ref[:, 3:4]
    total = jnp.sum(sums_ref[...][:, 0, :], axis=0, keepdims=True)
    square = (pairs, pairs)
    alike = (lax.broadcasted_iota(jnp.int32, square, 0) >> 3) == (
        lax.broadcasted_iota(jnp.int32, square, 1) >> 3
    )
    total = jnp.sum(jnp.where(alike, total, 0.0), axis=1, keepdims=True)
    scale = coef_scale * (weight / total - mark) * inverse
    inside = rows_ref[4:5, :]
    spread = lax.broadcasted_iota(jnp.int32, (rows, pairs), 0).astype(f32) == inside
    spread = jnp.where(spread, 1.0, 0.0).astype(bf16)
    spread = jnp.concatenate([spread, spread], axis=1)
    repeat = jnp.where(belongs((pairs, queries), 0), 1.0, 0.0).astype(bf16)
    copies = []
    for k in range(pieces):
        part = slice(k * piece, (k + 1) * piece)
        gain = gain_ref[:, part]
        row = (raw_ref[:, part].astype(f32) * gain * inverse).astype(bf16).astype(f32)
        term = (dot(repeat, unit_ref[:, part], nn_dims) - cos * row) * scale * gain
        made[:, part] = dot(spread, jnp.concatenate(split(term), axis=0), nn_dims)
        part = pl.ds(k * piece, piece)
        copies.append(pltpu.make_async_copy(made.at[:, part], out_ref.at[:, part], sems.at[k]))
        copies[-1].start()
    for copy in copies:
        copy.wait()


def final_kernel(got_ref, queries_ref, gain_ref, d_queries_ref, d_gain_ref):
    got = jnp.sum(got_ref[...].astype(f32), axis=0)
    query = queries_ref[...].astype(f32)
    norm = jnp.sqrt(jnp.sum(query * query, axis=1, keepdims=True))
    unit = query / norm
    d_unit = jnp.concatenate([got[k : k + 1] for k in range(4)], axis=1)
    d_queries_ref[...] = (d_unit - unit * jnp.sum(unit * d_unit, axis=1, keepdims=True)) / norm
    d_gain_ref[...] = jnp.concatenate([got[k : k + 1] for k in range(4, 8)], axis=1) / gain_ref[...]


def shape(dims, dtype=f32):
    return jax.ShapeDtypeStruct(dims, dtype)


def exchange(x):
    order = member_order(lax.axis_size("hash"))
    return lax.all_to_all(
        x, "hash", split_axis=0, concat_axis=0, axis_index_groups=[order], tiled=True
    )


def local(passages, queries, gain, candidates, teacher):
    count = lax.axis_size("hash")
    rows, width = passages.shape
    listed = candidates.shape[1]
    gain = gain.reshape(1, width)

    packed = pl.pallas_call(
        functools.partial(pack_kernel, rows),
        out_shape=shape((count, 8, width // 8 + listed), bf16),
        compiler_params=params(60),
        name="pack",
    )(queries, candidates, teacher)
    got = exchange(packed).reshape(count * 8, width // 8 + listed)

    pairs = count * 8
    near, far = pl.pallas_call(
        stage_kernel,
        in_specs=[outside()],
        out_specs=[whole(), outside()],
        out_shape=[shape((rows, width // 2), bf16), shape((10 * rows, width // 2), bf16)],
        scratch_shapes=[pltpu.SemaphoreType.DMA((4,))],
        compiler_params=params(48),
        name="stage",
        cost_estimate=pl.CostEstimate(
            flops=0, bytes_accessed=4 * rows * width, transcendentals=0
        ),
    )(passages)
    raw, unit, cols, lines, sums = pl.pallas_call(
        score_kernel,
        in_specs=[whole(), whole(), whole(), outside()],
        out_shape=[
            shape((pairs, width), bf16),
            shape((count, width), bf16),
            shape((pairs, 128)),
            shape((8, pairs)),
            shape((count, 1, pairs)),
        ],
        scratch_shapes=[
            pltpu.VMEM((rows, width // 2), bf16),
            pltpu.VMEM((width // 1024, pairs, 128), f32),
            pltpu.SemaphoreType.DMA((chunks // 2,)),
        ],
        compiler_params=params(48),
        name="score",
    )(got, gain, near, far)
    got_sums = exchange(sums)

    wide = shape((count, width))
    by_weight, by_teach, gain_weight, gain_teach = pl.pallas_call(
        mix_kernel,
        out_shape=[wide, wide, wide, shape((1, width))],
        compiler_params=params(48),
        name="mix",
        cost_estimate=pl.CostEstimate(
            flops=16 * count * pairs * width, bytes_accessed=8 * pairs * width, transcendentals=0
        ),
    )(unit, gain, raw, cols, lines)

    partial = pl.pallas_call(
        partial_kernel,
        out_shape=shape((pairs, width // 4), bf16),
        scratch_shapes=[pltpu.VMEM((width // 512, pairs, 128), f32)],
        compiler_params=params(48),
        name="partial",
    )(got_sums, by_weight, by_teach, gain_weight, gain_teach)
    got_partial = exchange(partial.reshape(count, 8, width // 4))

    d_passages = pl.pallas_call(
        passage_kernel,
        in_specs=[whole()] * 6,
        out_specs=outside(),
        out_shape=shape((rows, width)),
        scratch_shapes=[pltpu.VMEM((rows, width), f32), pltpu.SemaphoreType.DMA((pieces,))],
        compiler_params=params(48),
        name="d_passages",
        cost_estimate=pl.CostEstimate(
            flops=4 * pairs * rows * width, bytes_accessed=4 * rows * width, transcendentals=0
        ),
    )(got_sums, unit, gain, raw, cols, lines)

    d_queries, d_gain = pl.pallas_call(
        final_kernel,
        out_shape=[shape((1, width)), shape((1, width))],
        compiler_params=params(48),
        name="final",
    )(got_partial, queries, gain)
    return (d_passages, d_queries, d_gain.reshape(width))


def solution(mesh):
    in_specs = (
        P(("groups", "hash"), None),
        P(("groups", "hash"), None),
        P(),
        P(("groups", "hash"), None),
        P(("groups", "hash"), None),
    )
    out_specs = (P(("groups", "hash"), None), P(("groups", "hash"), None), P("groups"))
    return jax.shard_map(local, mesh=mesh, in_specs=in_specs, out_specs=out_specs, check_vma=False)
```

```python
import functools

import jax
import jax.numpy as jnp
from jax import lax
from jax.experimental import pallas as pl
from jax.experimental.pallas import tpu as pltpu
from jax.sharding import PartitionSpec as P

score_scale = 20.0
loss_scale = 8192.0
teacher_div = 2.0
coef_scale = loss_scale * score_scale
chunks = 4
pieces = 8
f32 = jnp.float32
bf16 = jnp.bfloat16
vmem = pltpu.VMEM
nn_dims = (((1,), (0,)), ((), ()))


def dot(a, b, dims):
    return lax.dot_general(a, b, dims, preferred_element_type=f32)


def split(x):
    high = x.astype(bf16)
    low = (x - high.astype(f32)).astype(bf16)
    return high, low


def member_order(count):
    return [(i + count // 2 + 1) % count for i in range(count)]


def params(megabytes):
    return pltpu.CompilerParams(vmem_limit_bytes=megabytes * 1024 * 1024)


def whole():
    return pl.BlockSpec(memory_space=vmem)


def outside():
    return pl.BlockSpec(memory_space=pltpu.HBM)


def pack_kernel(rows, queries_ref, candidates_ref, teacher_ref, out_ref):
    ids = candidates_ref[...]
    listed = ids.shape[1]
    count = out_ref.shape[0]
    width = queries_ref.shape[1] // 8
    query = queries_ref[...].astype(f32)
    query = jnp.concatenate([query[:, k * width : (k + 1) * width] for k in range(8)], axis=0)
    owner = lax.div(ids, rows)
    inside = ids - owner * rows
    slot = lax.rem(owner + (count - member_order(count)[0]), count)
    marks = jnp.exp(teacher_ref[...].astype(f32) * (1.0 / teacher_div))
    marks = marks / jnp.sum(marks, axis=1, keepdims=True)
    high, low = split(marks)
    values = jnp.concatenate(
        [
            (inside >> 8).astype(f32),
            (inside & 255).astype(f32),
            high.astype(f32),
            low.astype(f32),
            jnp.zeros((listed - 4, listed), f32),
        ],
        axis=0,
    )
    square = (listed, listed)
    across = jnp.broadcast_to(slot.astype(f32), square)
    same = across == jnp.transpose(across)
    earlier = same & (lax.broadcasted_iota(jnp.int32, square, 0) < lax.broadcasted_iota(jnp.int32, square, 1))
    rank = jnp.sum(jnp.where(earlier, 1.0, 0.0), axis=0, keepdims=True)
    place = slot * 8 + rank.astype(jnp.int32)
    spread = jnp.where(place == lax.broadcasted_iota(jnp.int32, (count * 8, listed), 0), 1.0, 0.0)
    lists = dot(spread.astype(bf16), jnp.transpose(values).astype(bf16), nn_dims)
    out_ref[:, :, :width] = jnp.broadcast_to(query.astype(bf16)[None], (count, 8, width))
    out_ref[:, :, width:] = lists.astype(bf16).reshape(count, 8, listed)


def belongs(dims, pair_axis):
    pair = lax.broadcasted_iota(jnp.int32, dims, pair_axis) >> 3
    return pair == lax.broadcasted_iota(jnp.int32, dims, 1 - pair_axis)


def stage_kernel(passages_ref, near_ref, far_ref, held, sems_in, sems_out):
    rows, width = near_ref.shape
    piece = rows // chunks
    copies_in, copies_out, copies_near = [], [], []
    for k in range(chunks):
        part = pl.ds(k * piece, piece)
        far = passages_ref.at[part, pl.ds(width, width)]
        near = passages_ref.at[part, pl.ds(0, width)]
        copies_in.append(pltpu.make_async_copy(far, held.at[part], sems_in.at[k]))
        copies_out.append(pltpu.make_async_copy(held.at[part], far_ref.at[part], sems_out.at[k]))
        copies_near.append(pltpu.make_async_copy(near, near_ref.at[part], sems_in.at[chunks + k]))
    for copy in copies_in + copies_near:
        copy.start()
    for k in range(chunks):
        copies_in[k].wait()
        copies_out[k].start()
    for copy in copies_near + copies_out:
        copy.wait()


def score_kernel(
    got_ref, gain_ref, near_ref, far_ref, raw_ref, unit_ref, cols_ref, rows_ref, sums_ref, held, wide, sems
):
    queries, width = unit_ref.shape
    pairs = queries * 8
    rows = held.shape[0]
    chunk = width // chunks
    half = chunks // 2
    copies = []
    for k in range(half):
        part = pl.ds(k * chunk, chunk)
        copies.append(pltpu.make_async_copy(far_ref.at[pl.ds(0, rows), part], held.at[:, part], sems.at[k]))
        copies[-1].start()
    tiles = wide.shape[0]
    loaded = [got_ref[:, j * 128 : (j + 1) * 128].astype(f32) for j in range(tiles + 1)]
    squares = sum(x * x for x in loaded[:-1])
    norm = jnp.sum(squares, axis=1, keepdims=True).reshape(queries, 8, 1)
    norm = jnp.sqrt(jnp.broadcast_to(jnp.sum(norm, axis=1, keepdims=True), (queries, 8, 1)))
    norm = norm.reshape(pairs, 1)
    for j in range(tiles):
        wide[j] = loaded[j] / norm
    unit = [wide[j, pl.ds(k, queries, stride=8), :] for k in range(8) for j in range(tiles)]
    unit = jnp.concatenate(unit, axis=1).astype(bf16)
    unit_ref[...] = unit
    lists = loaded[-1]
    inside = lists[:, 0:1] * 256.0 + lists[:, 1:2]
    mark = lists[:, 2:3] + lists[:, 3:4]
    lane = lax.broadcasted_iota(jnp.int32, (pairs, rows), 1).astype(f32)
    pick = jnp.where(inside == lane, 1.0, 0.0).astype(bf16)
    repeat = jnp.where(belongs((pairs, queries), 0), 1.0, 0.0).astype(bf16)
    size = jnp.zeros((pairs, 128), f32)
    along = jnp.zeros((pairs, 128), f32)
    for k in range(chunks):
        part = slice(k * chunk, (k + 1) * chunk)
        repeated = dot(repeat, unit[:, part], nn_dims)
        if k < half:
            passages = near_ref[:, part]
        else:
            copies[k - half].wait()
            passages = held[:, slice((k - half) * chunk, (k - half + 1) * chunk)]
        raw = dot(pick, passages, nn_dims)
        raw_ref[:, part] = raw.astype(bf16)
        lifted = raw * gain_ref[:, part]
        for j in range(chunk // 128):
            tile = slice(j * 128, (j + 1) * 128)
            size = size + lifted[:, tile] * lifted[:, tile]
            along = along + lifted[:, tile] * repeated[:, tile]
    inverse = 1.0 / jnp.sqrt(jnp.sum(size, axis=1, keepdims=True))
    cos = jnp.sum(along, axis=1, keepdims=True) * inverse
    weight = jnp.where(mark > 0.0, jnp.exp(cos * score_scale), 0.0)
    lane = lax.broadcasted_iota(jnp.int32, (pairs, 128), 1)
    cols = jnp.zeros((pairs, 128), f32)
    for k, column in enumerate((weight, mark, cos, inverse, inside)):
        cols = jnp.where(lane == k, column, cols)
    cols_ref[...] = cols
    flipped = jnp.transpose(cols)[:8]
    rows_ref[...] = flipped
    sums_ref[...] = jnp.broadcast_to(flipped[None, :1], sums_ref.shape)


def mix_kernel(base_ref, unit_ref, gain_ref, raw_ref, cols_ref, rows_ref, out_ref):
    queries = unit_ref.shape[0]
    pairs = raw_ref.shape[0]
    chunk = out_ref.shape[1] // 2
    cos, inverse = cols_ref[:, 2:3], cols_ref[:, 3:4]
    weight, mark = rows_ref[0:1, :], rows_ref[1:2, :]
    own = belongs((queries, pairs), 1)
    by_weight = split(jnp.where(own, weight, 0.0))
    by_mark = split(jnp.where(own, mark, 0.0))
    plain = jnp.concatenate([*by_weight, *by_mark], axis=0)
    repeat = jnp.where(belongs((pairs, queries), 0), 1.0, 0.0).astype(bf16)
    for k in range(2):
        part = slice(k * chunk, (k + 1) * chunk)
        there = pl.ds(pl.multiple_of(base_ref[0] + k * chunk, 128), chunk)
        row = (raw_ref[:, there].astype(f32) * gain_ref[:, there] * inverse).astype(bf16)
        mixed = dot(plain, row, nn_dims)
        out_ref[:queries, part] = mixed[:queries] + mixed[queries : 2 * queries]
        out_ref[queries : 2 * queries, part] = mixed[2 * queries : 3 * queries] + mixed[3 * queries :]
        row = row.astype(f32)
        turned = row * (dot(repeat, unit_ref[:, there], nn_dims) - cos * row)
        mixed = dot(plain, turned.astype(bf16), nn_dims)
        out_ref[2 * queries : 3 * queries, part] = mixed[:queries] + mixed[queries : 2 * queries]
        last = jnp.sum(mixed[2 * queries :], axis=0, keepdims=True)
        out_ref[3 * queries :, part] = jnp.broadcast_to(last, (8, chunk))


def partial_kernel(sums_ref, mine_ref, sibling_ref, out_ref, total_ref, laid):
    queries = sums_ref.shape[2] // 8
    width = mine_ref.shape[1]
    total = jnp.sum(sums_ref[...][:, 0, :], axis=0, keepdims=True)
    total_ref[...] = total
    own = belongs((queries, total.shape[1]), 1)
    inverse = 1.0 / jnp.sum(jnp.where(own, total, 0.0), axis=1, keepdims=True)
    both = mine_ref[...] + sibling_ref[...]
    partial = coef_scale * (both[:queries] * inverse - both[queries : 2 * queries])
    gain_part = jnp.sum(both[2 * queries : 3 * queries] * inverse, axis=0, keepdims=True)
    gain_part = coef_scale * (gain_part - both[3 * queries : 3 * queries + 1])
    tiles = laid.shape[0]
    for k in range(width // 128):
        row, tile = k // tiles, k % tiles
        part = slice(k * 128, (k + 1) * 128)
        laid[tile, pl.ds(row, queries, stride=8), :] = partial[:, part]
        laid[tile, pl.ds(4 + row, queries, stride=8), :] = jnp.broadcast_to(
            gain_part[:, part], (queries, 128)
        )
    for tile in range(tiles):
        out_ref[:, tile * 128 : (tile + 1) * 128] = laid[tile].astype(bf16)


def passage_kernel(total_ref, unit_ref, gain_ref, raw_ref, cols_ref, rows_ref, out_ref, made, sems):
    queries, width = unit_ref.shape
    rows, pairs = made.shape[0], raw_ref.shape[0]
    piece = width // pieces
    weight, mark = cols_ref[:, 0:1], cols_ref[:, 1:2]
    cos, inverse = cols_ref[:, 2:3], cols_ref[:, 3:4]
    square = (pairs, pairs)
    alike = (lax.broadcasted_iota(jnp.int32, square, 0) >> 3) == (
        lax.broadcasted_iota(jnp.int32, square, 1) >> 3
    )
    total = jnp.sum(jnp.where(alike, total_ref[...], 0.0), axis=1, keepdims=True)
    scale = coef_scale * (weight / total - mark) * inverse
    inside = rows_ref[4:5, :]
    spread = lax.broadcasted_iota(jnp.int32, (rows, pairs), 0).astype(f32) == inside
    spread = jnp.where(spread, 1.0, 0.0).astype(bf16)
    spread = jnp.concatenate([spread, spread], axis=1)
    repeat = jnp.where(belongs((pairs, queries), 0), 1.0, 0.0).astype(bf16)
    copies = []
    for k in range(pieces):
        part = slice(k * piece, (k + 1) * piece)
        gain = gain_ref[:, part]
        row = (raw_ref[:, part].astype(f32) * gain * inverse).astype(bf16).astype(f32)
        term = (dot(repeat, unit_ref[:, part], nn_dims) - cos * row) * scale * gain
        made[:, part] = dot(spread, jnp.concatenate(split(term), axis=0), nn_dims)
        part = pl.ds(k * piece, piece)
        copies.append(pltpu.make_async_copy(made.at[:, part], out_ref.at[:, part], sems.at[k]))
        copies[-1].start()
    for copy in copies:
        copy.wait()


def final_kernel(got_ref, queries_ref, gain_ref, d_queries_ref, d_gain_ref):
    count = got_ref.shape[0]
    got = got_ref[...].astype(f32).reshape(count // 2, 2, *got_ref.shape[1:])
    got = jnp.sum(got, axis=0)
    first = member_order(count)[0] % 2
    halves = [got[first], got[1 - first]]
    query = queries_ref[...].astype(f32)
    norm = jnp.sqrt(jnp.sum(query * query, axis=1, keepdims=True))
    unit = query / norm
    d_unit = jnp.concatenate([half[k : k + 1] for half in halves for k in range(4)], axis=1)
    d_queries_ref[...] = (d_unit - unit * jnp.sum(unit * d_unit, axis=1, keepdims=True)) / norm
    d_gain = jnp.concatenate([half[k : k + 1] for half in halves for k in range(4, 8)], axis=1)
    d_gain_ref[...] = d_gain / gain_ref[...]


def shape(dims, dtype=f32):
    return jax.ShapeDtypeStruct(dims, dtype)


def exchange(x):
    order = member_order(lax.axis_size("hash"))
    return lax.all_to_all(
        x, "hash", split_axis=0, concat_axis=0, axis_index_groups=[order], tiled=True
    )


def local(passages, queries, gain, candidates, teacher):
    count = lax.axis_size("hash")
    rows, width = passages.shape
    listed = candidates.shape[1]
    gain = gain.reshape(1, width)

    packed = pl.pallas_call(
        functools.partial(pack_kernel, rows),
        out_shape=shape((count, 8, width // 8 + listed), bf16),
        compiler_params=params(60),
        name="pack",
    )(queries, candidates, teacher)
    got = exchange(packed).reshape(count * 8, width // 8 + listed)

    pairs = count * 8
    near, far = pl.pallas_call(
        stage_kernel,
        in_specs=[outside()],
        out_specs=[whole(), outside()],
        out_shape=[shape((rows, width // 2), bf16), shape((10 * rows, width // 2), bf16)],
        scratch_shapes=[
            pltpu.VMEM((rows, width // 2), bf16),
            pltpu.SemaphoreType.DMA((2 * chunks,)),
            pltpu.SemaphoreType.DMA((chunks,)),
        ],
        compiler_params=params(48),
        name="stage",
        cost_estimate=pl.CostEstimate(
            flops=0, bytes_accessed=4 * rows * width, transcendentals=0
        ),
    )(passages)
    raw, unit, cols, lines, sums = pl.pallas_call(
        score_kernel,
        in_specs=[whole(), whole(), whole(), outside()],
        out_shape=[
            shape((pairs, width), bf16),
            shape((count, width), bf16),
            shape((pairs, 128)),
            shape((8, pairs)),
            shape((count, 1, pairs)),
        ],
        scratch_shapes=[
            pltpu.VMEM((rows, width // 2), bf16),
            pltpu.VMEM((width // 1024, pairs, 128), f32),
            pltpu.SemaphoreType.DMA((chunks // 2,)),
        ],
        compiler_params=params(48),
        name="score",
    )(got, gain, near, far)
    got_sums = exchange(sums)

    half = width // 2

    def mix(base):
        return pl.pallas_call(
            mix_kernel,
            in_specs=[pl.BlockSpec(memory_space=pltpu.SMEM)] + [whole()] * 5,
            out_shape=shape((3 * count + 8, half)),
            compiler_params=params(48),
            name="mix",
            cost_estimate=pl.CostEstimate(
                flops=8 * count * pairs * width, bytes_accessed=4 * pairs * width, transcendentals=0
            ),
        )(base.astype(jnp.int32).reshape(1), unit, gain, raw, cols, lines)

    core = lax.axis_index("hash") % 2
    theirs = mix((1 - core) * half)
    sibling = lax.ppermute(theirs, "hash", [(i, i ^ 1) for i in range(count)])
    mine = mix(core * half)

    partial, total = pl.pallas_call(
        partial_kernel,
        out_shape=[shape((pairs, half // 4), bf16), shape((1, pairs))],
        scratch_shapes=[pltpu.VMEM((half // 512, pairs, 128), f32)],
        compiler_params=params(48),
        name="partial",
    )(got_sums, mine, sibling)
    got_partial = exchange(partial.reshape(count, 8, half // 4))

    d_passages = pl.pallas_call(
        passage_kernel,
        in_specs=[whole()] * 6,
        out_specs=outside(),
        out_shape=shape((rows, width)),
        scratch_shapes=[pltpu.VMEM((rows, width), f32), pltpu.SemaphoreType.DMA((pieces,))],
        compiler_params=params(48),
        name="d_passages",
        cost_estimate=pl.CostEstimate(
            flops=4 * pairs * rows * width, bytes_accessed=4 * rows * width, transcendentals=0
        ),
    )(total, unit, gain, raw, cols, lines)

    d_queries, d_gain = pl.pallas_call(
        final_kernel,
        out_shape=[shape((1, width)), shape((1, width))],
        compiler_params=params(48),
        name="final",
    )(got_partial, queries, gain)
    return (d_passages, d_queries, d_gain.reshape(width))


def solution(mesh):
    in_specs = (
        P(("groups", "hash"), None),
        P(("groups", "hash"), None),
        P(),
        P(("groups", "hash"), None),
        P(("groups", "hash"), None),
    )
    out_specs = (P(("groups", "hash"), None), P(("groups", "hash"), None), P("groups"))
    return jax.shard_map(local, mesh=mesh, in_specs=in_specs, out_specs=out_specs, check_vma=False)
```

```python
import functools

import jax
import jax.numpy as jnp
from jax import lax
from jax.experimental import pallas as pl
from jax.experimental.pallas import tpu as pltpu
from jax.sharding import PartitionSpec as P

score_scale = 20.0
loss_scale = 8192.0
teacher_div = 2.0
coef_scale = loss_scale * score_scale
chunks = 4
f32 = jnp.float32
bf16 = jnp.bfloat16
vmem = pltpu.VMEM
nn_dims = (((1,), (0,)), ((), ()))


def dot(a, b, dims):
    return lax.dot_general(a, b, dims, preferred_element_type=f32)


def split(x):
    high = x.astype(bf16)
    low = (x - high.astype(f32)).astype(bf16)
    return high, low


def member_order(count):
    return [(i + count // 2 + 1) % count for i in range(count)]


def params(megabytes):
    return pltpu.CompilerParams(vmem_limit_bytes=megabytes * 1024 * 1024)


def whole():
    return pl.BlockSpec(memory_space=vmem)


def outside():
    return pl.BlockSpec(memory_space=pltpu.HBM)


def pack_kernel(rows, queries_ref, candidates_ref, teacher_ref, out_ref):
    ids = candidates_ref[...]
    listed = ids.shape[1]
    count = out_ref.shape[0]
    width = queries_ref.shape[1] // 8
    query = queries_ref[...].astype(f32)
    query = jnp.concatenate([query[:, k * width : (k + 1) * width] for k in range(8)], axis=0)
    owner = lax.div(ids, rows)
    inside = ids - owner * rows
    slot = lax.rem(owner + (count - member_order(count)[0]), count)
    marks = jnp.exp(teacher_ref[...].astype(f32) * (1.0 / teacher_div))
    marks = marks / jnp.sum(marks, axis=1, keepdims=True)
    high, low = split(marks)
    values = jnp.concatenate(
        [
            (inside >> 8).astype(f32),
            (inside & 255).astype(f32),
            high.astype(f32),
            low.astype(f32),
            jnp.zeros((listed - 4, listed), f32),
        ],
        axis=0,
    )
    square = (listed, listed)
    across = jnp.broadcast_to(slot.astype(f32), square)
    same = across == jnp.transpose(across)
    earlier = same & (lax.broadcasted_iota(jnp.int32, square, 0) < lax.broadcasted_iota(jnp.int32, square, 1))
    rank = jnp.sum(jnp.where(earlier, 1.0, 0.0), axis=0, keepdims=True)
    place = slot * 8 + rank.astype(jnp.int32)
    spread = jnp.where(place == lax.broadcasted_iota(jnp.int32, (count * 8, listed), 0), 1.0, 0.0)
    lists = dot(spread.astype(bf16), jnp.transpose(values).astype(bf16), nn_dims)
    out_ref[:, :, :width] = jnp.broadcast_to(query.astype(bf16)[None], (count, 8, width))
    out_ref[:, :, width:] = lists.astype(bf16).reshape(count, 8, listed)


def belongs(dims, pair_axis):
    pair = lax.broadcasted_iota(jnp.int32, dims, pair_axis) >> 3
    return pair == lax.broadcasted_iota(jnp.int32, dims, 1 - pair_axis)


def repeated(got_ref, eighth):
    pairs = got_ref.shape[0]
    width = got_ref.shape[1] - 128
    pair = lax.broadcasted_iota(jnp.int32, (pairs, pairs), 0)
    source = lax.broadcasted_iota(jnp.int32, (pairs, pairs), 1)
    pick = jnp.where(source == (pair & -8) + eighth, 1.0, 0.0).astype(bf16)
    return dot(pick, got_ref[:, :width], nn_dims)


def stage_kernel(passages_ref, gain_ref, near_ref, far_ref, gain_out_ref, held, sems_in, sems_out):
    gain_out_ref[...] = gain_ref[...]
    rows, width = near_ref.shape
    piece = rows // chunks
    copies_in, copies_out, copies_near = [], [], []
    for k in range(chunks):
        part = pl.ds(k * piece, piece)
        far = passages_ref.at[part, pl.ds(width, width)]
        near = passages_ref.at[part, pl.ds(0, width)]
        copies_in.append(pltpu.make_async_copy(far, held.at[part], sems_in.at[k]))
        copies_out.append(pltpu.make_async_copy(held.at[part], far_ref.at[part], sems_out.at[k]))
        copies_near.append(pltpu.make_async_copy(near, near_ref.at[part], sems_in.at[chunks + k]))
    for copy in copies_in + copies_near:
        copy.start()
    for k in range(chunks):
        copies_in[k].wait()
        copies_out[k].start()
    for copy in copies_near + copies_out:
        copy.wait()


def score_kernel(got_ref, gain_ref, near_ref, far_ref, raw_ref, cols_ref, rows_ref, sums_ref, held, sems):
    pairs, width = raw_ref.shape
    queries = pairs // 8
    rows = held.shape[0]
    chunk = width // 8
    half = held.shape[1] // chunk
    copies = []
    for k in range(half):
        part = pl.ds(k * chunk, chunk)
        copies.append(pltpu.make_async_copy(far_ref.at[pl.ds(0, rows), part], held.at[:, part], sems.at[k]))
        copies[-1].start()
    lists = got_ref[:, chunk:].astype(f32)
    inside = lists[:, 0:1] * 256.0 + lists[:, 1:2]
    mark = lists[:, 2:3] + lists[:, 3:4]
    lane = lax.broadcasted_iota(jnp.int32, (pairs, rows), 1).astype(f32)
    pick = jnp.where(inside == lane, 1.0, 0.0).astype(bf16)
    size = jnp.zeros((pairs, 128), f32)
    along = jnp.zeros((pairs, 128), f32)
    for k in range(8):
        part = slice(k * chunk, (k + 1) * chunk)
        query = repeated(got_ref, k)
        if k < half:
            passages = near_ref[:, part]
        else:
            copies[k - half].wait()
            passages = held[:, slice((k - half) * chunk, (k - half + 1) * chunk)]
        raw = dot(pick, passages, nn_dims)
        raw_ref[:, part] = raw.astype(bf16)
        lifted = raw * gain_ref[:, part]
        for j in range(chunk // 128):
            tile = slice(j * 128, (j + 1) * 128)
            size = size + lifted[:, tile] * lifted[:, tile]
            along = along + lifted[:, tile] * query[:, tile]
    squares = got_ref[:, :chunk].astype(f32)
    squares = jnp.sum(squares * squares, axis=1, keepdims=True).reshape(queries, 8, 1)
    squares = jnp.broadcast_to(jnp.sum(squares, axis=1, keepdims=True), (queries, 8, 1))
    query_inverse = 1.0 / jnp.sqrt(squares.reshape(pairs, 1))
    inverse = 1.0 / jnp.sqrt(jnp.sum(size, axis=1, keepdims=True))
    cos = jnp.sum(along, axis=1, keepdims=True) * inverse * query_inverse
    weight = jnp.where(mark > 0.0, jnp.exp(cos * score_scale), 0.0)
    lane = lax.broadcasted_iota(jnp.int32, (pairs, 128), 1)
    cols = jnp.zeros((pairs, 128), f32)
    for k, column in enumerate((weight, mark, cos, inverse, inside, query_inverse)):
        cols = jnp.where(lane == k, column, cols)
    cols_ref[...] = cols
    flipped = jnp.transpose(cols)[:8]
    rows_ref[...] = flipped
    sums_ref[...] = jnp.broadcast_to(flipped[None, :1], sums_ref.shape)


def mix_kernel(base_ref, got_ref, gain_ref, raw_ref, cols_ref, rows_ref, out_ref):
    pairs, width = raw_ref.shape
    queries = pairs // 8
    chunk = width // 8
    cos, inverse = cols_ref[:, 2:3], cols_ref[:, 3:4]
    weight, mark = rows_ref[0:1, :], rows_ref[1:2, :]
    own = belongs((queries, pairs), 1)
    by_weight = split(jnp.where(own, weight, 0.0))
    by_mark = split(jnp.where(own, mark, 0.0))
    plain = jnp.concatenate([*by_weight, *by_mark], axis=0)
    for k in range(out_ref.shape[1] // chunk):
        part = slice(k * chunk, (k + 1) * chunk)
        eighth = base_ref[0] + k
        there = pl.ds(pl.multiple_of(eighth * chunk, 128), chunk)
        row = (raw_ref[:, there].astype(f32) * gain_ref[:, there] * inverse).astype(bf16)
        mixed = dot(plain, row, nn_dims)
        out_ref[:queries, part] = mixed[:queries] + mixed[queries : 2 * queries]
        out_ref[queries : 2 * queries, part] = mixed[2 * queries : 3 * queries] + mixed[3 * queries :]
        row = row.astype(f32)
        query = (repeated(got_ref, eighth) * cols_ref[:, 5:6]).astype(bf16).astype(f32)
        turned = row * (query - cos * row)
        mixed = dot(plain, turned.astype(bf16), nn_dims)
        out_ref[2 * queries : 3 * queries, part] = mixed[:queries] + mixed[queries : 2 * queries]
        last = jnp.sum(mixed[2 * queries :], axis=0, keepdims=True)
        out_ref[3 * queries :, part] = jnp.broadcast_to(last, (8, chunk))


def partial_kernel(sums_ref, mine_ref, sibling_ref, out_ref, total_ref, laid):
    queries = sums_ref.shape[2] // 8
    width = mine_ref.shape[1]
    total = jnp.sum(sums_ref[...][:, 0, :], axis=0, keepdims=True)
    total_ref[...] = total
    own = belongs((queries, total.shape[1]), 1)
    inverse = 1.0 / jnp.sum(jnp.where(own, total, 0.0), axis=1, keepdims=True)
    both = mine_ref[...] + sibling_ref[...]
    partial = coef_scale * (both[:queries] * inverse - both[queries : 2 * queries])
    gain_part = jnp.sum(both[2 * queries : 3 * queries] * inverse, axis=0, keepdims=True)
    gain_part = coef_scale * (gain_part - both[3 * queries : 3 * queries + 1])
    tiles = laid.shape[0]
    for k in range(width // 128):
        row, tile = k // tiles, k % tiles
        part = slice(k * 128, (k + 1) * 128)
        laid[tile, pl.ds(row, queries, stride=8), :] = partial[:, part]
        laid[tile, pl.ds(4 + row, queries, stride=8), :] = jnp.broadcast_to(
            gain_part[:, part], (queries, 128)
        )
    for tile in range(tiles):
        out_ref[:, tile * 128 : (tile + 1) * 128] = laid[tile].astype(bf16)


def passage_kernel(total_ref, got_ref, gain_ref, raw_ref, cols_ref, rows_ref, out_ref, made, sems):
    pairs, width = raw_ref.shape
    rows = made.shape[0]
    piece = width // 8
    weight, mark = cols_ref[:, 0:1], cols_ref[:, 1:2]
    cos, inverse = cols_ref[:, 2:3], cols_ref[:, 3:4]
    square = (pairs, pairs)
    alike = (lax.broadcasted_iota(jnp.int32, square, 0) >> 3) == (
        lax.broadcasted_iota(jnp.int32, square, 1) >> 3
    )
    total = jnp.sum(jnp.where(alike, total_ref[...], 0.0), axis=1, keepdims=True)
    scale = coef_scale * (weight / total - mark) * inverse
    inside = rows_ref[4:5, :]
    spread = lax.broadcasted_iota(jnp.int32, (rows, pairs), 0).astype(f32) == inside
    spread = jnp.where(spread, 1.0, 0.0).astype(bf16)
    spread = jnp.concatenate([spread, spread], axis=1)
    copies = []
    for k in range(8):
        part = slice(k * piece, (k + 1) * piece)
        gain = gain_ref[:, part]
        row = (raw_ref[:, part].astype(f32) * gain * inverse).astype(bf16).astype(f32)
        query = (repeated(got_ref, k) * cols_ref[:, 5:6]).astype(bf16).astype(f32)
        term = (query - cos * row) * scale * gain
        made[:, part] = dot(spread, jnp.concatenate(split(term), axis=0), nn_dims)
        part = pl.ds(k * piece, piece)
        copies.append(pltpu.make_async_copy(made.at[:, part], out_ref.at[:, part], sems.at[k]))
        copies[-1].start()
    for copy in copies:
        copy.wait()


def final_kernel(got_ref, queries_ref, gain_ref, d_queries_ref, d_gain_ref):
    count = got_ref.shape[0]
    got = got_ref[...].astype(f32).reshape(count // 2, 2, *got_ref.shape[1:])
    got = jnp.sum(got, axis=0)
    first = member_order(count)[0] % 2
    halves = [got[first], got[1 - first]]
    query = queries_ref[...].astype(f32)
    norm = jnp.sqrt(jnp.sum(query * query, axis=1, keepdims=True))
    unit = query / norm
    d_unit = jnp.concatenate([half[k : k + 1] for half in halves for k in range(4)], axis=1)
    d_queries_ref[...] = (d_unit - unit * jnp.sum(unit * d_unit, axis=1, keepdims=True)) / norm
    d_gain = jnp.concatenate([half[k : k + 1] for half in halves for k in range(4, 8)], axis=1)
    d_gain_ref[...] = d_gain / gain_ref[...]


def shape(dims, dtype=f32):
    return jax.ShapeDtypeStruct(dims, dtype)


def exchange(x):
    order = member_order(lax.axis_size("hash"))
    return lax.all_to_all(
        x, "hash", split_axis=0, concat_axis=0, axis_index_groups=[order], tiled=True
    )


def local(passages, queries, gain, candidates, teacher):
    count = lax.axis_size("hash")
    rows, width = passages.shape
    listed = candidates.shape[1]
    gain = gain.reshape(1, width)

    packed = pl.pallas_call(
        functools.partial(pack_kernel, rows),
        out_shape=shape((count, 8, width // 8 + listed), bf16),
        compiler_params=params(60),
        name="pack",
    )(queries, candidates, teacher)
    got = exchange(packed).reshape(count * 8, width // 8 + listed)

    pairs = count * 8
    near, far, gain_near = pl.pallas_call(
        stage_kernel,
        in_specs=[outside(), whole()],
        out_specs=[whole(), outside(), whole()],
        out_shape=[
            shape((rows, width // 2), bf16),
            shape((10 * rows, width // 2), bf16),
            shape((1, width)),
        ],
        scratch_shapes=[
            pltpu.VMEM((rows, width // 2), bf16),
            pltpu.SemaphoreType.DMA((2 * chunks,)),
            pltpu.SemaphoreType.DMA((chunks,)),
        ],
        compiler_params=params(48),
        name="stage",
        cost_estimate=pl.CostEstimate(
            flops=0, bytes_accessed=4 * rows * width, transcendentals=0
        ),
    )(passages, gain)
    raw, cols, lines, sums = pl.pallas_call(
        score_kernel,
        in_specs=[whole(), whole(), whole(), outside()],
        out_shape=[
            shape((pairs, width), bf16),
            shape((pairs, 128)),
            shape((8, pairs)),
            shape((count, 1, pairs)),
        ],
        scratch_shapes=[
            pltpu.VMEM((rows, width // 2), bf16),
            pltpu.SemaphoreType.DMA((4,)),
        ],
        compiler_params=params(48),
        name="score",
    )(got, gain_near, near, far)
    got_sums = exchange(sums)

    half = width // 2

    def mix(base):
        return pl.pallas_call(
            mix_kernel,
            in_specs=[pl.BlockSpec(memory_space=pltpu.SMEM)] + [whole()] * 5,
            out_shape=shape((3 * count + 8, half)),
            compiler_params=params(48),
            name="mix",
            cost_estimate=pl.CostEstimate(
                flops=8 * count * pairs * width, bytes_accessed=64 * pairs * width, transcendentals=0
            ),
        )(base.astype(jnp.int32).reshape(1), got, gain_near, raw, cols, lines)

    core = lax.axis_index("hash") % 2
    theirs = mix((1 - core) * 4)
    sibling = lax.ppermute(theirs, "hash", [(i, i ^ 1) for i in range(count)])
    mine = mix(core * 4)

    partial, total = pl.pallas_call(
        partial_kernel,
        out_shape=[shape((pairs, half // 4), bf16), shape((1, pairs))],
        scratch_shapes=[pltpu.VMEM((half // 512, pairs, 128), f32)],
        compiler_params=params(48),
        name="partial",
    )(got_sums, mine, sibling)
    got_partial = exchange(partial.reshape(count, 8, half // 4))

    d_passages = pl.pallas_call(
        passage_kernel,
        in_specs=[whole()] * 6,
        out_specs=outside(),
        out_shape=shape((rows, width)),
        scratch_shapes=[pltpu.VMEM((rows, width), f32), pltpu.SemaphoreType.DMA((8,))],
        compiler_params=params(48),
        name="d_passages",
        cost_estimate=pl.CostEstimate(
            flops=4 * pairs * rows * width, bytes_accessed=4 * rows * width, transcendentals=0
        ),
    )(total, got, gain_near, raw, cols, lines)

    d_queries, d_gain = pl.pallas_call(
        final_kernel,
        out_shape=[shape((1, width)), shape((1, width))],
        compiler_params=params(48),
        name="final",
    )(got_partial, queries, gain)
    return (d_passages, d_queries, d_gain.reshape(width))


def solution(mesh):
    in_specs = (
        P(("groups", "hash"), None),
        P(("groups", "hash"), None),
        P(),
        P(("groups", "hash"), None),
        P(("groups", "hash"), None),
    )
    out_specs = (P(("groups", "hash"), None), P(("groups", "hash"), None), P("groups"))
    return jax.shard_map(local, mesh=mesh, in_specs=in_specs, out_specs=out_specs, check_vma=False)
```

```python
import functools

import jax
import jax.numpy as jnp
from jax import lax
from jax.experimental import pallas as pl
from jax.experimental.pallas import tpu as pltpu
from jax.sharding import PartitionSpec as P

score_scale = 20.0
loss_scale = 8192.0
teacher_div = 2.0
coef_scale = loss_scale * score_scale
chunks = 4
pieces = 8
f32 = jnp.float32
bf16 = jnp.bfloat16
vmem = pltpu.VMEM
nn_dims = (((1,), (0,)), ((), ()))


def dot(a, b, dims):
    return lax.dot_general(a, b, dims, preferred_element_type=f32)


def split(x):
    high = x.astype(bf16)
    low = (x - high.astype(f32)).astype(bf16)
    return high, low


def member_order(count):
    return [(i + count // 2 + 1) % count for i in range(count)]


def params(megabytes):
    return pltpu.CompilerParams(vmem_limit_bytes=megabytes * 1024 * 1024)


def whole():
    return pl.BlockSpec(memory_space=vmem)


def outside():
    return pl.BlockSpec(memory_space=pltpu.HBM)


def pack_kernel(rows, queries_ref, candidates_ref, teacher_ref, out_ref):
    ids = candidates_ref[...]
    listed = ids.shape[1]
    count = out_ref.shape[0]
    width = queries_ref.shape[1] // 8
    query = queries_ref[...].astype(f32)
    query = jnp.concatenate([query[:, k * width : (k + 1) * width] for k in range(8)], axis=0)
    owner = lax.div(ids, rows)
    inside = ids - owner * rows
    slot = lax.rem(owner + (count - member_order(count)[0]), count)
    marks = jnp.exp(teacher_ref[...].astype(f32) * (1.0 / teacher_div))
    marks = marks / jnp.sum(marks, axis=1, keepdims=True)
    high, low = split(marks)
    values = jnp.concatenate(
        [
            (inside >> 8).astype(f32),
            (inside & 255).astype(f32),
            high.astype(f32),
            low.astype(f32),
            jnp.zeros((listed - 4, listed), f32),
        ],
        axis=0,
    )
    square = (listed, listed)
    across = jnp.broadcast_to(slot.astype(f32), square)
    same = across == jnp.transpose(across)
    earlier = same & (lax.broadcasted_iota(jnp.int32, square, 0) < lax.broadcasted_iota(jnp.int32, square, 1))
    rank = jnp.sum(jnp.where(earlier, 1.0, 0.0), axis=0, keepdims=True)
    place = slot * 8 + rank.astype(jnp.int32)
    spread = jnp.where(place == lax.broadcasted_iota(jnp.int32, (count * 8, listed), 0), 1.0, 0.0)
    lists = dot(spread.astype(bf16), jnp.transpose(values).astype(bf16), nn_dims)
    out_ref[:, :, :width] = jnp.broadcast_to(query.astype(bf16)[None], (count, 8, width))
    out_ref[:, :, width:] = lists.astype(bf16).reshape(count, 8, listed)


def belongs(dims, pair_axis):
    pair = lax.broadcasted_iota(jnp.int32, dims, pair_axis) >> 3
    return pair == lax.broadcasted_iota(jnp.int32, dims, 1 - pair_axis)


def stage_kernel(passages_ref, gain_ref, near_ref, far_ref, gain_out_ref, held, sems_in, sems_out):
    gain_out_ref[...] = gain_ref[...]
    rows, width = near_ref.shape
    piece = rows // chunks
    copies_in, copies_out, copies_near = [], [], []
    for k in range(chunks):
        part = pl.ds(k * piece, piece)
        far = passages_ref.at[part, pl.ds(width, width)]
        near = passages_ref.at[part, pl.ds(0, width)]
        copies_in.append(pltpu.make_async_copy(far, held.at[part], sems_in.at[k]))
        copies_out.append(pltpu.make_async_copy(held.at[part], far_ref.at[part], sems_out.at[k]))
        copies_near.append(pltpu.make_async_copy(near, near_ref.at[part], sems_in.at[chunks + k]))
    for copy in copies_in + copies_near:
        copy.start()
    for k in range(chunks):
        copies_in[k].wait()
        copies_out[k].start()
    for copy in copies_near + copies_out:
        copy.wait()


def score_kernel(
    got_ref, gain_ref, near_ref, far_ref, raw_ref, query_ref, cols_ref, rows_ref, sums_ref, held, wide, sems
):
    queries, width = query_ref.shape
    pairs = queries * 8
    rows = held.shape[0]
    chunk = width // chunks
    half = chunks // 2
    copies = []
    for k in range(half):
        part = pl.ds(k * chunk, chunk)
        copies.append(pltpu.make_async_copy(far_ref.at[pl.ds(0, rows), part], held.at[:, part], sems.at[k]))
        copies[-1].start()
    tiles = wide.shape[0]
    loaded = [got_ref[:, j * 128 : (j + 1) * 128].astype(f32) for j in range(tiles + 1)]
    for j in range(tiles):
        wide[j] = loaded[j]
    query = [wide[j, pl.ds(k, queries, stride=8), :] for k in range(8) for j in range(tiles)]
    query = jnp.concatenate(query, axis=1).astype(bf16)
    query_ref[...] = query
    lists = loaded[-1]
    inside = lists[:, 0:1] * 256.0 + lists[:, 1:2]
    mark = lists[:, 2:3] + lists[:, 3:4]
    lane = lax.broadcasted_iota(jnp.int32, (pairs, rows), 1).astype(f32)
    pick = jnp.where(inside == lane, 1.0, 0.0).astype(bf16)
    repeat = jnp.where(belongs((pairs, queries), 0), 1.0, 0.0).astype(bf16)
    size = jnp.zeros((pairs, 128), f32)
    along = jnp.zeros((pairs, 128), f32)
    for k in range(chunks):
        part = slice(k * chunk, (k + 1) * chunk)
        repeated = dot(repeat, query[:, part], nn_dims)
        if k < half:
            passages = near_ref[:, part]
        else:
            copies[k - half].wait()
            passages = held[:, slice((k - half) * chunk, (k - half + 1) * chunk)]
        raw = dot(pick, passages, nn_dims)
        raw_ref[:, part] = raw.astype(bf16)
        lifted = raw * gain_ref[:, part]
        for j in range(chunk // 128):
            tile = slice(j * 128, (j + 1) * 128)
            size = size + lifted[:, tile] * lifted[:, tile]
            along = along + lifted[:, tile] * repeated[:, tile]
    inverse = 1.0 / jnp.sqrt(jnp.sum(size, axis=1, keepdims=True))
    squares = sum(x * x for x in loaded[:-1])
    squares = jnp.sum(squares, axis=1, keepdims=True).reshape(queries, 8, 1)
    squares = jnp.broadcast_to(jnp.sum(squares, axis=1, keepdims=True), (queries, 8, 1))
    query_inverse = 1.0 / jnp.sqrt(squares.reshape(pairs, 1))
    cos = jnp.sum(along, axis=1, keepdims=True) * inverse * query_inverse
    weight = jnp.where(mark > 0.0, jnp.exp(cos * score_scale), 0.0)
    lane = lax.broadcasted_iota(jnp.int32, (pairs, 128), 1)
    cols = jnp.zeros((pairs, 128), f32)
    for k, column in enumerate((weight, mark, cos, inverse, inside, query_inverse)):
        cols = jnp.where(lane == k, column, cols)
    cols_ref[...] = cols
    flipped = jnp.transpose(cols)[:8]
    rows_ref[...] = flipped
    sums_ref[...] = jnp.broadcast_to(flipped[None, :1], sums_ref.shape)


def mix_kernel(base_ref, query_ref, gain_ref, raw_ref, cols_ref, rows_ref, out_ref):
    queries = query_ref.shape[0]
    pairs = raw_ref.shape[0]
    chunk = out_ref.shape[1] // 2
    cos, inverse = cols_ref[:, 2:3], cols_ref[:, 3:4]
    weight, mark = rows_ref[0:1, :], rows_ref[1:2, :]
    own = belongs((queries, pairs), 1)
    by_weight = split(jnp.where(own, weight, 0.0))
    by_mark = split(jnp.where(own, mark, 0.0))
    plain = jnp.concatenate([*by_weight, *by_mark], axis=0)
    repeat = jnp.where(belongs((pairs, queries), 0), 1.0, 0.0).astype(bf16)
    for k in range(2):
        part = slice(k * chunk, (k + 1) * chunk)
        there = pl.ds(pl.multiple_of(base_ref[0] + k * chunk, 128), chunk)
        row = (raw_ref[:, there].astype(f32) * gain_ref[:, there] * inverse).astype(bf16)
        mixed = dot(plain, row, nn_dims)
        out_ref[:queries, part] = mixed[:queries] + mixed[queries : 2 * queries]
        out_ref[queries : 2 * queries, part] = mixed[2 * queries : 3 * queries] + mixed[3 * queries :]
        row = row.astype(f32)
        query = dot(repeat, query_ref[:, there], nn_dims) * cols_ref[:, 5:6]
        turned = row * (query.astype(bf16).astype(f32) - cos * row)
        mixed = dot(plain, turned.astype(bf16), nn_dims)
        out_ref[2 * queries : 3 * queries, part] = mixed[:queries] + mixed[queries : 2 * queries]
        last = jnp.sum(mixed[2 * queries :], axis=0, keepdims=True)
        out_ref[3 * queries :, part] = jnp.broadcast_to(last, (8, chunk))


def partial_kernel(sums_ref, mine_ref, sibling_ref, out_ref, total_ref, laid):
    queries = sums_ref.shape[2] // 8
    width = mine_ref.shape[1]
    total = jnp.sum(sums_ref[...][:, 0, :], axis=0, keepdims=True)
    total_ref[...] = total
    own = belongs((queries, total.shape[1]), 1)
    inverse = 1.0 / jnp.sum(jnp.where(own, total, 0.0), axis=1, keepdims=True)
    both = mine_ref[...] + sibling_ref[...]
    partial = coef_scale * (both[:queries] * inverse - both[queries : 2 * queries])
    gain_part = jnp.sum(both[2 * queries : 3 * queries] * inverse, axis=0, keepdims=True)
    gain_part = coef_scale * (gain_part - both[3 * queries : 3 * queries + 1])
    tiles = laid.shape[0]
    for k in range(width // 128):
        row, tile = k // tiles, k % tiles
        part = slice(k * 128, (k + 1) * 128)
        laid[tile, pl.ds(row, queries, stride=8), :] = partial[:, part]
        laid[tile, pl.ds(4 + row, queries, stride=8), :] = jnp.broadcast_to(
            gain_part[:, part], (queries, 128)
        )
    for tile in range(tiles):
        out_ref[:, tile * 128 : (tile + 1) * 128] = laid[tile].astype(bf16)


def passage_kernel(total_ref, query_ref, gain_ref, raw_ref, cols_ref, rows_ref, out_ref, made, sems):
    queries, width = query_ref.shape
    rows, pairs = made.shape[0], raw_ref.shape[0]
    piece = width // pieces
    weight, mark = cols_ref[:, 0:1], cols_ref[:, 1:2]
    cos, inverse = cols_ref[:, 2:3], cols_ref[:, 3:4]
    square = (pairs, pairs)
    alike = (lax.broadcasted_iota(jnp.int32, square, 0) >> 3) == (
        lax.broadcasted_iota(jnp.int32, square, 1) >> 3
    )
    total = jnp.sum(jnp.where(alike, total_ref[...], 0.0), axis=1, keepdims=True)
    scale = coef_scale * (weight / total - mark) * inverse
    inside = rows_ref[4:5, :]
    spread = lax.broadcasted_iota(jnp.int32, (rows, pairs), 0).astype(f32) == inside
    spread = jnp.where(spread, 1.0, 0.0).astype(bf16)
    spread = jnp.concatenate([spread, spread], axis=1)
    repeat = jnp.where(belongs((pairs, queries), 0), 1.0, 0.0).astype(bf16)
    copies = []
    for k in range(pieces):
        part = slice(k * piece, (k + 1) * piece)
        gain = gain_ref[:, part]
        row = (raw_ref[:, part].astype(f32) * gain * inverse).astype(bf16).astype(f32)
        query = dot(repeat, query_ref[:, part], nn_dims) * cols_ref[:, 5:6]
        term = (query.astype(bf16).astype(f32) - cos * row) * scale * gain
        made[:, part] = dot(spread, jnp.concatenate(split(term), axis=0), nn_dims)
        part = pl.ds(k * piece, piece)
        copies.append(pltpu.make_async_copy(made.at[:, part], out_ref.at[:, part], sems.at[k]))
        copies[-1].start()
    for copy in copies:
        copy.wait()


def final_kernel(got_ref, queries_ref, gain_ref, d_queries_ref, d_gain_ref):
    count = got_ref.shape[0]
    got = got_ref[...].astype(f32).reshape(count // 2, 2, *got_ref.shape[1:])
    got = jnp.sum(got, axis=0)
    first = member_order(count)[0] % 2
    halves = [got[first], got[1 - first]]
    query = queries_ref[...].astype(f32)
    norm = jnp.sqrt(jnp.sum(query * query, axis=1, keepdims=True))
    unit = query / norm
    d_unit = jnp.concatenate([half[k : k + 1] for half in halves for k in range(4)], axis=1)
    d_queries_ref[...] = (d_unit - unit * jnp.sum(unit * d_unit, axis=1, keepdims=True)) / norm
    d_gain = jnp.concatenate([half[k : k + 1] for half in halves for k in range(4, 8)], axis=1)
    d_gain_ref[...] = d_gain / gain_ref[...]


def shape(dims, dtype=f32):
    return jax.ShapeDtypeStruct(dims, dtype)


def exchange(x):
    order = member_order(lax.axis_size("hash"))
    return lax.all_to_all(
        x, "hash", split_axis=0, concat_axis=0, axis_index_groups=[order], tiled=True
    )


def local(passages, queries, gain, candidates, teacher):
    count = lax.axis_size("hash")
    rows, width = passages.shape
    listed = candidates.shape[1]
    gain = gain.reshape(1, width)

    packed = pl.pallas_call(
        functools.partial(pack_kernel, rows),
        out_shape=shape((count, 8, width // 8 + listed), bf16),
        compiler_params=params(60),
        name="pack",
    )(queries, candidates, teacher)
    got = exchange(packed).reshape(count * 8, width // 8 + listed)

    pairs = count * 8
    near, far, gain_near = pl.pallas_call(
        stage_kernel,
        in_specs=[outside(), whole()],
        out_specs=[whole(), outside(), whole()],
        out_shape=[
            shape((rows, width // 2), bf16),
            shape((10 * rows, width // 2), bf16),
            shape((1, width)),
        ],
        scratch_shapes=[
            pltpu.VMEM((rows, width // 2), bf16),
            pltpu.SemaphoreType.DMA((2 * chunks,)),
            pltpu.SemaphoreType.DMA((chunks,)),
        ],
        compiler_params=params(48),
        name="stage",
        cost_estimate=pl.CostEstimate(
            flops=0, bytes_accessed=4 * rows * width, transcendentals=0
        ),
    )(passages, gain)
    raw, query, cols, lines, sums = pl.pallas_call(
        score_kernel,
        in_specs=[whole(), whole(), whole(), outside()],
        out_shape=[
            shape((pairs, width), bf16),
            shape((count, width), bf16),
            shape((pairs, 128)),
            shape((8, pairs)),
            shape((count, 1, pairs)),
        ],
        scratch_shapes=[
            pltpu.VMEM((rows, width // 2), bf16),
            pltpu.VMEM((width // 1024, pairs, 128), f32),
            pltpu.SemaphoreType.DMA((chunks // 2,)),
        ],
        compiler_params=params(48),
        name="score",
    )(got, gain_near, near, far)

    half = width // 2

    def mix(base):
        return pl.pallas_call(
            mix_kernel,
            in_specs=[pl.BlockSpec(memory_space=pltpu.SMEM)] + [whole()] * 5,
            out_shape=shape((3 * count + 8, half)),
            compiler_params=params(48),
            name="mix",
            cost_estimate=pl.CostEstimate(
                flops=8 * count * pairs * width, bytes_accessed=4 * pairs * width, transcendentals=0
            ),
        )(base.astype(jnp.int32).reshape(1), query, gain_near, raw, cols, lines)

    core = lax.axis_index("hash") % 2
    theirs = mix((1 - core) * half)
    sibling = lax.ppermute(theirs, "hash", [(i, i ^ 1) for i in range(count)])
    mine = mix(core * half)
    got_sums = exchange(sums)

    partial, total = pl.pallas_call(
        partial_kernel,
        out_shape=[shape((pairs, half // 4), bf16), shape((1, pairs))],
        scratch_shapes=[pltpu.VMEM((half // 512, pairs, 128), f32)],
        compiler_params=params(48),
        name="partial",
    )(got_sums, mine, sibling)
    got_partial = exchange(partial.reshape(count, 8, half // 4))

    d_passages = pl.pallas_call(
        passage_kernel,
        in_specs=[whole()] * 6,
        out_specs=outside(),
        out_shape=shape((rows, width)),
        scratch_shapes=[pltpu.VMEM((rows, width), f32), pltpu.SemaphoreType.DMA((pieces,))],
        compiler_params=params(48),
        name="d_passages",
        cost_estimate=pl.CostEstimate(
            flops=4 * pairs * rows * width, bytes_accessed=4 * rows * width, transcendentals=0
        ),
    )(total, query, gain_near, raw, cols, lines)

    d_queries, d_gain = pl.pallas_call(
        final_kernel,
        out_shape=[shape((1, width)), shape((1, width))],
        compiler_params=params(48),
        name="final",
    )(got_partial, queries, gain)
    return (d_passages, d_queries, d_gain.reshape(width))


def solution(mesh):
    in_specs = (
        P(("groups", "hash"), None),
        P(("groups", "hash"), None),
        P(),
        P(("groups", "hash"), None),
        P(("groups", "hash"), None),
    )
    out_specs = (P(("groups", "hash"), None), P(("groups", "hash"), None), P("groups"))
    return jax.shard_map(local, mesh=mesh, in_specs=in_specs, out_specs=out_specs, check_vma=False)
```

```python
import functools

import jax
import jax.numpy as jnp
from jax import lax
from jax.experimental import pallas as pl
from jax.experimental.pallas import tpu as pltpu
from jax.sharding import PartitionSpec as P

score_scale = 20.0
loss_scale = 8192.0
teacher_div = 2.0
coef_scale = loss_scale * score_scale
chunks = 4
pieces = 8
f32 = jnp.float32
bf16 = jnp.bfloat16
vmem = pltpu.VMEM
nn_dims = (((1,), (0,)), ((), ()))


def dot(a, b, dims):
    return lax.dot_general(a, b, dims, preferred_element_type=f32)


def split(x):
    high = x.astype(bf16)
    low = (x - high.astype(f32)).astype(bf16)
    return high, low


def member_order(count):
    return [(i + count // 2 + 1) % count for i in range(count)]


def params(megabytes):
    return pltpu.CompilerParams(vmem_limit_bytes=megabytes * 1024 * 1024)


def whole():
    return pl.BlockSpec(memory_space=vmem)


def outside():
    return pl.BlockSpec(memory_space=pltpu.HBM)


def pack_kernel(rows, queries_ref, candidates_ref, teacher_ref, out_ref):
    ids = candidates_ref[...]
    listed = ids.shape[1]
    count = out_ref.shape[0]
    width = queries_ref.shape[1] // 8
    query = queries_ref[...].astype(f32)
    query = jnp.concatenate([query[:, k * width : (k + 1) * width] for k in range(8)], axis=0)
    owner = lax.div(ids, rows)
    inside = ids - owner * rows
    slot = lax.rem(owner + (count - member_order(count)[0]), count)
    marks = jnp.exp(teacher_ref[...].astype(f32) * (1.0 / teacher_div))
    marks = marks / jnp.sum(marks, axis=1, keepdims=True)
    high, low = split(marks)
    values = jnp.concatenate(
        [
            (inside >> 8).astype(f32),
            (inside & 255).astype(f32),
            high.astype(f32),
            low.astype(f32),
            jnp.zeros((listed - 4, listed), f32),
        ],
        axis=0,
    )
    square = (listed, listed)
    across = jnp.broadcast_to(slot.astype(f32), square)
    same = across == jnp.transpose(across)
    earlier = same & (lax.broadcasted_iota(jnp.int32, square, 0) < lax.broadcasted_iota(jnp.int32, square, 1))
    rank = jnp.sum(jnp.where(earlier, 1.0, 0.0), axis=0, keepdims=True)
    place = slot * 8 + rank.astype(jnp.int32)
    spread = jnp.where(place == lax.broadcasted_iota(jnp.int32, (count * 8, listed), 0), 1.0, 0.0)
    lists = dot(spread.astype(bf16), jnp.transpose(values).astype(bf16), nn_dims)
    out_ref[:, :, :width] = jnp.broadcast_to(query.astype(bf16)[None], (count, 8, width))
    out_ref[:, :, width:] = lists.astype(bf16).reshape(count, 8, listed)


def belongs(dims, pair_axis):
    pair = lax.broadcasted_iota(jnp.int32, dims, pair_axis) >> 3
    return pair == lax.broadcasted_iota(jnp.int32, dims, 1 - pair_axis)


def stage_kernel(passages_ref, gain_ref, near_ref, far_ref, gain_out_ref, held, sems_in, sems_out):
    gain_out_ref[...] = gain_ref[...]
    rows, width = near_ref.shape
    piece = rows // chunks
    copies_in, copies_out, copies_near = [], [], []
    for k in range(chunks):
        part = pl.ds(k * piece, piece)
        far = passages_ref.at[part, pl.ds(width, width)]
        near = passages_ref.at[part, pl.ds(0, width)]
        copies_in.append(pltpu.make_async_copy(far, held.at[part], sems_in.at[k]))
        copies_out.append(pltpu.make_async_copy(held.at[part], far_ref.at[part], sems_out.at[k]))
        copies_near.append(pltpu.make_async_copy(near, near_ref.at[part], sems_in.at[chunks + k]))
    for copy in copies_in + copies_near:
        copy.start()
    for k in range(chunks):
        copies_in[k].wait()
        copies_out[k].start()
    for copy in copies_near + copies_out:
        copy.wait()


def mix(base, query_ref, gain_ref, raw_ref, cols, lines, out_ref):
    queries = query_ref.shape[0]
    pairs = raw_ref.shape[0]
    chunk = out_ref.shape[1] // 2
    cos, inverse, query_inverse = cols[:, 2:3], cols[:, 3:4], cols[:, 5:6]
    own = belongs((queries, pairs), 1)
    by_weight = split(jnp.where(own, lines[0:1, :], 0.0))
    by_mark = split(jnp.where(own, lines[1:2, :], 0.0))
    plain = jnp.concatenate([*by_weight, *by_mark], axis=0)
    repeat = jnp.where(belongs((pairs, queries), 0), 1.0, 0.0).astype(bf16)
    for k in range(2):
        part = slice(k * chunk, (k + 1) * chunk)
        there = pl.ds(pl.multiple_of(base + k * chunk, 128), chunk)
        row = (raw_ref[:, there].astype(f32) * gain_ref[:, there] * inverse).astype(bf16)
        mixed = dot(plain, row, nn_dims)
        out_ref[:queries, part] = mixed[:queries] + mixed[queries : 2 * queries]
        out_ref[queries : 2 * queries, part] = mixed[2 * queries : 3 * queries] + mixed[3 * queries :]
        row = row.astype(f32)
        query = dot(repeat, query_ref[:, there], nn_dims) * query_inverse
        turned = row * (query.astype(bf16).astype(f32) - cos * row)
        mixed = dot(plain, turned.astype(bf16), nn_dims)
        out_ref[2 * queries : 3 * queries, part] = mixed[:queries] + mixed[queries : 2 * queries]
        last = jnp.sum(mixed[2 * queries :], axis=0, keepdims=True)
        out_ref[3 * queries :, part] = jnp.broadcast_to(last, (8, chunk))


def mix_kernel(core_ref, query_ref, gain_ref, raw_ref, cols_ref, rows_ref, out_ref):
    base = core_ref[0] * out_ref.shape[1]
    mix(base, query_ref, gain_ref, raw_ref, cols_ref[...], rows_ref[...], out_ref)


def score_kernel(
    core_ref, got_ref, gain_ref, near_ref, far_ref,
    raw_ref, query_ref, cols_ref, rows_ref, sums_ref, theirs_ref, held, wide, sems,
):
    queries, width = query_ref.shape
    pairs = queries * 8
    rows = held.shape[0]
    chunk = width // chunks
    half = chunks // 2
    copies = []
    for k in range(half):
        part = pl.ds(k * chunk, chunk)
        copies.append(pltpu.make_async_copy(far_ref.at[pl.ds(0, rows), part], held.at[:, part], sems.at[k]))
        copies[-1].start()
    tiles = wide.shape[0]
    loaded = [got_ref[:, j * 128 : (j + 1) * 128].astype(f32) for j in range(tiles + 1)]
    squares = sum(x * x for x in loaded[:-1])
    squares = jnp.sum(squares, axis=1, keepdims=True).reshape(queries, 8, 1)
    squares = jnp.broadcast_to(jnp.sum(squares, axis=1, keepdims=True), (queries, 8, 1))
    query_inverse = 1.0 / jnp.sqrt(squares.reshape(pairs, 1))
    for j in range(tiles):
        wide[j] = loaded[j]
    query = [wide[j, pl.ds(k, queries, stride=8), :] for k in range(8) for j in range(tiles)]
    query = jnp.concatenate(query, axis=1).astype(bf16)
    query_ref[...] = query
    lists = loaded[-1]
    inside = lists[:, 0:1] * 256.0 + lists[:, 1:2]
    mark = lists[:, 2:3] + lists[:, 3:4]
    lane = lax.broadcasted_iota(jnp.int32, (pairs, rows), 1).astype(f32)
    pick = jnp.where(inside == lane, 1.0, 0.0).astype(bf16)
    repeat = jnp.where(belongs((pairs, queries), 0), 1.0, 0.0).astype(bf16)
    size = jnp.zeros((pairs, 128), f32)
    along = jnp.zeros((pairs, 128), f32)
    for k in range(chunks):
        part = slice(k * chunk, (k + 1) * chunk)
        repeated = dot(repeat, query[:, part], nn_dims)
        if k < half:
            passages = near_ref[:, part]
        else:
            copies[k - half].wait()
            passages = held[:, slice((k - half) * chunk, (k - half + 1) * chunk)]
        raw = dot(pick, passages, nn_dims)
        raw_ref[:, part] = raw.astype(bf16)
        lifted = raw * gain_ref[:, part]
        for j in range(chunk // 128):
            tile = slice(j * 128, (j + 1) * 128)
            size = size + lifted[:, tile] * lifted[:, tile]
            along = along + lifted[:, tile] * repeated[:, tile]
    inverse = 1.0 / jnp.sqrt(jnp.sum(size, axis=1, keepdims=True))
    cos = jnp.sum(along, axis=1, keepdims=True) * inverse * query_inverse
    weight = jnp.where(mark > 0.0, jnp.exp(cos * score_scale), 0.0)
    lane = lax.broadcasted_iota(jnp.int32, (pairs, 128), 1)
    cols = jnp.zeros((pairs, 128), f32)
    for k, column in enumerate((weight, mark, cos, inverse, inside, query_inverse)):
        cols = jnp.where(lane == k, column, cols)
    cols_ref[...] = cols
    flipped = jnp.transpose(cols)[:8]
    rows_ref[...] = flipped
    sums_ref[...] = jnp.broadcast_to(flipped[None, :1], sums_ref.shape)
    base = (1 - core_ref[0]) * theirs_ref.shape[1]
    mix(base, query_ref, gain_ref, raw_ref, cols, flipped, theirs_ref)


def partial_kernel(sums_ref, mine_ref, sibling_ref, out_ref, total_ref, laid):
    queries = sums_ref.shape[2] // 8
    width = mine_ref.shape[1]
    total = jnp.sum(sums_ref[...][:, 0, :], axis=0, keepdims=True)
    total_ref[...] = total
    own = belongs((queries, total.shape[1]), 1)
    inverse = 1.0 / jnp.sum(jnp.where(own, total, 0.0), axis=1, keepdims=True)
    both = mine_ref[...] + sibling_ref[...]
    partial = coef_scale * (both[:queries] * inverse - both[queries : 2 * queries])
    gain_part = jnp.sum(both[2 * queries : 3 * queries] * inverse, axis=0, keepdims=True)
    gain_part = coef_scale * (gain_part - both[3 * queries : 3 * queries + 1])
    tiles = laid.shape[0]
    for k in range(width // 128):
        row, tile = k // tiles, k % tiles
        part = slice(k * 128, (k + 1) * 128)
        laid[tile, pl.ds(row, queries, stride=8), :] = partial[:, part]
        laid[tile, pl.ds(4 + row, queries, stride=8), :] = jnp.broadcast_to(
            gain_part[:, part], (queries, 128)
        )
    for tile in range(tiles):
        out_ref[:, tile * 128 : (tile + 1) * 128] = laid[tile].astype(bf16)


def passage_kernel(total_ref, query_ref, gain_ref, raw_ref, cols_ref, rows_ref, out_ref, made, sems):
    queries, width = query_ref.shape
    rows, pairs = made.shape[0], raw_ref.shape[0]
    piece = width // pieces
    weight, mark = cols_ref[:, 0:1], cols_ref[:, 1:2]
    cos, inverse = cols_ref[:, 2:3], cols_ref[:, 3:4]
    square = (pairs, pairs)
    alike = (lax.broadcasted_iota(jnp.int32, square, 0) >> 3) == (
        lax.broadcasted_iota(jnp.int32, square, 1) >> 3
    )
    total = jnp.sum(jnp.where(alike, total_ref[...], 0.0), axis=1, keepdims=True)
    scale = coef_scale * (weight / total - mark) * inverse
    inside = rows_ref[4:5, :]
    spread = lax.broadcasted_iota(jnp.int32, (rows, pairs), 0).astype(f32) == inside
    spread = jnp.where(spread, 1.0, 0.0).astype(bf16)
    spread = jnp.concatenate([spread, spread], axis=1)
    repeat = jnp.where(belongs((pairs, queries), 0), 1.0, 0.0).astype(bf16)
    copies = []
    for k in range(pieces):
        part = slice(k * piece, (k + 1) * piece)
        gain = gain_ref[:, part]
        row = (raw_ref[:, part].astype(f32) * gain * inverse).astype(bf16).astype(f32)
        query = dot(repeat, query_ref[:, part], nn_dims) * cols_ref[:, 5:6]
        term = (query.astype(bf16).astype(f32) - cos * row) * scale * gain
        made[:, part] = dot(spread, jnp.concatenate(split(term), axis=0), nn_dims)
        part = pl.ds(k * piece, piece)
        copies.append(pltpu.make_async_copy(made.at[:, part], out_ref.at[:, part], sems.at[k]))
        copies[-1].start()
    for copy in copies:
        copy.wait()


def final_kernel(got_ref, queries_ref, gain_ref, d_queries_ref, d_gain_ref):
    count = got_ref.shape[0]
    got = got_ref[...].astype(f32).reshape(count // 2, 2, *got_ref.shape[1:])
    got = jnp.sum(got, axis=0)
    first = member_order(count)[0] % 2
    halves = [got[first], got[1 - first]]
    query = queries_ref[...].astype(f32)
    norm = jnp.sqrt(jnp.sum(query * query, axis=1, keepdims=True))
    unit = query / norm
    d_unit = jnp.concatenate([half[k : k + 1] for half in halves for k in range(4)], axis=1)
    d_queries_ref[...] = (d_unit - unit * jnp.sum(unit * d_unit, axis=1, keepdims=True)) / norm
    d_gain = jnp.concatenate([half[k : k + 1] for half in halves for k in range(4, 8)], axis=1)
    d_gain_ref[...] = d_gain / gain_ref[...]


def shape(dims, dtype=f32):
    return jax.ShapeDtypeStruct(dims, dtype)


def exchange(x):
    order = member_order(lax.axis_size("hash"))
    return lax.all_to_all(
        x, "hash", split_axis=0, concat_axis=0, axis_index_groups=[order], tiled=True
    )


def local(passages, queries, gain, candidates, teacher):
    count = lax.axis_size("hash")
    rows, width = passages.shape
    listed = candidates.shape[1]
    gain = gain.reshape(1, width)

    packed = pl.pallas_call(
        functools.partial(pack_kernel, rows),
        out_shape=shape((count, 8, width // 8 + listed), bf16),
        compiler_params=params(60),
        name="pack",
    )(queries, candidates, teacher)
    got = exchange(packed).reshape(count * 8, width // 8 + listed)

    pairs = count * 8
    near, far, gain_near = pl.pallas_call(
        stage_kernel,
        in_specs=[outside(), whole()],
        out_specs=[whole(), outside(), whole()],
        out_shape=[
            shape((rows, width // 2), bf16),
            shape((10 * rows, width // 2), bf16),
            shape((1, width)),
        ],
        scratch_shapes=[
            pltpu.VMEM((rows, width // 2), bf16),
            pltpu.SemaphoreType.DMA((2 * chunks,)),
            pltpu.SemaphoreType.DMA((chunks,)),
        ],
        compiler_params=params(48),
        name="stage",
        cost_estimate=pl.CostEstimate(
            flops=0, bytes_accessed=4 * rows * width, transcendentals=0
        ),
    )(passages, gain)
    half = width // 2
    core = (lax.axis_index("hash") % 2).astype(jnp.int32).reshape(1)
    raw, query, cols, lines, sums, theirs = pl.pallas_call(
        score_kernel,
        in_specs=[pl.BlockSpec(memory_space=pltpu.SMEM), whole(), whole(), whole(), outside()],
        out_shape=[
            shape((pairs, width), bf16),
            shape((count, width), bf16),
            shape((pairs, 128)),
            shape((8, pairs)),
            shape((count, 1, pairs)),
            shape((3 * count + 8, half)),
        ],
        scratch_shapes=[
            pltpu.VMEM((rows, width // 2), bf16),
            pltpu.VMEM((width // 1024, pairs, 128), f32),
            pltpu.SemaphoreType.DMA((chunks // 2,)),
        ],
        compiler_params=params(48),
        name="score",
    )(core, got, gain_near, near, far)

    got_sums = exchange(sums)
    sibling = lax.ppermute(theirs, "hash", [(i, i ^ 1) for i in range(count)])
    mine = pl.pallas_call(
        mix_kernel,
        in_specs=[pl.BlockSpec(memory_space=pltpu.SMEM)] + [whole()] * 5,
        out_shape=shape((3 * count + 8, half)),
        compiler_params=params(48),
        name="mix",
        cost_estimate=pl.CostEstimate(
            flops=8 * count * pairs * width, bytes_accessed=4 * pairs * width, transcendentals=0
        ),
    )(core, query, gain_near, raw, cols, lines)

    partial, total = pl.pallas_call(
        partial_kernel,
        out_shape=[shape((pairs, half // 4), bf16), shape((1, pairs))],
        scratch_shapes=[pltpu.VMEM((half // 512, pairs, 128), f32)],
        compiler_params=params(48),
        name="partial",
    )(got_sums, mine, sibling)
    got_partial = exchange(partial.reshape(count, 8, half // 4))

    d_passages = pl.pallas_call(
        passage_kernel,
        in_specs=[whole()] * 6,
        out_specs=outside(),
        out_shape=shape((rows, width)),
        scratch_shapes=[pltpu.VMEM((rows, width), f32), pltpu.SemaphoreType.DMA((pieces,))],
        compiler_params=params(48),
        name="d_passages",
        cost_estimate=pl.CostEstimate(
            flops=4 * pairs * rows * width, bytes_accessed=4 * rows * width, transcendentals=0
        ),
    )(total, query, gain_near, raw, cols, lines)

    d_queries, d_gain = pl.pallas_call(
        final_kernel,
        out_shape=[shape((1, width)), shape((1, width))],
        compiler_params=params(48),
        name="final",
    )(got_partial, queries, gain)
    return (d_passages, d_queries, d_gain.reshape(width))


def solution(mesh):
    in_specs = (
        P(("groups", "hash"), None),
        P(("groups", "hash"), None),
        P(),
        P(("groups", "hash"), None),
        P(("groups", "hash"), None),
    )
    out_specs = (P(("groups", "hash"), None), P(("groups", "hash"), None), P("groups"))
    return jax.shard_map(local, mesh=mesh, in_specs=in_specs, out_specs=out_specs, check_vma=False)
```

```python
import functools

import jax
import jax.numpy as jnp
from jax import lax
from jax.experimental import pallas as pl
from jax.experimental.pallas import tpu as pltpu
from jax.sharding import PartitionSpec as P

score_scale = 20.0
loss_scale = 8192.0
teacher_div = 2.0
coef_scale = loss_scale * score_scale
chunks = 4
pieces = 8
f32 = jnp.float32
bf16 = jnp.bfloat16
vmem = pltpu.VMEM
nn_dims = (((1,), (0,)), ((), ()))


def dot(a, b, dims):
    return lax.dot_general(a, b, dims, preferred_element_type=f32)


def split(x):
    high = x.astype(bf16)
    low = (x - high.astype(f32)).astype(bf16)
    return high, low


def member_order(count):
    return [(i + count // 2 + 1) % count for i in range(count)]


def params(megabytes):
    return pltpu.CompilerParams(vmem_limit_bytes=megabytes * 1024 * 1024)


def whole():
    return pl.BlockSpec(memory_space=vmem)


def outside():
    return pl.BlockSpec(memory_space=pltpu.HBM)


def pack_kernel(rows, queries_ref, candidates_ref, teacher_ref, out_ref):
    ids = candidates_ref[...]
    listed = ids.shape[1]
    count = out_ref.shape[0]
    width = queries_ref.shape[1] // 8
    query = queries_ref[...].astype(f32)
    query = jnp.concatenate([query[:, k * width : (k + 1) * width] for k in range(8)], axis=0)
    owner = lax.div(ids, rows)
    inside = ids - owner * rows
    slot = lax.rem(owner + (count - member_order(count)[0]), count)
    marks = jnp.exp(teacher_ref[...].astype(f32) * (1.0 / teacher_div))
    marks = marks / jnp.sum(marks, axis=1, keepdims=True)
    high, low = split(marks)
    values = jnp.concatenate(
        [
            (inside >> 8).astype(f32),
            (inside & 255).astype(f32),
            high.astype(f32),
            low.astype(f32),
            jnp.zeros((listed - 4, listed), f32),
        ],
        axis=0,
    )
    square = (listed, listed)
    across = jnp.broadcast_to(slot.astype(f32), square)
    same = across == jnp.transpose(across)
    earlier = same & (lax.broadcasted_iota(jnp.int32, square, 0) < lax.broadcasted_iota(jnp.int32, square, 1))
    rank = jnp.sum(jnp.where(earlier, 1.0, 0.0), axis=0, keepdims=True)
    place = slot * 8 + rank.astype(jnp.int32)
    spread = jnp.where(place == lax.broadcasted_iota(jnp.int32, (count * 8, listed), 0), 1.0, 0.0)
    lists = dot(spread.astype(bf16), jnp.transpose(values).astype(bf16), nn_dims)
    out_ref[:, :, :width] = jnp.broadcast_to(query.astype(bf16)[None], (count, 8, width))
    out_ref[:, :, width:] = lists.astype(bf16).reshape(count, 8, listed)


def belongs(dims, pair_axis):
    pair = lax.broadcasted_iota(jnp.int32, dims, pair_axis) >> 3
    return pair == lax.broadcasted_iota(jnp.int32, dims, 1 - pair_axis)


def stage_kernel(passages_ref, gain_ref, near_ref, far_ref, gain_out_ref, held, sems_in, sems_out):
    gain_out_ref[...] = gain_ref[...]
    rows, width = near_ref.shape
    piece = rows // chunks
    copies_in, copies_out, copies_near = [], [], []
    for k in range(chunks):
        part = pl.ds(k * piece, piece)
        far = passages_ref.at[part, pl.ds(width, width)]
        near = passages_ref.at[part, pl.ds(0, width)]
        copies_in.append(pltpu.make_async_copy(far, held.at[part], sems_in.at[k]))
        copies_out.append(pltpu.make_async_copy(held.at[part], far_ref.at[part], sems_out.at[k]))
        copies_near.append(pltpu.make_async_copy(near, near_ref.at[part], sems_in.at[chunks + k]))
    for copy in copies_in + copies_near:
        copy.start()
    for k in range(chunks):
        copies_in[k].wait()
        copies_out[k].start()
    for copy in copies_near + copies_out:
        copy.wait()


def mix(base, first, query_ref, gain_ref, raw_ref, lines, out_ref, before_ref):
    queries = query_ref.shape[0]
    pairs = raw_ref.shape[0]
    chunk = out_ref.shape[1] // 2
    cols = jnp.transpose(jnp.concatenate([lines, jnp.zeros((120, pairs), f32)], axis=0))
    cos, inverse, query_inverse = cols[:, 2:3], cols[:, 3:4], cols[:, 5:6]
    own = belongs((queries, pairs), 1)
    by_weight = split(jnp.where(own, lines[0:1, :], 0.0))
    by_mark = split(jnp.where(own, lines[1:2, :], 0.0))
    plain = jnp.concatenate([*by_weight, *by_mark], axis=0)
    repeat = jnp.where(belongs((pairs, queries), 0), 1.0, 0.0).astype(bf16)
    for k in range(2):
        part = slice(k * chunk, (k + 1) * chunk)
        there = pl.ds(pl.multiple_of(base + k * chunk, 128), chunk)
        here = pl.ds(pl.multiple_of(first + k * chunk, 128), chunk)
        row = (raw_ref[:, here].astype(f32) * gain_ref[:, there] * inverse).astype(bf16)
        plainly = dot(plain, row, nn_dims)
        row = row.astype(f32)
        query = dot(repeat, query_ref[:, there], nn_dims) * query_inverse
        turned = row * (query.astype(bf16).astype(f32) - cos * row)
        turned = dot(plain, turned.astype(bf16), nn_dims)
        last = jnp.sum(turned[2 * queries :], axis=0, keepdims=True)
        sums = jnp.concatenate(
            [
                plainly[:queries] + plainly[queries : 2 * queries],
                plainly[2 * queries : 3 * queries] + plainly[3 * queries :],
                turned[:queries] + turned[queries : 2 * queries],
                jnp.broadcast_to(last, (8, chunk)),
            ],
            axis=0,
        )
        out_ref[:, part] = sums if before_ref is None else sums + before_ref[:, part]


def mine_kernel(core_ref, query_ref, gain_ref, raw_ref, rows_ref, out_ref):
    base = core_ref[0] * out_ref.shape[1]
    mix(base, base, query_ref, gain_ref, raw_ref, rows_ref[...], out_ref, None)


def both_kernel(core_ref, query_ref, gain_ref, raw_ref, rows_ref, mine_ref, out_ref):
    base = core_ref[0] * out_ref.shape[1]
    mix(base, 0, query_ref, gain_ref, raw_ref, rows_ref[...], out_ref, mine_ref)


def score_kernel(
    core_ref, got_ref, gain_ref, near_ref, far_ref,
    raw_ref, query_ref, cols_ref, rows_ref, sums_ref, theirs_ref, held, wide, sems,
):
    queries, width = query_ref.shape
    pairs = queries * 8
    rows = held.shape[0]
    chunk = width // chunks
    half = chunks // 2
    copies = []
    for k in range(half):
        part = pl.ds(k * chunk, chunk)
        copies.append(pltpu.make_async_copy(far_ref.at[pl.ds(0, rows), part], held.at[:, part], sems.at[k]))
        copies[-1].start()
    tiles = wide.shape[0]
    loaded = [got_ref[:, j * 128 : (j + 1) * 128].astype(f32) for j in range(tiles + 1)]
    squares = sum(x * x for x in loaded[:-1])
    squares = jnp.sum(squares, axis=1, keepdims=True).reshape(queries, 8, 1)
    squares = jnp.broadcast_to(jnp.sum(squares, axis=1, keepdims=True), (queries, 8, 1))
    query_inverse = 1.0 / jnp.sqrt(squares.reshape(pairs, 1))
    for j in range(tiles):
        wide[j] = loaded[j]
    query = [wide[j, pl.ds(k, queries, stride=8), :] for k in range(8) for j in range(tiles)]
    query = jnp.concatenate(query, axis=1).astype(bf16)
    query_ref[...] = query
    lists = loaded[-1]
    inside = lists[:, 0:1] * 256.0 + lists[:, 1:2]
    mark = lists[:, 2:3] + lists[:, 3:4]
    lane = lax.broadcasted_iota(jnp.int32, (pairs, rows), 1).astype(f32)
    pick = jnp.where(inside == lane, 1.0, 0.0).astype(bf16)
    repeat = jnp.where(belongs((pairs, queries), 0), 1.0, 0.0).astype(bf16)
    size = jnp.zeros((pairs, 128), f32)
    along = jnp.zeros((pairs, 128), f32)
    for k in range(chunks):
        part = slice(k * chunk, (k + 1) * chunk)
        repeated = dot(repeat, query[:, part], nn_dims)
        if k < half:
            passages = near_ref[:, part]
        else:
            copies[k - half].wait()
            passages = held[:, slice((k - half) * chunk, (k - half + 1) * chunk)]
        raw = dot(pick, passages, nn_dims)
        raw_ref[:, part] = raw.astype(bf16)
        lifted = raw * gain_ref[:, part]
        for j in range(chunk // 128):
            tile = slice(j * 128, (j + 1) * 128)
            size = size + lifted[:, tile] * lifted[:, tile]
            along = along + lifted[:, tile] * repeated[:, tile]
    there = theirs_ref.shape[1]
    theirs_ref[...] = raw_ref[:, pl.ds(pl.multiple_of((1 - core_ref[0]) * there, 128), there)]
    inverse = 1.0 / jnp.sqrt(jnp.sum(size, axis=1, keepdims=True))
    cos = jnp.sum(along, axis=1, keepdims=True) * inverse * query_inverse
    weight = jnp.where(mark > 0.0, jnp.exp(cos * score_scale), 0.0)
    lane = lax.broadcasted_iota(jnp.int32, (pairs, 128), 1)
    cols = jnp.zeros((pairs, 128), f32)
    for k, column in enumerate((weight, mark, cos, inverse, inside, query_inverse)):
        cols = jnp.where(lane == k, column, cols)
    cols_ref[...] = cols
    flipped = jnp.transpose(cols)[:8]
    rows_ref[...] = flipped
    sums_ref[...] = jnp.broadcast_to(flipped[None, :1], sums_ref.shape)


def partial_kernel(sums_ref, both_ref, out_ref, total_ref, laid):
    queries = sums_ref.shape[2] // 8
    width = both_ref.shape[1]
    total = jnp.sum(sums_ref[...][:, 0, :], axis=0, keepdims=True)
    total_ref[...] = total
    own = belongs((queries, total.shape[1]), 1)
    inverse = 1.0 / jnp.sum(jnp.where(own, total, 0.0), axis=1, keepdims=True)
    both = both_ref[...]
    partial = coef_scale * (both[:queries] * inverse - both[queries : 2 * queries])
    gain_part = jnp.sum(both[2 * queries : 3 * queries] * inverse, axis=0, keepdims=True)
    gain_part = coef_scale * (gain_part - both[3 * queries : 3 * queries + 1])
    tiles = laid.shape[0]
    for k in range(width // 128):
        row, tile = k // tiles, k % tiles
        part = slice(k * 128, (k + 1) * 128)
        laid[tile, pl.ds(row, queries, stride=8), :] = partial[:, part]
        laid[tile, pl.ds(4 + row, queries, stride=8), :] = jnp.broadcast_to(
            gain_part[:, part], (queries, 128)
        )
    for tile in range(tiles):
        out_ref[:, tile * 128 : (tile + 1) * 128] = laid[tile].astype(bf16)


def passage_kernel(total_ref, query_ref, gain_ref, raw_ref, cols_ref, rows_ref, out_ref, made, sems):
    queries, width = query_ref.shape
    rows, pairs = made.shape[0], raw_ref.shape[0]
    piece = width // pieces
    weight, mark = cols_ref[:, 0:1], cols_ref[:, 1:2]
    cos, inverse = cols_ref[:, 2:3], cols_ref[:, 3:4]
    square = (pairs, pairs)
    alike = (lax.broadcasted_iota(jnp.int32, square, 0) >> 3) == (
        lax.broadcasted_iota(jnp.int32, square, 1) >> 3
    )
    total = jnp.sum(jnp.where(alike, total_ref[...], 0.0), axis=1, keepdims=True)
    scale = coef_scale * (weight / total - mark) * inverse
    inside = rows_ref[4:5, :]
    spread = lax.broadcasted_iota(jnp.int32, (rows, pairs), 0).astype(f32) == inside
    spread = jnp.where(spread, 1.0, 0.0).astype(bf16)
    spread = jnp.concatenate([spread, spread], axis=1)
    repeat = jnp.where(belongs((pairs, queries), 0), 1.0, 0.0).astype(bf16)
    copies = []
    for k in range(pieces):
        part = slice(k * piece, (k + 1) * piece)
        gain = gain_ref[:, part]
        row = (raw_ref[:, part].astype(f32) * gain * inverse).astype(bf16).astype(f32)
        query = dot(repeat, query_ref[:, part], nn_dims) * cols_ref[:, 5:6]
        term = (query.astype(bf16).astype(f32) - cos * row) * scale * gain
        made[:, part] = dot(spread, jnp.concatenate(split(term), axis=0), nn_dims)
        part = pl.ds(k * piece, piece)
        copies.append(pltpu.make_async_copy(made.at[:, part], out_ref.at[:, part], sems.at[k]))
        copies[-1].start()
    for copy in copies:
        copy.wait()


def final_kernel(got_ref, queries_ref, gain_ref, d_queries_ref, d_gain_ref):
    count = got_ref.shape[0]
    got = got_ref[...].astype(f32).reshape(count // 2, 2, *got_ref.shape[1:])
    got = jnp.sum(got, axis=0)
    first = member_order(count)[0] % 2
    halves = [got[first], got[1 - first]]
    query = queries_ref[...].astype(f32)
    norm = jnp.sqrt(jnp.sum(query * query, axis=1, keepdims=True))
    unit = query / norm
    d_unit = jnp.concatenate([half[k : k + 1] for half in halves for k in range(4)], axis=1)
    d_queries_ref[...] = (d_unit - unit * jnp.sum(unit * d_unit, axis=1, keepdims=True)) / norm
    d_gain = jnp.concatenate([half[k : k + 1] for half in halves for k in range(4, 8)], axis=1)
    d_gain_ref[...] = d_gain / gain_ref[...]


def shape(dims, dtype=f32):
    return jax.ShapeDtypeStruct(dims, dtype)


def exchange(x):
    order = member_order(lax.axis_size("hash"))
    return lax.all_to_all(
        x, "hash", split_axis=0, concat_axis=0, axis_index_groups=[order], tiled=True
    )


def local(passages, queries, gain, candidates, teacher):
    count = lax.axis_size("hash")
    rows, width = passages.shape
    listed = candidates.shape[1]
    gain = gain.reshape(1, width)

    packed = pl.pallas_call(
        functools.partial(pack_kernel, rows),
        out_shape=shape((count, 8, width // 8 + listed), bf16),
        compiler_params=params(60),
        name="pack",
    )(queries, candidates, teacher)
    got = exchange(packed).reshape(count * 8, width // 8 + listed)

    pairs = count * 8
    near, far, gain_near = pl.pallas_call(
        stage_kernel,
        in_specs=[outside(), whole()],
        out_specs=[whole(), outside(), whole()],
        out_shape=[
            shape((rows, width // 2), bf16),
            shape((10 * rows, width // 2), bf16),
            shape((1, width)),
        ],
        scratch_shapes=[
            pltpu.VMEM((rows, width // 2), bf16),
            pltpu.SemaphoreType.DMA((2 * chunks,)),
            pltpu.SemaphoreType.DMA((chunks,)),
        ],
        compiler_params=params(48),
        name="stage",
        cost_estimate=pl.CostEstimate(
            flops=0, bytes_accessed=4 * rows * width, transcendentals=0
        ),
    )(passages, gain)
    half = width // 2
    core = (lax.axis_index("hash") % 2).astype(jnp.int32).reshape(1)
    raw, query, cols, lines, sums, theirs = pl.pallas_call(
        score_kernel,
        in_specs=[pl.BlockSpec(memory_space=pltpu.SMEM), whole(), whole(), whole(), outside()],
        out_shape=[
            shape((pairs, width), bf16),
            shape((count, width), bf16),
            shape((pairs, 128)),
            shape((8, pairs)),
            shape((count, 1, pairs)),
            shape((pairs, half), bf16),
        ],
        scratch_shapes=[
            pltpu.VMEM((rows, width // 2), bf16),
            pltpu.VMEM((width // 1024, pairs, 128), f32),
            pltpu.SemaphoreType.DMA((chunks // 2,)),
        ],
        compiler_params=params(48),
        name="score",
    )(core, got, gain_near, near, far)

    got_sums = exchange(sums)
    swap = [(i, i ^ 1) for i in range(count)]
    sibling_raw = lax.ppermute(theirs, "hash", swap)
    sibling_lines = lax.ppermute(lines, "hash", swap)

    def mixed(kernel, *operands):
        return pl.pallas_call(
            kernel,
            in_specs=[pl.BlockSpec(memory_space=pltpu.SMEM)] + [whole()] * (len(operands) + 2),
            out_shape=shape((3 * count + 8, half)),
            compiler_params=params(48),
            name="mix",
            cost_estimate=pl.CostEstimate(
                flops=8 * count * pairs * width, bytes_accessed=4 * pairs * width, transcendentals=0
            ),
        )(core, query, gain_near, *operands)

    mine = mixed(mine_kernel, raw, lines)
    both = mixed(both_kernel, sibling_raw, sibling_lines, mine)

    partial, total = pl.pallas_call(
        partial_kernel,
        out_shape=[shape((pairs, half // 4), bf16), shape((1, pairs))],
        scratch_shapes=[pltpu.VMEM((half // 512, pairs, 128), f32)],
        compiler_params=params(48),
        name="partial",
    )(got_sums, both)
    got_partial = exchange(partial.reshape(count, 8, half // 4))

    d_passages = pl.pallas_call(
        passage_kernel,
        in_specs=[whole()] * 6,
        out_specs=outside(),
        out_shape=shape((rows, width)),
        scratch_shapes=[pltpu.VMEM((rows, width), f32), pltpu.SemaphoreType.DMA((pieces,))],
        compiler_params=params(48),
        name="d_passages",
        cost_estimate=pl.CostEstimate(
            flops=4 * pairs * rows * width, bytes_accessed=4 * rows * width, transcendentals=0
        ),
    )(total, query, gain_near, raw, cols, lines)

    d_queries, d_gain = pl.pallas_call(
        final_kernel,
        out_shape=[shape((1, width)), shape((1, width))],
        compiler_params=params(48),
        name="final",
    )(got_partial, queries, gain)
    return (d_passages, d_queries, d_gain.reshape(width))


def solution(mesh):
    in_specs = (
        P(("groups", "hash"), None),
        P(("groups", "hash"), None),
        P(),
        P(("groups", "hash"), None),
        P(("groups", "hash"), None),
    )
    out_specs = (P(("groups", "hash"), None), P(("groups", "hash"), None), P("groups"))
    return jax.shard_map(local, mesh=mesh, in_specs=in_specs, out_specs=out_specs, check_vma=False)
```

```python
import functools

import jax
import jax.numpy as jnp
from jax import lax
from jax.experimental import pallas as pl
from jax.experimental.pallas import tpu as pltpu
from jax.sharding import PartitionSpec as P

score_scale = 20.0
loss_scale = 8192.0
teacher_div = 2.0
coef_scale = loss_scale * score_scale
chunks = 4
pieces = 8
f32 = jnp.float32
bf16 = jnp.bfloat16
vmem = pltpu.VMEM
nn_dims = (((1,), (0,)), ((), ()))


def dot(a, b, dims):
    return lax.dot_general(a, b, dims, preferred_element_type=f32)


def split(x):
    high = x.astype(bf16)
    low = (x - high.astype(f32)).astype(bf16)
    return high, low


def member_order(count):
    first = count // 2 + 1
    return [first, *range(0, count, 2), *(i for i in range(1, count, 2) if i != first)]


def member_slot(owner, count):
    first = count // 2 + 1
    half = owner >> 1
    odd = 1 + count // 2 + half - jnp.where(owner > first, 1, 0)
    return jnp.where((owner & 1) == 0, 1 + half, jnp.where(owner == first, 0, odd))


def params(megabytes):
    return pltpu.CompilerParams(vmem_limit_bytes=megabytes * 1024 * 1024)


def whole():
    return pl.BlockSpec(memory_space=vmem)


def outside():
    return pl.BlockSpec(memory_space=pltpu.HBM)


def pack_kernel(rows, queries_ref, candidates_ref, teacher_ref, out_ref):
    ids = candidates_ref[...]
    listed = ids.shape[1]
    count = out_ref.shape[0]
    width = queries_ref.shape[1] // 8
    query = queries_ref[...].astype(f32)
    query = jnp.concatenate([query[:, k * width : (k + 1) * width] for k in range(8)], axis=0)
    owner = lax.div(ids, rows)
    inside = ids - owner * rows
    slot = member_slot(owner, count)
    marks = jnp.exp(teacher_ref[...].astype(f32) * (1.0 / teacher_div))
    marks = marks / jnp.sum(marks, axis=1, keepdims=True)
    high, low = split(marks)
    values = jnp.concatenate(
        [
            (inside >> 8).astype(f32),
            (inside & 255).astype(f32),
            high.astype(f32),
            low.astype(f32),
            jnp.zeros((listed - 4, listed), f32),
        ],
        axis=0,
    )
    square = (listed, listed)
    across = jnp.broadcast_to(slot.astype(f32), square)
    same = across == jnp.transpose(across)
    earlier = same & (lax.broadcasted_iota(jnp.int32, square, 0) < lax.broadcasted_iota(jnp.int32, square, 1))
    rank = jnp.sum(jnp.where(earlier, 1.0, 0.0), axis=0, keepdims=True)
    place = slot * 8 + rank.astype(jnp.int32)
    spread = jnp.where(place == lax.broadcasted_iota(jnp.int32, (count * 8, listed), 0), 1.0, 0.0)
    lists = dot(spread.astype(bf16), jnp.transpose(values).astype(bf16), nn_dims)
    out_ref[:, :, :width] = jnp.broadcast_to(query.astype(bf16)[None], (count, 8, width))
    out_ref[:, :, width:] = lists.astype(bf16).reshape(count, 8, listed)


def belongs(dims, pair_axis):
    pair = lax.broadcasted_iota(jnp.int32, dims, pair_axis) >> 3
    return pair == lax.broadcasted_iota(jnp.int32, dims, 1 - pair_axis)


def stage_kernel(passages_ref, gain_ref, near_ref, far_ref, gain_out_ref, held, sems_in, sems_out):
    gain_out_ref[...] = gain_ref[...]
    rows, width = near_ref.shape
    piece = rows // chunks
    copies_in, copies_out, copies_near = [], [], []
    for k in range(chunks):
        part = pl.ds(k * piece, piece)
        far = passages_ref.at[part, pl.ds(width, width)]
        near = passages_ref.at[part, pl.ds(0, width)]
        copies_in.append(pltpu.make_async_copy(far, held.at[part], sems_in.at[k]))
        copies_out.append(pltpu.make_async_copy(held.at[part], far_ref.at[part], sems_out.at[k]))
        copies_near.append(pltpu.make_async_copy(near, near_ref.at[part], sems_in.at[chunks + k]))
    for copy in copies_in + copies_near:
        copy.start()
    for k in range(chunks):
        copies_in[k].wait()
        copies_out[k].start()
    for copy in copies_near + copies_out:
        copy.wait()


def mix(base, first, query_ref, gain_ref, raw_ref, lines, out_ref, before_ref):
    queries = query_ref.shape[0]
    pairs = raw_ref.shape[0]
    chunk = out_ref.shape[1] // 2
    cols = jnp.transpose(jnp.concatenate([lines, jnp.zeros((120, pairs), f32)], axis=0))
    cos, inverse, query_inverse = cols[:, 2:3], cols[:, 3:4], cols[:, 5:6]
    own = belongs((queries, pairs), 1)
    by_weight = split(jnp.where(own, lines[0:1, :], 0.0))
    by_mark = split(jnp.where(own, lines[1:2, :], 0.0))
    plain = jnp.concatenate([*by_weight, *by_mark], axis=0)
    repeat = jnp.where(belongs((pairs, queries), 0), 1.0, 0.0).astype(bf16)
    for k in range(2):
        part = slice(k * chunk, (k + 1) * chunk)
        there = pl.ds(pl.multiple_of(base + k * chunk, 128), chunk)
        here = pl.ds(pl.multiple_of(first + k * chunk, 128), chunk)
        row = (raw_ref[:, here].astype(f32) * gain_ref[:, there] * inverse).astype(bf16)
        plainly = dot(plain, row, nn_dims)
        row = row.astype(f32)
        query = dot(repeat, query_ref[:, there], nn_dims) * query_inverse
        turned = row * (query.astype(bf16).astype(f32) - cos * row)
        turned = dot(plain, turned.astype(bf16), nn_dims)
        last = jnp.sum(turned[2 * queries :], axis=0, keepdims=True)
        sums = jnp.concatenate(
            [
                plainly[:queries] + plainly[queries : 2 * queries],
                plainly[2 * queries : 3 * queries] + plainly[3 * queries :],
                turned[:queries] + turned[queries : 2 * queries],
                jnp.broadcast_to(last, (8, chunk)),
            ],
            axis=0,
        )
        out_ref[:, part] = sums if before_ref is None else sums + before_ref[:, part]


def mine_kernel(core_ref, query_ref, gain_ref, raw_ref, rows_ref, out_ref):
    base = core_ref[0] * out_ref.shape[1]
    mix(base, base, query_ref, gain_ref, raw_ref, rows_ref[...], out_ref, None)


def both_kernel(core_ref, query_ref, gain_ref, raw_ref, rows_ref, mine_ref, out_ref):
    base = core_ref[0] * out_ref.shape[1]
    mix(base, 0, query_ref, gain_ref, raw_ref, rows_ref[...], out_ref, mine_ref)


def score_kernel(
    core_ref, got_ref, gain_ref, near_ref, far_ref,
    raw_ref, query_ref, cols_ref, rows_ref, sums_ref, theirs_ref, held, wide, sems,
):
    queries, width = query_ref.shape
    pairs = queries * 8
    rows = held.shape[0]
    chunk = width // chunks
    half = chunks // 2
    copies = []
    for k in range(half):
        part = pl.ds(k * chunk, chunk)
        copies.append(pltpu.make_async_copy(far_ref.at[pl.ds(0, rows), part], held.at[:, part], sems.at[k]))
        copies[-1].start()
    tiles = wide.shape[0]
    loaded = [got_ref[:, j * 128 : (j + 1) * 128].astype(f32) for j in range(tiles + 1)]
    squares = sum(x * x for x in loaded[:-1])
    squares = jnp.sum(squares, axis=1, keepdims=True).reshape(queries, 8, 1)
    squares = jnp.broadcast_to(jnp.sum(squares, axis=1, keepdims=True), (queries, 8, 1))
    query_inverse = 1.0 / jnp.sqrt(squares.reshape(pairs, 1))
    for j in range(tiles):
        wide[j] = loaded[j]
    query = [wide[j, pl.ds(k, queries, stride=8), :] for k in range(8) for j in range(tiles)]
    query = jnp.concatenate(query, axis=1).astype(bf16)
    query_ref[...] = query
    lists = loaded[-1]
    inside = lists[:, 0:1] * 256.0 + lists[:, 1:2]
    mark = lists[:, 2:3] + lists[:, 3:4]
    lane = lax.broadcasted_iota(jnp.int32, (pairs, rows), 1).astype(f32)
    pick = jnp.where(inside == lane, 1.0, 0.0).astype(bf16)
    size = jnp.zeros((pairs, 128), f32)
    along = [jnp.zeros((8, 128), f32)] * queries
    for k in range(chunks):
        part = slice(k * chunk, (k + 1) * chunk)
        if k < half:
            passages = near_ref[:, part]
        else:
            copies[k - half].wait()
            passages = held[:, slice((k - half) * chunk, (k - half + 1) * chunk)]
        raw = dot(pick, passages, nn_dims)
        raw_ref[:, part] = raw.astype(bf16)
        lifted = raw * gain_ref[:, part]
        for j in range(chunk // 128):
            tile = slice(j * 128, (j + 1) * 128)
            size = size + lifted[:, tile] * lifted[:, tile]
            eighth, place = divmod(k * chunk // 128 + j, tiles)
            for i in range(queries):
                row = wide[place, i * 8 + eighth : i * 8 + eighth + 1, :]
                along[i] = along[i] + lifted[i * 8 : i * 8 + 8, tile] * row
    there = theirs_ref.shape[1]
    theirs_ref[...] = raw_ref[:, pl.ds(pl.multiple_of((1 - core_ref[0]) * there, 128), there)]
    inverse = 1.0 / jnp.sqrt(jnp.sum(size, axis=1, keepdims=True))
    along = jnp.concatenate(along, axis=0)
    cos = jnp.sum(along, axis=1, keepdims=True) * inverse * query_inverse
    weight = jnp.where(mark > 0.0, jnp.exp(cos * score_scale), 0.0)
    lane = lax.broadcasted_iota(jnp.int32, (pairs, 128), 1)
    cols = jnp.zeros((pairs, 128), f32)
    for k, column in enumerate((weight, mark, cos, inverse, inside, query_inverse)):
        cols = jnp.where(lane == k, column, cols)
    cols_ref[...] = cols
    flipped = jnp.transpose(cols)[:8]
    rows_ref[...] = flipped
    sums_ref[...] = jnp.broadcast_to(flipped[None, :1], sums_ref.shape)


def partial_kernel(sums_ref, both_ref, out_ref, total_ref, laid):
    queries = sums_ref.shape[2] // 8
    width = both_ref.shape[1]
    total = jnp.sum(sums_ref[...][:, 0, :], axis=0, keepdims=True)
    total_ref[...] = total
    own = belongs((queries, total.shape[1]), 1)
    inverse = 1.0 / jnp.sum(jnp.where(own, total, 0.0), axis=1, keepdims=True)
    both = both_ref[...]
    partial = coef_scale * (both[:queries] * inverse - both[queries : 2 * queries])
    gain_part = jnp.sum(both[2 * queries : 3 * queries] * inverse, axis=0, keepdims=True)
    gain_part = coef_scale * (gain_part - both[3 * queries : 3 * queries + 1])
    tiles = laid.shape[0]
    for k in range(width // 128):
        row, tile = k // tiles, k % tiles
        part = slice(k * 128, (k + 1) * 128)
        laid[tile, pl.ds(row, queries, stride=8), :] = partial[:, part]
        laid[tile, pl.ds(4 + row, queries, stride=8), :] = jnp.broadcast_to(
            gain_part[:, part], (queries, 128)
        )
    for tile in range(tiles):
        out_ref[:, tile * 128 : (tile + 1) * 128] = laid[tile].astype(bf16)


def passage_kernel(total_ref, query_ref, gain_ref, raw_ref, cols_ref, rows_ref, out_ref, made, sems):
    queries, width = query_ref.shape
    rows, pairs = made.shape[0], raw_ref.shape[0]
    piece = width // pieces
    weight, mark = cols_ref[:, 0:1], cols_ref[:, 1:2]
    cos, inverse = cols_ref[:, 2:3], cols_ref[:, 3:4]
    square = (pairs, pairs)
    alike = (lax.broadcasted_iota(jnp.int32, square, 0) >> 3) == (
        lax.broadcasted_iota(jnp.int32, square, 1) >> 3
    )
    total = jnp.sum(jnp.where(alike, total_ref[...], 0.0), axis=1, keepdims=True)
    scale = coef_scale * (weight / total - mark) * inverse
    inside = rows_ref[4:5, :]
    spread = lax.broadcasted_iota(jnp.int32, (rows, pairs), 0).astype(f32) == inside
    spread = jnp.where(spread, 1.0, 0.0).astype(bf16)
    spread = jnp.concatenate([spread, spread], axis=1)
    repeat = jnp.where(belongs((pairs, queries), 0), 1.0, 0.0).astype(bf16)
    copies = []
    for k in range(pieces):
        part = slice(k * piece, (k + 1) * piece)
        gain = gain_ref[:, part]
        row = (raw_ref[:, part].astype(f32) * gain * inverse).astype(bf16).astype(f32)
        query = dot(repeat, query_ref[:, part], nn_dims) * cols_ref[:, 5:6]
        term = (query.astype(bf16).astype(f32) - cos * row) * scale * gain
        made[:, part] = dot(spread, jnp.concatenate(split(term), axis=0), nn_dims)
        part = pl.ds(k * piece, piece)
        copies.append(pltpu.make_async_copy(made.at[:, part], out_ref.at[:, part], sems.at[k]))
        copies[-1].start()
    for copy in copies:
        copy.wait()


def final_kernel(got_ref, queries_ref, gain_ref, d_queries_ref, d_gain_ref):
    count = got_ref.shape[0]
    got = got_ref[...].astype(f32)
    middle = 1 + count // 2
    halves = [jnp.sum(got[1:middle], axis=0), got[0] + jnp.sum(got[middle:], axis=0)]
    query = queries_ref[...].astype(f32)
    norm = jnp.sqrt(jnp.sum(query * query, axis=1, keepdims=True))
    unit = query / norm
    d_unit = jnp.concatenate([half[k : k + 1] for half in halves for k in range(4)], axis=1)
    d_queries_ref[...] = (d_unit - unit * jnp.sum(unit * d_unit, axis=1, keepdims=True)) / norm
    d_gain = jnp.concatenate([half[k : k + 1] for half in halves for k in range(4, 8)], axis=1)
    d_gain_ref[...] = d_gain / gain_ref[...]


def shape(dims, dtype=f32):
    return jax.ShapeDtypeStruct(dims, dtype)


def exchange(x):
    order = member_order(lax.axis_size("hash"))
    return lax.all_to_all(
        x, "hash", split_axis=0, concat_axis=0, axis_index_groups=[order], tiled=True
    )


def local(passages, queries, gain, candidates, teacher):
    count = lax.axis_size("hash")
    rows, width = passages.shape
    listed = candidates.shape[1]
    gain = gain.reshape(1, width)

    packed = pl.pallas_call(
        functools.partial(pack_kernel, rows),
        out_shape=shape((count, 8, width // 8 + listed), bf16),
        compiler_params=params(60),
        name="pack",
    )(queries, candidates, teacher)
    got = exchange(packed).reshape(count * 8, width // 8 + listed)

    pairs = count * 8
    near, far, gain_near = pl.pallas_call(
        stage_kernel,
        in_specs=[outside(), whole()],
        out_specs=[whole(), outside(), whole()],
        out_shape=[
            shape((rows, width // 2), bf16),
            shape((10 * rows, width // 2), bf16),
            shape((1, width)),
        ],
        scratch_shapes=[
            pltpu.VMEM((rows, width // 2), bf16),
            pltpu.SemaphoreType.DMA((2 * chunks,)),
            pltpu.SemaphoreType.DMA((chunks,)),
        ],
        compiler_params=params(48),
        name="stage",
        cost_estimate=pl.CostEstimate(
            flops=0, bytes_accessed=4 * rows * width, transcendentals=0
        ),
    )(passages, gain)
    half = width // 2
    core = (lax.axis_index("hash") % 2).astype(jnp.int32).reshape(1)
    raw, query, cols, lines, sums, theirs = pl.pallas_call(
        score_kernel,
        in_specs=[pl.BlockSpec(memory_space=pltpu.SMEM), whole(), whole(), whole(), outside()],
        out_shape=[
            shape((pairs, width), bf16),
            shape((count, width), bf16),
            shape((pairs, 128)),
            shape((8, pairs)),
            shape((count, 1, pairs)),
            shape((pairs, half), bf16),
        ],
        scratch_shapes=[
            pltpu.VMEM((rows, width // 2), bf16),
            pltpu.VMEM((width // 1024, pairs, 128), f32),
            pltpu.SemaphoreType.DMA((chunks // 2,)),
        ],
        compiler_params=params(48),
        name="score",
    )(core, got, gain_near, near, far)

    got_sums = exchange(sums)
    swap = [(i, i ^ 1) for i in range(count)]
    sibling_raw = lax.ppermute(theirs, "hash", swap)
    sibling_lines = lax.ppermute(lines, "hash", swap)

    def mixed(kernel, *operands):
        return pl.pallas_call(
            kernel,
            in_specs=[pl.BlockSpec(memory_space=pltpu.SMEM)] + [whole()] * (len(operands) + 2),
            out_shape=shape((3 * count + 8, half)),
            compiler_params=params(48),
            name="mix",
            cost_estimate=pl.CostEstimate(
                flops=8 * count * pairs * width, bytes_accessed=4 * pairs * width, transcendentals=0
            ),
        )(core, query, gain_near, *operands)

    mine = mixed(mine_kernel, raw, lines)
    both = mixed(both_kernel, sibling_raw, sibling_lines, mine)

    partial, total = pl.pallas_call(
        partial_kernel,
        out_shape=[shape((pairs, half // 4), bf16), shape((1, pairs))],
        scratch_shapes=[pltpu.VMEM((half // 512, pairs, 128), f32)],
        compiler_params=params(48),
        name="partial",
    )(got_sums, both)
    got_partial = exchange(partial.reshape(count, 8, half // 4))

    d_passages = pl.pallas_call(
        passage_kernel,
        in_specs=[whole()] * 6,
        out_specs=outside(),
        out_shape=shape((rows, width)),
        scratch_shapes=[pltpu.VMEM((rows, width), f32), pltpu.SemaphoreType.DMA((pieces,))],
        compiler_params=params(48),
        name="d_passages",
        cost_estimate=pl.CostEstimate(
            flops=4 * pairs * rows * width, bytes_accessed=4 * rows * width, transcendentals=0
        ),
    )(total, query, gain_near, raw, cols, lines)

    d_queries, d_gain = pl.pallas_call(
        final_kernel,
        out_shape=[shape((1, width)), shape((1, width))],
        compiler_params=params(48),
        name="final",
    )(got_partial, queries, gain)
    return (d_passages, d_queries, d_gain.reshape(width))


def solution(mesh):
    in_specs = (
        P(("groups", "hash"), None),
        P(("groups", "hash"), None),
        P(),
        P(("groups", "hash"), None),
        P(("groups", "hash"), None),
    )
    out_specs = (P(("groups", "hash"), None), P(("groups", "hash"), None), P("groups"))
    return jax.shard_map(local, mesh=mesh, in_specs=in_specs, out_specs=out_specs, check_vma=False)
```

```python
import functools

import jax
import jax.numpy as jnp
from jax import lax
from jax.experimental import pallas as pl
from jax.experimental.pallas import tpu as pltpu
from jax.sharding import PartitionSpec as P

score_scale = 20.0
loss_scale = 8192.0
teacher_div = 2.0
coef_scale = loss_scale * score_scale
chunks = 4
pieces = 8
f32 = jnp.float32
bf16 = jnp.bfloat16
vmem = pltpu.VMEM
nn_dims = (((1,), (0,)), ((), ()))


def dot(a, b, dims):
    return lax.dot_general(a, b, dims, preferred_element_type=f32)


def split(x):
    high = x.astype(bf16)
    low = (x - high.astype(f32)).astype(bf16)
    return high, low


def member_order(count):
    first = count // 2 + 1
    return [first, *range(0, count, 2), *(i for i in range(1, count, 2) if i != first)]


def member_slot(owner, count):
    first = count // 2 + 1
    half = owner >> 1
    odd = 1 + count // 2 + half - jnp.where(owner > first, 1, 0)
    return jnp.where((owner & 1) == 0, 1 + half, jnp.where(owner == first, 0, odd))


def params(megabytes):
    return pltpu.CompilerParams(vmem_limit_bytes=megabytes * 1024 * 1024)


def whole():
    return pl.BlockSpec(memory_space=vmem)


def outside():
    return pl.BlockSpec(memory_space=pltpu.HBM)


def pack_kernel(rows, queries_ref, candidates_ref, teacher_ref, out_ref):
    ids = candidates_ref[...]
    listed = ids.shape[1]
    count = out_ref.shape[0]
    width = queries_ref.shape[1] // 8
    query = queries_ref[...].astype(f32)
    query = jnp.concatenate([query[:, k * width : (k + 1) * width] for k in range(8)], axis=0)
    owner = lax.div(ids, rows)
    inside = ids - owner * rows
    slot = member_slot(owner, count)
    marks = jnp.exp(teacher_ref[...].astype(f32) * (1.0 / teacher_div))
    marks = marks / jnp.sum(marks, axis=1, keepdims=True)
    high, low = split(marks)
    values = jnp.concatenate(
        [
            (inside >> 8).astype(f32),
            (inside & 255).astype(f32),
            high.astype(f32),
            low.astype(f32),
            jnp.zeros((listed - 4, listed), f32),
        ],
        axis=0,
    )
    square = (listed, listed)
    across = jnp.broadcast_to(slot.astype(f32), square)
    same = across == jnp.transpose(across)
    earlier = same & (lax.broadcasted_iota(jnp.int32, square, 0) < lax.broadcasted_iota(jnp.int32, square, 1))
    rank = jnp.sum(jnp.where(earlier, 1.0, 0.0), axis=0, keepdims=True)
    place = slot * 8 + rank.astype(jnp.int32)
    spread = jnp.where(place == lax.broadcasted_iota(jnp.int32, (count * 8, listed), 0), 1.0, 0.0)
    lists = dot(spread.astype(bf16), jnp.transpose(values).astype(bf16), nn_dims)
    out_ref[:, :, :width] = jnp.broadcast_to(query.astype(bf16)[None], (count, 8, width))
    out_ref[:, :, width:] = lists.astype(bf16).reshape(count, 8, listed)


def belongs(dims, pair_axis):
    pair = lax.broadcasted_iota(jnp.int32, dims, pair_axis) >> 3
    return pair == lax.broadcasted_iota(jnp.int32, dims, 1 - pair_axis)


def stage_kernel(passages_ref, gain_ref, near_ref, far_ref, gain_out_ref, held, sems_in, sems_out):
    gain_out_ref[...] = gain_ref[...]
    rows, width = near_ref.shape
    rest = held.shape[1]
    piece = rows // chunks
    copies_in, copies_out, copies_near = [], [], []
    for k in range(chunks):
        part = pl.ds(k * piece, piece)
        far = passages_ref.at[part, pl.ds(width, rest)]
        near = passages_ref.at[part, pl.ds(0, width)]
        copies_in.append(pltpu.make_async_copy(far, held.at[part], sems_in.at[k]))
        copies_out.append(pltpu.make_async_copy(held.at[part], far_ref.at[part], sems_out.at[k]))
        copies_near.append(pltpu.make_async_copy(near, near_ref.at[part], sems_in.at[chunks + k]))
    for copy in copies_in + copies_near:
        copy.start()
    for k in range(chunks):
        copies_in[k].wait()
        copies_out[k].start()
    for copy in copies_near + copies_out:
        copy.wait()


def mix(base, first, query_ref, gain_ref, raw_ref, lines, out_ref, before_ref):
    queries = query_ref.shape[0]
    pairs = raw_ref.shape[0]
    chunk = out_ref.shape[1] // 2
    cols = jnp.transpose(jnp.concatenate([lines, jnp.zeros((120, pairs), f32)], axis=0))
    cos, inverse, query_inverse = cols[:, 2:3], cols[:, 3:4], cols[:, 5:6]
    own = belongs((queries, pairs), 1)
    by_weight = split(jnp.where(own, lines[0:1, :], 0.0))
    by_mark = split(jnp.where(own, lines[1:2, :], 0.0))
    plain = jnp.concatenate([*by_weight, *by_mark], axis=0)
    repeat = jnp.where(belongs((pairs, queries), 0), 1.0, 0.0).astype(bf16)
    for k in range(2):
        part = slice(k * chunk, (k + 1) * chunk)
        there = pl.ds(pl.multiple_of(base + k * chunk, 128), chunk)
        here = pl.ds(pl.multiple_of(first + k * chunk, 128), chunk)
        row = (raw_ref[:, here].astype(f32) * gain_ref[:, there] * inverse).astype(bf16)
        plainly = dot(plain, row, nn_dims)
        row = row.astype(f32)
        query = dot(repeat, query_ref[:, there], nn_dims) * query_inverse
        turned = row * (query.astype(bf16).astype(f32) - cos * row)
        turned = dot(plain, turned.astype(bf16), nn_dims)
        last = jnp.sum(turned[2 * queries :], axis=0, keepdims=True)
        sums = jnp.concatenate(
            [
                plainly[:queries] + plainly[queries : 2 * queries],
                plainly[2 * queries : 3 * queries] + plainly[3 * queries :],
                turned[:queries] + turned[queries : 2 * queries],
                jnp.broadcast_to(last, (8, chunk)),
            ],
            axis=0,
        )
        out_ref[:, part] = sums if before_ref is None else sums + before_ref[:, part]


def mine_kernel(core_ref, query_ref, gain_ref, raw_ref, rows_ref, out_ref):
    base = core_ref[0] * out_ref.shape[1]
    mix(base, base, query_ref, gain_ref, raw_ref, rows_ref[...], out_ref, None)


def both_kernel(core_ref, query_ref, gain_ref, raw_ref, rows_ref, mine_ref, out_ref):
    base = core_ref[0] * out_ref.shape[1]
    mix(base, 0, query_ref, gain_ref, raw_ref, rows_ref[...], out_ref, mine_ref)


def score_kernel(
    core_ref, got_ref, gain_ref, near_ref, far_ref,
    raw_ref, query_ref, cols_ref, rows_ref, sums_ref, theirs_ref, held, wide, sems,
):
    queries, width = query_ref.shape
    pairs = queries * 8
    rows = held.shape[0]
    chunk = width // chunks
    close = near_ref.shape[1] // chunk
    copies = []
    for k in range(chunks - close):
        part = pl.ds(k * chunk, chunk)
        copies.append(pltpu.make_async_copy(far_ref.at[pl.ds(0, rows), part], held.at[:, part], sems.at[k]))
        copies[-1].start()
    tiles = wide.shape[0]
    loaded = [got_ref[:, j * 128 : (j + 1) * 128].astype(f32) for j in range(tiles + 1)]
    squares = sum(x * x for x in loaded[:-1])
    squares = jnp.sum(squares, axis=1, keepdims=True).reshape(queries, 8, 1)
    squares = jnp.broadcast_to(jnp.sum(squares, axis=1, keepdims=True), (queries, 8, 1))
    query_inverse = 1.0 / jnp.sqrt(squares.reshape(pairs, 1))
    for j in range(tiles):
        wide[j] = loaded[j]
    query = [wide[j, pl.ds(k, queries, stride=8), :] for k in range(8) for j in range(tiles)]
    query = jnp.concatenate(query, axis=1).astype(bf16)
    query_ref[...] = query
    lists = loaded[-1]
    inside = lists[:, 0:1] * 256.0 + lists[:, 1:2]
    mark = lists[:, 2:3] + lists[:, 3:4]
    lane = lax.broadcasted_iota(jnp.int32, (pairs, rows), 1).astype(f32)
    pick = jnp.where(inside == lane, 1.0, 0.0).astype(bf16)
    size = jnp.zeros((pairs, 128), f32)
    along = [jnp.zeros((8, 128), f32)] * queries
    for k in range(chunks):
        part = slice(k * chunk, (k + 1) * chunk)
        if k < close:
            passages = near_ref[:, part]
        else:
            copies[k - close].wait()
            passages = held[:, slice((k - close) * chunk, (k - close + 1) * chunk)]
        raw = dot(pick, passages, nn_dims)
        raw_ref[:, part] = raw.astype(bf16)
        lifted = raw * gain_ref[:, part]
        for j in range(chunk // 128):
            tile = slice(j * 128, (j + 1) * 128)
            size = size + lifted[:, tile] * lifted[:, tile]
            eighth, place = divmod(k * chunk // 128 + j, tiles)
            for i in range(queries):
                row = wide[place, i * 8 + eighth : i * 8 + eighth + 1, :]
                along[i] = along[i] + lifted[i * 8 : i * 8 + 8, tile] * row
    there = theirs_ref.shape[1]
    theirs_ref[...] = raw_ref[:, pl.ds(pl.multiple_of((1 - core_ref[0]) * there, 128), there)]
    inverse = 1.0 / jnp.sqrt(jnp.sum(size, axis=1, keepdims=True))
    along = jnp.concatenate(along, axis=0)
    cos = jnp.sum(along, axis=1, keepdims=True) * inverse * query_inverse
    weight = jnp.where(mark > 0.0, jnp.exp(cos * score_scale), 0.0)
    lane = lax.broadcasted_iota(jnp.int32, (pairs, 128), 1)
    cols = jnp.zeros((pairs, 128), f32)
    for k, column in enumerate((weight, mark, cos, inverse, inside, query_inverse)):
        cols = jnp.where(lane == k, column, cols)
    cols_ref[...] = cols
    flipped = jnp.transpose(cols)[:8]
    rows_ref[...] = flipped
    sums_ref[...] = jnp.broadcast_to(flipped[None, :1], sums_ref.shape)


def partial_kernel(sums_ref, both_ref, out_ref, total_ref, laid):
    queries = sums_ref.shape[2] // 8
    width = both_ref.shape[1]
    total = jnp.sum(sums_ref[...][:, 0, :], axis=0, keepdims=True)
    total_ref[...] = total
    own = belongs((queries, total.shape[1]), 1)
    inverse = 1.0 / jnp.sum(jnp.where(own, total, 0.0), axis=1, keepdims=True)
    both = both_ref[...]
    partial = coef_scale * (both[:queries] * inverse - both[queries : 2 * queries])
    gain_part = jnp.sum(both[2 * queries : 3 * queries] * inverse, axis=0, keepdims=True)
    gain_part = coef_scale * (gain_part - both[3 * queries : 3 * queries + 1])
    tiles = laid.shape[0]
    for k in range(width // 128):
        row, tile = k // tiles, k % tiles
        part = slice(k * 128, (k + 1) * 128)
        laid[tile, pl.ds(row, queries, stride=8), :] = partial[:, part]
        laid[tile, pl.ds(4 + row, queries, stride=8), :] = jnp.broadcast_to(
            gain_part[:, part], (queries, 128)
        )
    for tile in range(tiles):
        out_ref[:, tile * 128 : (tile + 1) * 128] = laid[tile].astype(bf16)


def passage_kernel(total_ref, query_ref, gain_ref, raw_ref, cols_ref, rows_ref, out_ref, made, sems):
    queries, width = query_ref.shape
    rows, pairs = made.shape[0], raw_ref.shape[0]
    piece = width // pieces
    weight, mark = cols_ref[:, 0:1], cols_ref[:, 1:2]
    cos, inverse = cols_ref[:, 2:3], cols_ref[:, 3:4]
    square = (pairs, pairs)
    alike = (lax.broadcasted_iota(jnp.int32, square, 0) >> 3) == (
        lax.broadcasted_iota(jnp.int32, square, 1) >> 3
    )
    total = jnp.sum(jnp.where(alike, total_ref[...], 0.0), axis=1, keepdims=True)
    scale = coef_scale * (weight / total - mark) * inverse
    inside = rows_ref[4:5, :]
    spread = lax.broadcasted_iota(jnp.int32, (rows, pairs), 0).astype(f32) == inside
    spread = jnp.where(spread, 1.0, 0.0).astype(bf16)
    spread = jnp.concatenate([spread, spread], axis=1)
    repeat = jnp.where(belongs((pairs, queries), 0), 1.0, 0.0).astype(bf16)
    copies = []
    for k in range(pieces):
        part = slice(k * piece, (k + 1) * piece)
        gain = gain_ref[:, part]
        row = (raw_ref[:, part].astype(f32) * gain * inverse).astype(bf16).astype(f32)
        query = dot(repeat, query_ref[:, part], nn_dims) * cols_ref[:, 5:6]
        term = (query.astype(bf16).astype(f32) - cos * row) * scale * gain
        made[:, part] = dot(spread, jnp.concatenate(split(term), axis=0), nn_dims)
        part = pl.ds(k * piece, piece)
        copies.append(pltpu.make_async_copy(made.at[:, part], out_ref.at[:, part], sems.at[k]))
        copies[-1].start()
    for copy in copies:
        copy.wait()


def final_kernel(got_ref, queries_ref, gain_ref, d_queries_ref, d_gain_ref):
    count = got_ref.shape[0]
    got = got_ref[...].astype(f32)
    middle = 1 + count // 2
    halves = [jnp.sum(got[1:middle], axis=0), got[0] + jnp.sum(got[middle:], axis=0)]
    query = queries_ref[...].astype(f32)
    norm = jnp.sqrt(jnp.sum(query * query, axis=1, keepdims=True))
    unit = query / norm
    d_unit = jnp.concatenate([half[k : k + 1] for half in halves for k in range(4)], axis=1)
    d_queries_ref[...] = (d_unit - unit * jnp.sum(unit * d_unit, axis=1, keepdims=True)) / norm
    d_gain = jnp.concatenate([half[k : k + 1] for half in halves for k in range(4, 8)], axis=1)
    d_gain_ref[...] = d_gain / gain_ref[...]


def shape(dims, dtype=f32):
    return jax.ShapeDtypeStruct(dims, dtype)


def exchange(x):
    order = member_order(lax.axis_size("hash"))
    return lax.all_to_all(
        x, "hash", split_axis=0, concat_axis=0, axis_index_groups=[order], tiled=True
    )


def local(passages, queries, gain, candidates, teacher):
    count = lax.axis_size("hash")
    rows, width = passages.shape
    listed = candidates.shape[1]
    gain = gain.reshape(1, width)

    packed = pl.pallas_call(
        functools.partial(pack_kernel, rows),
        out_shape=shape((count, 8, width // 8 + listed), bf16),
        compiler_params=params(60),
        name="pack",
    )(queries, candidates, teacher)
    got = exchange(packed).reshape(count * 8, width // 8 + listed)

    pairs = count * 8
    near, far, gain_near = pl.pallas_call(
        stage_kernel,
        in_specs=[outside(), whole()],
        out_specs=[whole(), outside(), whole()],
        out_shape=[
            shape((rows, width - width // chunks), bf16),
            shape((20 * rows, width // chunks), bf16),
            shape((1, width)),
        ],
        scratch_shapes=[
            pltpu.VMEM((rows, width // chunks), bf16),
            pltpu.SemaphoreType.DMA((2 * chunks,)),
            pltpu.SemaphoreType.DMA((chunks,)),
        ],
        compiler_params=params(48),
        name="stage",
        cost_estimate=pl.CostEstimate(
            flops=0, bytes_accessed=4 * rows * width, transcendentals=0
        ),
    )(passages, gain)
    half = width // 2
    core = (lax.axis_index("hash") % 2).astype(jnp.int32).reshape(1)
    raw, query, cols, lines, sums, theirs = pl.pallas_call(
        score_kernel,
        in_specs=[pl.BlockSpec(memory_space=pltpu.SMEM), whole(), whole(), whole(), outside()],
        out_shape=[
            shape((pairs, width), bf16),
            shape((count, width), bf16),
            shape((pairs, 128)),
            shape((8, pairs)),
            shape((count, 1, pairs)),
            shape((pairs, half), bf16),
        ],
        scratch_shapes=[
            pltpu.VMEM((rows, width // chunks), bf16),
            pltpu.VMEM((width // 1024, pairs, 128), f32),
            pltpu.SemaphoreType.DMA((chunks // 2,)),
        ],
        compiler_params=params(48),
        name="score",
    )(core, got, gain_near, near, far)

    got_sums = exchange(sums)
    swap = [(i, i ^ 1) for i in range(count)]
    sibling_raw = lax.ppermute(theirs, "hash", swap)
    sibling_lines = lax.ppermute(lines, "hash", swap)

    def mixed(kernel, *operands):
        return pl.pallas_call(
            kernel,
            in_specs=[pl.BlockSpec(memory_space=pltpu.SMEM)] + [whole()] * (len(operands) + 2),
            out_shape=shape((3 * count + 8, half)),
            compiler_params=params(48),
            name="mix",
            cost_estimate=pl.CostEstimate(
                flops=8 * count * pairs * width, bytes_accessed=4 * pairs * width, transcendentals=0
            ),
        )(core, query, gain_near, *operands)

    mine = mixed(mine_kernel, raw, lines)
    both = mixed(both_kernel, sibling_raw, sibling_lines, mine)

    partial, total = pl.pallas_call(
        partial_kernel,
        out_shape=[shape((pairs, half // 4), bf16), shape((1, pairs))],
        scratch_shapes=[pltpu.VMEM((half // 512, pairs, 128), f32)],
        compiler_params=params(48),
        name="partial",
    )(got_sums, both)
    got_partial = exchange(partial.reshape(count, 8, half // 4))

    d_passages = pl.pallas_call(
        passage_kernel,
        in_specs=[whole()] * 6,
        out_specs=outside(),
        out_shape=shape((rows, width)),
        scratch_shapes=[pltpu.VMEM((rows, width), f32), pltpu.SemaphoreType.DMA((pieces,))],
        compiler_params=params(48),
        name="d_passages",
        cost_estimate=pl.CostEstimate(
            flops=4 * pairs * rows * width, bytes_accessed=4 * rows * width, transcendentals=0
        ),
    )(total, query, gain_near, raw, cols, lines)

    d_queries, d_gain = pl.pallas_call(
        final_kernel,
        out_shape=[shape((1, width)), shape((1, width))],
        compiler_params=params(48),
        name="final",
    )(got_partial, queries, gain)
    return (d_passages, d_queries, d_gain.reshape(width))


def solution(mesh):
    in_specs = (
        P(("groups", "hash"), None),
        P(("groups", "hash"), None),
        P(),
        P(("groups", "hash"), None),
        P(("groups", "hash"), None),
    )
    out_specs = (P(("groups", "hash"), None), P(("groups", "hash"), None), P("groups"))
    return jax.shard_map(local, mesh=mesh, in_specs=in_specs, out_specs=out_specs, check_vma=False)
```

```python
import functools

import jax
import jax.numpy as jnp
from jax import lax
from jax.experimental import pallas as pl
from jax.experimental.pallas import tpu as pltpu
from jax.sharding import PartitionSpec as P

score_scale = 20.0
loss_scale = 8192.0
teacher_div = 2.0
coef_scale = loss_scale * score_scale
chunks = 4
taken = 16
close = 11
pieces = 8
f32 = jnp.float32
bf16 = jnp.bfloat16
vmem = pltpu.VMEM
nn_dims = (((1,), (0,)), ((), ()))


def dot(a, b, dims):
    return lax.dot_general(a, b, dims, preferred_element_type=f32)


def split(x):
    high = x.astype(bf16)
    low = (x - high.astype(f32)).astype(bf16)
    return high, low


def member_order(count):
    first = count // 2 + 1
    return [first, *range(0, count, 2), *(i for i in range(1, count, 2) if i != first)]


def member_slot(owner, count):
    first = count // 2 + 1
    half = owner >> 1
    odd = 1 + count // 2 + half - jnp.where(owner > first, 1, 0)
    return jnp.where((owner & 1) == 0, 1 + half, jnp.where(owner == first, 0, odd))


def params(megabytes):
    return pltpu.CompilerParams(vmem_limit_bytes=megabytes * 1024 * 1024)


def whole():
    return pl.BlockSpec(memory_space=vmem)


def outside():
    return pl.BlockSpec(memory_space=pltpu.HBM)


def pack_kernel(rows, queries_ref, candidates_ref, teacher_ref, out_ref):
    ids = candidates_ref[...]
    listed = ids.shape[1]
    count = out_ref.shape[0]
    width = queries_ref.shape[1] // 8
    query = queries_ref[...].astype(f32)
    query = jnp.concatenate([query[:, k * width : (k + 1) * width] for k in range(8)], axis=0)
    owner = lax.div(ids, rows)
    inside = ids - owner * rows
    slot = member_slot(owner, count)
    marks = jnp.exp(teacher_ref[...].astype(f32) * (1.0 / teacher_div))
    marks = marks / jnp.sum(marks, axis=1, keepdims=True)
    high, low = split(marks)
    values = jnp.concatenate(
        [
            (inside >> 8).astype(f32),
            (inside & 255).astype(f32),
            high.astype(f32),
            low.astype(f32),
            jnp.zeros((listed - 4, listed), f32),
        ],
        axis=0,
    )
    square = (listed, listed)
    across = jnp.broadcast_to(slot.astype(f32), square)
    same = across == jnp.transpose(across)
    earlier = same & (lax.broadcasted_iota(jnp.int32, square, 0) < lax.broadcasted_iota(jnp.int32, square, 1))
    rank = jnp.sum(jnp.where(earlier, 1.0, 0.0), axis=0, keepdims=True)
    place = slot * 8 + rank.astype(jnp.int32)
    spread = jnp.where(place == lax.broadcasted_iota(jnp.int32, (count * 8, listed), 0), 1.0, 0.0)
    lists = dot(spread.astype(bf16), jnp.transpose(values).astype(bf16), nn_dims)
    out_ref[:, :, :width] = jnp.broadcast_to(query.astype(bf16)[None], (count, 8, width))
    out_ref[:, :, width:] = lists.astype(bf16).reshape(count, 8, listed)


def belongs(dims, pair_axis):
    pair = lax.broadcasted_iota(jnp.int32, dims, pair_axis) >> 3
    return pair == lax.broadcasted_iota(jnp.int32, dims, 1 - pair_axis)


def stage_kernel(passages_ref, gain_ref, near_ref, far_ref, gain_out_ref, held, sems_in, sems_out):
    gain_out_ref[...] = gain_ref[...]
    rows, width = near_ref.shape
    rest = held.shape[1]
    piece = rows // chunks
    copies_in, copies_out, copies_near = [], [], []
    for k in range(chunks):
        part = pl.ds(k * piece, piece)
        far = passages_ref.at[part, pl.ds(width, rest)]
        near = passages_ref.at[part, pl.ds(0, width)]
        copies_in.append(pltpu.make_async_copy(far, held.at[part], sems_in.at[k]))
        copies_out.append(pltpu.make_async_copy(held.at[part], far_ref.at[part], sems_out.at[k]))
        copies_near.append(pltpu.make_async_copy(near, near_ref.at[part], sems_in.at[chunks + k]))
    for copy in copies_in + copies_near:
        copy.start()
    for k in range(chunks):
        copies_in[k].wait()
        copies_out[k].start()
    for copy in copies_near + copies_out:
        copy.wait()


def mix(base, first, query_ref, gain_ref, raw_ref, lines, out_ref, before_ref):
    queries = query_ref.shape[0]
    pairs = raw_ref.shape[0]
    chunk = out_ref.shape[1] // 2
    cols = jnp.transpose(jnp.concatenate([lines, jnp.zeros((120, pairs), f32)], axis=0))
    cos, inverse, query_inverse = cols[:, 2:3], cols[:, 3:4], cols[:, 5:6]
    own = belongs((queries, pairs), 1)
    by_weight = split(jnp.where(own, lines[0:1, :], 0.0))
    by_mark = split(jnp.where(own, lines[1:2, :], 0.0))
    plain = jnp.concatenate([*by_weight, *by_mark], axis=0)
    repeat = jnp.where(belongs((pairs, queries), 0), 1.0, 0.0).astype(bf16)
    for k in range(2):
        part = slice(k * chunk, (k + 1) * chunk)
        there = pl.ds(pl.multiple_of(base + k * chunk, 128), chunk)
        here = pl.ds(pl.multiple_of(first + k * chunk, 128), chunk)
        row = (raw_ref[:, here].astype(f32) * gain_ref[:, there] * inverse).astype(bf16)
        plainly = dot(plain, row, nn_dims)
        row = row.astype(f32)
        query = dot(repeat, query_ref[:, there], nn_dims) * query_inverse
        turned = row * (query.astype(bf16).astype(f32) - cos * row)
        turned = dot(plain, turned.astype(bf16), nn_dims)
        last = jnp.sum(turned[2 * queries :], axis=0, keepdims=True)
        sums = jnp.concatenate(
            [
                plainly[:queries] + plainly[queries : 2 * queries],
                plainly[2 * queries : 3 * queries] + plainly[3 * queries :],
                turned[:queries] + turned[queries : 2 * queries],
                jnp.broadcast_to(last, (8, chunk)),
            ],
            axis=0,
        )
        out_ref[:, part] = sums if before_ref is None else sums + before_ref[:, part]


def mine_kernel(core_ref, query_ref, gain_ref, raw_ref, rows_ref, out_ref):
    base = core_ref[0] * out_ref.shape[1]
    mix(base, base, query_ref, gain_ref, raw_ref, rows_ref[...], out_ref, None)


def both_kernel(core_ref, query_ref, gain_ref, raw_ref, rows_ref, mine_ref, out_ref):
    base = core_ref[0] * out_ref.shape[1]
    mix(base, 0, query_ref, gain_ref, raw_ref, rows_ref[...], out_ref, mine_ref)


def score_kernel(
    core_ref, got_ref, gain_ref, near_ref, far_ref,
    raw_ref, query_ref, cols_ref, rows_ref, sums_ref, theirs_ref, held, wide, sems,
):
    queries, width = query_ref.shape
    pairs = queries * 8
    rows = held.shape[0]
    chunk = width // taken
    copies = []
    for k in range(taken - close):
        part = pl.ds(k * chunk, chunk)
        copies.append(pltpu.make_async_copy(far_ref.at[pl.ds(0, rows), part], held.at[:, part], sems.at[k]))
        copies[-1].start()
    tiles = wide.shape[0]
    loaded = [got_ref[:, j * 128 : (j + 1) * 128].astype(f32) for j in range(tiles + 1)]
    squares = sum(x * x for x in loaded[:-1])
    squares = jnp.sum(squares, axis=1, keepdims=True).reshape(queries, 8, 1)
    squares = jnp.broadcast_to(jnp.sum(squares, axis=1, keepdims=True), (queries, 8, 1))
    query_inverse = 1.0 / jnp.sqrt(squares.reshape(pairs, 1))
    for j in range(tiles):
        wide[j] = loaded[j]
    query = [wide[j, pl.ds(k, queries, stride=8), :] for k in range(8) for j in range(tiles)]
    query = jnp.concatenate(query, axis=1).astype(bf16)
    query_ref[...] = query
    lists = loaded[-1]
    inside = lists[:, 0:1] * 256.0 + lists[:, 1:2]
    mark = lists[:, 2:3] + lists[:, 3:4]
    lane = lax.broadcasted_iota(jnp.int32, (pairs, rows), 1).astype(f32)
    pick = jnp.where(inside == lane, 1.0, 0.0).astype(bf16)
    size = jnp.zeros((pairs, 128), f32)
    along = [jnp.zeros((8, 128), f32)] * queries
    for k in range(taken):
        part = slice(k * chunk, (k + 1) * chunk)
        if k < close:
            passages = near_ref[:, part]
        else:
            copies[k - close].wait()
            passages = held[:, slice((k - close) * chunk, (k - close + 1) * chunk)]
        raw = dot(pick, passages, nn_dims)
        raw_ref[:, part] = raw.astype(bf16)
        lifted = raw * gain_ref[:, part]
        for j in range(chunk // 128):
            tile = slice(j * 128, (j + 1) * 128)
            size = size + lifted[:, tile] * lifted[:, tile]
            eighth, place = divmod(k * chunk // 128 + j, tiles)
            for i in range(queries):
                row = wide[place, i * 8 + eighth : i * 8 + eighth + 1, :]
                along[i] = along[i] + lifted[i * 8 : i * 8 + 8, tile] * row
    there = theirs_ref.shape[1]
    theirs_ref[...] = raw_ref[:, pl.ds(pl.multiple_of((1 - core_ref[0]) * there, 128), there)]
    inverse = 1.0 / jnp.sqrt(jnp.sum(size, axis=1, keepdims=True))
    along = jnp.concatenate(along, axis=0)
    cos = jnp.sum(along, axis=1, keepdims=True) * inverse * query_inverse
    weight = jnp.where(mark > 0.0, jnp.exp(cos * score_scale), 0.0)
    lane = lax.broadcasted_iota(jnp.int32, (pairs, 128), 1)
    cols = jnp.zeros((pairs, 128), f32)
    for k, column in enumerate((weight, mark, cos, inverse, inside, query_inverse)):
        cols = jnp.where(lane == k, column, cols)
    cols_ref[...] = cols
    flipped = jnp.transpose(cols)[:8]
    rows_ref[...] = flipped
    sums_ref[...] = jnp.broadcast_to(flipped[None, :1], sums_ref.shape)


def partial_kernel(sums_ref, both_ref, out_ref, total_ref, laid):
    queries = sums_ref.shape[2] // 8
    width = both_ref.shape[1]
    total = jnp.sum(sums_ref[...][:, 0, :], axis=0, keepdims=True)
    total_ref[...] = total
    own = belongs((queries, total.shape[1]), 1)
    inverse = 1.0 / jnp.sum(jnp.where(own, total, 0.0), axis=1, keepdims=True)
    both = both_ref[...]
    partial = coef_scale * (both[:queries] * inverse - both[queries : 2 * queries])
    gain_part = jnp.sum(both[2 * queries : 3 * queries] * inverse, axis=0, keepdims=True)
    gain_part = coef_scale * (gain_part - both[3 * queries : 3 * queries + 1])
    tiles = laid.shape[0]
    for k in range(width // 128):
        row, tile = k // tiles, k % tiles
        part = slice(k * 128, (k + 1) * 128)
        laid[tile, pl.ds(row, queries, stride=8), :] = partial[:, part]
        laid[tile, pl.ds(4 + row, queries, stride=8), :] = jnp.broadcast_to(
            gain_part[:, part], (queries, 128)
        )
    for tile in range(tiles):
        out_ref[:, tile * 128 : (tile + 1) * 128] = laid[tile].astype(bf16)


def passage_kernel(total_ref, query_ref, gain_ref, raw_ref, cols_ref, rows_ref, out_ref, made, sems):
    queries, width = query_ref.shape
    rows, pairs = made.shape[0], raw_ref.shape[0]
    piece = width // pieces
    weight, mark = cols_ref[:, 0:1], cols_ref[:, 1:2]
    cos, inverse = cols_ref[:, 2:3], cols_ref[:, 3:4]
    square = (pairs, pairs)
    alike = (lax.broadcasted_iota(jnp.int32, square, 0) >> 3) == (
        lax.broadcasted_iota(jnp.int32, square, 1) >> 3
    )
    total = jnp.sum(jnp.where(alike, total_ref[...], 0.0), axis=1, keepdims=True)
    scale = coef_scale * (weight / total - mark) * inverse
    inside = rows_ref[4:5, :]
    spread = lax.broadcasted_iota(jnp.int32, (rows, pairs), 0).astype(f32) == inside
    spread = jnp.where(spread, 1.0, 0.0).astype(bf16)
    spread = jnp.concatenate([spread, spread], axis=1)
    repeat = jnp.where(belongs((pairs, queries), 0), 1.0, 0.0).astype(bf16)
    copies = []
    for k in range(pieces):
        part = slice(k * piece, (k + 1) * piece)
        gain = gain_ref[:, part]
        row = (raw_ref[:, part].astype(f32) * gain * inverse).astype(bf16).astype(f32)
        query = dot(repeat, query_ref[:, part], nn_dims) * cols_ref[:, 5:6]
        term = (query.astype(bf16).astype(f32) - cos * row) * scale * gain
        made[:, part] = dot(spread, jnp.concatenate(split(term), axis=0), nn_dims)
        part = pl.ds(k * piece, piece)
        copies.append(pltpu.make_async_copy(made.at[:, part], out_ref.at[:, part], sems.at[k]))
        copies[-1].start()
    for copy in copies:
        copy.wait()


def final_kernel(got_ref, queries_ref, gain_ref, d_queries_ref, d_gain_ref):
    count = got_ref.shape[0]
    got = got_ref[...].astype(f32)
    middle = 1 + count // 2
    halves = [jnp.sum(got[1:middle], axis=0), got[0] + jnp.sum(got[middle:], axis=0)]
    query = queries_ref[...].astype(f32)
    norm = jnp.sqrt(jnp.sum(query * query, axis=1, keepdims=True))
    unit = query / norm
    d_unit = jnp.concatenate([half[k : k + 1] for half in halves for k in range(4)], axis=1)
    d_queries_ref[...] = (d_unit - unit * jnp.sum(unit * d_unit, axis=1, keepdims=True)) / norm
    d_gain = jnp.concatenate([half[k : k + 1] for half in halves for k in range(4, 8)], axis=1)
    d_gain_ref[...] = d_gain / gain_ref[...]


def shape(dims, dtype=f32):
    return jax.ShapeDtypeStruct(dims, dtype)


def exchange(x):
    order = member_order(lax.axis_size("hash"))
    return lax.all_to_all(
        x, "hash", split_axis=0, concat_axis=0, axis_index_groups=[order], tiled=True
    )


def local(passages, queries, gain, candidates, teacher):
    count = lax.axis_size("hash")
    rows, width = passages.shape
    listed = candidates.shape[1]
    gain = gain.reshape(1, width)

    packed = pl.pallas_call(
        functools.partial(pack_kernel, rows),
        out_shape=shape((count, 8, width // 8 + listed), bf16),
        compiler_params=params(60),
        name="pack",
    )(queries, candidates, teacher)
    got = exchange(packed).reshape(count * 8, width // 8 + listed)

    pairs = count * 8
    far_width = (taken - close) * width // taken
    near, far, gain_near = pl.pallas_call(
        stage_kernel,
        in_specs=[outside(), whole()],
        out_specs=[whole(), outside(), whole()],
        out_shape=[
            shape((rows, close * width // taken), bf16),
            shape((16 * rows, far_width), bf16),
            shape((1, width)),
        ],
        scratch_shapes=[
            pltpu.VMEM((rows, far_width), bf16),
            pltpu.SemaphoreType.DMA((2 * chunks,)),
            pltpu.SemaphoreType.DMA((chunks,)),
        ],
        compiler_params=params(48),
        name="stage",
        cost_estimate=pl.CostEstimate(
            flops=0, bytes_accessed=4 * rows * width, transcendentals=0
        ),
    )(passages, gain)
    half = width // 2
    core = (lax.axis_index("hash") % 2).astype(jnp.int32).reshape(1)
    raw, query, cols, lines, sums, theirs = pl.pallas_call(
        score_kernel,
        in_specs=[pl.BlockSpec(memory_space=pltpu.SMEM), whole(), whole(), whole(), outside()],
        out_shape=[
            shape((pairs, width), bf16),
            shape((count, width), bf16),
            shape((pairs, 128)),
            shape((8, pairs)),
            shape((count, 1, pairs)),
            shape((pairs, half), bf16),
        ],
        scratch_shapes=[
            pltpu.VMEM((rows, far_width), bf16),
            pltpu.VMEM((width // 1024, pairs, 128), f32),
            pltpu.SemaphoreType.DMA((taken - close,)),
        ],
        compiler_params=params(48),
        name="score",
    )(core, got, gain_near, near, far)

    got_sums = exchange(sums)
    swap = [(i, i ^ 1) for i in range(count)]
    sibling_raw = lax.ppermute(theirs, "hash", swap)
    sibling_lines = lax.ppermute(lines, "hash", swap)

    def mixed(kernel, *operands):
        return pl.pallas_call(
            kernel,
            in_specs=[pl.BlockSpec(memory_space=pltpu.SMEM)] + [whole()] * (len(operands) + 2),
            out_shape=shape((3 * count + 8, half)),
            compiler_params=params(48),
            name="mix",
            cost_estimate=pl.CostEstimate(
                flops=8 * count * pairs * width, bytes_accessed=4 * pairs * width, transcendentals=0
            ),
        )(core, query, gain_near, *operands)

    mine = mixed(mine_kernel, raw, lines)
    both = mixed(both_kernel, sibling_raw, sibling_lines, mine)

    partial, total = pl.pallas_call(
        partial_kernel,
        out_shape=[shape((pairs, half // 4), bf16), shape((1, pairs))],
        scratch_shapes=[pltpu.VMEM((half // 512, pairs, 128), f32)],
        compiler_params=params(48),
        name="partial",
    )(got_sums, both)
    got_partial = exchange(partial.reshape(count, 8, half // 4))

    d_passages = pl.pallas_call(
        passage_kernel,
        in_specs=[whole()] * 6,
        out_specs=outside(),
        out_shape=shape((rows, width)),
        scratch_shapes=[pltpu.VMEM((rows, width), f32), pltpu.SemaphoreType.DMA((pieces,))],
        compiler_params=params(48),
        name="d_passages",
        cost_estimate=pl.CostEstimate(
            flops=4 * pairs * rows * width, bytes_accessed=4 * rows * width, transcendentals=0
        ),
    )(total, query, gain_near, raw, cols, lines)

    d_queries, d_gain = pl.pallas_call(
        final_kernel,
        out_shape=[shape((1, width)), shape((1, width))],
        compiler_params=params(48),
        name="final",
    )(got_partial, queries, gain)
    return (d_passages, d_queries, d_gain.reshape(width))


def solution(mesh):
    in_specs = (
        P(("groups", "hash"), None),
        P(("groups", "hash"), None),
        P(),
        P(("groups", "hash"), None),
        P(("groups", "hash"), None),
    )
    out_specs = (P(("groups", "hash"), None), P(("groups", "hash"), None), P("groups"))
    return jax.shard_map(local, mesh=mesh, in_specs=in_specs, out_specs=out_specs, check_vma=False)
```

```python
import functools

import jax
import jax.numpy as jnp
from jax import lax
from jax.experimental import pallas as pl
from jax.experimental.pallas import tpu as pltpu
from jax.sharding import PartitionSpec as P

score_scale = 20.0
loss_scale = 8192.0
teacher_div = 2.0
coef_scale = loss_scale * score_scale
chunks = 4
taken = 8
close = 5
pieces = 8
f32 = jnp.float32
bf16 = jnp.bfloat16
vmem = pltpu.VMEM
nn_dims = (((1,), (0,)), ((), ()))


def dot(a, b, dims):
    return lax.dot_general(a, b, dims, preferred_element_type=f32)


def split(x):
    high = x.astype(bf16)
    low = (x - high.astype(f32)).astype(bf16)
    return high, low


def member_order(count):
    first = count // 2 + 1
    return [first, *range(0, count, 2), *(i for i in range(1, count, 2) if i != first)]


def member_slot(owner, count):
    first = count // 2 + 1
    half = owner >> 1
    odd = 1 + count // 2 + half - jnp.where(owner > first, 1, 0)
    return jnp.where((owner & 1) == 0, 1 + half, jnp.where(owner == first, 0, odd))


def params(megabytes):
    return pltpu.CompilerParams(vmem_limit_bytes=megabytes * 1024 * 1024)


def whole():
    return pl.BlockSpec(memory_space=vmem)


def outside():
    return pl.BlockSpec(memory_space=pltpu.HBM)


def pack_kernel(rows, queries_ref, candidates_ref, teacher_ref, out_ref):
    ids = candidates_ref[...]
    listed = ids.shape[1]
    count = out_ref.shape[0]
    width = queries_ref.shape[1] // 8
    query = queries_ref[...].astype(f32)
    query = jnp.concatenate([query[:, k * width : (k + 1) * width] for k in range(8)], axis=0)
    owner = lax.div(ids, rows)
    inside = ids - owner * rows
    slot = member_slot(owner, count)
    marks = jnp.exp(teacher_ref[...].astype(f32) * (1.0 / teacher_div))
    marks = marks / jnp.sum(marks, axis=1, keepdims=True)
    high, low = split(marks)
    values = jnp.concatenate(
        [
            (inside >> 8).astype(f32),
            (inside & 255).astype(f32),
            high.astype(f32),
            low.astype(f32),
            jnp.zeros((listed - 4, listed), f32),
        ],
        axis=0,
    )
    square = (listed, listed)
    across = jnp.broadcast_to(slot.astype(f32), square)
    same = across == jnp.transpose(across)
    earlier = same & (lax.broadcasted_iota(jnp.int32, square, 0) < lax.broadcasted_iota(jnp.int32, square, 1))
    rank = jnp.sum(jnp.where(earlier, 1.0, 0.0), axis=0, keepdims=True)
    place = slot * 8 + rank.astype(jnp.int32)
    spread = jnp.where(place == lax.broadcasted_iota(jnp.int32, (count * 8, listed), 0), 1.0, 0.0)
    lists = dot(spread.astype(bf16), jnp.transpose(values).astype(bf16), nn_dims)
    out_ref[:, :, :width] = jnp.broadcast_to(query.astype(bf16)[None], (count, 8, width))
    out_ref[:, :, width:] = lists.astype(bf16).reshape(count, 8, listed)


def belongs(dims, pair_axis):
    pair = lax.broadcasted_iota(jnp.int32, dims, pair_axis) >> 3
    return pair == lax.broadcasted_iota(jnp.int32, dims, 1 - pair_axis)


def stage_kernel(passages_ref, gain_ref, near_ref, far_ref, gain_out_ref, held, sems_in, sems_out):
    gain_out_ref[...] = gain_ref[...]
    rows, width = near_ref.shape
    rest = held.shape[1]
    piece = rows // chunks
    copies_in, copies_out, copies_near = [], [], []
    for k in range(chunks):
        part = pl.ds(k * piece, piece)
        far = passages_ref.at[part, pl.ds(width, rest)]
        near = passages_ref.at[part, pl.ds(0, width)]
        copies_in.append(pltpu.make_async_copy(far, held.at[part], sems_in.at[k]))
        copies_out.append(pltpu.make_async_copy(held.at[part], far_ref.at[part], sems_out.at[k]))
        copies_near.append(pltpu.make_async_copy(near, near_ref.at[part], sems_in.at[chunks + k]))
    for copy in copies_in + copies_near:
        copy.start()
    for k in range(chunks):
        copies_in[k].wait()
        copies_out[k].start()
    for copy in copies_near + copies_out:
        copy.wait()


def mix(base, first, query_ref, gain_ref, raw_ref, lines, out_ref, before_ref):
    queries = query_ref.shape[0]
    pairs = raw_ref.shape[0]
    chunk = out_ref.shape[1] // 2
    cols = jnp.transpose(jnp.concatenate([lines, jnp.zeros((120, pairs), f32)], axis=0))
    cos, inverse, query_inverse = cols[:, 2:3], cols[:, 3:4], cols[:, 5:6]
    own = belongs((queries, pairs), 1)
    by_weight = split(jnp.where(own, lines[0:1, :], 0.0))
    by_mark = split(jnp.where(own, lines[1:2, :], 0.0))
    plain = jnp.concatenate([*by_weight, *by_mark], axis=0)
    repeat = jnp.where(belongs((pairs, queries), 0), 1.0, 0.0).astype(bf16)
    for k in range(2):
        part = slice(k * chunk, (k + 1) * chunk)
        there = pl.ds(pl.multiple_of(base + k * chunk, 128), chunk)
        here = pl.ds(pl.multiple_of(first + k * chunk, 128), chunk)
        row = (raw_ref[:, here].astype(f32) * gain_ref[:, there] * inverse).astype(bf16)
        plainly = dot(plain, row, nn_dims)
        row = row.astype(f32)
        query = dot(repeat, query_ref[:, there], nn_dims) * query_inverse
        turned = row * (query.astype(bf16).astype(f32) - cos * row)
        turned = dot(plain, turned.astype(bf16), nn_dims)
        last = jnp.sum(turned[2 * queries :], axis=0, keepdims=True)
        sums = jnp.concatenate(
            [
                plainly[:queries] + plainly[queries : 2 * queries],
                plainly[2 * queries : 3 * queries] + plainly[3 * queries :],
                turned[:queries] + turned[queries : 2 * queries],
                jnp.broadcast_to(last, (8, chunk)),
            ],
            axis=0,
        )
        out_ref[:, part] = sums if before_ref is None else sums + before_ref[:, part]


def mine_kernel(core_ref, query_ref, gain_ref, raw_ref, rows_ref, out_ref):
    base = core_ref[0] * out_ref.shape[1]
    mix(base, base, query_ref, gain_ref, raw_ref, rows_ref[...], out_ref, None)


def both_kernel(core_ref, query_ref, gain_ref, raw_ref, rows_ref, mine_ref, out_ref):
    base = core_ref[0] * out_ref.shape[1]
    mix(base, 0, query_ref, gain_ref, raw_ref, rows_ref[...], out_ref, mine_ref)


def score_kernel(
    core_ref, got_ref, gain_ref, near_ref, far_ref,
    raw_ref, query_ref, cols_ref, rows_ref, sums_ref, theirs_ref, held, wide, sems,
):
    queries, width = query_ref.shape
    pairs = queries * 8
    rows = held.shape[0]
    split_at = near_ref.shape[1]
    copy = pltpu.make_async_copy(far_ref.at[pl.ds(0, rows)], held, sems.at[0])
    copy.start()
    tiles = wide.shape[0]
    loaded = [got_ref[:, j * 128 : (j + 1) * 128].astype(f32) for j in range(tiles + 1)]
    squares = sum(x * x for x in loaded[:-1])
    squares = jnp.sum(squares, axis=1, keepdims=True).reshape(queries, 8, 1)
    squares = jnp.broadcast_to(jnp.sum(squares, axis=1, keepdims=True), (queries, 8, 1))
    query_inverse = 1.0 / jnp.sqrt(squares.reshape(pairs, 1))
    for j in range(tiles):
        wide[j] = loaded[j]
    query = [wide[j, pl.ds(k, queries, stride=8), :] for k in range(8) for j in range(tiles)]
    query = jnp.concatenate(query, axis=1).astype(bf16)
    query_ref[...] = query
    lists = loaded[-1]
    inside = lists[:, 0:1] * 256.0 + lists[:, 1:2]
    mark = lists[:, 2:3] + lists[:, 3:4]
    lane = lax.broadcasted_iota(jnp.int32, (pairs, rows), 1).astype(f32)
    pick = jnp.where(inside == lane, 1.0, 0.0).astype(bf16)
    size = jnp.zeros((pairs, 128), f32)
    along = [jnp.zeros((8, 128), f32)] * queries
    for begin, end, source in ((0, split_at, near_ref), (split_at, width, held)):
        if source is held:
            copy.wait()
        raw = dot(pick, source[...], nn_dims)
        raw_ref[:, begin:end] = raw.astype(bf16)
        lifted = raw * gain_ref[:, begin:end]
        for j in range((end - begin) // 128):
            tile = lifted[:, j * 128 : (j + 1) * 128]
            size = size + tile * tile
            eighth, place = divmod(begin // 128 + j, tiles)
            for i in range(queries):
                row = wide[place, i * 8 + eighth : i * 8 + eighth + 1, :]
                along[i] = along[i] + tile[i * 8 : i * 8 + 8] * row
    there = theirs_ref.shape[1]
    theirs_ref[...] = raw_ref[:, pl.ds(pl.multiple_of((1 - core_ref[0]) * there, 128), there)]
    inverse = 1.0 / jnp.sqrt(jnp.sum(size, axis=1, keepdims=True))
    along = jnp.concatenate(along, axis=0)
    cos = jnp.sum(along, axis=1, keepdims=True) * inverse * query_inverse
    weight = jnp.where(mark > 0.0, jnp.exp(cos * score_scale), 0.0)
    lane = lax.broadcasted_iota(jnp.int32, (pairs, 128), 1)
    cols = jnp.zeros((pairs, 128), f32)
    for k, column in enumerate((weight, mark, cos, inverse, inside, query_inverse)):
        cols = jnp.where(lane == k, column, cols)
    cols_ref[...] = cols
    flipped = jnp.transpose(cols)[:8]
    rows_ref[...] = flipped
    sums_ref[...] = jnp.broadcast_to(flipped[None, :1], sums_ref.shape)


def partial_kernel(sums_ref, both_ref, out_ref, total_ref, laid):
    queries = sums_ref.shape[2] // 8
    width = both_ref.shape[1]
    total = jnp.sum(sums_ref[...][:, 0, :], axis=0, keepdims=True)
    total_ref[...] = total
    own = belongs((queries, total.shape[1]), 1)
    inverse = 1.0 / jnp.sum(jnp.where(own, total, 0.0), axis=1, keepdims=True)
    both = both_ref[...]
    partial = coef_scale * (both[:queries] * inverse - both[queries : 2 * queries])
    gain_part = jnp.sum(both[2 * queries : 3 * queries] * inverse, axis=0, keepdims=True)
    gain_part = coef_scale * (gain_part - both[3 * queries : 3 * queries + 1])
    tiles = laid.shape[0]
    for k in range(width // 128):
        row, tile = k // tiles, k % tiles
        part = slice(k * 128, (k + 1) * 128)
        laid[tile, pl.ds(row, queries, stride=8), :] = partial[:, part]
        laid[tile, pl.ds(4 + row, queries, stride=8), :] = jnp.broadcast_to(
            gain_part[:, part], (queries, 128)
        )
    for tile in range(tiles):
        out_ref[:, tile * 128 : (tile + 1) * 128] = laid[tile].astype(bf16)


def passage_kernel(total_ref, query_ref, gain_ref, raw_ref, cols_ref, rows_ref, out_ref, made, sems):
    queries, width = query_ref.shape
    rows, pairs = made.shape[0], raw_ref.shape[0]
    piece = width // pieces
    weight, mark = cols_ref[:, 0:1], cols_ref[:, 1:2]
    cos, inverse = cols_ref[:, 2:3], cols_ref[:, 3:4]
    square = (pairs, pairs)
    alike = (lax.broadcasted_iota(jnp.int32, square, 0) >> 3) == (
        lax.broadcasted_iota(jnp.int32, square, 1) >> 3
    )
    total = jnp.sum(jnp.where(alike, total_ref[...], 0.0), axis=1, keepdims=True)
    scale = coef_scale * (weight / total - mark) * inverse
    inside = rows_ref[4:5, :]
    spread = lax.broadcasted_iota(jnp.int32, (rows, pairs), 0).astype(f32) == inside
    spread = jnp.where(spread, 1.0, 0.0).astype(bf16)
    spread = jnp.concatenate([spread, spread], axis=1)
    repeat = jnp.where(belongs((pairs, queries), 0), 1.0, 0.0).astype(bf16)
    copies = []
    for k in range(pieces):
        part = slice(k * piece, (k + 1) * piece)
        gain = gain_ref[:, part]
        row = (raw_ref[:, part].astype(f32) * gain * inverse).astype(bf16).astype(f32)
        query = dot(repeat, query_ref[:, part], nn_dims) * cols_ref[:, 5:6]
        term = (query.astype(bf16).astype(f32) - cos * row) * scale * gain
        made[:, part] = dot(spread, jnp.concatenate(split(term), axis=0), nn_dims)
        part = pl.ds(k * piece, piece)
        copies.append(pltpu.make_async_copy(made.at[:, part], out_ref.at[:, part], sems.at[k]))
        copies[-1].start()
    for copy in copies:
        copy.wait()


def final_kernel(got_ref, queries_ref, gain_ref, d_queries_ref, d_gain_ref):
    count = got_ref.shape[0]
    got = got_ref[...].astype(f32)
    middle = 1 + count // 2
    halves = [jnp.sum(got[1:middle], axis=0), got[0] + jnp.sum(got[middle:], axis=0)]
    query = queries_ref[...].astype(f32)
    norm = jnp.sqrt(jnp.sum(query * query, axis=1, keepdims=True))
    unit = query / norm
    d_unit = jnp.concatenate([half[k : k + 1] for half in halves for k in range(4)], axis=1)
    d_queries_ref[...] = (d_unit - unit * jnp.sum(unit * d_unit, axis=1, keepdims=True)) / norm
    d_gain = jnp.concatenate([half[k : k + 1] for half in halves for k in range(4, 8)], axis=1)
    d_gain_ref[...] = d_gain / gain_ref[...]


def shape(dims, dtype=f32):
    return jax.ShapeDtypeStruct(dims, dtype)


def exchange(x):
    order = member_order(lax.axis_size("hash"))
    return lax.all_to_all(
        x, "hash", split_axis=0, concat_axis=0, axis_index_groups=[order], tiled=True
    )


def local(passages, queries, gain, candidates, teacher):
    count = lax.axis_size("hash")
    rows, width = passages.shape
    listed = candidates.shape[1]
    gain = gain.reshape(1, width)

    packed = pl.pallas_call(
        functools.partial(pack_kernel, rows),
        out_shape=shape((count, 8, width // 8 + listed), bf16),
        compiler_params=params(60),
        name="pack",
    )(queries, candidates, teacher)
    got = exchange(packed).reshape(count * 8, width // 8 + listed)

    pairs = count * 8
    far_width = (taken - close) * width // taken
    near, far, gain_near = pl.pallas_call(
        stage_kernel,
        in_specs=[outside(), whole()],
        out_specs=[whole(), outside(), whole()],
        out_shape=[
            shape((rows, close * width // taken), bf16),
            shape((16 * rows, far_width), bf16),
            shape((1, width)),
        ],
        scratch_shapes=[
            pltpu.VMEM((rows, far_width), bf16),
            pltpu.SemaphoreType.DMA((2 * chunks,)),
            pltpu.SemaphoreType.DMA((chunks,)),
        ],
        compiler_params=params(48),
        name="stage",
        cost_estimate=pl.CostEstimate(
            flops=0, bytes_accessed=4 * rows * width, transcendentals=0
        ),
    )(passages, gain)
    half = width // 2
    core = (lax.axis_index("hash") % 2).astype(jnp.int32).reshape(1)
    raw, query, cols, lines, sums, theirs = pl.pallas_call(
        score_kernel,
        in_specs=[pl.BlockSpec(memory_space=pltpu.SMEM), whole(), whole(), whole(), outside()],
        out_shape=[
            shape((pairs, width), bf16),
            shape((count, width), bf16),
            shape((pairs, 128)),
            shape((8, pairs)),
            shape((count, 1, pairs)),
            shape((pairs, half), bf16),
        ],
        scratch_shapes=[
            pltpu.VMEM((rows, far_width), bf16),
            pltpu.VMEM((width // 1024, pairs, 128), f32),
            pltpu.SemaphoreType.DMA((1,)),
        ],
        compiler_params=params(48),
        name="score",
    )(core, got, gain_near, near, far)

    got_sums = exchange(sums)
    swap = [(i, i ^ 1) for i in range(count)]
    sibling_raw = lax.ppermute(theirs, "hash", swap)
    sibling_lines = lax.ppermute(lines, "hash", swap)

    def mixed(kernel, *operands):
        return pl.pallas_call(
            kernel,
            in_specs=[pl.BlockSpec(memory_space=pltpu.SMEM)] + [whole()] * (len(operands) + 2),
            out_shape=shape((3 * count + 8, half)),
            compiler_params=params(48),
            name="mix",
            cost_estimate=pl.CostEstimate(
                flops=8 * count * pairs * width, bytes_accessed=4 * pairs * width, transcendentals=0
            ),
        )(core, query, gain_near, *operands)

    mine = mixed(mine_kernel, raw, lines)
    both = mixed(both_kernel, sibling_raw, sibling_lines, mine)

    partial, total = pl.pallas_call(
        partial_kernel,
        out_shape=[shape((pairs, half // 4), bf16), shape((1, pairs))],
        scratch_shapes=[pltpu.VMEM((half // 512, pairs, 128), f32)],
        compiler_params=params(48),
        name="partial",
    )(got_sums, both)
    got_partial = exchange(partial.reshape(count, 8, half // 4))

    d_passages = pl.pallas_call(
        passage_kernel,
        in_specs=[whole()] * 6,
        out_specs=outside(),
        out_shape=shape((rows, width)),
        scratch_shapes=[pltpu.VMEM((rows, width), f32), pltpu.SemaphoreType.DMA((pieces,))],
        compiler_params=params(48),
        name="d_passages",
        cost_estimate=pl.CostEstimate(
            flops=4 * pairs * rows * width, bytes_accessed=4 * rows * width, transcendentals=0
        ),
    )(total, query, gain_near, raw, cols, lines)

    d_queries, d_gain = pl.pallas_call(
        final_kernel,
        out_shape=[shape((1, width)), shape((1, width))],
        compiler_params=params(48),
        name="final",
    )(got_partial, queries, gain)
    return (d_passages, d_queries, d_gain.reshape(width))


def solution(mesh):
    in_specs = (
        P(("groups", "hash"), None),
        P(("groups", "hash"), None),
        P(),
        P(("groups", "hash"), None),
        P(("groups", "hash"), None),
    )
    out_specs = (P(("groups", "hash"), None), P(("groups", "hash"), None), P("groups"))
    return jax.shard_map(local, mesh=mesh, in_specs=in_specs, out_specs=out_specs, check_vma=False)
```

```python
import functools

import jax
import jax.numpy as jnp
from jax import lax
from jax.experimental import pallas as pl
from jax.experimental.pallas import tpu as pltpu
from jax.sharding import PartitionSpec as P

score_scale = 20.0
loss_scale = 8192.0
teacher_div = 2.0
coef_scale = loss_scale * score_scale
chunks = 4
pieces = 8
f32 = jnp.float32
bf16 = jnp.bfloat16
vmem = pltpu.VMEM
nn_dims = (((1,), (0,)), ((), ()))


def dot(a, b, dims):
    return lax.dot_general(a, b, dims, preferred_element_type=f32)


def split(x):
    high = x.astype(bf16)
    low = (x - high.astype(f32)).astype(bf16)
    return high, low


def member_order(count):
    first = count // 2 + 1
    return [first, *range(0, count, 2), *(i for i in range(1, count, 2) if i != first)]


def member_slot(owner, count):
    first = count // 2 + 1
    half = owner >> 1
    odd = 1 + count // 2 + half - jnp.where(owner > first, 1, 0)
    return jnp.where((owner & 1) == 0, 1 + half, jnp.where(owner == first, 0, odd))


def params(megabytes):
    return pltpu.CompilerParams(vmem_limit_bytes=megabytes * 1024 * 1024)


def whole():
    return pl.BlockSpec(memory_space=vmem)


def outside():
    return pl.BlockSpec(memory_space=pltpu.HBM)


def pack_kernel(rows, queries_ref, candidates_ref, teacher_ref, out_ref):
    ids = candidates_ref[...]
    listed = ids.shape[1]
    count = out_ref.shape[0]
    width = queries_ref.shape[1] // 8
    query = queries_ref[...].astype(f32)
    query = jnp.concatenate([query[:, k * width : (k + 1) * width] for k in range(8)], axis=0)
    owner = lax.div(ids, rows)
    inside = ids - owner * rows
    slot = member_slot(owner, count)
    marks = jnp.exp(teacher_ref[...].astype(f32) * (1.0 / teacher_div))
    marks = marks / jnp.sum(marks, axis=1, keepdims=True)
    high, low = split(marks)
    values = jnp.concatenate(
        [
            (inside >> 8).astype(f32),
            (inside & 255).astype(f32),
            high.astype(f32),
            low.astype(f32),
            jnp.zeros((listed - 4, listed), f32),
        ],
        axis=0,
    )
    square = (listed, listed)
    across = jnp.broadcast_to(slot.astype(f32), square)
    same = across == jnp.transpose(across)
    earlier = same & (lax.broadcasted_iota(jnp.int32, square, 0) < lax.broadcasted_iota(jnp.int32, square, 1))
    rank = jnp.sum(jnp.where(earlier, 1.0, 0.0), axis=0, keepdims=True)
    place = slot * 8 + rank.astype(jnp.int32)
    spread = jnp.where(place == lax.broadcasted_iota(jnp.int32, (count * 8, listed), 0), 1.0, 0.0)
    lists = dot(spread.astype(bf16), jnp.transpose(values).astype(bf16), nn_dims)
    out_ref[:, :, :width] = jnp.broadcast_to(query.astype(bf16)[None], (count, 8, width))
    out_ref[:, :, width:] = lists.astype(bf16).reshape(count, 8, listed)


def belongs(dims, pair_axis):
    pair = lax.broadcasted_iota(jnp.int32, dims, pair_axis) >> 3
    return pair == lax.broadcasted_iota(jnp.int32, dims, 1 - pair_axis)


def stage_kernel(passages_ref, gain_ref, near_ref, far_ref, norms_ref, raw, gains, held, sems_in, sems_out, sem):
    rows, width = near_ref.shape
    piece = rows // pieces
    gain_copy = pltpu.make_async_copy(gain_ref, gains, sem.at[0])
    gain_copy.start()
    copies_in, copies_out, inverses = [], [], []
    for k in range(pieces):
        part = pl.ds(k * piece, piece)
        copies_in.append(pltpu.make_async_copy(passages_ref.at[part], raw.at[part], sems_in.at[k]))
        copies_out.append(pltpu.make_async_copy(held.at[part], far_ref.at[part], sems_out.at[k]))
        copies_in[-1].start()
    gain_copy.wait()
    for k in range(pieces):
        part = pl.ds(k * piece, piece)
        copies_in[k].wait()
        lifted = raw[part, :].astype(f32) * gains[...]
        inverse = 1.0 / jnp.sqrt(jnp.sum(lifted * lifted, axis=1, keepdims=True))
        unit = (lifted * inverse).astype(bf16)
        held[part, :] = unit[:, width:]
        copies_out[k].start()
        near_ref[part, :] = unit[:, :width]
        inverses.append(inverse)
    inverse = jnp.concatenate(inverses, axis=0)
    norms_ref[...] = jnp.transpose(jnp.broadcast_to(inverse, (rows, 128)))[:1, :]
    for copy in copies_out:
        copy.wait()


def mix(base, first, query_ref, units_ref, lines, out_ref, before_ref):
    queries = query_ref.shape[0]
    pairs = units_ref.shape[0]
    chunk = out_ref.shape[1] // 2
    cols = jnp.transpose(jnp.concatenate([lines, jnp.zeros((120, pairs), f32)], axis=0))
    cos, query_inverse = cols[:, 2:3], cols[:, 5:6]
    own = belongs((queries, pairs), 1)
    by_weight = split(jnp.where(own, lines[0:1, :], 0.0))
    by_mark = split(jnp.where(own, lines[1:2, :], 0.0))
    plain = jnp.concatenate([*by_weight, *by_mark], axis=0)
    repeat = jnp.where(belongs((pairs, queries), 0), 1.0, 0.0).astype(bf16)
    for k in range(2):
        part = slice(k * chunk, (k + 1) * chunk)
        there = pl.ds(pl.multiple_of(base + k * chunk, 128), chunk)
        here = pl.ds(pl.multiple_of(first + k * chunk, 128), chunk)
        row = units_ref[:, here]
        plainly = dot(plain, row, nn_dims)
        row = row.astype(f32)
        query = dot(repeat, query_ref[:, there], nn_dims) * query_inverse
        turned = row * (query.astype(bf16).astype(f32) - cos * row)
        turned = dot(plain, turned.astype(bf16), nn_dims)
        last = jnp.sum(turned[2 * queries :], axis=0, keepdims=True)
        sums = jnp.concatenate(
            [
                plainly[:queries] + plainly[queries : 2 * queries],
                plainly[2 * queries : 3 * queries] + plainly[3 * queries :],
                turned[:queries] + turned[queries : 2 * queries],
                jnp.broadcast_to(last, (8, chunk)),
            ],
            axis=0,
        )
        out_ref[:, part] = sums if before_ref is None else sums + before_ref[:, part]


def mine_kernel(core_ref, query_ref, units_ref, rows_ref, out_ref):
    base = core_ref[0] * out_ref.shape[1]
    mix(base, base, query_ref, units_ref, rows_ref[...], out_ref, None)


def both_kernel(core_ref, query_ref, units_ref, rows_ref, mine_ref, out_ref):
    base = core_ref[0] * out_ref.shape[1]
    mix(base, 0, query_ref, units_ref, rows_ref[...], out_ref, mine_ref)


def score_kernel(
    core_ref, got_ref, norms_ref, near_ref, far_ref,
    units_ref, query_ref, cols_ref, rows_ref, sums_ref, theirs_ref, held, wide, sems,
):
    queries, width = query_ref.shape
    pairs = queries * 8
    rows = held.shape[0]
    chunk = width // chunks
    half = chunks // 2
    copies = []
    for k in range(half):
        part = pl.ds(k * chunk, chunk)
        copies.append(pltpu.make_async_copy(far_ref.at[pl.ds(0, rows), part], held.at[:, part], sems.at[k]))
        copies[-1].start()
    tiles = wide.shape[0]
    loaded = [got_ref[:, j * 128 : (j + 1) * 128].astype(f32) for j in range(tiles + 1)]
    squares = sum(x * x for x in loaded[:-1])
    squares = jnp.sum(squares, axis=1, keepdims=True).reshape(queries, 8, 1)
    squares = jnp.broadcast_to(jnp.sum(squares, axis=1, keepdims=True), (queries, 8, 1))
    query_inverse = 1.0 / jnp.sqrt(squares.reshape(pairs, 1))
    for j in range(tiles):
        wide[j] = loaded[j]
    query = [wide[j, pl.ds(k, queries, stride=8), :] for k in range(8) for j in range(tiles)]
    query = jnp.concatenate(query, axis=1).astype(bf16)
    query_ref[...] = query
    lists = loaded[-1]
    inside = lists[:, 0:1] * 256.0 + lists[:, 1:2]
    mark = lists[:, 2:3] + lists[:, 3:4]
    lane = lax.broadcasted_iota(jnp.int32, (pairs, rows), 1).astype(f32)
    here = inside == lane
    inverse = jnp.sum(jnp.where(here, norms_ref[...], 0.0), axis=1, keepdims=True)
    pick = jnp.where(here, 1.0, 0.0).astype(bf16)
    along = [jnp.zeros((8, 128), f32)] * queries
    for k in range(chunks):
        part = slice(k * chunk, (k + 1) * chunk)
        if k < half:
            passages = near_ref[:, part]
        else:
            copies[k - half].wait()
            passages = held[:, slice((k - half) * chunk, (k - half + 1) * chunk)]
        units = dot(pick, passages, nn_dims)
        units_ref[:, part] = units.astype(bf16)
        for j in range(chunk // 128):
            tile = slice(j * 128, (j + 1) * 128)
            eighth, place = divmod(k * chunk // 128 + j, tiles)
            for i in range(queries):
                row = wide[place, i * 8 + eighth : i * 8 + eighth + 1, :]
                along[i] = along[i] + units[i * 8 : i * 8 + 8, tile] * row
    there = theirs_ref.shape[1]
    theirs_ref[...] = units_ref[:, pl.ds(pl.multiple_of((1 - core_ref[0]) * there, 128), there)]
    along = jnp.concatenate(along, axis=0)
    cos = jnp.sum(along, axis=1, keepdims=True) * query_inverse
    weight = jnp.where(mark > 0.0, jnp.exp(cos * score_scale), 0.0)
    lane = lax.broadcasted_iota(jnp.int32, (pairs, 128), 1)
    cols = jnp.zeros((pairs, 128), f32)
    for k, column in enumerate((weight, mark, cos, inverse, inside, query_inverse)):
        cols = jnp.where(lane == k, column, cols)
    cols_ref[...] = cols
    flipped = jnp.transpose(cols)[:8]
    rows_ref[...] = flipped
    sums_ref[...] = jnp.broadcast_to(flipped[None, :1], sums_ref.shape)


def partial_kernel(sums_ref, both_ref, out_ref, total_ref, laid):
    queries = sums_ref.shape[2] // 8
    width = both_ref.shape[1]
    total = jnp.sum(sums_ref[...][:, 0, :], axis=0, keepdims=True)
    total_ref[...] = total
    own = belongs((queries, total.shape[1]), 1)
    inverse = 1.0 / jnp.sum(jnp.where(own, total, 0.0), axis=1, keepdims=True)
    both = both_ref[...]
    partial = coef_scale * (both[:queries] * inverse - both[queries : 2 * queries])
    gain_part = jnp.sum(both[2 * queries : 3 * queries] * inverse, axis=0, keepdims=True)
    gain_part = coef_scale * (gain_part - both[3 * queries : 3 * queries + 1])
    tiles = laid.shape[0]
    for k in range(width // 128):
        row, tile = k // tiles, k % tiles
        part = slice(k * 128, (k + 1) * 128)
        laid[tile, pl.ds(row, queries, stride=8), :] = partial[:, part]
        laid[tile, pl.ds(4 + row, queries, stride=8), :] = jnp.broadcast_to(
            gain_part[:, part], (queries, 128)
        )
    for tile in range(tiles):
        out_ref[:, tile * 128 : (tile + 1) * 128] = laid[tile].astype(bf16)


def passage_kernel(total_ref, query_ref, gain_ref, units_ref, cols_ref, rows_ref, out_ref, made, sems):
    queries, width = query_ref.shape
    rows, pairs = made.shape[0], units_ref.shape[0]
    piece = width // pieces
    weight, mark = cols_ref[:, 0:1], cols_ref[:, 1:2]
    cos, inverse = cols_ref[:, 2:3], cols_ref[:, 3:4]
    square = (pairs, pairs)
    alike = (lax.broadcasted_iota(jnp.int32, square, 0) >> 3) == (
        lax.broadcasted_iota(jnp.int32, square, 1) >> 3
    )
    total = jnp.sum(jnp.where(alike, total_ref[...], 0.0), axis=1, keepdims=True)
    scale = coef_scale * (weight / total - mark) * inverse
    inside = rows_ref[4:5, :]
    spread = lax.broadcasted_iota(jnp.int32, (rows, pairs), 0).astype(f32) == inside
    spread = jnp.where(spread, 1.0, 0.0).astype(bf16)
    spread = jnp.concatenate([spread, spread], axis=1)
    repeat = jnp.where(belongs((pairs, queries), 0), 1.0, 0.0).astype(bf16)
    copies = []
    for k in range(pieces):
        part = slice(k * piece, (k + 1) * piece)
        gain = gain_ref[:, part]
        row = units_ref[:, part].astype(f32)
        query = dot(repeat, query_ref[:, part], nn_dims) * cols_ref[:, 5:6]
        term = (query.astype(bf16).astype(f32) - cos * row) * scale * gain
        made[:, part] = dot(spread, jnp.concatenate(split(term), axis=0), nn_dims)
        part = pl.ds(k * piece, piece)
        copies.append(pltpu.make_async_copy(made.at[:, part], out_ref.at[:, part], sems.at[k]))
        copies[-1].start()
    for copy in copies:
        copy.wait()


def final_kernel(got_ref, queries_ref, gain_ref, d_queries_ref, d_gain_ref):
    count = got_ref.shape[0]
    got = got_ref[...].astype(f32)
    middle = 1 + count // 2
    halves = [jnp.sum(got[1:middle], axis=0), got[0] + jnp.sum(got[middle:], axis=0)]
    query = queries_ref[...].astype(f32)
    norm = jnp.sqrt(jnp.sum(query * query, axis=1, keepdims=True))
    unit = query / norm
    d_unit = jnp.concatenate([half[k : k + 1] for half in halves for k in range(4)], axis=1)
    d_queries_ref[...] = (d_unit - unit * jnp.sum(unit * d_unit, axis=1, keepdims=True)) / norm
    d_gain = jnp.concatenate([half[k : k + 1] for half in halves for k in range(4, 8)], axis=1)
    d_gain_ref[...] = d_gain / gain_ref[...]


def shape(dims, dtype=f32):
    return jax.ShapeDtypeStruct(dims, dtype)


def exchange(x):
    order = member_order(lax.axis_size("hash"))
    return lax.all_to_all(
        x, "hash", split_axis=0, concat_axis=0, axis_index_groups=[order], tiled=True
    )


def local(passages, queries, gain, candidates, teacher):
    count = lax.axis_size("hash")
    rows, width = passages.shape
    listed = candidates.shape[1]
    gain = gain.reshape(1, width)

    packed = pl.pallas_call(
        functools.partial(pack_kernel, rows),
        out_shape=shape((count, 8, width // 8 + listed), bf16),
        compiler_params=params(60),
        name="pack",
    )(queries, candidates, teacher)
    got = exchange(packed).reshape(count * 8, width // 8 + listed)

    pairs = count * 8
    near, far, norms = pl.pallas_call(
        stage_kernel,
        in_specs=[outside(), outside()],
        out_specs=[whole(), outside(), whole()],
        out_shape=[
            shape((rows, width // 2), bf16),
            shape((10 * rows, width // 2), bf16),
            shape((1, rows)),
        ],
        scratch_shapes=[
            pltpu.VMEM((rows, width), bf16),
            pltpu.VMEM((1, width), f32),
            pltpu.VMEM((rows, width // 2), bf16),
            pltpu.SemaphoreType.DMA((pieces,)),
            pltpu.SemaphoreType.DMA((pieces,)),
            pltpu.SemaphoreType.DMA((1,)),
        ],
        compiler_params=params(48),
        name="stage",
        cost_estimate=pl.CostEstimate(
            flops=0, bytes_accessed=4 * rows * width, transcendentals=0
        ),
    )(passages, gain)
    half = width // 2
    core = (lax.axis_index("hash") % 2).astype(jnp.int32).reshape(1)
    units, query, cols, lines, sums, theirs = pl.pallas_call(
        score_kernel,
        in_specs=[pl.BlockSpec(memory_space=pltpu.SMEM), whole(), whole(), whole(), outside()],
        out_shape=[
            shape((pairs, width), bf16),
            shape((count, width), bf16),
            shape((pairs, 128)),
            shape((8, pairs)),
            shape((count, 1, pairs)),
            shape((pairs, half), bf16),
        ],
        scratch_shapes=[
            pltpu.VMEM((rows, width // 2), bf16),
            pltpu.VMEM((width // 1024, pairs, 128), f32),
            pltpu.SemaphoreType.DMA((chunks // 2,)),
        ],
        compiler_params=params(48),
        name="score",
    )(core, got, norms, near, far)

    got_sums = exchange(sums)
    swap = [(i, i ^ 1) for i in range(count)]
    sibling_units = lax.ppermute(theirs, "hash", swap)
    sibling_lines = lax.ppermute(lines, "hash", swap)

    def mixed(kernel, *operands):
        return pl.pallas_call(
            kernel,
            in_specs=[pl.BlockSpec(memory_space=pltpu.SMEM)] + [whole()] * (len(operands) + 1),
            out_shape=shape((3 * count + 8, half)),
            compiler_params=params(48),
            name="mix",
            cost_estimate=pl.CostEstimate(
                flops=8 * count * pairs * width, bytes_accessed=4 * pairs * width, transcendentals=0
            ),
        )(core, query, *operands)

    mine = mixed(mine_kernel, units, lines)
    both = mixed(both_kernel, sibling_units, sibling_lines, mine)

    partial, total = pl.pallas_call(
        partial_kernel,
        out_shape=[shape((pairs, half // 4), bf16), shape((1, pairs))],
        scratch_shapes=[pltpu.VMEM((half // 512, pairs, 128), f32)],
        compiler_params=params(48),
        name="partial",
    )(got_sums, both)
    got_partial = exchange(partial.reshape(count, 8, half // 4))

    d_passages = pl.pallas_call(
        passage_kernel,
        in_specs=[whole()] * 6,
        out_specs=outside(),
        out_shape=shape((rows, width)),
        scratch_shapes=[pltpu.VMEM((rows, width), f32), pltpu.SemaphoreType.DMA((pieces,))],
        compiler_params=params(48),
        name="d_passages",
        cost_estimate=pl.CostEstimate(
            flops=4 * pairs * rows * width, bytes_accessed=4 * rows * width, transcendentals=0
        ),
    )(total, query, gain, units, cols, lines)

    d_queries, d_gain = pl.pallas_call(
        final_kernel,
        out_shape=[shape((1, width)), shape((1, width))],
        compiler_params=params(48),
        name="final",
    )(got_partial, queries, gain)
    return (d_passages, d_queries, d_gain.reshape(width))


def solution(mesh):
    in_specs = (
        P(("groups", "hash"), None),
        P(("groups", "hash"), None),
        P(),
        P(("groups", "hash"), None),
        P(("groups", "hash"), None),
    )
    out_specs = (P(("groups", "hash"), None), P(("groups", "hash"), None), P("groups"))
    return jax.shard_map(local, mesh=mesh, in_specs=in_specs, out_specs=out_specs, check_vma=False)
```

```python
import functools

import jax
import jax.numpy as jnp
from jax import lax
from jax.experimental import pallas as pl
from jax.experimental.pallas import tpu as pltpu
from jax.sharding import PartitionSpec as P

score_scale = 20.0
loss_scale = 8192.0
teacher_div = 2.0
coef_scale = loss_scale * score_scale
chunks = 4
pieces = 8
f32 = jnp.float32
bf16 = jnp.bfloat16
vmem = pltpu.VMEM
nn_dims = (((1,), (0,)), ((), ()))


def dot(a, b, dims):
    return lax.dot_general(a, b, dims, preferred_element_type=f32)


def split(x):
    high = x.astype(bf16)
    low = (x - high.astype(f32)).astype(bf16)
    return high, low


def member_order(count):
    first = count // 2 + 1
    return [first, *range(0, count, 2), *(i for i in range(1, count, 2) if i != first)]


def member_slot(owner, count):
    first = count // 2 + 1
    half = owner >> 1
    odd = 1 + count // 2 + half - jnp.where(owner > first, 1, 0)
    return jnp.where((owner & 1) == 0, 1 + half, jnp.where(owner == first, 0, odd))


def params(megabytes):
    return pltpu.CompilerParams(vmem_limit_bytes=megabytes * 1024 * 1024)


def whole():
    return pl.BlockSpec(memory_space=vmem)


def outside():
    return pl.BlockSpec(memory_space=pltpu.HBM)


def pack_kernel(rows, queries_ref, candidates_ref, teacher_ref, out_ref):
    ids = candidates_ref[...]
    listed = ids.shape[1]
    count = out_ref.shape[0]
    width = queries_ref.shape[1] // 8
    query = queries_ref[...].astype(f32)
    query = jnp.concatenate([query[:, k * width : (k + 1) * width] for k in range(8)], axis=0)
    owner = lax.div(ids, rows)
    inside = ids - owner * rows
    slot = member_slot(owner, count)
    marks = jnp.exp(teacher_ref[...].astype(f32) * (1.0 / teacher_div))
    marks = marks / jnp.sum(marks, axis=1, keepdims=True)
    high, low = split(marks)
    values = jnp.concatenate(
        [
            (inside >> 8).astype(f32),
            (inside & 255).astype(f32),
            high.astype(f32),
            low.astype(f32),
            jnp.zeros((listed - 4, listed), f32),
        ],
        axis=0,
    )
    square = (listed, listed)
    across = jnp.broadcast_to(slot.astype(f32), square)
    same = across == jnp.transpose(across)
    earlier = same & (lax.broadcasted_iota(jnp.int32, square, 0) < lax.broadcasted_iota(jnp.int32, square, 1))
    rank = jnp.sum(jnp.where(earlier, 1.0, 0.0), axis=0, keepdims=True)
    place = slot * 8 + rank.astype(jnp.int32)
    spread = jnp.where(place == lax.broadcasted_iota(jnp.int32, (count * 8, listed), 0), 1.0, 0.0)
    lists = dot(spread.astype(bf16), jnp.transpose(values).astype(bf16), nn_dims)
    out_ref[:, :, :width] = jnp.broadcast_to(query.astype(bf16)[None], (count, 8, width))
    out_ref[:, :, width:] = lists.astype(bf16).reshape(count, 8, listed)


def belongs(dims, pair_axis):
    pair = lax.broadcasted_iota(jnp.int32, dims, pair_axis) >> 3
    return pair == lax.broadcasted_iota(jnp.int32, dims, 1 - pair_axis)


def stage_kernel(passages_ref, gain_ref, near_ref, far_ref, gain_out_ref, held, sems_in, sems_out):
    gain_out_ref[...] = gain_ref[...]
    rows, width = near_ref.shape
    piece = rows // chunks
    copies_in, copies_out, copies_near = [], [], []
    for k in range(chunks):
        part = pl.ds(k * piece, piece)
        far = passages_ref.at[part, pl.ds(width, width)]
        near = passages_ref.at[part, pl.ds(0, width)]
        copies_in.append(pltpu.make_async_copy(far, held.at[part], sems_in.at[k]))
        copies_out.append(pltpu.make_async_copy(held.at[part], far_ref.at[part], sems_out.at[k]))
        copies_near.append(pltpu.make_async_copy(near, near_ref.at[part], sems_in.at[chunks + k]))
    for copy in copies_in + copies_near:
        copy.start()
    for k in range(chunks):
        copies_in[k].wait()
        copies_out[k].start()
    for copy in copies_near + copies_out:
        copy.wait()


def mix(base, first, query_ref, gain_ref, raw_ref, lines, out_ref, before_ref):
    queries = query_ref.shape[0]
    pairs = raw_ref.shape[0]
    chunk = out_ref.shape[1] // 2
    cols = jnp.transpose(jnp.concatenate([lines, jnp.zeros((120, pairs), f32)], axis=0))
    cos, inverse, query_inverse = cols[:, 2:3], cols[:, 3:4], cols[:, 5:6]
    own = belongs((queries, pairs), 1)
    by_weight = split(jnp.where(own, lines[0:1, :], 0.0))
    by_mark = split(jnp.where(own, lines[1:2, :], 0.0))
    plain = jnp.concatenate([*by_weight, *by_mark], axis=0)
    repeat = jnp.where(belongs((pairs, queries), 0), 1.0, 0.0).astype(bf16)
    for k in range(2):
        part = slice(k * chunk, (k + 1) * chunk)
        there = pl.ds(pl.multiple_of(base + k * chunk, 128), chunk)
        here = pl.ds(pl.multiple_of(first + k * chunk, 128), chunk)
        row = (raw_ref[:, here].astype(f32) * gain_ref[:, there] * inverse).astype(bf16)
        plainly = dot(plain, row, nn_dims)
        row = row.astype(f32)
        query = dot(repeat, query_ref[:, there], nn_dims) * query_inverse
        turned = row * (query.astype(bf16).astype(f32) - cos * row)
        turned = dot(plain, turned.astype(bf16), nn_dims)
        last = jnp.sum(turned[2 * queries :], axis=0, keepdims=True)
        sums = jnp.concatenate(
            [
                plainly[:queries] + plainly[queries : 2 * queries],
                plainly[2 * queries : 3 * queries] + plainly[3 * queries :],
                turned[:queries] + turned[queries : 2 * queries],
                jnp.broadcast_to(last, (8, chunk)),
            ],
            axis=0,
        )
        out_ref[:, part] = sums if before_ref is None else sums + before_ref[:, part]


def mine_kernel(core_ref, query_ref, gain_ref, raw_ref, rows_ref, out_ref):
    base = core_ref[0] * out_ref.shape[1]
    mix(base, base, query_ref, gain_ref, raw_ref, rows_ref[...], out_ref, None)


def both_kernel(core_ref, query_ref, gain_ref, raw_ref, rows_ref, mine_ref, out_ref):
    base = core_ref[0] * out_ref.shape[1]
    mix(base, 0, query_ref, gain_ref, raw_ref, rows_ref[...], out_ref, mine_ref)


def score_kernel(
    core_ref, got_ref, gain_ref, near_ref, far_ref,
    raw_ref, query_ref, cols_ref, rows_ref, sums_ref, theirs_ref, held, wide, sems,
):
    queries, width = query_ref.shape
    pairs = queries * 8
    rows = held.shape[0]
    chunk = width // chunks
    half = chunks // 2
    copies = []
    piece = rows // chunks
    for k in range(half):
        part = pl.ds(k * chunk, chunk)
        copies.append([])
        for j in range(chunks):
            down = pl.ds(j * piece, piece)
            there, here = far_ref.at[down, part], held.at[down, part]
            copies[k].append(pltpu.make_async_copy(there, here, sems.at[k * chunks + j]))
            copies[k][j].start()
    tiles = wide.shape[0]
    loaded = [got_ref[:, j * 128 : (j + 1) * 128].astype(f32) for j in range(tiles + 1)]
    squares = sum(x * x for x in loaded[:-1])
    squares = jnp.sum(squares, axis=1, keepdims=True).reshape(queries, 8, 1)
    squares = jnp.broadcast_to(jnp.sum(squares, axis=1, keepdims=True), (queries, 8, 1))
    query_inverse = 1.0 / jnp.sqrt(squares.reshape(pairs, 1))
    for j in range(tiles):
        wide[j] = loaded[j]
    query = [wide[j, pl.ds(k, queries, stride=8), :] for k in range(8) for j in range(tiles)]
    query = jnp.concatenate(query, axis=1).astype(bf16)
    query_ref[...] = query
    lists = loaded[-1]
    inside = lists[:, 0:1] * 256.0 + lists[:, 1:2]
    mark = lists[:, 2:3] + lists[:, 3:4]
    lane = lax.broadcasted_iota(jnp.int32, (pairs, rows), 1).astype(f32)
    pick = jnp.where(inside == lane, 1.0, 0.0).astype(bf16)
    size = jnp.zeros((pairs, 128), f32)
    along = [jnp.zeros((8, 128), f32)] * queries
    for k in range(chunks):
        part = slice(k * chunk, (k + 1) * chunk)
        if k < half:
            passages = near_ref[:, part]
        else:
            for copy in copies[k - half]:
                copy.wait()
            passages = held[:, slice((k - half) * chunk, (k - half + 1) * chunk)]
        raw = dot(pick, passages, nn_dims)
        raw_ref[:, part] = raw.astype(bf16)
        lifted = raw * gain_ref[:, part]
        for j in range(chunk // 128):
            tile = slice(j * 128, (j + 1) * 128)
            size = size + lifted[:, tile] * lifted[:, tile]
            eighth, place = divmod(k * chunk // 128 + j, tiles)
            for i in range(queries):
                row = wide[place, i * 8 + eighth : i * 8 + eighth + 1, :]
                along[i] = along[i] + lifted[i * 8 : i * 8 + 8, tile] * row
    there = theirs_ref.shape[1]
    theirs_ref[...] = raw_ref[:, pl.ds(pl.multiple_of((1 - core_ref[0]) * there, 128), there)]
    inverse = 1.0 / jnp.sqrt(jnp.sum(size, axis=1, keepdims=True))
    along = jnp.concatenate(along, axis=0)
    cos = jnp.sum(along, axis=1, keepdims=True) * inverse * query_inverse
    weight = jnp.where(mark > 0.0, jnp.exp(cos * score_scale), 0.0)
    lane = lax.broadcasted_iota(jnp.int32, (pairs, 128), 1)
    cols = jnp.zeros((pairs, 128), f32)
    for k, column in enumerate((weight, mark, cos, inverse, inside, query_inverse)):
        cols = jnp.where(lane == k, column, cols)
    cols_ref[...] = cols
    flipped = jnp.transpose(cols)[:8]
    rows_ref[...] = flipped
    sums_ref[...] = jnp.broadcast_to(flipped[None, :1], sums_ref.shape)


def partial_kernel(sums_ref, both_ref, out_ref, total_ref, laid):
    queries = sums_ref.shape[2] // 8
    width = both_ref.shape[1]
    total = jnp.sum(sums_ref[...][:, 0, :], axis=0, keepdims=True)
    total_ref[...] = total
    own = belongs((queries, total.shape[1]), 1)
    inverse = 1.0 / jnp.sum(jnp.where(own, total, 0.0), axis=1, keepdims=True)
    both = both_ref[...]
    partial = coef_scale * (both[:queries] * inverse - both[queries : 2 * queries])
    gain_part = jnp.sum(both[2 * queries : 3 * queries] * inverse, axis=0, keepdims=True)
    gain_part = coef_scale * (gain_part - both[3 * queries : 3 * queries + 1])
    tiles = laid.shape[0]
    for k in range(width // 128):
        row, tile = k // tiles, k % tiles
        part = slice(k * 128, (k + 1) * 128)
        laid[tile, pl.ds(row, queries, stride=8), :] = partial[:, part]
        laid[tile, pl.ds(4 + row, queries, stride=8), :] = jnp.broadcast_to(
            gain_part[:, part], (queries, 128)
        )
    for tile in range(tiles):
        out_ref[:, tile * 128 : (tile + 1) * 128] = laid[tile].astype(bf16)


def passage_kernel(total_ref, query_ref, gain_ref, raw_ref, cols_ref, rows_ref, out_ref, made, sems):
    queries, width = query_ref.shape
    rows, pairs = made.shape[0], raw_ref.shape[0]
    piece = width // pieces
    weight, mark = cols_ref[:, 0:1], cols_ref[:, 1:2]
    cos, inverse = cols_ref[:, 2:3], cols_ref[:, 3:4]
    square = (pairs, pairs)
    alike = (lax.broadcasted_iota(jnp.int32, square, 0) >> 3) == (
        lax.broadcasted_iota(jnp.int32, square, 1) >> 3
    )
    total = jnp.sum(jnp.where(alike, total_ref[...], 0.0), axis=1, keepdims=True)
    scale = coef_scale * (weight / total - mark) * inverse
    inside = rows_ref[4:5, :]
    spread = lax.broadcasted_iota(jnp.int32, (rows, pairs), 0).astype(f32) == inside
    spread = jnp.where(spread, 1.0, 0.0).astype(bf16)
    spread = jnp.concatenate([spread, spread], axis=1)
    repeat = jnp.where(belongs((pairs, queries), 0), 1.0, 0.0).astype(bf16)
    copies = []
    for k in range(pieces):
        part = slice(k * piece, (k + 1) * piece)
        gain = gain_ref[:, part]
        row = (raw_ref[:, part].astype(f32) * gain * inverse).astype(bf16).astype(f32)
        query = dot(repeat, query_ref[:, part], nn_dims) * cols_ref[:, 5:6]
        term = (query.astype(bf16).astype(f32) - cos * row) * scale * gain
        made[:, part] = dot(spread, jnp.concatenate(split(term), axis=0), nn_dims)
        part = pl.ds(k * piece, piece)
        copies.append(pltpu.make_async_copy(made.at[:, part], out_ref.at[:, part], sems.at[k]))
        copies[-1].start()
    for copy in copies:
        copy.wait()


def final_kernel(got_ref, queries_ref, gain_ref, d_queries_ref, d_gain_ref):
    count = got_ref.shape[0]
    got = got_ref[...].astype(f32)
    middle = 1 + count // 2
    halves = [jnp.sum(got[1:middle], axis=0), got[0] + jnp.sum(got[middle:], axis=0)]
    query = queries_ref[...].astype(f32)
    norm = jnp.sqrt(jnp.sum(query * query, axis=1, keepdims=True))
    unit = query / norm
    d_unit = jnp.concatenate([half[k : k + 1] for half in halves for k in range(4)], axis=1)
    d_queries_ref[...] = (d_unit - unit * jnp.sum(unit * d_unit, axis=1, keepdims=True)) / norm
    d_gain = jnp.concatenate([half[k : k + 1] for half in halves for k in range(4, 8)], axis=1)
    d_gain_ref[...] = d_gain / gain_ref[...]


def shape(dims, dtype=f32):
    return jax.ShapeDtypeStruct(dims, dtype)


def exchange(x):
    order = member_order(lax.axis_size("hash"))
    return lax.all_to_all(
        x, "hash", split_axis=0, concat_axis=0, axis_index_groups=[order], tiled=True
    )


def local(passages, queries, gain, candidates, teacher):
    count = lax.axis_size("hash")
    rows, width = passages.shape
    listed = candidates.shape[1]
    gain = gain.reshape(1, width)

    packed = pl.pallas_call(
        functools.partial(pack_kernel, rows),
        out_shape=shape((count, 8, width // 8 + listed), bf16),
        compiler_params=params(60),
        name="pack",
    )(queries, candidates, teacher)
    got = exchange(packed).reshape(count * 8, width // 8 + listed)

    pairs = count * 8
    near, far, gain_near = pl.pallas_call(
        stage_kernel,
        in_specs=[outside(), whole()],
        out_specs=[whole(), outside(), whole()],
        out_shape=[
            shape((rows, width // 2), bf16),
            shape((10 * rows, width // 2), bf16),
            shape((1, width)),
        ],
        scratch_shapes=[
            pltpu.VMEM((rows, width // 2), bf16),
            pltpu.SemaphoreType.DMA((2 * chunks,)),
            pltpu.SemaphoreType.DMA((chunks,)),
        ],
        compiler_params=params(48),
        name="stage",
        cost_estimate=pl.CostEstimate(
            flops=0, bytes_accessed=4 * rows * width, transcendentals=0
        ),
    )(passages, gain)
    half = width // 2
    core = (lax.axis_index("hash") % 2).astype(jnp.int32).reshape(1)
    raw, query, cols, lines, sums, theirs = pl.pallas_call(
        score_kernel,
        in_specs=[pl.BlockSpec(memory_space=pltpu.SMEM), whole(), whole(), whole(), outside()],
        out_shape=[
            shape((pairs, width), bf16),
            shape((count, width), bf16),
            shape((pairs, 128)),
            shape((8, pairs)),
            shape((count, 1, pairs)),
            shape((pairs, half), bf16),
        ],
        scratch_shapes=[
            pltpu.VMEM((rows, width // 2), bf16),
            pltpu.VMEM((width // 1024, pairs, 128), f32),
            pltpu.SemaphoreType.DMA((chunks // 2 * chunks,)),
        ],
        compiler_params=params(48),
        name="score",
    )(core, got, gain_near, near, far)

    got_sums = exchange(sums)
    swap = [(i, i ^ 1) for i in range(count)]
    sibling_raw = lax.ppermute(theirs, "hash", swap)
    sibling_lines = lax.ppermute(lines, "hash", swap)

    def mixed(kernel, *operands):
        return pl.pallas_call(
            kernel,
            in_specs=[pl.BlockSpec(memory_space=pltpu.SMEM)] + [whole()] * (len(operands) + 2),
            out_shape=shape((3 * count + 8, half)),
            compiler_params=params(48),
            name="mix",
            cost_estimate=pl.CostEstimate(
                flops=8 * count * pairs * width, bytes_accessed=4 * pairs * width, transcendentals=0
            ),
        )(core, query, gain_near, *operands)

    mine = mixed(mine_kernel, raw, lines)
    both = mixed(both_kernel, sibling_raw, sibling_lines, mine)

    partial, total = pl.pallas_call(
        partial_kernel,
        out_shape=[shape((pairs, half // 4), bf16), shape((1, pairs))],
        scratch_shapes=[pltpu.VMEM((half // 512, pairs, 128), f32)],
        compiler_params=params(48),
        name="partial",
    )(got_sums, both)
    got_partial = exchange(partial.reshape(count, 8, half // 4))

    d_passages = pl.pallas_call(
        passage_kernel,
        in_specs=[whole()] * 6,
        out_specs=outside(),
        out_shape=shape((rows, width)),
        scratch_shapes=[pltpu.VMEM((rows, width), f32), pltpu.SemaphoreType.DMA((pieces,))],
        compiler_params=params(48),
        name="d_passages",
        cost_estimate=pl.CostEstimate(
            flops=4 * pairs * rows * width, bytes_accessed=4 * rows * width, transcendentals=0
        ),
    )(total, query, gain_near, raw, cols, lines)

    d_queries, d_gain = pl.pallas_call(
        final_kernel,
        out_shape=[shape((1, width)), shape((1, width))],
        compiler_params=params(48),
        name="final",
    )(got_partial, queries, gain)
    return (d_passages, d_queries, d_gain.reshape(width))


def solution(mesh):
    in_specs = (
        P(("groups", "hash"), None),
        P(("groups", "hash"), None),
        P(),
        P(("groups", "hash"), None),
        P(("groups", "hash"), None),
    )
    out_specs = (P(("groups", "hash"), None), P(("groups", "hash"), None), P("groups"))
    return jax.shard_map(local, mesh=mesh, in_specs=in_specs, out_specs=out_specs, check_vma=False)
```

```python
import functools

import jax
import jax.numpy as jnp
from jax import lax
from jax.experimental import pallas as pl
from jax.experimental.pallas import tpu as pltpu
from jax.sharding import PartitionSpec as P

score_scale = 20.0
loss_scale = 8192.0
teacher_div = 2.0
coef_scale = loss_scale * score_scale
chunks = 4
pieces = 8
f32 = jnp.float32
bf16 = jnp.bfloat16
vmem = pltpu.VMEM
nn_dims = (((1,), (0,)), ((), ()))


def dot(a, b, dims):
    return lax.dot_general(a, b, dims, preferred_element_type=f32)


def split(x):
    high = x.astype(bf16)
    low = (x - high.astype(f32)).astype(bf16)
    return high, low


def member_order(count):
    first = count // 2 + 1
    return [first, *range(0, count, 2), *(i for i in range(1, count, 2) if i != first)]


def member_slot(owner, count):
    first = count // 2 + 1
    half = owner >> 1
    odd = 1 + count // 2 + half - jnp.where(owner > first, 1, 0)
    return jnp.where((owner & 1) == 0, 1 + half, jnp.where(owner == first, 0, odd))


def params(megabytes):
    return pltpu.CompilerParams(vmem_limit_bytes=megabytes * 1024 * 1024)


def whole():
    return pl.BlockSpec(memory_space=vmem)


def outside():
    return pl.BlockSpec(memory_space=pltpu.HBM)


def pack_kernel(rows, queries_ref, candidates_ref, teacher_ref, out_ref):
    ids = candidates_ref[...]
    listed = ids.shape[1]
    count = out_ref.shape[0]
    width = queries_ref.shape[1] // 8
    query = queries_ref[...].astype(f32)
    query = jnp.concatenate([query[:, k * width : (k + 1) * width] for k in range(8)], axis=0)
    owner = lax.div(ids, rows)
    inside = ids - owner * rows
    slot = member_slot(owner, count)
    marks = jnp.exp(teacher_ref[...].astype(f32) * (1.0 / teacher_div))
    marks = marks / jnp.sum(marks, axis=1, keepdims=True)
    high, low = split(marks)
    values = jnp.concatenate(
        [
            (inside >> 8).astype(f32),
            (inside & 255).astype(f32),
            high.astype(f32),
            low.astype(f32),
            jnp.zeros((listed - 4, listed), f32),
        ],
        axis=0,
    )
    square = (listed, listed)
    across = jnp.broadcast_to(slot.astype(f32), square)
    same = across == jnp.transpose(across)
    earlier = same & (lax.broadcasted_iota(jnp.int32, square, 0) < lax.broadcasted_iota(jnp.int32, square, 1))
    rank = jnp.sum(jnp.where(earlier, 1.0, 0.0), axis=0, keepdims=True)
    place = slot * 8 + rank.astype(jnp.int32)
    spread = jnp.where(place == lax.broadcasted_iota(jnp.int32, (count * 8, listed), 0), 1.0, 0.0)
    lists = dot(spread.astype(bf16), jnp.transpose(values).astype(bf16), nn_dims)
    out_ref[:, :, :width] = jnp.broadcast_to(query.astype(bf16)[None], (count, 8, width))
    out_ref[:, :, width:] = lists.astype(bf16).reshape(count, 8, listed)


def belongs(dims, pair_axis):
    pair = lax.broadcasted_iota(jnp.int32, dims, pair_axis) >> 3
    return pair == lax.broadcasted_iota(jnp.int32, dims, 1 - pair_axis)


def stage_kernel(passages_ref, gain_ref, near_ref, far_ref, gain_out_ref, held, sems_in, sems_out):
    gain_out_ref[...] = gain_ref[...]
    rows, width = near_ref.shape
    half = width // 2
    piece = rows // chunks
    copies_in, copies_out, copies_near = [], [], []
    for k in range(chunks):
        part = pl.ds(k * piece, piece)
        far = passages_ref.at[part, pl.ds(width, width)]
        near = passages_ref.at[part, pl.ds(0, width)]
        copies_in.append(pltpu.make_async_copy(far, held.at[part], sems_in.at[k]))
        copies_near.append(pltpu.make_async_copy(near, near_ref.at[part], sems_in.at[chunks + k]))
        for j in range(2):
            there = far_ref.at[pl.ds(j * rows + k * piece, piece)]
            here = held.at[part, pl.ds(j * half, half)]
            copies_out.append(pltpu.make_async_copy(here, there, sems_out.at[2 * k + j]))
    for copy in copies_in + copies_near:
        copy.start()
    for k in range(chunks):
        copies_in[k].wait()
        copies_out[2 * k].start()
        copies_out[2 * k + 1].start()
    for copy in copies_near + copies_out:
        copy.wait()


def mix(base, first, query_ref, gain_ref, raw_ref, lines, out_ref, before_ref):
    queries = query_ref.shape[0]
    pairs = raw_ref.shape[0]
    chunk = out_ref.shape[1] // 2
    cols = jnp.transpose(jnp.concatenate([lines, jnp.zeros((120, pairs), f32)], axis=0))
    cos, inverse, query_inverse = cols[:, 2:3], cols[:, 3:4], cols[:, 5:6]
    own = belongs((queries, pairs), 1)
    by_weight = split(jnp.where(own, lines[0:1, :], 0.0))
    by_mark = split(jnp.where(own, lines[1:2, :], 0.0))
    plain = jnp.concatenate([*by_weight, *by_mark], axis=0)
    repeat = jnp.where(belongs((pairs, queries), 0), 1.0, 0.0).astype(bf16)
    for k in range(2):
        part = slice(k * chunk, (k + 1) * chunk)
        there = pl.ds(pl.multiple_of(base + k * chunk, 128), chunk)
        here = pl.ds(pl.multiple_of(first + k * chunk, 128), chunk)
        row = (raw_ref[:, here].astype(f32) * gain_ref[:, there] * inverse).astype(bf16)
        plainly = dot(plain, row, nn_dims)
        row = row.astype(f32)
        query = dot(repeat, query_ref[:, there], nn_dims) * query_inverse
        turned = row * (query.astype(bf16).astype(f32) - cos * row)
        turned = dot(plain, turned.astype(bf16), nn_dims)
        last = jnp.sum(turned[2 * queries :], axis=0, keepdims=True)
        sums = jnp.concatenate(
            [
                plainly[:queries] + plainly[queries : 2 * queries],
                plainly[2 * queries : 3 * queries] + plainly[3 * queries :],
                turned[:queries] + turned[queries : 2 * queries],
                jnp.broadcast_to(last, (8, chunk)),
            ],
            axis=0,
        )
        out_ref[:, part] = sums if before_ref is None else sums + before_ref[:, part]


def mine_kernel(core_ref, query_ref, gain_ref, raw_ref, rows_ref, out_ref):
    base = core_ref[0] * out_ref.shape[1]
    mix(base, base, query_ref, gain_ref, raw_ref, rows_ref[...], out_ref, None)


def both_kernel(core_ref, query_ref, gain_ref, raw_ref, rows_ref, mine_ref, out_ref):
    base = core_ref[0] * out_ref.shape[1]
    mix(base, 0, query_ref, gain_ref, raw_ref, rows_ref[...], out_ref, mine_ref)


def score_kernel(
    core_ref, got_ref, gain_ref, near_ref, far_ref,
    raw_ref, query_ref, cols_ref, rows_ref, sums_ref, theirs_ref, held, wide, sems,
):
    queries, width = query_ref.shape
    pairs = queries * 8
    rows = held.shape[1]
    chunk = width // chunks
    half = chunks // 2
    copies = []
    for k in range(half):
        copies.append(pltpu.make_async_copy(far_ref.at[pl.ds(k * rows, rows)], held.at[k], sems.at[k]))
        copies[-1].start()
    tiles = wide.shape[0]
    loaded = [got_ref[:, j * 128 : (j + 1) * 128].astype(f32) for j in range(tiles + 1)]
    squares = sum(x * x for x in loaded[:-1])
    squares = jnp.sum(squares, axis=1, keepdims=True).reshape(queries, 8, 1)
    squares = jnp.broadcast_to(jnp.sum(squares, axis=1, keepdims=True), (queries, 8, 1))
    query_inverse = 1.0 / jnp.sqrt(squares.reshape(pairs, 1))
    for j in range(tiles):
        wide[j] = loaded[j]
    query = [wide[j, pl.ds(k, queries, stride=8), :] for k in range(8) for j in range(tiles)]
    query = jnp.concatenate(query, axis=1).astype(bf16)
    query_ref[...] = query
    lists = loaded[-1]
    inside = lists[:, 0:1] * 256.0 + lists[:, 1:2]
    mark = lists[:, 2:3] + lists[:, 3:4]
    lane = lax.broadcasted_iota(jnp.int32, (pairs, rows), 1).astype(f32)
    pick = jnp.where(inside == lane, 1.0, 0.0).astype(bf16)
    size = jnp.zeros((pairs, 128), f32)
    along = [jnp.zeros((8, 128), f32)] * queries
    for k in range(chunks):
        part = slice(k * chunk, (k + 1) * chunk)
        if k < half:
            passages = near_ref[:, part]
        else:
            copies[k - half].wait()
            passages = held[k - half]
        raw = dot(pick, passages, nn_dims)
        raw_ref[:, part] = raw.astype(bf16)
        lifted = raw * gain_ref[:, part]
        for j in range(chunk // 128):
            tile = slice(j * 128, (j + 1) * 128)
            size = size + lifted[:, tile] * lifted[:, tile]
            eighth, place = divmod(k * chunk // 128 + j, tiles)
            for i in range(queries):
                row = wide[place, i * 8 + eighth : i * 8 + eighth + 1, :]
                along[i] = along[i] + lifted[i * 8 : i * 8 + 8, tile] * row
    there = theirs_ref.shape[1]
    theirs_ref[...] = raw_ref[:, pl.ds(pl.multiple_of((1 - core_ref[0]) * there, 128), there)]
    inverse = 1.0 / jnp.sqrt(jnp.sum(size, axis=1, keepdims=True))
    along = jnp.concatenate(along, axis=0)
    cos = jnp.sum(along, axis=1, keepdims=True) * inverse * query_inverse
    weight = jnp.where(mark > 0.0, jnp.exp(cos * score_scale), 0.0)
    lane = lax.broadcasted_iota(jnp.int32, (pairs, 128), 1)
    cols = jnp.zeros((pairs, 128), f32)
    for k, column in enumerate((weight, mark, cos, inverse, inside, query_inverse)):
        cols = jnp.where(lane == k, column, cols)
    cols_ref[...] = cols
    flipped = jnp.transpose(cols)[:8]
    rows_ref[...] = flipped
    sums_ref[...] = jnp.broadcast_to(flipped[None, :1], sums_ref.shape)


def partial_kernel(sums_ref, both_ref, out_ref, total_ref, laid):
    queries = sums_ref.shape[2] // 8
    width = both_ref.shape[1]
    total = jnp.sum(sums_ref[...][:, 0, :], axis=0, keepdims=True)
    total_ref[...] = total
    own = belongs((queries, total.shape[1]), 1)
    inverse = 1.0 / jnp.sum(jnp.where(own, total, 0.0), axis=1, keepdims=True)
    both = both_ref[...]
    partial = coef_scale * (both[:queries] * inverse - both[queries : 2 * queries])
    gain_part = jnp.sum(both[2 * queries : 3 * queries] * inverse, axis=0, keepdims=True)
    gain_part = coef_scale * (gain_part - both[3 * queries : 3 * queries + 1])
    tiles = laid.shape[0]
    for k in range(width // 128):
        row, tile = k // tiles, k % tiles
        part = slice(k * 128, (k + 1) * 128)
        laid[tile, pl.ds(row, queries, stride=8), :] = partial[:, part]
        laid[tile, pl.ds(4 + row, queries, stride=8), :] = jnp.broadcast_to(
            gain_part[:, part], (queries, 128)
        )
    for tile in range(tiles):
        out_ref[:, tile * 128 : (tile + 1) * 128] = laid[tile].astype(bf16)


def passage_kernel(total_ref, query_ref, gain_ref, raw_ref, cols_ref, rows_ref, out_ref, made, sems):
    queries, width = query_ref.shape
    rows, pairs = made.shape[0], raw_ref.shape[0]
    piece = width // pieces
    weight, mark = cols_ref[:, 0:1], cols_ref[:, 1:2]
    cos, inverse = cols_ref[:, 2:3], cols_ref[:, 3:4]
    square = (pairs, pairs)
    alike = (lax.broadcasted_iota(jnp.int32, square, 0) >> 3) == (
        lax.broadcasted_iota(jnp.int32, square, 1) >> 3
    )
    total = jnp.sum(jnp.where(alike, total_ref[...], 0.0), axis=1, keepdims=True)
    scale = coef_scale * (weight / total - mark) * inverse
    inside = rows_ref[4:5, :]
    spread = lax.broadcasted_iota(jnp.int32, (rows, pairs), 0).astype(f32) == inside
    spread = jnp.where(spread, 1.0, 0.0).astype(bf16)
    spread = jnp.concatenate([spread, spread], axis=1)
    repeat = jnp.where(belongs((pairs, queries), 0), 1.0, 0.0).astype(bf16)
    copies = []
    for k in range(pieces):
        part = slice(k * piece, (k + 1) * piece)
        gain = gain_ref[:, part]
        row = (raw_ref[:, part].astype(f32) * gain * inverse).astype(bf16).astype(f32)
        query = dot(repeat, query_ref[:, part], nn_dims) * cols_ref[:, 5:6]
        term = (query.astype(bf16).astype(f32) - cos * row) * scale * gain
        made[:, part] = dot(spread, jnp.concatenate(split(term), axis=0), nn_dims)
        part = pl.ds(k * piece, piece)
        copies.append(pltpu.make_async_copy(made.at[:, part], out_ref.at[:, part], sems.at[k]))
        copies[-1].start()
    for copy in copies:
        copy.wait()


def final_kernel(got_ref, queries_ref, gain_ref, d_queries_ref, d_gain_ref):
    count = got_ref.shape[0]
    got = got_ref[...].astype(f32)
    middle = 1 + count // 2
    halves = [jnp.sum(got[1:middle], axis=0), got[0] + jnp.sum(got[middle:], axis=0)]
    query = queries_ref[...].astype(f32)
    norm = jnp.sqrt(jnp.sum(query * query, axis=1, keepdims=True))
    unit = query / norm
    d_unit = jnp.concatenate([half[k : k + 1] for half in halves for k in range(4)], axis=1)
    d_queries_ref[...] = (d_unit - unit * jnp.sum(unit * d_unit, axis=1, keepdims=True)) / norm
    d_gain = jnp.concatenate([half[k : k + 1] for half in halves for k in range(4, 8)], axis=1)
    d_gain_ref[...] = d_gain / gain_ref[...]


def shape(dims, dtype=f32):
    return jax.ShapeDtypeStruct(dims, dtype)


def exchange(x):
    order = member_order(lax.axis_size("hash"))
    return lax.all_to_all(
        x, "hash", split_axis=0, concat_axis=0, axis_index_groups=[order], tiled=True
    )


def local(passages, queries, gain, candidates, teacher):
    count = lax.axis_size("hash")
    rows, width = passages.shape
    listed = candidates.shape[1]
    gain = gain.reshape(1, width)

    packed = pl.pallas_call(
        functools.partial(pack_kernel, rows),
        out_shape=shape((count, 8, width // 8 + listed), bf16),
        compiler_params=params(60),
        name="pack",
    )(queries, candidates, teacher)
    got = exchange(packed).reshape(count * 8, width // 8 + listed)

    pairs = count * 8
    near, far, gain_near = pl.pallas_call(
        stage_kernel,
        in_specs=[outside(), whole()],
        out_specs=[whole(), outside(), whole()],
        out_shape=[
            shape((rows, width // 2), bf16),
            shape((20 * rows, width // 4), bf16),
            shape((1, width)),
        ],
        scratch_shapes=[
            pltpu.VMEM((rows, width // 2), bf16),
            pltpu.SemaphoreType.DMA((2 * chunks,)),
            pltpu.SemaphoreType.DMA((2 * chunks,)),
        ],
        compiler_params=params(48),
        name="stage",
        cost_estimate=pl.CostEstimate(
            flops=0, bytes_accessed=4 * rows * width, transcendentals=0
        ),
    )(passages, gain)
    half = width // 2
    core = (lax.axis_index("hash") % 2).astype(jnp.int32).reshape(1)
    raw, query, cols, lines, sums, theirs = pl.pallas_call(
        score_kernel,
        in_specs=[pl.BlockSpec(memory_space=pltpu.SMEM), whole(), whole(), whole(), outside()],
        out_shape=[
            shape((pairs, width), bf16),
            shape((count, width), bf16),
            shape((pairs, 128)),
            shape((8, pairs)),
            shape((count, 1, pairs)),
            shape((pairs, half), bf16),
        ],
        scratch_shapes=[
            pltpu.VMEM((chunks // 2, rows, width // chunks), bf16),
            pltpu.VMEM((width // 1024, pairs, 128), f32),
            pltpu.SemaphoreType.DMA((chunks // 2,)),
        ],
        compiler_params=params(48),
        name="score",
    )(core, got, gain_near, near, far)

    got_sums = exchange(sums)
    swap = [(i, i ^ 1) for i in range(count)]
    sibling_raw = lax.ppermute(theirs, "hash", swap)
    sibling_lines = lax.ppermute(lines, "hash", swap)

    def mixed(kernel, *operands):
        return pl.pallas_call(
            kernel,
            in_specs=[pl.BlockSpec(memory_space=pltpu.SMEM)] + [whole()] * (len(operands) + 2),
            out_shape=shape((3 * count + 8, half)),
            compiler_params=params(48),
            name="mix",
            cost_estimate=pl.CostEstimate(
                flops=8 * count * pairs * width, bytes_accessed=4 * pairs * width, transcendentals=0
            ),
        )(core, query, gain_near, *operands)

    mine = mixed(mine_kernel, raw, lines)
    both = mixed(both_kernel, sibling_raw, sibling_lines, mine)

    partial, total = pl.pallas_call(
        partial_kernel,
        out_shape=[shape((pairs, half // 4), bf16), shape((1, pairs))],
        scratch_shapes=[pltpu.VMEM((half // 512, pairs, 128), f32)],
        compiler_params=params(48),
        name="partial",
    )(got_sums, both)
    got_partial = exchange(partial.reshape(count, 8, half // 4))

    d_passages = pl.pallas_call(
        passage_kernel,
        in_specs=[whole()] * 6,
        out_specs=outside(),
        out_shape=shape((rows, width)),
        scratch_shapes=[pltpu.VMEM((rows, width), f32), pltpu.SemaphoreType.DMA((pieces,))],
        compiler_params=params(48),
        name="d_passages",
        cost_estimate=pl.CostEstimate(
            flops=4 * pairs * rows * width, bytes_accessed=4 * rows * width, transcendentals=0
        ),
    )(total, query, gain_near, raw, cols, lines)

    d_queries, d_gain = pl.pallas_call(
        final_kernel,
        out_shape=[shape((1, width)), shape((1, width))],
        compiler_params=params(48),
        name="final",
    )(got_partial, queries, gain)
    return (d_passages, d_queries, d_gain.reshape(width))


def solution(mesh):
    in_specs = (
        P(("groups", "hash"), None),
        P(("groups", "hash"), None),
        P(),
        P(("groups", "hash"), None),
        P(("groups", "hash"), None),
    )
    out_specs = (P(("groups", "hash"), None), P(("groups", "hash"), None), P("groups"))
    return jax.shard_map(local, mesh=mesh, in_specs=in_specs, out_specs=out_specs, check_vma=False)
```

```python
import functools

import jax
import jax.numpy as jnp
from jax import lax
from jax.experimental import pallas as pl
from jax.experimental.pallas import tpu as pltpu
from jax.sharding import PartitionSpec as P

score_scale = 20.0
loss_scale = 8192.0
teacher_div = 2.0
coef_scale = loss_scale * score_scale
chunks = 4
pieces = 8
f32 = jnp.float32
bf16 = jnp.bfloat16
vmem = pltpu.VMEM
nn_dims = (((1,), (0,)), ((), ()))
nt_dims = (((1,), (1,)), ((), ()))


def dot(a, b, dims):
    return lax.dot_general(a, b, dims, preferred_element_type=f32)


def split(x):
    high = x.astype(bf16)
    low = (x - high.astype(f32)).astype(bf16)
    return high, low


def member_order(count):
    first = count // 2 + 1
    return [first, *range(0, count, 2), *(i for i in range(1, count, 2) if i != first)]


def member_slot(owner, count):
    first = count // 2 + 1
    half = owner >> 1
    odd = 1 + count // 2 + half - jnp.where(owner > first, 1, 0)
    return jnp.where((owner & 1) == 0, 1 + half, jnp.where(owner == first, 0, odd))


def params(megabytes):
    return pltpu.CompilerParams(vmem_limit_bytes=megabytes * 1024 * 1024)


def whole():
    return pl.BlockSpec(memory_space=vmem)


def outside():
    return pl.BlockSpec(memory_space=pltpu.HBM)


def pack_kernel(rows, queries_ref, candidates_ref, teacher_ref, out_ref):
    ids = candidates_ref[...]
    listed = ids.shape[1]
    count = out_ref.shape[0]
    width = queries_ref.shape[1] // 8
    query = queries_ref[...].astype(f32)
    query = jnp.concatenate([query[:, k * width : (k + 1) * width] for k in range(8)], axis=0)
    owner = ids >> (rows.bit_length() - 1) if rows & (rows - 1) == 0 else lax.div(ids, rows)
    inside = ids - owner * rows
    slot = member_slot(owner, count)
    marks = jnp.exp(teacher_ref[...].astype(f32) * (1.0 / teacher_div))
    marks = marks / jnp.sum(marks, axis=1, keepdims=True)
    high, low = split(marks)
    values = jnp.concatenate(
        [
            (inside >> 8).astype(f32),
            (inside & 255).astype(f32),
            high.astype(f32),
            low.astype(f32),
            jnp.zeros((12, listed), f32),
        ],
        axis=0,
    )
    square = (listed, listed)
    across = jnp.broadcast_to(slot.astype(f32), square)
    same = across == jnp.transpose(across)
    earlier = same & (lax.broadcasted_iota(jnp.int32, square, 0) < lax.broadcasted_iota(jnp.int32, square, 1))
    rank = jnp.sum(jnp.where(earlier, 1.0, 0.0), axis=0, keepdims=True)
    place = slot * 8 + rank.astype(jnp.int32)
    spread = jnp.where(place == lax.broadcasted_iota(jnp.int32, (count * 8, listed), 0), 1.0, 0.0)
    lists = dot(spread.astype(bf16), values.astype(bf16), nt_dims)
    lists = jnp.concatenate([lists, jnp.zeros((count * 8, listed - 16), f32)], axis=1)
    out_ref[:, :, :width] = jnp.broadcast_to(query.astype(bf16)[None], (count, 8, width))
    out_ref[:, :, width:] = lists.astype(bf16).reshape(count, 8, listed)


def belongs(dims, pair_axis):
    pair = lax.broadcasted_iota(jnp.int32, dims, pair_axis) >> 3
    return pair == lax.broadcasted_iota(jnp.int32, dims, 1 - pair_axis)


def stage_kernel(passages_ref, gain_ref, near_ref, far_ref, gain_out_ref, held, sems_in, sems_out):
    gain_out_ref[...] = gain_ref[...]
    rows, width = near_ref.shape
    half = width // 2
    piece = rows // chunks
    copies_in, copies_out, copies_near = [], [], []
    for k in range(chunks):
        part = pl.ds(k * piece, piece)
        far = passages_ref.at[part, pl.ds(width, width)]
        near = passages_ref.at[part, pl.ds(0, width)]
        copies_in.append(pltpu.make_async_copy(far, held.at[part], sems_in.at[k]))
        copies_near.append(pltpu.make_async_copy(near, near_ref.at[part], sems_in.at[chunks + k]))
        for j in range(2):
            there = far_ref.at[pl.ds(j * rows + k * piece, piece)]
            here = held.at[part, pl.ds(j * half, half)]
            copies_out.append(pltpu.make_async_copy(here, there, sems_out.at[2 * k + j]))
    for copy in copies_in + copies_near:
        copy.start()
    for k in range(chunks):
        copies_in[k].wait()
        copies_out[2 * k].start()
        copies_out[2 * k + 1].start()
    for copy in copies_near + copies_out:
        copy.wait()


def mix(base, first, query_ref, gain_ref, raw_ref, lines, width):
    queries = query_ref.shape[0]
    pairs = raw_ref.shape[0]
    chunk = width // 2
    cols = jnp.transpose(jnp.concatenate([lines, jnp.zeros((120, pairs), f32)], axis=0))
    cos, inverse, query_inverse = cols[:, 2:3], cols[:, 3:4], cols[:, 5:6]
    own = belongs((queries, pairs), 1)
    by_weight = split(jnp.where(own, lines[0:1, :], 0.0))
    by_mark = split(jnp.where(own, lines[1:2, :], 0.0))
    plain = jnp.concatenate([*by_weight, *by_mark], axis=0)
    repeat = jnp.where(belongs((pairs, queries), 0), 1.0, 0.0).astype(bf16)
    for k in range(2):
        there = pl.ds(pl.multiple_of(base + k * chunk, 128), chunk)
        here = pl.ds(pl.multiple_of(first + k * chunk, 128), chunk)
        row = (raw_ref[:, here].astype(f32) * gain_ref[:, there] * inverse).astype(bf16)
        plainly = dot(plain, row, nn_dims)
        row = row.astype(f32)
        query = dot(repeat, query_ref[:, there], nn_dims) * query_inverse
        turned = row * (query.astype(bf16).astype(f32) - cos * row)
        turned = dot(plain, turned.astype(bf16), nn_dims)
        last = jnp.sum(turned[2 * queries :], axis=0, keepdims=True)
        sums = jnp.concatenate(
            [
                plainly[:queries] + plainly[queries : 2 * queries],
                plainly[2 * queries : 3 * queries] + plainly[3 * queries :],
                turned[:queries] + turned[queries : 2 * queries],
                jnp.broadcast_to(last, (8, chunk)),
            ],
            axis=0,
        )
        yield slice(k * chunk, (k + 1) * chunk), sums


def mine_kernel(core_ref, query_ref, gain_ref, raw_ref, rows_ref, out_ref):
    width = out_ref.shape[1]
    base = core_ref[0] * width
    for part, sums in mix(base, base, query_ref, gain_ref, raw_ref, rows_ref[...], width):
        out_ref[:, part] = sums


def both_kernel(core_ref, query_ref, gain_ref, raw_ref, rows_ref, mine_ref, scaled_ref, plain_ref):
    queries = query_ref.shape[0]
    width = mine_ref.shape[1]
    tiles = scaled_ref.shape[0]
    base = core_ref[0] * width
    for part, sums in mix(base, 0, query_ref, gain_ref, raw_ref, rows_ref[...], width):
        sums = sums + mine_ref[:, part]
        for j in range((part.stop - part.start) // 128):
            row, tile = divmod(part.start // 128 + j, tiles)
            piece = sums[:, j * 128 : (j + 1) * 128]
            last = piece[3 * queries : 3 * queries + 1] * (1.0 / queries)
            scaled_ref[tile, pl.ds(row, queries, stride=8), :] = piece[:queries]
            scaled_ref[tile, pl.ds(4 + row, queries, stride=8), :] = piece[2 * queries : 3 * queries]
            plain_ref[tile, pl.ds(row, queries, stride=8), :] = piece[queries : 2 * queries]
            plain_ref[tile, pl.ds(4 + row, queries, stride=8), :] = jnp.broadcast_to(last, (queries, 128))


def score_kernel(
    core_ref, got_ref, gain_ref, near_ref, far_ref,
    raw_ref, query_ref, cols_ref, rows_ref, sums_ref, theirs_ref, held, wide, sems,
):
    queries, width = query_ref.shape
    pairs = queries * 8
    rows = held.shape[1]
    chunk = width // chunks
    half = chunks // 2
    copies = []
    for k in range(half):
        copies.append(pltpu.make_async_copy(far_ref.at[pl.ds(k * rows, rows)], held.at[k], sems.at[k]))
        copies[-1].start()
    tiles = wide.shape[0]
    loaded = [got_ref[:, j * 128 : (j + 1) * 128].astype(f32) for j in range(tiles + 1)]
    squares = sum(x * x for x in loaded[:-1])
    squares = jnp.sum(squares, axis=1, keepdims=True).reshape(queries, 8, 1)
    squares = jnp.broadcast_to(jnp.sum(squares, axis=1, keepdims=True), (queries, 8, 1))
    query_inverse = 1.0 / jnp.sqrt(squares.reshape(pairs, 1))
    for j in range(tiles):
        wide[j] = loaded[j]
    query = [wide[j, pl.ds(k, queries, stride=8), :] for k in range(8) for j in range(tiles)]
    query = jnp.concatenate(query, axis=1).astype(bf16)
    query_ref[...] = query
    lists = loaded[-1]
    inside = lists[:, 0:1] * 256.0 + lists[:, 1:2]
    mark = lists[:, 2:3] + lists[:, 3:4]
    lane = lax.broadcasted_iota(jnp.int32, (pairs, rows), 1).astype(f32)
    pick = jnp.where(inside == lane, 1.0, 0.0).astype(bf16)
    size = jnp.zeros((pairs, 128), f32)
    along = [jnp.zeros((8, 128), f32)] * queries
    for k in range(chunks):
        part = slice(k * chunk, (k + 1) * chunk)
        if k < half:
            passages = near_ref[:, part]
        else:
            copies[k - half].wait()
            passages = held[k - half]
        raw = dot(pick, passages, nn_dims)
        raw_ref[:, part] = raw.astype(bf16)
        lifted = raw * gain_ref[:, part]
        for j in range(chunk // 128):
            tile = slice(j * 128, (j + 1) * 128)
            size = size + lifted[:, tile] * lifted[:, tile]
            eighth, place = divmod(k * chunk // 128 + j, tiles)
            for i in range(queries):
                row = wide[place, i * 8 + eighth : i * 8 + eighth + 1, :]
                along[i] = along[i] + lifted[i * 8 : i * 8 + 8, tile] * row
    there = theirs_ref.shape[1]
    theirs_ref[...] = raw_ref[:, pl.ds(pl.multiple_of((1 - core_ref[0]) * there, 128), there)]
    inverse = 1.0 / jnp.sqrt(jnp.sum(size, axis=1, keepdims=True))
    along = jnp.concatenate(along, axis=0)
    cos = jnp.sum(along, axis=1, keepdims=True) * inverse * query_inverse
    weight = jnp.where(mark > 0.0, jnp.exp(cos * score_scale), 0.0)
    lane = lax.broadcasted_iota(jnp.int32, (pairs, 128), 1)
    cols = jnp.zeros((pairs, 128), f32)
    for k, column in enumerate((weight, mark, cos, inverse, inside, query_inverse)):
        cols = jnp.where(lane == k, column, cols)
    cols_ref[...] = cols
    flipped = jnp.transpose(cols)[:8]
    rows_ref[...] = flipped
    sums_ref[...] = jnp.broadcast_to(flipped[None, :1], sums_ref.shape)


def partial_kernel(sums_ref, scaled_ref, plain_ref, out_ref, total_ref):
    tiles, pairs, _ = scaled_ref.shape
    queries = pairs // 8
    total = jnp.sum(sums_ref[...][:, 0, :], axis=0, keepdims=True)
    total_ref[...] = total
    alike = (lax.broadcasted_iota(jnp.int32, (pairs, pairs), 0) >> 3) == (
        lax.broadcasted_iota(jnp.int32, (pairs, pairs), 1) >> 3
    )
    inverse = coef_scale / jnp.sum(jnp.where(alike, total, 0.0), axis=1, keepdims=True)
    single = (lax.broadcasted_iota(jnp.int32, (pairs, 128), 0) & 7) < 4
    for tile in range(tiles):
        terms = scaled_ref[tile] * inverse - coef_scale * plain_ref[tile]
        added = jnp.sum(terms.reshape(queries, 8, 128), axis=0, keepdims=True)
        added = jnp.broadcast_to(added, (queries, 8, 128)).reshape(pairs, 128)
        out_ref[:, tile * 128 : (tile + 1) * 128] = jnp.where(single, terms, added).astype(bf16)


def passage_kernel(total_ref, query_ref, gain_ref, raw_ref, cols_ref, rows_ref, out_ref, made, sems):
    queries, width = query_ref.shape
    rows, pairs = made.shape[0], raw_ref.shape[0]
    piece = width // pieces
    weight, mark = cols_ref[:, 0:1], cols_ref[:, 1:2]
    cos, inverse = cols_ref[:, 2:3], cols_ref[:, 3:4]
    square = (pairs, pairs)
    alike = (lax.broadcasted_iota(jnp.int32, square, 0) >> 3) == (
        lax.broadcasted_iota(jnp.int32, square, 1) >> 3
    )
    total = jnp.sum(jnp.where(alike, total_ref[...], 0.0), axis=1, keepdims=True)
    scale = coef_scale * (weight / total - mark) * inverse
    inside = rows_ref[4:5, :]
    spread = lax.broadcasted_iota(jnp.int32, (rows, pairs), 0).astype(f32) == inside
    spread = jnp.where(spread, 1.0, 0.0).astype(bf16)
    spread = jnp.concatenate([spread, spread], axis=1)
    repeat = jnp.where(belongs((pairs, queries), 0), 1.0, 0.0).astype(bf16)
    copies = []
    for k in range(pieces):
        part = slice(k * piece, (k + 1) * piece)
        gain = gain_ref[:, part]
        row = (raw_ref[:, part].astype(f32) * gain * inverse).astype(bf16).astype(f32)
        query = dot(repeat, query_ref[:, part], nn_dims) * cols_ref[:, 5:6]
        term = (query.astype(bf16).astype(f32) - cos * row) * scale * gain
        made[:, part] = dot(spread, jnp.concatenate(split(term), axis=0), nn_dims)
        part = pl.ds(k * piece, piece)
        copies.append(pltpu.make_async_copy(made.at[:, part], out_ref.at[:, part], sems.at[k]))
        copies[-1].start()
    for copy in copies:
        copy.wait()


def final_kernel(got_ref, queries_ref, gain_ref, d_queries_ref, d_gain_ref):
    count = got_ref.shape[0]
    got = got_ref[...].astype(f32)
    middle = 1 + count // 2
    halves = [jnp.sum(got[1:middle], axis=0), got[0] + jnp.sum(got[middle:], axis=0)]
    query = queries_ref[...].astype(f32)
    norm = jnp.sqrt(jnp.sum(query * query, axis=1, keepdims=True))
    unit = query / norm
    d_unit = jnp.concatenate([half[k : k + 1] for half in halves for k in range(4)], axis=1)
    d_queries_ref[...] = (d_unit - unit * jnp.sum(unit * d_unit, axis=1, keepdims=True)) / norm
    d_gain = jnp.concatenate([half[k : k + 1] for half in halves for k in range(4, 8)], axis=1)
    d_gain_ref[...] = d_gain / gain_ref[...]


def shape(dims, dtype=f32):
    return jax.ShapeDtypeStruct(dims, dtype)


def exchange(x):
    order = member_order(lax.axis_size("hash"))
    return lax.all_to_all(
        x, "hash", split_axis=0, concat_axis=0, axis_index_groups=[order], tiled=True
    )


def local(passages, queries, gain, candidates, teacher):
    count = lax.axis_size("hash")
    rows, width = passages.shape
    listed = candidates.shape[1]
    gain = gain.reshape(1, width)

    packed = pl.pallas_call(
        functools.partial(pack_kernel, rows),
        out_shape=shape((count, 8, width // 8 + listed), bf16),
        compiler_params=params(60),
        name="pack",
    )(queries, candidates, teacher)
    got = exchange(packed).reshape(count * 8, width // 8 + listed)

    pairs = count * 8
    near, far, gain_near = pl.pallas_call(
        stage_kernel,
        in_specs=[outside(), whole()],
        out_specs=[whole(), outside(), whole()],
        out_shape=[
            shape((rows, width // 2), bf16),
            shape((20 * rows, width // 4), bf16),
            shape((1, width)),
        ],
        scratch_shapes=[
            pltpu.VMEM((rows, width // 2), bf16),
            pltpu.SemaphoreType.DMA((2 * chunks,)),
            pltpu.SemaphoreType.DMA((2 * chunks,)),
        ],
        compiler_params=params(48),
        name="stage",
        cost_estimate=pl.CostEstimate(
            flops=0, bytes_accessed=4 * rows * width, transcendentals=0
        ),
    )(passages, gain)
    half = width // 2
    core = (lax.axis_index("hash") % 2).astype(jnp.int32).reshape(1)
    raw, query, cols, lines, sums, theirs = pl.pallas_call(
        score_kernel,
        in_specs=[pl.BlockSpec(memory_space=pltpu.SMEM), whole(), whole(), whole(), outside()],
        out_shape=[
            shape((pairs, width), bf16),
            shape((count, width), bf16),
            shape((pairs, 128)),
            shape((8, pairs)),
            shape((count, 1, pairs)),
            shape((pairs, half), bf16),
        ],
        scratch_shapes=[
            pltpu.VMEM((chunks // 2, rows, width // chunks), bf16),
            pltpu.VMEM((width // 1024, pairs, 128), f32),
            pltpu.SemaphoreType.DMA((chunks // 2,)),
        ],
        compiler_params=params(48),
        name="score",
    )(core, got, gain_near, near, far)

    got_sums = exchange(sums)
    swap = [(i, i ^ 1) for i in range(count)]
    sibling_raw = lax.ppermute(theirs, "hash", swap)
    sibling_lines = lax.ppermute(lines, "hash", swap)

    def mixed(kernel, out_shape, *operands):
        return pl.pallas_call(
            kernel,
            in_specs=[pl.BlockSpec(memory_space=pltpu.SMEM)] + [whole()] * (len(operands) + 2),
            out_shape=out_shape,
            compiler_params=params(48),
            name="mix",
            cost_estimate=pl.CostEstimate(
                flops=8 * count * pairs * width, bytes_accessed=4 * pairs * width, transcendentals=0
            ),
        )(core, query, gain_near, *operands)

    mine = mixed(mine_kernel, shape((3 * count + 8, half)), raw, lines)
    laid = shape((half // 512, pairs, 128))
    scaled, plain = mixed(both_kernel, [laid, laid], sibling_raw, sibling_lines, mine)

    partial, total = pl.pallas_call(
        partial_kernel,
        out_shape=[shape((pairs, half // 4), bf16), shape((1, pairs))],
        compiler_params=params(48),
        name="partial",
    )(got_sums, scaled, plain)
    got_partial = exchange(partial.reshape(count, 8, half // 4))

    d_passages = pl.pallas_call(
        passage_kernel,
        in_specs=[whole()] * 6,
        out_specs=outside(),
        out_shape=shape((rows, width)),
        scratch_shapes=[pltpu.VMEM((rows, width), f32), pltpu.SemaphoreType.DMA((pieces,))],
        compiler_params=params(48),
        name="d_passages",
        cost_estimate=pl.CostEstimate(
            flops=4 * pairs * rows * width, bytes_accessed=4 * rows * width, transcendentals=0
        ),
    )(total, query, gain_near, raw, cols, lines)

    d_queries, d_gain = pl.pallas_call(
        final_kernel,
        out_shape=[shape((1, width)), shape((1, width))],
        compiler_params=params(48),
        name="final",
    )(got_partial, queries, gain)
    return (d_passages, d_queries, d_gain.reshape(width))


def solution(mesh):
    in_specs = (
        P(("groups", "hash"), None),
        P(("groups", "hash"), None),
        P(),
        P(("groups", "hash"), None),
        P(("groups", "hash"), None),
    )
    out_specs = (P(("groups", "hash"), None), P(("groups", "hash"), None), P("groups"))
    return jax.shard_map(local, mesh=mesh, in_specs=in_specs, out_specs=out_specs, check_vma=False)
```

```python
import functools

import jax
import jax.numpy as jnp
from jax import lax
from jax.experimental import pallas as pl
from jax.experimental.pallas import tpu as pltpu
from jax.sharding import PartitionSpec as P

score_scale = 20.0
loss_scale = 8192.0
teacher_div = 2.0
coef_scale = loss_scale * score_scale
chunks = 4
pieces = 8
f32 = jnp.float32
bf16 = jnp.bfloat16
vmem = pltpu.VMEM
nn_dims = (((1,), (0,)), ((), ()))


def dot(a, b, dims):
    return lax.dot_general(a, b, dims, preferred_element_type=f32)


def split(x):
    high = x.astype(bf16)
    low = (x - high.astype(f32)).astype(bf16)
    return high, low


def member_order(count):
    first = count // 2 + 1
    return [first, *range(0, count, 2), *(i for i in range(1, count, 2) if i != first)]


def member_slot(owner, count):
    first = count // 2 + 1
    half = owner >> 1
    odd = 1 + count // 2 + half - jnp.where(owner > first, 1, 0)
    return jnp.where((owner & 1) == 0, 1 + half, jnp.where(owner == first, 0, odd))


def params(megabytes):
    return pltpu.CompilerParams(vmem_limit_bytes=megabytes * 1024 * 1024)


def whole():
    return pl.BlockSpec(memory_space=vmem)


def outside():
    return pl.BlockSpec(memory_space=pltpu.HBM)


def pack_kernel(rows, queries_ref, candidates_ref, teacher_ref, out_ref):
    ids = candidates_ref[...]
    listed = ids.shape[1]
    count = out_ref.shape[0]
    width = queries_ref.shape[1] // 8
    query = queries_ref[...].astype(f32)
    query = jnp.concatenate([query[:, k * width : (k + 1) * width] for k in range(8)], axis=0)
    owner = lax.div(ids, rows)
    inside = ids - owner * rows
    slot = member_slot(owner, count)
    marks = jnp.exp(teacher_ref[...].astype(f32) * (1.0 / teacher_div))
    marks = marks / jnp.sum(marks, axis=1, keepdims=True)
    high, low = split(marks)
    values = jnp.concatenate(
        [
            (inside >> 8).astype(f32),
            (inside & 255).astype(f32),
            high.astype(f32),
            low.astype(f32),
            jnp.zeros((listed - 4, listed), f32),
        ],
        axis=0,
    )
    square = (listed, listed)
    across = jnp.broadcast_to(slot.astype(f32), square)
    same = across == jnp.transpose(across)
    earlier = same & (lax.broadcasted_iota(jnp.int32, square, 0) < lax.broadcasted_iota(jnp.int32, square, 1))
    rank = jnp.sum(jnp.where(earlier, 1.0, 0.0), axis=0, keepdims=True)
    place = slot * 8 + rank.astype(jnp.int32)
    spread = jnp.where(place == lax.broadcasted_iota(jnp.int32, (count * 8, listed), 0), 1.0, 0.0)
    lists = dot(spread.astype(bf16), jnp.transpose(values).astype(bf16), nn_dims)
    out_ref[:, :, :width] = jnp.broadcast_to(query.astype(bf16)[None], (count, 8, width))
    out_ref[:, :, width:] = lists.astype(bf16).reshape(count, 8, listed)


def belongs(dims, pair_axis):
    pair = lax.broadcasted_iota(jnp.int32, dims, pair_axis) >> 3
    return pair == lax.broadcasted_iota(jnp.int32, dims, 1 - pair_axis)


def stage_kernel(passages_ref, gain_ref, near_ref, far_ref, gain_out_ref, held, sems_in, sems_out):
    gain_out_ref[...] = gain_ref[...]
    rows, width = near_ref.shape
    half = width // 2
    piece = rows // chunks
    copies_in, copies_out, copies_near = [], [], []
    for k in range(chunks):
        part = pl.ds(k * piece, piece)
        far = passages_ref.at[part, pl.ds(width, width)]
        near = passages_ref.at[part, pl.ds(0, width)]
        copies_in.append(pltpu.make_async_copy(far, held.at[part], sems_in.at[k]))
        copies_near.append(pltpu.make_async_copy(near, near_ref.at[part], sems_in.at[chunks + k]))
        for j in range(2):
            there = far_ref.at[pl.ds(j * rows + k * piece, piece)]
            here = held.at[part, pl.ds(j * half, half)]
            copies_out.append(pltpu.make_async_copy(here, there, sems_out.at[2 * k + j]))
    for copy in copies_in + copies_near:
        copy.start()
    for k in range(chunks):
        copies_in[k].wait()
        copies_out[2 * k].start()
        copies_out[2 * k + 1].start()
    for copy in copies_near + copies_out:
        copy.wait()


def mix(base, first, query_ref, gain_ref, raw_ref, lines, out_ref, before_ref):
    queries = query_ref.shape[0]
    pairs = raw_ref.shape[0]
    chunk = out_ref.shape[1] // 2
    cols = jnp.transpose(jnp.concatenate([lines, jnp.zeros((120, pairs), f32)], axis=0))
    cos, inverse, query_inverse = cols[:, 2:3], cols[:, 3:4], cols[:, 5:6]
    own = belongs((queries, pairs), 1)
    by_weight = split(jnp.where(own, lines[0:1, :], 0.0))
    by_mark = split(jnp.where(own, lines[1:2, :], 0.0))
    plain = jnp.concatenate([*by_weight, *by_mark], axis=0)
    repeat = jnp.where(belongs((pairs, queries), 0), 1.0, 0.0).astype(bf16)
    for k in range(2):
        part = slice(k * chunk, (k + 1) * chunk)
        there = pl.ds(pl.multiple_of(base + k * chunk, 128), chunk)
        here = pl.ds(pl.multiple_of(first + k * chunk, 128), chunk)
        row = (raw_ref[:, here].astype(f32) * gain_ref[:, there] * inverse).astype(bf16)
        plainly = dot(plain, row, nn_dims)
        row = row.astype(f32)
        query = dot(repeat, query_ref[:, there], nn_dims) * query_inverse
        turned = row * (query.astype(bf16).astype(f32) - cos * row)
        turned = dot(plain, turned.astype(bf16), nn_dims)
        last = jnp.sum(turned[2 * queries :], axis=0, keepdims=True)
        sums = jnp.concatenate(
            [
                plainly[:queries] + plainly[queries : 2 * queries],
                plainly[2 * queries : 3 * queries] + plainly[3 * queries :],
                turned[:queries] + turned[queries : 2 * queries],
                jnp.broadcast_to(last, (8, chunk)),
            ],
            axis=0,
        )
        out_ref[:, part] = sums if before_ref is None else sums + before_ref[:, part]


def mine_kernel(core_ref, got_ref, gain_ref, raw_ref, rows_ref, out_ref, query_ref, wide):
    queries = query_ref.shape[0]
    tiles = wide.shape[0]
    for j in range(tiles):
        wide[j] = got_ref[:, j * 128 : (j + 1) * 128].astype(f32)
    query = [wide[j, pl.ds(k, queries, stride=8), :] for k in range(8) for j in range(tiles)]
    query_ref[...] = jnp.concatenate(query, axis=1).astype(bf16)
    base = core_ref[0] * out_ref.shape[1]
    mix(base, base, query_ref, gain_ref, raw_ref, rows_ref[...], out_ref, None)


def both_kernel(core_ref, query_ref, gain_ref, raw_ref, rows_ref, mine_ref, out_ref):
    base = core_ref[0] * out_ref.shape[1]
    mix(base, 0, query_ref, gain_ref, raw_ref, rows_ref[...], out_ref, mine_ref)


def score_kernel(
    core_ref, got_ref, gain_ref, near_ref, far_ref,
    raw_ref, cols_ref, rows_ref, sums_ref, theirs_ref, held, wide, sems,
):
    pairs, width = raw_ref.shape
    queries = pairs // 8
    rows = held.shape[1]
    chunk = width // chunks
    half = chunks // 2
    copies = []
    for k in range(half):
        copies.append(pltpu.make_async_copy(far_ref.at[pl.ds(k * rows, rows)], held.at[k], sems.at[k]))
        copies[-1].start()
    tiles = wide.shape[0]
    loaded = [got_ref[:, j * 128 : (j + 1) * 128].astype(f32) for j in range(tiles + 1)]
    squares = sum(x * x for x in loaded[:-1])
    squares = jnp.sum(squares, axis=1, keepdims=True).reshape(queries, 8, 1)
    squares = jnp.broadcast_to(jnp.sum(squares, axis=1, keepdims=True), (queries, 8, 1))
    query_inverse = 1.0 / jnp.sqrt(squares.reshape(pairs, 1))
    for j in range(tiles):
        wide[j] = loaded[j]
    lists = loaded[-1]
    inside = lists[:, 0:1] * 256.0 + lists[:, 1:2]
    mark = lists[:, 2:3] + lists[:, 3:4]
    lane = lax.broadcasted_iota(jnp.int32, (pairs, rows), 1).astype(f32)
    pick = jnp.where(inside == lane, 1.0, 0.0).astype(bf16)
    size = jnp.zeros((pairs, 128), f32)
    along = [jnp.zeros((8, 128), f32)] * queries
    for k in range(chunks):
        part = slice(k * chunk, (k + 1) * chunk)
        if k < half:
            passages = near_ref[:, part]
        else:
            copies[k - half].wait()
            passages = held[k - half]
        raw = dot(pick, passages, nn_dims)
        raw_ref[:, part] = raw.astype(bf16)
        lifted = raw * gain_ref[:, part]
        for j in range(chunk // 128):
            tile = slice(j * 128, (j + 1) * 128)
            size = size + lifted[:, tile] * lifted[:, tile]
            eighth, place = divmod(k * chunk // 128 + j, tiles)
            for i in range(queries):
                row = wide[place, i * 8 + eighth : i * 8 + eighth + 1, :]
                along[i] = along[i] + lifted[i * 8 : i * 8 + 8, tile] * row
    there = theirs_ref.shape[1]
    theirs_ref[...] = raw_ref[:, pl.ds(pl.multiple_of((1 - core_ref[0]) * there, 128), there)]
    inverse = 1.0 / jnp.sqrt(jnp.sum(size, axis=1, keepdims=True))
    along = jnp.concatenate(along, axis=0)
    cos = jnp.sum(along, axis=1, keepdims=True) * inverse * query_inverse
    weight = jnp.where(mark > 0.0, jnp.exp(cos * score_scale), 0.0)
    lane = lax.broadcasted_iota(jnp.int32, (pairs, 128), 1)
    cols = jnp.zeros((pairs, 128), f32)
    for k, column in enumerate((weight, mark, cos, inverse, inside, query_inverse)):
        cols = jnp.where(lane == k, column, cols)
    cols_ref[...] = cols
    flipped = jnp.transpose(cols)[:8]
    rows_ref[...] = flipped
    sums_ref[...] = jnp.broadcast_to(flipped[None, :1], sums_ref.shape)


def partial_kernel(sums_ref, both_ref, out_ref, total_ref, laid):
    queries = sums_ref.shape[2] // 8
    width = both_ref.shape[1]
    total = jnp.sum(sums_ref[...][:, 0, :], axis=0, keepdims=True)
    total_ref[...] = total
    own = belongs((queries, total.shape[1]), 1)
    inverse = 1.0 / jnp.sum(jnp.where(own, total, 0.0), axis=1, keepdims=True)
    both = both_ref[...]
    partial = coef_scale * (both[:queries] * inverse - both[queries : 2 * queries])
    gain_part = jnp.sum(both[2 * queries : 3 * queries] * inverse, axis=0, keepdims=True)
    gain_part = coef_scale * (gain_part - both[3 * queries : 3 * queries + 1])
    tiles = laid.shape[0]
    for k in range(width // 128):
        row, tile = k // tiles, k % tiles
        part = slice(k * 128, (k + 1) * 128)
        laid[tile, pl.ds(row, queries, stride=8), :] = partial[:, part]
        laid[tile, pl.ds(4 + row, queries, stride=8), :] = jnp.broadcast_to(
            gain_part[:, part], (queries, 128)
        )
    for tile in range(tiles):
        out_ref[:, tile * 128 : (tile + 1) * 128] = laid[tile].astype(bf16)


def passage_kernel(total_ref, query_ref, gain_ref, raw_ref, cols_ref, rows_ref, out_ref, made, sems):
    queries, width = query_ref.shape
    rows, pairs = made.shape[0], raw_ref.shape[0]
    piece = width // pieces
    weight, mark = cols_ref[:, 0:1], cols_ref[:, 1:2]
    cos, inverse = cols_ref[:, 2:3], cols_ref[:, 3:4]
    square = (pairs, pairs)
    alike = (lax.broadcasted_iota(jnp.int32, square, 0) >> 3) == (
        lax.broadcasted_iota(jnp.int32, square, 1) >> 3
    )
    total = jnp.sum(jnp.where(alike, total_ref[...], 0.0), axis=1, keepdims=True)
    scale = coef_scale * (weight / total - mark) * inverse
    inside = rows_ref[4:5, :]
    spread = lax.broadcasted_iota(jnp.int32, (rows, pairs), 0).astype(f32) == inside
    spread = jnp.where(spread, 1.0, 0.0).astype(bf16)
    spread = jnp.concatenate([spread, spread], axis=1)
    repeat = jnp.where(belongs((pairs, queries), 0), 1.0, 0.0).astype(bf16)
    copies = []
    for k in range(pieces):
        part = slice(k * piece, (k + 1) * piece)
        gain = gain_ref[:, part]
        row = (raw_ref[:, part].astype(f32) * gain * inverse).astype(bf16).astype(f32)
        query = dot(repeat, query_ref[:, part], nn_dims) * cols_ref[:, 5:6]
        term = (query.astype(bf16).astype(f32) - cos * row) * scale * gain
        made[:, part] = dot(spread, jnp.concatenate(split(term), axis=0), nn_dims)
        part = pl.ds(k * piece, piece)
        copies.append(pltpu.make_async_copy(made.at[:, part], out_ref.at[:, part], sems.at[k]))
        copies[-1].start()
    for copy in copies:
        copy.wait()


def final_kernel(got_ref, queries_ref, gain_ref, d_queries_ref, d_gain_ref):
    count = got_ref.shape[0]
    got = got_ref[...].astype(f32)
    middle = 1 + count // 2
    halves = [jnp.sum(got[1:middle], axis=0), got[0] + jnp.sum(got[middle:], axis=0)]
    query = queries_ref[...].astype(f32)
    norm = jnp.sqrt(jnp.sum(query * query, axis=1, keepdims=True))
    unit = query / norm
    d_unit = jnp.concatenate([half[k : k + 1] for half in halves for k in range(4)], axis=1)
    d_queries_ref[...] = (d_unit - unit * jnp.sum(unit * d_unit, axis=1, keepdims=True)) / norm
    d_gain = jnp.concatenate([half[k : k + 1] for half in halves for k in range(4, 8)], axis=1)
    d_gain_ref[...] = d_gain / gain_ref[...]


def shape(dims, dtype=f32):
    return jax.ShapeDtypeStruct(dims, dtype)


def exchange(x):
    order = member_order(lax.axis_size("hash"))
    return lax.all_to_all(
        x, "hash", split_axis=0, concat_axis=0, axis_index_groups=[order], tiled=True
    )


def local(passages, queries, gain, candidates, teacher):
    count = lax.axis_size("hash")
    rows, width = passages.shape
    listed = candidates.shape[1]
    gain = gain.reshape(1, width)

    packed = pl.pallas_call(
        functools.partial(pack_kernel, rows),
        out_shape=shape((count, 8, width // 8 + listed), bf16),
        compiler_params=params(60),
        name="pack",
    )(queries, candidates, teacher)
    got = exchange(packed).reshape(count * 8, width // 8 + listed)

    pairs = count * 8
    near, far, gain_near = pl.pallas_call(
        stage_kernel,
        in_specs=[outside(), whole()],
        out_specs=[whole(), outside(), whole()],
        out_shape=[
            shape((rows, width // 2), bf16),
            shape((20 * rows, width // 4), bf16),
            shape((1, width)),
        ],
        scratch_shapes=[
            pltpu.VMEM((rows, width // 2), bf16),
            pltpu.SemaphoreType.DMA((2 * chunks,)),
            pltpu.SemaphoreType.DMA((2 * chunks,)),
        ],
        compiler_params=params(48),
        name="stage",
        cost_estimate=pl.CostEstimate(
            flops=0, bytes_accessed=4 * rows * width, transcendentals=0
        ),
    )(passages, gain)
    half = width // 2
    core = (lax.axis_index("hash") % 2).astype(jnp.int32).reshape(1)
    raw, cols, lines, sums, theirs = pl.pallas_call(
        score_kernel,
        in_specs=[pl.BlockSpec(memory_space=pltpu.SMEM), whole(), whole(), whole(), outside()],
        out_shape=[
            shape((pairs, width), bf16),
            shape((pairs, 128)),
            shape((8, pairs)),
            shape((count, 1, pairs)),
            shape((pairs, half), bf16),
        ],
        scratch_shapes=[
            pltpu.VMEM((chunks // 2, rows, width // chunks), bf16),
            pltpu.VMEM((width // 1024, pairs, 128), f32),
            pltpu.SemaphoreType.DMA((chunks // 2,)),
        ],
        compiler_params=params(48),
        name="score",
    )(core, got, gain_near, near, far)

    got_sums = exchange(sums)
    swap = [(i, i ^ 1) for i in range(count)]
    sibling_raw = lax.ppermute(theirs, "hash", swap)
    sibling_lines = lax.ppermute(lines, "hash", swap)

    def mixed(kernel, out_shape, scratch, *operands):
        return pl.pallas_call(
            kernel,
            in_specs=[pl.BlockSpec(memory_space=pltpu.SMEM)] + [whole()] * len(operands),
            out_shape=out_shape,
            scratch_shapes=scratch,
            compiler_params=params(48),
            name="mix",
            cost_estimate=pl.CostEstimate(
                flops=8 * count * pairs * width, bytes_accessed=4 * pairs * width, transcendentals=0
            ),
        )(core, *operands)

    wide = [pltpu.VMEM((width // 1024, pairs, 128), f32)]
    added = shape((3 * count + 8, half))
    mine, query = mixed(
        mine_kernel, [added, shape((count, width), bf16)], wide, got, gain_near, raw, lines
    )
    both = mixed(both_kernel, added, [], query, gain_near, sibling_raw, sibling_lines, mine)

    partial, total = pl.pallas_call(
        partial_kernel,
        out_shape=[shape((pairs, half // 4), bf16), shape((1, pairs))],
        scratch_shapes=[pltpu.VMEM((half // 512, pairs, 128), f32)],
        compiler_params=params(48),
        name="partial",
    )(got_sums, both)
    got_partial = exchange(partial.reshape(count, 8, half // 4))

    d_passages = pl.pallas_call(
        passage_kernel,
        in_specs=[whole()] * 6,
        out_specs=outside(),
        out_shape=shape((rows, width)),
        scratch_shapes=[pltpu.VMEM((rows, width), f32), pltpu.SemaphoreType.DMA((pieces,))],
        compiler_params=params(48),
        name="d_passages",
        cost_estimate=pl.CostEstimate(
            flops=4 * pairs * rows * width, bytes_accessed=4 * rows * width, transcendentals=0
        ),
    )(total, query, gain_near, raw, cols, lines)

    d_queries, d_gain = pl.pallas_call(
        final_kernel,
        out_shape=[shape((1, width)), shape((1, width))],
        compiler_params=params(48),
        name="final",
    )(got_partial, queries, gain)
    return (d_passages, d_queries, d_gain.reshape(width))


def solution(mesh):
    in_specs = (
        P(("groups", "hash"), None),
        P(("groups", "hash"), None),
        P(),
        P(("groups", "hash"), None),
        P(("groups", "hash"), None),
    )
    out_specs = (P(("groups", "hash"), None), P(("groups", "hash"), None), P("groups"))
    return jax.shard_map(local, mesh=mesh, in_specs=in_specs, out_specs=out_specs, check_vma=False)
```

```python
import functools

import jax
import jax.numpy as jnp
from jax import lax
from jax.experimental import pallas as pl
from jax.experimental.pallas import tpu as pltpu
from jax.sharding import PartitionSpec as P

score_scale = 20.0
loss_scale = 8192.0
teacher_div = 2.0
coef_scale = loss_scale * score_scale
chunks = 4
pieces = 8
f32 = jnp.float32
bf16 = jnp.bfloat16
vmem = pltpu.VMEM
nn_dims = (((1,), (0,)), ((), ()))


def dot(a, b, dims):
    return lax.dot_general(a, b, dims, preferred_element_type=f32)


def split(x):
    high = x.astype(bf16)
    low = (x - high.astype(f32)).astype(bf16)
    return high, low


def member_order(count):
    first = count // 2 + 1
    return [first, *range(0, count, 2), *(i for i in range(1, count, 2) if i != first)]


def member_slot(owner, count):
    first = count // 2 + 1
    half = owner >> 1
    odd = 1 + count // 2 + half - jnp.where(owner > first, 1, 0)
    return jnp.where((owner & 1) == 0, 1 + half, jnp.where(owner == first, 0, odd))


def params(megabytes):
    return pltpu.CompilerParams(vmem_limit_bytes=megabytes * 1024 * 1024)


def whole():
    return pl.BlockSpec(memory_space=vmem)


def outside():
    return pl.BlockSpec(memory_space=pltpu.HBM)


def pack_kernel(rows, queries_ref, candidates_ref, teacher_ref, out_ref):
    ids = candidates_ref[...]
    listed = ids.shape[1]
    count = out_ref.shape[0]
    width = queries_ref.shape[1] // 8
    query = queries_ref[...].astype(f32)
    query = jnp.concatenate([query[:, k * width : (k + 1) * width] for k in range(8)], axis=0)
    owner = lax.div(ids, rows)
    inside = ids - owner * rows
    slot = member_slot(owner, count)
    marks = jnp.exp(teacher_ref[...].astype(f32) * (1.0 / teacher_div))
    marks = marks / jnp.sum(marks, axis=1, keepdims=True)
    high, low = split(marks)
    values = jnp.concatenate(
        [
            (inside >> 8).astype(f32),
            (inside & 255).astype(f32),
            high.astype(f32),
            low.astype(f32),
            jnp.zeros((listed - 4, listed), f32),
        ],
        axis=0,
    )
    square = (listed, listed)
    across = jnp.broadcast_to(slot.astype(f32), square)
    same = across == jnp.transpose(across)
    earlier = same & (lax.broadcasted_iota(jnp.int32, square, 0) < lax.broadcasted_iota(jnp.int32, square, 1))
    rank = jnp.sum(jnp.where(earlier, 1.0, 0.0), axis=0, keepdims=True)
    place = slot * 8 + rank.astype(jnp.int32)
    spread = jnp.where(place == lax.broadcasted_iota(jnp.int32, (count * 8, listed), 0), 1.0, 0.0)
    lists = dot(spread.astype(bf16), jnp.transpose(values).astype(bf16), nn_dims)
    out_ref[:, :, :width] = jnp.broadcast_to(query.astype(bf16)[None], (count, 8, width))
    out_ref[:, :, width:] = lists.astype(bf16).reshape(count, 8, listed)


def belongs(dims, pair_axis):
    pair = lax.broadcasted_iota(jnp.int32, dims, pair_axis) >> 3
    return pair == lax.broadcasted_iota(jnp.int32, dims, 1 - pair_axis)


def stage_kernel(passages_ref, gain_ref, near_ref, far_ref, gain_out_ref, held, sems_in, sems_out):
    gain_out_ref[...] = gain_ref[...]
    rows, width = near_ref.shape
    half = width // 2
    piece = rows // chunks
    copies_in, copies_out, copies_near = [], [], []
    for k in range(chunks):
        part = pl.ds(k * piece, piece)
        far = passages_ref.at[part, pl.ds(width, width)]
        near = passages_ref.at[part, pl.ds(0, width)]
        copies_in.append(pltpu.make_async_copy(far, held.at[part], sems_in.at[k]))
        copies_near.append(pltpu.make_async_copy(near, near_ref.at[part], sems_in.at[chunks + k]))
        for j in range(2):
            there = far_ref.at[pl.ds(j * rows + k * piece, piece)]
            here = held.at[part, pl.ds(j * half, half)]
            copies_out.append(pltpu.make_async_copy(here, there, sems_out.at[2 * k + j]))
    for copy in copies_in + copies_near:
        copy.start()
    for k in range(chunks):
        copies_in[k].wait()
        copies_out[2 * k].start()
        copies_out[2 * k + 1].start()
    for copy in copies_near + copies_out:
        copy.wait()


def mix(base, first, query_ref, gain_ref, raw_ref, lines, out_ref, before_ref):
    queries = query_ref.shape[0]
    pairs = raw_ref.shape[0]
    chunk = out_ref.shape[1] // 2
    cols = jnp.transpose(jnp.concatenate([lines, jnp.zeros((120, pairs), f32)], axis=0))
    cos, inverse, query_inverse = cols[:, 2:3], cols[:, 3:4], cols[:, 5:6]
    own = belongs((queries, pairs), 1)
    by_weight = split(jnp.where(own, lines[0:1, :], 0.0))
    by_mark = split(jnp.where(own, lines[1:2, :], 0.0))
    plain = jnp.concatenate([*by_weight, *by_mark], axis=0)
    repeat = jnp.where(belongs((pairs, queries), 0), 1.0, 0.0).astype(bf16)
    for k in range(2):
        part = slice(k * chunk, (k + 1) * chunk)
        there = pl.ds(pl.multiple_of(base + k * chunk, 128), chunk)
        here = pl.ds(pl.multiple_of(first + k * chunk, 128), chunk)
        row = (raw_ref[:, here].astype(f32) * gain_ref[:, there] * inverse).astype(bf16)
        plainly = dot(plain, row, nn_dims)
        row = row.astype(f32)
        query = dot(repeat, query_ref[:, there], nn_dims) * query_inverse
        turned = row * (query.astype(bf16).astype(f32) - cos * row)
        turned = dot(plain, turned.astype(bf16), nn_dims)
        last = jnp.sum(turned[2 * queries :], axis=0, keepdims=True)
        sums = jnp.concatenate(
            [
                plainly[:queries] + plainly[queries : 2 * queries],
                plainly[2 * queries : 3 * queries] + plainly[3 * queries :],
                turned[:queries] + turned[queries : 2 * queries],
                jnp.broadcast_to(last, (8, chunk)),
            ],
            axis=0,
        )
        out_ref[:, part] = sums if before_ref is None else sums + before_ref[:, part]


def mine_kernel(core_ref, got_ref, gain_ref, raw_ref, rows_ref, out_ref, query_ref, wide):
    queries = query_ref.shape[0]
    tiles = wide.shape[0]
    for j in range(tiles):
        wide[j, : 8 * queries, :] = got_ref[:, j * 128 : (j + 1) * 128].astype(f32)
    query = [wide[j, pl.ds(k, queries, stride=8), :] for k in range(8) for j in range(tiles)]
    query_ref[...] = jnp.concatenate(query, axis=1).astype(bf16)
    base = core_ref[0] * out_ref.shape[1]
    mix(base, base, query_ref, gain_ref, raw_ref, rows_ref[...], out_ref, None)


def both_kernel(core_ref, query_ref, gain_ref, raw_ref, rows_ref, mine_ref, out_ref):
    base = core_ref[0] * out_ref.shape[1]
    mix(base, 0, query_ref, gain_ref, raw_ref, rows_ref[...], out_ref, mine_ref)


def score_kernel(
    core_ref, got_ref, gain_ref, near_ref, far_ref,
    raw_ref, cols_ref, rows_ref, sums_ref, theirs_ref, held, wide, sems,
):
    pairs, width = raw_ref.shape
    queries = pairs // 8
    rows = held.shape[1]
    chunk = width // chunks
    half = chunks // 2
    copies = []
    for k in range(half):
        copies.append(pltpu.make_async_copy(far_ref.at[pl.ds(k * rows, rows)], held.at[k], sems.at[k]))
        copies[-1].start()
    tiles = wide.shape[0]
    loaded = [got_ref[:, j * 128 : (j + 1) * 128].astype(f32) for j in range(tiles + 1)]
    squares = sum(x * x for x in loaded[:-1])
    squares = jnp.sum(squares, axis=1, keepdims=True).reshape(queries, 8, 1)
    squares = jnp.broadcast_to(jnp.sum(squares, axis=1, keepdims=True), (queries, 8, 1))
    query_inverse = 1.0 / jnp.sqrt(squares.reshape(pairs, 1))
    for j in range(tiles):
        wide[j, :pairs, :] = loaded[j]
    lists = loaded[-1]
    inside = lists[:, 0:1] * 256.0 + lists[:, 1:2]
    mark = lists[:, 2:3] + lists[:, 3:4]
    lane = lax.broadcasted_iota(jnp.int32, (pairs, rows), 1).astype(f32)
    pick = jnp.where(inside == lane, 1.0, 0.0).astype(bf16)
    size = jnp.zeros((pairs, 128), f32)
    along = [jnp.zeros((8, 128), f32)] * queries
    for k in range(chunks):
        part = slice(k * chunk, (k + 1) * chunk)
        if k < half:
            passages = near_ref[:, part]
        else:
            copies[k - half].wait()
            passages = held[k - half]
        raw = dot(pick, passages, nn_dims)
        raw_ref[:, part] = raw.astype(bf16)
        lifted = raw * gain_ref[:, part]
        for j in range(chunk // 128):
            tile = slice(j * 128, (j + 1) * 128)
            size = size + lifted[:, tile] * lifted[:, tile]
            eighth, place = divmod(k * chunk // 128 + j, tiles)
            for i in range(queries):
                row = wide[place, i * 8 + eighth : i * 8 + eighth + 1, :]
                along[i] = along[i] + lifted[i * 8 : i * 8 + 8, tile] * row
    there = theirs_ref.shape[1]
    theirs_ref[...] = raw_ref[:, pl.ds(pl.multiple_of((1 - core_ref[0]) * there, 128), there)]
    inverse = 1.0 / jnp.sqrt(jnp.sum(size, axis=1, keepdims=True))
    along = jnp.concatenate(along, axis=0)
    cos = jnp.sum(along, axis=1, keepdims=True) * inverse * query_inverse
    weight = jnp.where(mark > 0.0, jnp.exp(cos * score_scale), 0.0)
    lane = lax.broadcasted_iota(jnp.int32, (pairs, 128), 1)
    cols = jnp.zeros((pairs, 128), f32)
    for k, column in enumerate((weight, mark, cos, inverse, inside, query_inverse)):
        cols = jnp.where(lane == k, column, cols)
    cols_ref[...] = cols
    flipped = jnp.transpose(cols)[:8]
    rows_ref[...] = flipped
    sums_ref[...] = jnp.broadcast_to(flipped[None, :1], sums_ref.shape)


def partial_kernel(sums_ref, both_ref, out_ref, total_ref, laid):
    queries = sums_ref.shape[2] // 8
    width = both_ref.shape[1]
    total = jnp.sum(sums_ref[...][:, 0, :], axis=0, keepdims=True)
    total_ref[...] = total
    own = belongs((queries, total.shape[1]), 1)
    inverse = 1.0 / jnp.sum(jnp.where(own, total, 0.0), axis=1, keepdims=True)
    both = both_ref[...]
    partial = coef_scale * (both[:queries] * inverse - both[queries : 2 * queries])
    gain_part = jnp.sum(both[2 * queries : 3 * queries] * inverse, axis=0, keepdims=True)
    gain_part = coef_scale * (gain_part - both[3 * queries : 3 * queries + 1])
    tiles = laid.shape[0]
    for k in range(width // 128):
        row, tile = k // tiles, k % tiles
        part = slice(k * 128, (k + 1) * 128)
        laid[tile, pl.ds(row, queries, stride=8), :] = partial[:, part]
        laid[tile, pl.ds(4 + row, queries, stride=8), :] = jnp.broadcast_to(
            gain_part[:, part], (queries, 128)
        )
    for tile in range(tiles):
        out_ref[:, tile * 128 : (tile + 1) * 128] = laid[tile, : 8 * queries, :].astype(bf16)


def passage_kernel(total_ref, query_ref, gain_ref, raw_ref, cols_ref, rows_ref, out_ref, made, sems):
    queries, width = query_ref.shape
    rows, pairs = made.shape[0], raw_ref.shape[0]
    piece = width // pieces
    weight, mark = cols_ref[:, 0:1], cols_ref[:, 1:2]
    cos, inverse = cols_ref[:, 2:3], cols_ref[:, 3:4]
    square = (pairs, pairs)
    alike = (lax.broadcasted_iota(jnp.int32, square, 0) >> 3) == (
        lax.broadcasted_iota(jnp.int32, square, 1) >> 3
    )
    total = jnp.sum(jnp.where(alike, total_ref[...], 0.0), axis=1, keepdims=True)
    scale = coef_scale * (weight / total - mark) * inverse
    inside = rows_ref[4:5, :]
    spread = lax.broadcasted_iota(jnp.int32, (rows, pairs), 0).astype(f32) == inside
    spread = jnp.where(spread, 1.0, 0.0).astype(bf16)
    spread = jnp.concatenate([spread, spread], axis=1)
    repeat = jnp.where(belongs((pairs, queries), 0), 1.0, 0.0).astype(bf16)
    copies = []
    for k in range(pieces):
        part = slice(k * piece, (k + 1) * piece)
        gain = gain_ref[:, part]
        row = (raw_ref[:, part].astype(f32) * gain * inverse).astype(bf16).astype(f32)
        query = dot(repeat, query_ref[:, part], nn_dims) * cols_ref[:, 5:6]
        term = (query.astype(bf16).astype(f32) - cos * row) * scale * gain
        made[:, part] = dot(spread, jnp.concatenate(split(term), axis=0), nn_dims)
        part = pl.ds(k * piece, piece)
        copies.append(pltpu.make_async_copy(made.at[:, part], out_ref.at[:, part], sems.at[k]))
        copies[-1].start()
    for copy in copies:
        copy.wait()


def final_kernel(got_ref, queries_ref, gain_ref, d_queries_ref, d_gain_ref):
    count = got_ref.shape[0]
    got = got_ref[...].astype(f32)
    middle = 1 + count // 2
    halves = [jnp.sum(got[1:middle], axis=0), got[0] + jnp.sum(got[middle:], axis=0)]
    query = queries_ref[...].astype(f32)
    norm = jnp.sqrt(jnp.sum(query * query, axis=1, keepdims=True))
    unit = query / norm
    d_unit = jnp.concatenate([half[k : k + 1] for half in halves for k in range(4)], axis=1)
    d_queries_ref[...] = (d_unit - unit * jnp.sum(unit * d_unit, axis=1, keepdims=True)) / norm
    d_gain = jnp.concatenate([half[k : k + 1] for half in halves for k in range(4, 8)], axis=1)
    d_gain_ref[...] = d_gain / gain_ref[...]


def shape(dims, dtype=f32):
    return jax.ShapeDtypeStruct(dims, dtype)


def exchange(x):
    order = member_order(lax.axis_size("hash"))
    return lax.all_to_all(
        x, "hash", split_axis=0, concat_axis=0, axis_index_groups=[order], tiled=True
    )


def local(passages, queries, gain, candidates, teacher):
    count = lax.axis_size("hash")
    rows, width = passages.shape
    listed = candidates.shape[1]
    gain = gain.reshape(1, width)

    packed = pl.pallas_call(
        functools.partial(pack_kernel, rows),
        out_shape=shape((count, 8, width // 8 + listed), bf16),
        compiler_params=params(60),
        name="pack",
    )(queries, candidates, teacher)
    got = exchange(packed).reshape(count * 8, width // 8 + listed)

    pairs = count * 8
    near, far, gain_near = pl.pallas_call(
        stage_kernel,
        in_specs=[outside(), whole()],
        out_specs=[whole(), outside(), whole()],
        out_shape=[
            shape((rows, width // 2), bf16),
            shape((20 * rows, width // 4), bf16),
            shape((1, width)),
        ],
        scratch_shapes=[
            pltpu.VMEM((rows, width // 2), bf16),
            pltpu.SemaphoreType.DMA((2 * chunks,)),
            pltpu.SemaphoreType.DMA((2 * chunks,)),
        ],
        compiler_params=params(48),
        name="stage",
        cost_estimate=pl.CostEstimate(
            flops=0, bytes_accessed=4 * rows * width, transcendentals=0
        ),
    )(passages, gain)
    half = width // 2
    core = (lax.axis_index("hash") % 2).astype(jnp.int32).reshape(1)
    raw, cols, lines, sums, theirs = pl.pallas_call(
        score_kernel,
        in_specs=[pl.BlockSpec(memory_space=pltpu.SMEM), whole(), whole(), whole(), outside()],
        out_shape=[
            shape((pairs, width), bf16),
            shape((pairs, 128)),
            shape((8, pairs)),
            shape((count, 1, pairs)),
            shape((pairs, half), bf16),
        ],
        scratch_shapes=[
            pltpu.VMEM((chunks // 2, rows, width // chunks), bf16),
            pltpu.VMEM((width // 1024, pairs + 8, 128), f32),
            pltpu.SemaphoreType.DMA((chunks // 2,)),
        ],
        compiler_params=params(48),
        name="score",
    )(core, got, gain_near, near, far)

    got_sums = exchange(sums)
    swap = [(i, i ^ 1) for i in range(count)]
    sibling_raw = lax.ppermute(theirs, "hash", swap)
    sibling_lines = lax.ppermute(lines, "hash", swap)

    def mixed(kernel, out_shape, scratch, *operands):
        return pl.pallas_call(
            kernel,
            in_specs=[pl.BlockSpec(memory_space=pltpu.SMEM)] + [whole()] * len(operands),
            out_shape=out_shape,
            scratch_shapes=scratch,
            compiler_params=params(48),
            name="mix",
            cost_estimate=pl.CostEstimate(
                flops=8 * count * pairs * width, bytes_accessed=4 * pairs * width, transcendentals=0
            ),
        )(core, *operands)

    wide = [pltpu.VMEM((width // 1024, pairs + 8, 128), f32)]
    added = shape((3 * count + 8, half))
    mine, query = mixed(
        mine_kernel, [added, shape((count, width), bf16)], wide, got, gain_near, raw, lines
    )
    both = mixed(both_kernel, added, [], query, gain_near, sibling_raw, sibling_lines, mine)

    partial, total = pl.pallas_call(
        partial_kernel,
        out_shape=[shape((pairs, half // 4), bf16), shape((1, pairs))],
        scratch_shapes=[pltpu.VMEM((half // 512, pairs + 8, 128), f32)],
        compiler_params=params(48),
        name="partial",
    )(got_sums, both)
    got_partial = exchange(partial.reshape(count, 8, half // 4))

    d_passages = pl.pallas_call(
        passage_kernel,
        in_specs=[whole()] * 6,
        out_specs=outside(),
        out_shape=shape((rows, width)),
        scratch_shapes=[pltpu.VMEM((rows, width), f32), pltpu.SemaphoreType.DMA((pieces,))],
        compiler_params=params(48),
        name="d_passages",
        cost_estimate=pl.CostEstimate(
            flops=4 * pairs * rows * width, bytes_accessed=4 * rows * width, transcendentals=0
        ),
    )(total, query, gain_near, raw, cols, lines)

    d_queries, d_gain = pl.pallas_call(
        final_kernel,
        out_shape=[shape((1, width)), shape((1, width))],
        compiler_params=params(48),
        name="final",
    )(got_partial, queries, gain)
    return (d_passages, d_queries, d_gain.reshape(width))


def solution(mesh):
    in_specs = (
        P(("groups", "hash"), None),
        P(("groups", "hash"), None),
        P(),
        P(("groups", "hash"), None),
        P(("groups", "hash"), None),
    )
    out_specs = (P(("groups", "hash"), None), P(("groups", "hash"), None), P("groups"))
    return jax.shard_map(local, mesh=mesh, in_specs=in_specs, out_specs=out_specs, check_vma=False)
```

```python
import functools

import jax
import jax.numpy as jnp
from jax import lax
from jax.experimental import pallas as pl
from jax.experimental.pallas import tpu as pltpu
from jax.sharding import PartitionSpec as P

score_scale = 20.0
loss_scale = 8192.0
teacher_div = 2.0
coef_scale = loss_scale * score_scale
chunks = 4
pieces = 8
f32 = jnp.float32
bf16 = jnp.bfloat16
vmem = pltpu.VMEM
nn_dims = (((1,), (0,)), ((), ()))


def dot(a, b, dims):
    return lax.dot_general(a, b, dims, preferred_element_type=f32)


def split(x):
    high = x.astype(bf16)
    low = (x - high.astype(f32)).astype(bf16)
    return high, low


def member_order(count):
    first = count // 2 + 1
    return [first, *range(0, count, 2), *(i for i in range(1, count, 2) if i != first)]


def member_slot(owner, count):
    first = count // 2 + 1
    half = owner >> 1
    odd = 1 + count // 2 + half - jnp.where(owner > first, 1, 0)
    return jnp.where((owner & 1) == 0, 1 + half, jnp.where(owner == first, 0, odd))


def params(megabytes):
    return pltpu.CompilerParams(vmem_limit_bytes=megabytes * 1024 * 1024)


def whole():
    return pl.BlockSpec(memory_space=vmem)


def outside():
    return pl.BlockSpec(memory_space=pltpu.HBM)


def pack_kernel(rows, queries_ref, candidates_ref, teacher_ref, out_ref):
    ids = candidates_ref[...]
    listed = ids.shape[1]
    count = out_ref.shape[0]
    width = queries_ref.shape[1] // 8
    query = queries_ref[...].astype(f32)
    query = jnp.concatenate([query[:, k * width : (k + 1) * width] for k in range(8)], axis=0)
    owner = lax.div(ids, rows)
    inside = ids - owner * rows
    slot = member_slot(owner, count)
    marks = jnp.exp(teacher_ref[...].astype(f32) * (1.0 / teacher_div))
    marks = marks / jnp.sum(marks, axis=1, keepdims=True)
    high, low = split(marks)
    values = jnp.concatenate(
        [
            (inside >> 8).astype(f32),
            (inside & 255).astype(f32),
            high.astype(f32),
            low.astype(f32),
            jnp.zeros((listed - 4, listed), f32),
        ],
        axis=0,
    )
    square = (listed, listed)
    across = jnp.broadcast_to(slot.astype(f32), square)
    same = across == jnp.transpose(across)
    earlier = same & (lax.broadcasted_iota(jnp.int32, square, 0) < lax.broadcasted_iota(jnp.int32, square, 1))
    rank = jnp.sum(jnp.where(earlier, 1.0, 0.0), axis=0, keepdims=True)
    place = slot * 8 + rank.astype(jnp.int32)
    spread = jnp.where(place == lax.broadcasted_iota(jnp.int32, (count * 8, listed), 0), 1.0, 0.0)
    lists = dot(spread.astype(bf16), jnp.transpose(values).astype(bf16), nn_dims)
    out_ref[:, :, :width] = jnp.broadcast_to(query.astype(bf16)[None], (count, 8, width))
    out_ref[:, :, width:] = lists.astype(bf16).reshape(count, 8, listed)


def belongs(dims, pair_axis):
    pair = lax.broadcasted_iota(jnp.int32, dims, pair_axis) >> 3
    return pair == lax.broadcasted_iota(jnp.int32, dims, 1 - pair_axis)


def stage_kernel(passages_ref, gain_ref, near_ref, far_ref, gain_out_ref, held, sems_in, sems_out):
    gain_out_ref[...] = gain_ref[...]
    rows, width = near_ref.shape
    rest = held.shape[1]
    half = rest // 2
    piece = rows // chunks
    copies_in, copies_out, copies_near = [], [], []
    for k in range(chunks):
        part = pl.ds(k * piece, piece)
        far = passages_ref.at[part, pl.ds(width, rest)]
        near = passages_ref.at[part, pl.ds(0, width)]
        copies_in.append(pltpu.make_async_copy(far, held.at[part], sems_in.at[k]))
        copies_near.append(pltpu.make_async_copy(near, near_ref.at[part], sems_in.at[chunks + k]))
        for j in range(2):
            there = far_ref.at[pl.ds(j * rows + k * piece, piece)]
            here = held.at[part, pl.ds(j * half, half)]
            copies_out.append(pltpu.make_async_copy(here, there, sems_out.at[2 * k + j]))
    for copy in copies_in + copies_near:
        copy.start()
    for k in range(chunks):
        copies_in[k].wait()
        copies_out[2 * k].start()
        copies_out[2 * k + 1].start()
    for copy in copies_near + copies_out:
        copy.wait()


def mix(base, first, query_ref, gain_ref, raw_ref, lines, out_ref, before_ref):
    queries = query_ref.shape[0]
    pairs = raw_ref.shape[0]
    chunk = out_ref.shape[1] // 2
    cols = jnp.transpose(jnp.concatenate([lines, jnp.zeros((120, pairs), f32)], axis=0))
    cos, inverse, query_inverse = cols[:, 2:3], cols[:, 3:4], cols[:, 5:6]
    own = belongs((queries, pairs), 1)
    by_weight = split(jnp.where(own, lines[0:1, :], 0.0))
    by_mark = split(jnp.where(own, lines[1:2, :], 0.0))
    plain = jnp.concatenate([*by_weight, *by_mark], axis=0)
    repeat = jnp.where(belongs((pairs, queries), 0), 1.0, 0.0).astype(bf16)
    for k in range(2):
        part = slice(k * chunk, (k + 1) * chunk)
        there = pl.ds(pl.multiple_of(base + k * chunk, 128), chunk)
        here = pl.ds(pl.multiple_of(first + k * chunk, 128), chunk)
        row = (raw_ref[:, here].astype(f32) * gain_ref[:, there] * inverse).astype(bf16)
        plainly = dot(plain, row, nn_dims)
        row = row.astype(f32)
        query = dot(repeat, query_ref[:, there], nn_dims) * query_inverse
        turned = row * (query.astype(bf16).astype(f32) - cos * row)
        turned = dot(plain, turned.astype(bf16), nn_dims)
        last = jnp.sum(turned[2 * queries :], axis=0, keepdims=True)
        sums = jnp.concatenate(
            [
                plainly[:queries] + plainly[queries : 2 * queries],
                plainly[2 * queries : 3 * queries] + plainly[3 * queries :],
                turned[:queries] + turned[queries : 2 * queries],
                jnp.broadcast_to(last, (8, chunk)),
            ],
            axis=0,
        )
        out_ref[:, part] = sums if before_ref is None else sums + before_ref[:, part]


def mine_kernel(core_ref, got_ref, gain_ref, raw_ref, rows_ref, out_ref, query_ref, wide):
    queries = query_ref.shape[0]
    tiles = wide.shape[0]
    for j in range(tiles):
        wide[j, : 8 * queries, :] = got_ref[:, j * 128 : (j + 1) * 128].astype(f32)
    query = [wide[j, pl.ds(k, queries, stride=8), :] for k in range(8) for j in range(tiles)]
    query_ref[...] = jnp.concatenate(query, axis=1).astype(bf16)
    base = core_ref[0] * out_ref.shape[1]
    mix(base, base, query_ref, gain_ref, raw_ref, rows_ref[...], out_ref, None)


def both_kernel(core_ref, query_ref, gain_ref, raw_ref, rows_ref, mine_ref, out_ref):
    base = core_ref[0] * out_ref.shape[1]
    mix(base, 0, query_ref, gain_ref, raw_ref, rows_ref[...], out_ref, mine_ref)


def score_kernel(
    core_ref, got_ref, gain_ref, near_ref, far_ref,
    raw_ref, cols_ref, rows_ref, sums_ref, theirs_ref, held, wide, sems,
):
    pairs, width = raw_ref.shape
    queries = pairs // 8
    rows = held.shape[1]
    chunk = width // chunks
    half = chunks // 2
    copies = []
    for k in range(half):
        copies.append(pltpu.make_async_copy(far_ref.at[pl.ds(k * rows, rows)], held.at[k], sems.at[k]))
        copies[-1].start()
    tiles = wide.shape[0]
    loaded = [got_ref[:, j * 128 : (j + 1) * 128].astype(f32) for j in range(tiles + 1)]
    squares = sum(x * x for x in loaded[:-1])
    squares = jnp.sum(squares, axis=1, keepdims=True).reshape(queries, 8, 1)
    squares = jnp.broadcast_to(jnp.sum(squares, axis=1, keepdims=True), (queries, 8, 1))
    query_inverse = 1.0 / jnp.sqrt(squares.reshape(pairs, 1))
    for j in range(tiles):
        wide[j, :pairs, :] = loaded[j]
    lists = loaded[-1]
    inside = lists[:, 0:1] * 256.0 + lists[:, 1:2]
    mark = lists[:, 2:3] + lists[:, 3:4]
    lane = lax.broadcasted_iota(jnp.int32, (pairs, rows), 1).astype(f32)
    pick = jnp.where(inside == lane, 1.0, 0.0).astype(bf16)
    size = jnp.zeros((pairs, 128), f32)
    along = [jnp.zeros((8, 128), f32)] * queries
    close, chunk = near_ref.shape[1] // 2, held.shape[2]
    ends = [0, close, 2 * close, 2 * close + chunk, width]
    for k in range(chunks):
        part = slice(ends[k], ends[k + 1])
        if k < half:
            passages = near_ref[:, part]
        else:
            copies[k - half].wait()
            passages = held[k - half]
        raw = dot(pick, passages, nn_dims)
        raw_ref[:, part] = raw.astype(bf16)
        lifted = raw * gain_ref[:, part]
        for j in range((ends[k + 1] - ends[k]) // 128):
            tile = slice(j * 128, (j + 1) * 128)
            size = size + lifted[:, tile] * lifted[:, tile]
            eighth, place = divmod(ends[k] // 128 + j, tiles)
            for i in range(queries):
                row = wide[place, i * 8 + eighth : i * 8 + eighth + 1, :]
                along[i] = along[i] + lifted[i * 8 : i * 8 + 8, tile] * row
    there = theirs_ref.shape[1]
    theirs_ref[...] = raw_ref[:, pl.ds(pl.multiple_of((1 - core_ref[0]) * there, 128), there)]
    inverse = 1.0 / jnp.sqrt(jnp.sum(size, axis=1, keepdims=True))
    along = jnp.concatenate(along, axis=0)
    cos = jnp.sum(along, axis=1, keepdims=True) * inverse * query_inverse
    weight = jnp.where(mark > 0.0, jnp.exp(cos * score_scale), 0.0)
    lane = lax.broadcasted_iota(jnp.int32, (pairs, 128), 1)
    cols = jnp.zeros((pairs, 128), f32)
    for k, column in enumerate((weight, mark, cos, inverse, inside, query_inverse)):
        cols = jnp.where(lane == k, column, cols)
    cols_ref[...] = cols
    flipped = jnp.transpose(cols)[:8]
    rows_ref[...] = flipped
    sums_ref[...] = jnp.broadcast_to(flipped[None, :1], sums_ref.shape)


def partial_kernel(sums_ref, both_ref, out_ref, total_ref, laid):
    queries = sums_ref.shape[2] // 8
    width = both_ref.shape[1]
    total = jnp.sum(sums_ref[...][:, 0, :], axis=0, keepdims=True)
    total_ref[...] = total
    own = belongs((queries, total.shape[1]), 1)
    inverse = 1.0 / jnp.sum(jnp.where(own, total, 0.0), axis=1, keepdims=True)
    both = both_ref[...]
    partial = coef_scale * (both[:queries] * inverse - both[queries : 2 * queries])
    gain_part = jnp.sum(both[2 * queries : 3 * queries] * inverse, axis=0, keepdims=True)
    gain_part = coef_scale * (gain_part - both[3 * queries : 3 * queries + 1])
    tiles = laid.shape[0]
    for k in range(width // 128):
        row, tile = k // tiles, k % tiles
        part = slice(k * 128, (k + 1) * 128)
        laid[tile, pl.ds(row, queries, stride=8), :] = partial[:, part]
        laid[tile, pl.ds(4 + row, queries, stride=8), :] = jnp.broadcast_to(
            gain_part[:, part], (queries, 128)
        )
    for tile in range(tiles):
        out_ref[:, tile * 128 : (tile + 1) * 128] = laid[tile, : 8 * queries, :].astype(bf16)


def passage_kernel(total_ref, query_ref, gain_ref, raw_ref, cols_ref, rows_ref, out_ref, made, sems):
    queries, width = query_ref.shape
    rows, pairs = made.shape[0], raw_ref.shape[0]
    piece = width // pieces
    weight, mark = cols_ref[:, 0:1], cols_ref[:, 1:2]
    cos, inverse = cols_ref[:, 2:3], cols_ref[:, 3:4]
    square = (pairs, pairs)
    alike = (lax.broadcasted_iota(jnp.int32, square, 0) >> 3) == (
        lax.broadcasted_iota(jnp.int32, square, 1) >> 3
    )
    total = jnp.sum(jnp.where(alike, total_ref[...], 0.0), axis=1, keepdims=True)
    scale = coef_scale * (weight / total - mark) * inverse
    inside = rows_ref[4:5, :]
    spread = lax.broadcasted_iota(jnp.int32, (rows, pairs), 0).astype(f32) == inside
    spread = jnp.where(spread, 1.0, 0.0).astype(bf16)
    spread = jnp.concatenate([spread, spread], axis=1)
    repeat = jnp.where(belongs((pairs, queries), 0), 1.0, 0.0).astype(bf16)
    copies = []
    for k in range(pieces):
        part = slice(k * piece, (k + 1) * piece)
        gain = gain_ref[:, part]
        row = (raw_ref[:, part].astype(f32) * gain * inverse).astype(bf16).astype(f32)
        query = dot(repeat, query_ref[:, part], nn_dims) * cols_ref[:, 5:6]
        term = (query.astype(bf16).astype(f32) - cos * row) * scale * gain
        made[:, part] = dot(spread, jnp.concatenate(split(term), axis=0), nn_dims)
        part = pl.ds(k * piece, piece)
        copies.append(pltpu.make_async_copy(made.at[:, part], out_ref.at[:, part], sems.at[k]))
        copies[-1].start()
    for copy in copies:
        copy.wait()


def final_kernel(got_ref, queries_ref, gain_ref, d_queries_ref, d_gain_ref):
    count = got_ref.shape[0]
    got = got_ref[...].astype(f32)
    middle = 1 + count // 2
    halves = [jnp.sum(got[1:middle], axis=0), got[0] + jnp.sum(got[middle:], axis=0)]
    query = queries_ref[...].astype(f32)
    norm = jnp.sqrt(jnp.sum(query * query, axis=1, keepdims=True))
    unit = query / norm
    d_unit = jnp.concatenate([half[k : k + 1] for half in halves for k in range(4)], axis=1)
    d_queries_ref[...] = (d_unit - unit * jnp.sum(unit * d_unit, axis=1, keepdims=True)) / norm
    d_gain = jnp.concatenate([half[k : k + 1] for half in halves for k in range(4, 8)], axis=1)
    d_gain_ref[...] = d_gain / gain_ref[...]


def shape(dims, dtype=f32):
    return jax.ShapeDtypeStruct(dims, dtype)


def exchange(x):
    order = member_order(lax.axis_size("hash"))
    return lax.all_to_all(
        x, "hash", split_axis=0, concat_axis=0, axis_index_groups=[order], tiled=True
    )


def local(passages, queries, gain, candidates, teacher):
    count = lax.axis_size("hash")
    rows, width = passages.shape
    listed = candidates.shape[1]
    gain = gain.reshape(1, width)

    packed = pl.pallas_call(
        functools.partial(pack_kernel, rows),
        out_shape=shape((count, 8, width // 8 + listed), bf16),
        compiler_params=params(60),
        name="pack",
    )(queries, candidates, teacher)
    got = exchange(packed).reshape(count * 8, width // 8 + listed)

    pairs = count * 8
    near, far, gain_near = pl.pallas_call(
        stage_kernel,
        in_specs=[outside(), whole()],
        out_specs=[whole(), outside(), whole()],
        out_shape=[
            shape((rows, 9 * width // 16), bf16),
            shape((24 * rows, 7 * width // 32), bf16),
            shape((1, width)),
        ],
        scratch_shapes=[
            pltpu.VMEM((rows, 7 * width // 16), bf16),
            pltpu.SemaphoreType.DMA((2 * chunks,)),
            pltpu.SemaphoreType.DMA((2 * chunks,)),
        ],
        compiler_params=params(48),
        name="stage",
        cost_estimate=pl.CostEstimate(
            flops=0, bytes_accessed=4 * rows * width, transcendentals=0
        ),
    )(passages, gain)
    half = width // 2
    core = (lax.axis_index("hash") % 2).astype(jnp.int32).reshape(1)
    raw, cols, lines, sums, theirs = pl.pallas_call(
        score_kernel,
        in_specs=[pl.BlockSpec(memory_space=pltpu.SMEM), whole(), whole(), whole(), outside()],
        out_shape=[
            shape((pairs, width), bf16),
            shape((pairs, 128)),
            shape((8, pairs)),
            shape((count, 1, pairs)),
            shape((pairs, half), bf16),
        ],
        scratch_shapes=[
            pltpu.VMEM((chunks // 2, rows, 7 * width // 32), bf16),
            pltpu.VMEM((width // 1024, pairs + 8, 128), f32),
            pltpu.SemaphoreType.DMA((chunks // 2,)),
        ],
        compiler_params=params(48),
        name="score",
    )(core, got, gain_near, near, far)

    got_sums = exchange(sums)
    swap = [(i, i ^ 1) for i in range(count)]
    sibling_raw = lax.ppermute(theirs, "hash", swap)
    sibling_lines = lax.ppermute(lines, "hash", swap)

    def mixed(kernel, out_shape, scratch, *operands):
        return pl.pallas_call(
            kernel,
            in_specs=[pl.BlockSpec(memory_space=pltpu.SMEM)] + [whole()] * len(operands),
            out_shape=out_shape,
            scratch_shapes=scratch,
            compiler_params=params(48),
            name="mix",
            cost_estimate=pl.CostEstimate(
                flops=8 * count * pairs * width, bytes_accessed=4 * pairs * width, transcendentals=0
            ),
        )(core, *operands)

    wide = [pltpu.VMEM((width // 1024, pairs + 8, 128), f32)]
    added = shape((3 * count + 8, half))
    mine, query = mixed(
        mine_kernel, [added, shape((count, width), bf16)], wide, got, gain_near, raw, lines
    )
    both = mixed(both_kernel, added, [], query, gain_near, sibling_raw, sibling_lines, mine)

    partial, total = pl.pallas_call(
        partial_kernel,
        out_shape=[shape((pairs, half // 4), bf16), shape((1, pairs))],
        scratch_shapes=[pltpu.VMEM((half // 512, pairs + 8, 128), f32)],
        compiler_params=params(48),
        name="partial",
    )(got_sums, both)
    got_partial = exchange(partial.reshape(count, 8, half // 4))

    d_passages = pl.pallas_call(
        passage_kernel,
        in_specs=[whole()] * 6,
        out_specs=outside(),
        out_shape=shape((rows, width)),
        scratch_shapes=[pltpu.VMEM((rows, width), f32), pltpu.SemaphoreType.DMA((pieces,))],
        compiler_params=params(48),
        name="d_passages",
        cost_estimate=pl.CostEstimate(
            flops=4 * pairs * rows * width, bytes_accessed=4 * rows * width, transcendentals=0
        ),
    )(total, query, gain_near, raw, cols, lines)

    d_queries, d_gain = pl.pallas_call(
        final_kernel,
        out_shape=[shape((1, width)), shape((1, width))],
        compiler_params=params(48),
        name="final",
    )(got_partial, queries, gain)
    return (d_passages, d_queries, d_gain.reshape(width))


def solution(mesh):
    in_specs = (
        P(("groups", "hash"), None),
        P(("groups", "hash"), None),
        P(),
        P(("groups", "hash"), None),
        P(("groups", "hash"), None),
    )
    out_specs = (P(("groups", "hash"), None), P(("groups", "hash"), None), P("groups"))
    return jax.shard_map(local, mesh=mesh, in_specs=in_specs, out_specs=out_specs, check_vma=False)
```
